32 devices in a mesh: fsdp: 16 (over z, y, x), tp: 2 (over core).
Axes of the slice: x: 2, y: 2, z: 4, core: 2. Of those that a mesh axis runs over, the one named last changes fastest.
Arguments:
- tokens: bfloat16 [8192, 768], P('fsdp'), may hold values from -6 to 6
- cotangent: bfloat16 [8192, 768], P('fsdp'), may hold values from -6 to 6
- w_qkv: float32 [2, 768, 3, 768], P(None, 'fsdp', None, 'tp'), may hold values from -0.21875 to 0.21875
- w_out: float32 [2, 768, 768], P(None, 'tp', 'fsdp'), may hold values from -0.875 to 0.875
- w_up: float32 [2, 768, 3072], P(None, 'fsdp', 'tp'), may hold values from -0.21875 to 0.21875
- w_down: float32 [2, 3072, 768], P(None, 'tp', 'fsdp'), may hold values from -0.109375 to 0.109375
- mom_qkv: float32 [2, 768, 3, 768], P(None, 'fsdp', None, 'tp'), may hold values from -384 to 384
- mom_out: float32 [2, 768, 768], P(None, 'tp', 'fsdp'), may hold values from -112 to 112
- mom_up: float32 [2, 768, 3072], P(None, 'fsdp', 'tp'), may hold values from -160 to 160
- mom_down: float32 [2, 3072, 768], P(None, 'tp', 'fsdp'), may hold values from -320 to 320
- vectors: float32 [2, 9984], replicated, may hold values from -1.2 to 1.4
- vec_first: float32 [2, 9984], replicated, may hold values from -80 to 80
- vec_second: float32 [2, 9984], replicated, may hold values from 409.6 to 3276.8
- lengths: int32 [16], replicated, may hold values from 1 to 1024, 8192 in all
Outputs:
- block_out: float32 [8192, 768], P('fsdp')
- input_grad: float32 [8192, 768], P('fsdp')
- grad_qkv: float32 [2, 768, 3, 768], P(None, 'fsdp', None, 'tp')
- grad_out: float32 [2, 768, 768], P(None, 'tp', 'fsdp')
- grad_up: float32 [2, 768, 3072], P(None, 'fsdp', 'tp')
- grad_down: float32 [2, 3072, 768], P(None, 'tp', 'fsdp')
- new_mom_qkv: float32 [2, 768, 3, 768], P(None, 'fsdp', None, 'tp')
- new_mom_out: float32 [2, 768, 768], P(None, 'tp', 'fsdp')
- new_mom_up: float32 [2, 768, 3072], P(None, 'fsdp', 'tp')
- new_mom_down: float32 [2, 3072, 768], P(None, 'tp', 'fsdp')
- new_qkv: float32 [2, 768, 3, 768], P(None, 'fsdp', None, 'tp')
- new_out: float32 [2, 768, 768], P(None, 'tp', 'fsdp')
- new_up: float32 [2, 768, 3072], P(None, 'fsdp', 'tp')
- new_down: float32 [2, 3072, 768], P(None, 'tp', 'fsdp')
- new_vec_first: float32 [2, 9984], replicated
- new_vec_second: float32 [2, 9984], replicated
- new_vectors: float32 [2, 9984], replicated
- grad_bias_up: float32 [2, 3072], replicated
The draws below stay inside these ranges and needn't reach their ends.
All inputs are finite; a program needn't handle non-finite values.
Results may differ from the reference program's by a relative error of at most 0.025.
Values may be sent and summed in bfloat16 or wider, within the bound.
No kernel may reach another device: no remote copies, remote signals or barrier semaphores. Data moves between devices by JAX's collectives and lax.ppermute only.
A program may use at most 320 MiB of HBM per device.

```python
import math
import jax
import jax.numpy as jnp
import numpy as np
from jax import lax

D = 768
HEADS = 12
HEAD = 64
ROT = 16
FF = 3072
LAYERS = 2
STEP = 10
MAXLEN = 1024
TOKENS = 8192
SEQS = 16
VEC = 9984


def draw_vectors(key, part):
    key = jax.random.fold_in(key, 11)
    noise = jnp.clip(jax.random.normal(key, (LAYERS, 9 * D + FF), jnp.float32), -4.0, 4.0)
    column = jnp.arange(9 * D + FF)
    is_gain = (column < D) | (column >= 2 * D) & (column < 3 * D)
    return jnp.where(is_gain[None, :], 1.0 + 0.1 * noise, 0.3 * noise)


def block_scale(key, extent, split, low, high):
    def one(dim, parts):
        steps = jax.random.uniform(jax.random.fold_in(jax.random.fold_in(key, 6), dim), (parts,), jnp.float32, low / len(split), high / len(split))
        return jnp.repeat(jnp.exp(steps), extent[dim] // parts).reshape((-1,) + (1,) * (len(extent) - dim - 1))

    level = one(*split[0])
    for cut in split[1:]:
        level = level * one(*cut)
    return level


def split_up(count, total, limit, lean):
    weights = [(1 << 20) // math.isqrt(grade ** lean) + 1 for grade in range(2, count + 1)]
    surplus, counts = total - limit - (count - 1), [1] * (count - 1)
    while surplus > 0:
        movable = [i for i in range(count - 1) if counts[i] < limit]
        mass, budget = sum([weights[i] for i in movable]), surplus
        for i in movable:
            extra = min(limit - counts[i], max(1, budget * weights[i] // mass), surplus)
            counts[i] = counts[i] + extra
            surplus = surplus - extra
    return np.array([limit] + counts)


def uneven(key, count, total, limit, slope):
    if count == 2:
        one = jax.random.randint(key, (), max(1, total - limit), min(limit, total - 1) + 1)
        return jnp.stack([one, total - one])
    sizes = jnp.asarray(split_up(count, total, limit, slope), jnp.int32)
    twos = (count - 1) // 2
    donor, taker = sizes[1:1 + 2 * twos:2], sizes[2:2 + 2 * twos:2]
    slack = jnp.minimum(donor - 1, limit - taker)
    shifted = jax.random.randint(jax.random.fold_in(key, 1), (twos,), 0, 1 << 20) % (slack + 1)
    sizes = sizes.at[1:1 + 2 * twos:2].set(donor - shifted).at[2:2 + 2 * twos:2].set(taker + shifted)
    return sizes[jax.random.permutation(jax.random.fold_in(key, 2), count)]


def scatter_about(key, dims, spread, bound, cuts=(), held_as=jnp.bfloat16):
    loudness = block_scale(key, dims, cuts, -0.22, 0.18) if cuts else 1.0
    drawn = jax.random.normal(key, dims, jnp.float32) * spread * loudness
    return jnp.minimum(jnp.maximum(drawn, -bound), bound).astype(held_as)


def setup_inputs(seed: int = 0) -> dict:
    keys = jax.random.split(jax.random.key(seed), 15)
    tokens = scatter_about(keys[0], (TOKENS, D), 1.0, 6.0, ((0, 16),))
    cotangent = scatter_about(keys[1], (TOKENS, D), 1.0, 6.0, ((0, 16),))
    w_qkv = scatter_about(keys[2], (LAYERS, D, 3, D), D ** -0.5, 0.21875, ((1, 16), (3, 2)), jnp.float32)
    w_out = scatter_about(keys[3], (LAYERS, D, D), (D // 16) ** -0.5, 0.875, ((1, 2), (2, 16)), jnp.float32)
    w_up = scatter_about(keys[4], (LAYERS, D, FF), D ** -0.5, 0.21875, ((1, 16), (2, 2)), jnp.float32)
    w_down = scatter_about(keys[5], (LAYERS, FF, D), FF ** -0.5, 0.109375, ((1, 2), (2, 16)), jnp.float32)
    mom_qkv = scatter_about(keys[6], (LAYERS, D, 3, D), (0.7 * TOKENS ** 0.5), 384.0, ((1, 16), (3, 2)), jnp.float32)
    mom_out = scatter_about(keys[7], (LAYERS, D, D), (0.2 * TOKENS ** 0.5), 112.0, ((1, 2), (2, 16)), jnp.float32)
    mom_up = scatter_about(keys[8], (LAYERS, D, FF), (0.3 * TOKENS ** 0.5), 160.0, ((1, 16), (2, 2)), jnp.float32)
    mom_down = scatter_about(keys[9], (LAYERS, FF, D), (0.6 * TOKENS ** 0.5), 320.0, ((1, 2), (2, 16)), jnp.float32)
    vectors = draw_vectors(jax.random.fold_in(keys[14], 71), 0)
    vec_first = scatter_about(keys[11], (LAYERS, VEC), (0.15 * TOKENS ** 0.5), 80.0, (), jnp.float32)
    vec_second = jnp.clip(jnp.exp(jax.random.uniform(keys[12], (LAYERS, VEC), jnp.float32, math.log(409.6), math.log(3276.8))), 409.6, 3276.8)
    lengths = uneven(keys[13], SEQS, TOKENS, MAXLEN, 2).astype(jnp.int32)
    return {"tokens": tokens, "cotangent": cotangent, "w_qkv": w_qkv, "w_out": w_out, "w_up": w_up, "w_down": w_down, "mom_qkv": mom_qkv, "mom_out": mom_out, "mom_up": mom_up, "mom_down": mom_down, "vectors": vectors, "vec_first": vec_first, "vec_second": vec_second, "lengths": lengths}


@jax.custom_vjp
def low(v):
    return lax.optimization_barrier(v.astype(jnp.bfloat16)).astype(jnp.float32)

@jax.custom_vjp
def low_back(v):
    return v

def low_keep(v):
    return (low(v), None)

def low_pass(kept, grad):
    return (grad,)

def back_keep(v):
    return (v, None)

def back_low(kept, grad):
    return (low(grad),)
low.defvjp(low_keep, low_pass)
low_back.defvjp(back_keep, back_low)
HIGHEST = lax.Precision.HIGHEST
MASKED = -1000000000.0
NS_A = 3.4445
NS_B = -4.775
NS_C = 2.0315
MOMENTUM = 0.95
RATE_MAT = 0.02
SHRINK = 0.99
RATE_VEC = 0.25
BETA_ONE = 0.9
BETA_TWO = 0.95
ADAM_EPS = 1e-08

def normalize(inputs, gain_vec, shift_vec):
    average = lax.optimization_barrier(jnp.mean(inputs, axis=-1, keepdims=True))
    centered = inputs - average
    variance = lax.optimization_barrier(jnp.mean(centered * centered, axis=-1, keepdims=True))
    return centered * lax.rsqrt(variance + 1e-05) * gain_vec + shift_vec

def rotate(entries, cosine, sine_rows):
    half_rot = ROT // 2
    front_half = entries[..., :half_rot]
    back_half = entries[..., half_rot:ROT]
    cos_rows = cosine[:, None, :]
    sin_rows = sine_rows[:, None, :]
    return jnp.concatenate([front_half * cos_rows - back_half * sin_rows, back_half * cos_rows + front_half * sin_rows, entries[..., ROT:]], axis=-1)

def angles(positions):
    freqs = jnp.exp(jnp.arange(ROT // 2, dtype=jnp.float32) * (-2.0 * math.log(10000.0) / ROT))
    phase = positions.astype(jnp.float32)[:, None] * freqs[None, :]
    return (jnp.cos(phase), jnp.sin(phase))

def sequence_starts(lengths, token_index):
    ends_at = jnp.cumsum(lengths).astype(jnp.int32)
    picked = jnp.where(ends_at[None, :] <= token_index[:, None], lengths[None, :], 0)
    return lax.optimization_barrier(jnp.sum(picked, axis=1)).astype(jnp.int32)

def lowered(array_in):
    return lax.optimization_barrier(array_in.astype(jnp.bfloat16))

def orthogonalize(matrix):
    is_tall = matrix.shape[0] > matrix.shape[1]
    working = matrix.T if is_tall else matrix
    norm_size = jnp.sqrt(jnp.sum(working * working)) + 1e-07
    current = lowered(working / norm_size)
    for sweep_index in range(5):
        gram_mat = lowered(jnp.dot(current, current.T, preferred_element_type=jnp.float32))
        square = jnp.dot(gram_mat, gram_mat, preferred_element_type=jnp.float32)
        mixer = lowered(NS_B * gram_mat.astype(jnp.float32) + NS_C * square)
        current = lowered(NS_A * current.astype(jnp.float32) + jnp.dot(mixer, current, preferred_element_type=jnp.float32))
    return current.T if is_tall else current

def attention(query_rows, key_rows, value_rows, token_index, starts):
    block_rows = math.gcd(TOKENS, 512)
    block_count = TOKENS // block_rows
    span = block_rows + MAXLEN
    key_pad = jnp.pad(key_rows, ((MAXLEN, 0), (0, 0), (0, 0)))
    value_pad = jnp.pad(value_rows, ((MAXLEN, 0), (0, 0), (0, 0)))

    def one_block(block_index):
        begin = block_index * block_rows
        query_part = lax.dynamic_slice_in_dim(query_rows, begin, block_rows, 0)
        key_part = lax.dynamic_slice_in_dim(key_pad, begin, span, 0)
        value_part = lax.dynamic_slice_in_dim(value_pad, begin, span, 0)
        query_index = lax.dynamic_slice_in_dim(token_index, begin, block_rows, 0)
        query_start = lax.dynamic_slice_in_dim(starts, begin, block_rows, 0)
        key_index = begin - MAXLEN + jnp.arange(span, dtype=jnp.int32)
        visible = (key_index[None, :] >= query_start[:, None]) & (key_index[None, :] <= query_index[:, None])
        score_rows = jnp.einsum('qhd,khd->hqk', query_part, key_part, precision=HIGHEST)
        score_rows = low_back(jnp.where(visible[None], score_rows, MASKED))
        prob_rows = low(jax.nn.softmax(score_rows, axis=-1))
        return jnp.einsum('hqk,khd->qhd', prob_rows, value_part, precision=HIGHEST)
    result = lax.map(jax.checkpoint(one_block), jnp.arange(block_count, dtype=jnp.int32))
    return result.reshape(TOKENS, HEADS, HEAD)

def reference(tokens, cotangent, w_qkv, w_out, w_up, w_down, mom_qkv, mom_out, mom_up, mom_down, vectors, vec_first, vec_second, lengths):
    token_index = jnp.arange(TOKENS, dtype=jnp.int32)
    starts = sequence_starts(lengths, token_index)
    cosine, sine_rows = angles(token_index - starts)
    scale_q = HEAD ** (-0.5)

    def forward_pass(hidden_x, qkv_all, out_all, up_all, down_all, vector_all):
        for layer_index in range(LAYERS):
            row_vec = vector_all[layer_index]
            normed = low(normalize(hidden_x, row_vec[0:D], row_vec[D:2 * D]))
            pre_qkv = jnp.dot(normed, low(qkv_all[layer_index]).reshape(D, 3 * D), precision=HIGHEST) + row_vec[6 * D:9 * D]
            pre_qkv = low_back(pre_qkv).reshape(TOKENS, 3, HEADS, HEAD)
            query_rows = low(rotate(pre_qkv[:, 0], cosine, sine_rows) * scale_q)
            key_rows = low(rotate(pre_qkv[:, 1], cosine, sine_rows))
            value_rows = low(pre_qkv[:, 2])
            attn_out = attention(query_rows, key_rows, value_rows, token_index, starts).reshape(TOKENS, D)
            attn_out = low(low_back(attn_out))
            normed_two = low(normalize(hidden_x, row_vec[2 * D:3 * D], row_vec[3 * D:4 * D]))
            hidden_pre = low_back(jnp.dot(normed_two, low(up_all[layer_index]), precision=HIGHEST) + row_vec[9 * D:])
            hidden_low = low(jax.nn.gelu(hidden_pre, approximate=False))
            branch = jnp.dot(attn_out, low(out_all[layer_index]), precision=HIGHEST) + jnp.dot(hidden_low, low(down_all[layer_index]), precision=HIGHEST)
            hidden_x = hidden_x + low_back(branch) + row_vec[4 * D:5 * D] + row_vec[5 * D:6 * D]
        return hidden_x
    block_out, pullback = jax.vjp(forward_pass, tokens.astype(jnp.float32), w_qkv, w_out, w_up, w_down, vectors)
    input_grad, grad_qkv, grad_out, grad_up, grad_down, grad_vectors = pullback(cotangent.astype(jnp.float32))
    shapes = ((D, 3 * D), (D, D), (D, FF), (FF, D))
    weights = (w_qkv, w_out, w_up, w_down)
    moments = (mom_qkv, mom_out, mom_up, mom_down)
    gradients = (grad_qkv, grad_out, grad_up, grad_down)
    new_moments = []
    new_weights = []
    for kind_index in range(4):
        rows_n, cols_n = shapes[kind_index]
        moment_list = []
        weight_list = []
        for layer_index in range(LAYERS):
            grad_matrix = gradients[kind_index][layer_index].reshape(rows_n, cols_n)
            moment_new = MOMENTUM * moments[kind_index][layer_index].reshape(rows_n, cols_n) + grad_matrix
            update = orthogonalize(moment_new).astype(jnp.float32)
            weight_new = weights[kind_index][layer_index].reshape(rows_n, cols_n) * SHRINK - RATE_MAT * math.sqrt(max(rows_n, cols_n)) * update
            moment_list.append(moment_new.reshape(weights[kind_index].shape[1:]))
            weight_list.append(weight_new.reshape(weights[kind_index].shape[1:]))
        new_moments.append(jnp.stack(moment_list))
        new_weights.append(jnp.stack(weight_list))
    first_new = BETA_ONE * vec_first + (1.0 - BETA_ONE) * grad_vectors
    second_new = BETA_TWO * vec_second + (1.0 - BETA_TWO) * grad_vectors * grad_vectors
    first_hat = first_new / (1.0 - BETA_ONE ** STEP)
    second_hat = second_new / (1.0 - BETA_TWO ** STEP)
    vectors_new = vectors - RATE_VEC * first_hat / (jnp.sqrt(second_hat) + ADAM_EPS)
    grad_bias_up = grad_vectors[:, 9 * D:]
    return (block_out, input_grad, grad_qkv, grad_out, grad_up, grad_down, new_moments[0], new_moments[1], new_moments[2], new_moments[3], new_weights[0], new_weights[1], new_weights[2], new_weights[3], first_new, second_new, vectors_new, grad_bias_up)
```

```python
import functools
import math

import jax
import jax.numpy as jnp
from jax import lax
from jax.experimental import pallas as pl
from jax.experimental.pallas import tpu as pltpu
from jax.sharding import PartitionSpec as P

D = 768
HEAD = 64
ROT = 16
FF = 3072
LAYERS = 2
SEQ_DEV = 64
STEP = 10
PAIR = 2 * HEAD
BLK = 256
KINDS = 4

MASKED = -1000000000.0
EPS_NORM = 1e-05
NS_A = 3.4445
NS_B = -4.775
NS_C = 2.0315
MOMENTUM = 0.95
RATE_MAT = 0.02
SHRINK = 0.99
RATE_VEC = 0.25
BETA_ONE = 0.9
BETA_TWO = 0.95
ADAM_EPS = 1e-08
VMEM_CAP = 56 * 1024 * 1024

bf16 = jnp.bfloat16
f32 = jnp.float32


def permute(x, pairs):
    return lax.ppermute(x, "fsdp", pairs)


def xor_pairs(count, by):
    return [(i, i ^ by) for i in range(count)]


def core_swap(x):
    count = lax.axis_size("tp")
    return lax.ppermute(x, "tp", [(i, i ^ 1) for i in range(count)])


def from_behind(x, by):
    devices = lax.axis_size("fsdp")
    return lax.ppermute(
        x, "fsdp", [(i, i + by) for i in range(devices) if 0 <= i + by < devices]
    )


def dims_of(count):
    if count == 16:
        return [(4, 4), (2, 2), (2, 1)]
    return [(2, 1 << s) for s in range(count.bit_length() - 2, -1, -1)]


def line_pairs(count, stride, moves):
    pairs = []
    for i in range(count):
        pos = (i // stride) % 4
        if pos in moves:
            pairs.append((i, i + (moves[pos] - pos) * stride))
    return pairs


def position(dim):
    size, stride = dim
    return (lax.axis_index("fsdp") // stride) % size


def gather_bit(block, axis, dim, count):
    other = permute(block, xor_pairs(count, dim[1]))
    first = position(dim) == 0
    return jnp.where(
        first,
        jnp.concatenate([block, other], axis),
        jnp.concatenate([other, block], axis),
    )


def gather_line(block, axis, dim, count):
    pos = position(dim)
    pairs = functools.partial(line_pairs, count, dim[1])
    left_one = permute(block, pairs({0: 1, 1: 2, 2: 3}))
    right_one = permute(block, pairs({3: 2, 2: 1, 1: 0}))
    left_two = permute(left_one, pairs({1: 2, 2: 3}))
    right_two = permute(right_one, pairs({2: 1, 1: 0}))
    far = permute(jnp.where(pos == 1, right_two, left_two), pairs({2: 3, 1: 0}))

    def pick(options):
        out = options[3]
        for k in (2, 1, 0):
            out = jnp.where(pos == k, options[k], out)
        return out

    return jnp.concatenate(
        [
            pick([block, left_one, left_two, far]),
            pick([right_one, block, left_one, left_two]),
            pick([right_two, right_one, block, left_one]),
            pick([far, right_two, right_one, block]),
        ],
        axis,
    )


def gather_rows(piece, order=None):
    count = lax.axis_size("fsdp")
    dims = dims_of(count)
    rows, cols = piece.shape
    block = piece.reshape((1,) * len(dims) + (rows, cols))
    order = range(len(dims)) if order is None or len(dims) != 3 else order
    for axis in order:
        step = gather_line if dims[axis][0] == 4 else gather_bit
        block = step(block, axis, dims[axis], count)
    return block.reshape(count * rows, cols)


def take(block, index, axis):
    return lax.dynamic_slice_in_dim(block, index, 1, axis)


def scatter_bit(block, axis, dim, count):
    pos = position(dim)
    other = permute(take(block, 1 - pos, axis).astype(bf16), xor_pairs(count, dim[1]))
    return take(block, pos, axis).astype(f32) + other.astype(f32)


def scatter_line(block, axis, dim, count):
    pos = position(dim)
    pairs = functools.partial(line_pairs, count, dim[1])
    right = [{0: 1}, {0: 1, 1: 2}, {0: 1, 1: 2, 2: 3}]
    left = [{3: 2}, {3: 2, 2: 1}, {3: 2, 2: 1, 1: 0}]
    from_left = from_right = None
    for step in range(3):
        up = take(block, jnp.minimum(pos + 3 - step, 3), axis).astype(f32)
        down = take(block, jnp.maximum(pos - 3 + step, 0), axis).astype(f32)
        if step:
            up = up + from_left.astype(f32)
            down = down + from_right.astype(f32)
        from_left = permute(up.astype(bf16), pairs(right[step]))
        from_right = permute(down.astype(bf16), pairs(left[step]))
    return take(block, pos, axis).astype(f32) + from_left.astype(f32) + from_right.astype(f32)


def scatter_rows(full, order=None):
    count = lax.axis_size("fsdp")
    dims = dims_of(count)
    cols = full.shape[1]
    rows = full.shape[0] // count
    block = full.reshape(tuple(d[0] for d in dims) + (rows, cols))
    order = range(len(dims)) if order is None or len(dims) != 3 else order
    order = list(order)
    for place, axis in enumerate(order):
        step = scatter_line if dims[axis][0] == 4 else scatter_bit
        block = step(block, axis, dims[axis], count)
        if place < len(order) - 1:
            block = block.astype(bf16)
    return block.reshape(rows, cols)


def gather_streams(piece):
    half = piece.shape[1] // 256 * 128
    return jnp.concatenate(
        [gather_rows(piece[:, :half], (0, 2, 1)), gather_rows(piece[:, half:], (2, 1, 0))],
        axis=1,
    )


def scatter_streams(full):
    half = full.shape[1] // 256 * 128
    return jnp.concatenate(
        [scatter_rows(full[:, :half], (1, 2, 0)), scatter_rows(full[:, half:], (0, 1, 2))],
        axis=1,
    )


def sum_everywhere(x):
    count = lax.axis_size("fsdp")
    x = x + core_swap(x)
    step = 1
    while step < count:
        x = x + permute(x, xor_pairs(count, step))
        step *= 2
    return x


def normalize(inputs):
    average = jnp.mean(inputs, axis=-1, keepdims=True)
    centered = inputs - average
    variance = jnp.mean(centered * centered, axis=-1, keepdims=True)
    inverse = lax.rsqrt(variance + EPS_NORM)
    return centered * inverse, inverse


def gelu_slope(preact):
    normal_cdf = 0.5 * (1.0 + lax.erf(preact * (1.0 / math.sqrt(2.0))))
    return normal_cdf + preact * jnp.exp(-0.5 * preact * preact) * (1.0 / math.sqrt(2.0 * math.pi))


def sequence_starts(lengths, token_index):
    ends_at = jnp.cumsum(lengths)
    picked = jnp.where(ends_at[None, :] <= token_index[:, None], lengths[None, :], 0)
    return jnp.sum(picked, axis=1)


def rope_tables(positions):
    lane = jnp.arange(PAIR, dtype=jnp.int32) % HEAD
    half = ROT // 2
    freqs = jnp.exp((lane % half).astype(f32) * (-2.0 * math.log(10000.0) / ROT))
    freqs = jnp.where(lane < ROT, freqs, 0.0)
    phase = positions.astype(f32)[:, None] * freqs[None, :]
    sine = jnp.sin(phase)
    front = jnp.where(lane < half, -sine, 0.0)
    back = jnp.where((lane >= half) & (lane < ROT), sine, 0.0)
    return jnp.stack([jnp.cos(phase), front, back])


def rope(u, tables, sign):
    half = ROT // 2
    return u * tables[0] + sign * (
        pltpu.roll(u, PAIR - half, 1) * tables[1] + pltpu.roll(u, half, 1) * tables[2]
    )


def rope_kernel(pre_ref, table_ref, q_ref, kv_ref):
    width = q_ref.shape[1]
    tables = [table_ref[i] for i in range(3)]
    for p in range(width // PAIR):
        at = slice(p * PAIR, (p + 1) * PAIR)
        query = rope(pre_ref[:, p * PAIR : (p + 1) * PAIR], tables, 1.0)
        q_ref[:, at] = (query * HEAD ** (-0.5)).astype(bf16)
        key = rope(pre_ref[:, width + p * PAIR : width + (p + 1) * PAIR], tables, 1.0)
        kv_ref[0, :, at] = key.astype(bf16)
        kv_ref[1, :, at] = pre_ref[:, 2 * width + p * PAIR : 2 * width + (p + 1) * PAIR].astype(bf16)


def rope_forward(pre, tables):
    rows, width = pre.shape[0], pre.shape[1] // 3
    step = BLK
    return pl.pallas_call(
        rope_kernel,
        grid=(rows // step,),
        in_specs=[
            pl.BlockSpec((step, 3 * width), lambda i: (i, 0)),
            pl.BlockSpec((3, step, PAIR), lambda i: (0, i, 0)),
        ],
        out_specs=[
            pl.BlockSpec((step, width), lambda i: (i, 0)),
            pl.BlockSpec((2, step, width), lambda i: (0, i, 0)),
        ],
        out_shape=[
            jax.ShapeDtypeStruct((rows, width), bf16),
            jax.ShapeDtypeStruct((2, rows, width), bf16),
        ],
        compiler_params=pltpu.CompilerParams(vmem_limit_bytes=VMEM_CAP),
        cost_estimate=pl.CostEstimate(flops=rows * width * 12, bytes_accessed=rows * width * 18, transcendentals=0),
        name="rope_forward",
    )(pre, tables)


def rope_back_kernel(steps, *refs):
    dq_a, dq_b, own, *rest = refs
    halos = rest[:steps]
    table_ref, out_ref, sum_ref = rest[steps:]
    width = dq_a.shape[1]
    tables = [table_ref[i] for i in range(3)]

    @pl.when(pl.program_id(0) == 0)
    def _():
        sum_ref[...] = jnp.zeros_like(sum_ref)

    def put(at, value):
        low = value.astype(bf16)
        out_ref[:, at] = low
        sum_ref[:, at] += jnp.sum(low.astype(f32), axis=0, keepdims=True)

    for p in range(width // PAIR):
        lanes = slice(p * PAIR, (p + 1) * PAIR)
        query = (dq_a[:, lanes] + dq_b[:, lanes]) * HEAD ** (-0.5)
        put(slice(p * PAIR, (p + 1) * PAIR), rope(query, tables, -1.0))
        key, value = own[0, :, lanes], own[1, :, lanes]
        for halo in halos:
            key = key + halo[0, :, lanes].astype(f32)
            value = value + halo[1, :, lanes].astype(f32)
        put(slice(width + p * PAIR, width + (p + 1) * PAIR), rope(key, tables, -1.0))
        put(slice(2 * width + p * PAIR, 2 * width + (p + 1) * PAIR), value)


def rope_backward(dq_a, dq_b, own, halos, tables):
    rows, width = dq_a.shape
    step = BLK
    flat = pl.BlockSpec((step, width), lambda i: (i, 0))
    pair = pl.BlockSpec((2, step, width), lambda i: (0, i, 0))
    return pl.pallas_call(
        functools.partial(rope_back_kernel, len(halos)),
        grid=(rows // step,),
        in_specs=[flat, flat, pair]
        + [pair] * len(halos)
        + [pl.BlockSpec((3, step, PAIR), lambda i: (0, i, 0))],
        out_specs=[
            pl.BlockSpec((step, 3 * width), lambda i: (i, 0)),
            pl.BlockSpec((1, 3 * width), lambda i: (0, 0)),
        ],
        out_shape=[
            jax.ShapeDtypeStruct((rows, 3 * width), bf16),
            jax.ShapeDtypeStruct((1, 3 * width), f32),
        ],
        compiler_params=pltpu.CompilerParams(vmem_limit_bytes=VMEM_CAP),
        cost_estimate=pl.CostEstimate(flops=rows * width * 16, bytes_accessed=rows * width * 28, transcendentals=0),
        name="rope_backward",
    )(dq_a, dq_b, own, *halos, tables)


def low_lanes():
    return lax.broadcasted_iota(jnp.int32, (1, PAIR), 1) < HEAD


def attend_kernel(sources, scal_ref, q_ref, start_ref, *refs):
    kv_refs = refs[:sources]
    o_ref, lse_ref, m_ref, l_ref, acc_ref = refs[sources:]
    rows = q_ref.shape[0]
    base = scal_ref[0]
    low = low_lanes()
    for qb in range(rows // BLK):
        at = pl.ds(qb * BLK, BLK)
        q_pair = q_ref[at, :]
        zero = jnp.zeros_like(q_pair)
        queries = [jnp.where(low, q_pair, zero), jnp.where(low, zero, q_pair)]
        m_ref[...] = jnp.full_like(m_ref, -1e30)
        l_ref[...] = jnp.zeros_like(l_ref)
        acc_ref[...] = jnp.zeros_like(acc_ref)
        first_start = scal_ref[1 + qb]
        row_start = start_ref[at, 0:1]
        row_index = base + qb * BLK + lax.broadcasted_iota(jnp.int32, (BLK, 1), 0)
        for src in range(sources - 1, -1, -1):
            for kb in range(rows // BLK - 1, -1, -1):
                offset = (src - (sources - 1)) * rows + kb * BLK
                if offset > qb * BLK:
                    continue
                key_base = base + offset

                def work(src=src, kb=kb, key_base=key_base):
                    keys = kv_refs[src][0, pl.ds(kb * BLK, BLK), :]
                    values = kv_refs[src][1, pl.ds(kb * BLK, BLK), :]
                    key_index = key_base + lax.broadcasted_iota(jnp.int32, (1, BLK), 1)
                    seen = (key_index >= row_start) & (key_index <= row_index)
                    for h in range(2):
                        s = lax.dot_general(
                            queries[h], keys, (((1,), (1,)), ((), ())), preferred_element_type=f32
                        )
                        s = jnp.where(seen, s, MASKED)
                        m_old = m_ref[h]
                        m_new = jnp.maximum(m_old, jnp.max(s, axis=1, keepdims=True))
                        scale = jnp.exp(m_old - m_new)
                        e = jnp.exp(s - m_new[:, 0:1])
                        m_ref[h] = m_new
                        l_ref[h] = l_ref[h] * scale + jnp.sum(e, axis=1, keepdims=True)
                        acc_ref[h] = acc_ref[h] * scale + jnp.dot(
                            e.astype(bf16), values, preferred_element_type=f32
                        )

                if offset == qb * BLK:
                    work()
                else:
                    pl.when(key_base + BLK > first_start)(work)
        out = jnp.where(low, acc_ref[0] / l_ref[0], acc_ref[1] / l_ref[1])
        o_ref[at, :] = out.astype(bf16)
        for h in range(2):
            lse_ref[0, h : h + 1, at] = jnp.transpose(m_ref[h] + jnp.log(l_ref[h]))[0:1, :]


def attend(scalars, q, start_cols, kvs):
    rows, width = q.shape
    pairs = width // PAIR
    sources = len(kvs)
    return pl.pallas_call(
        functools.partial(attend_kernel, sources),
        grid=(pairs,),
        in_specs=[
            pl.BlockSpec(memory_space=pltpu.SMEM),
            pl.BlockSpec((rows, PAIR), lambda p: (0, p)),
            pl.BlockSpec((rows, PAIR), lambda p: (0, 0)),
        ]
        + [pl.BlockSpec((2, rows, PAIR), lambda p: (0, 0, p))] * sources,
        out_specs=[
            pl.BlockSpec((rows, PAIR), lambda p: (0, p)),
            pl.BlockSpec((1, 8, rows), lambda p: (p, 0, 0)),
        ],
        out_shape=[
            jax.ShapeDtypeStruct((rows, width), bf16),
            jax.ShapeDtypeStruct((pairs, 8, rows), f32),
        ],
        scratch_shapes=[
            pltpu.VMEM((2, BLK, PAIR), f32),
            pltpu.VMEM((2, BLK, PAIR), f32),
            pltpu.VMEM((2, BLK, PAIR), f32),
        ],
        compiler_params=pltpu.CompilerParams(vmem_limit_bytes=VMEM_CAP),
        cost_estimate=pl.CostEstimate(
            flops=4 * rows * rows * width * 2,
            bytes_accessed=rows * width * 2 * (2 + 2 * sources),
            transcendentals=rows * rows * 12,
        ),
        name="attend",
    )(scalars, q, start_cols, *kvs)


def attend_back_kernel(sources, offset_rows, scal_ref, q_ref, g_ref, lse_ref, delta_ref, start_ref, *refs):
    kv_refs = refs[:sources]
    dq_ref, *dkv_refs = refs[sources:]
    rows = q_ref.shape[0]
    base = scal_ref[0]
    low = low_lanes()
    dq_ref[...] = jnp.zeros_like(dq_ref)
    for src in range(sources):
        for kb in range(rows // BLK):
            key_at = pl.ds(kb * BLK, BLK)
            offset = offset_rows[src] + kb * BLK
            dkv_refs[src][0, key_at, :] = jnp.zeros((BLK, PAIR), dkv_refs[src].dtype)
            dkv_refs[src][1, key_at, :] = jnp.zeros((BLK, PAIR), dkv_refs[src].dtype)
            key_base = base + offset
            last = rows // BLK - 1

            def key_block(src=src, key_at=key_at, offset=offset, key_base=key_base):
                keys = kv_refs[src][0, key_at, :]
                values = kv_refs[src][1, key_at, :]
                zero = jnp.zeros_like(keys)
                halves = [jnp.where(low, keys, zero), jnp.where(low, zero, keys)]
                key_index = key_base + lax.broadcasted_iota(jnp.int32, (BLK, 1), 0)
                for qb in range(rows // BLK):
                    if offset > qb * BLK:
                        continue

                    def work(qb=qb):
                        at = pl.ds(qb * BLK, BLK)
                        q_pair = q_ref[at, :]
                        g_pair = g_ref[at, :]
                        row_index = base + qb * BLK + lax.broadcasted_iota(jnp.int32, (1, BLK), 1)
                        seen = (key_index >= start_ref[0:1, at]) & (key_index <= row_index)
                        d_key = jnp.zeros((BLK, PAIR), f32)
                        d_value = jnp.zeros((BLK, PAIR), f32)
                        d_query = jnp.zeros((BLK, PAIR), f32)
                        for h in range(2):
                            keep = low if h == 0 else jnp.logical_not(low)
                            q_h = jnp.where(keep, q_pair, zero)
                            g_h = jnp.where(keep, g_pair, zero)
                            s = lax.dot_general(
                                keys, q_h, (((1,), (1,)), ((), ())), preferred_element_type=f32
                            )
                            s = jnp.where(seen, s, MASKED)
                            prob = jnp.exp(s - lse_ref[0, h : h + 1, at])
                            d_prob = lax.dot_general(
                                values, g_h, (((1,), (1,)), ((), ())), preferred_element_type=f32
                            )
                            d_score = (prob * (d_prob - delta_ref[0, h : h + 1, at])).astype(bf16)
                            d_value += jnp.dot(prob.astype(bf16), g_h, preferred_element_type=f32)
                            d_key += jnp.dot(d_score, q_h, preferred_element_type=f32)
                            d_query += lax.dot_general(
                                d_score, halves[h], (((0,), (0,)), ((), ())), preferred_element_type=f32
                            )
                        kind = dkv_refs[src].dtype
                        dkv_refs[src][0, key_at, :] = (
                            dkv_refs[src][0, key_at, :].astype(f32) + d_key
                        ).astype(kind)
                        dkv_refs[src][1, key_at, :] = (
                            dkv_refs[src][1, key_at, :].astype(f32) + d_value
                        ).astype(kind)
                        dq_ref[at, :] += d_query

                    if offset == qb * BLK:
                        work()
                    else:
                        pl.when(key_base + BLK > scal_ref[1 + qb])(work)

            key_block()


def attend_back(scalars, q, g, lse, delta, start_rows, kvs, offset_rows, kind):
    rows, width = q.shape
    pairs = width // PAIR
    sources = len(kvs)
    flat = pl.BlockSpec((rows, PAIR), lambda p: (0, p))
    stat = pl.BlockSpec((1, 8, rows), lambda p: (p, 0, 0))
    pair = pl.BlockSpec((2, rows, PAIR), lambda p: (0, 0, p))
    return pl.pallas_call(
        functools.partial(attend_back_kernel, sources, tuple(offset_rows)),
        grid=(pairs,),
        in_specs=[
            pl.BlockSpec(memory_space=pltpu.SMEM),
            flat,
            flat,
            stat,
            stat,
            pl.BlockSpec((8, rows), lambda p: (0, 0)),
        ]
        + [pair] * sources,
        out_specs=[flat] + [pair] * sources,
        out_shape=[jax.ShapeDtypeStruct((rows, width), f32)]
        + [jax.ShapeDtypeStruct((2, rows, width), kind)] * sources,
        compiler_params=pltpu.CompilerParams(vmem_limit_bytes=VMEM_CAP),
        cost_estimate=pl.CostEstimate(
            flops=10 * rows * rows * width * sources // 2,
            bytes_accessed=rows * width * (8 + 8 * sources),
            transcendentals=rows * rows * 6,
        ),
        name="attend_back",
    )(scalars, q, g, lse, delta, start_rows, *kvs)


def orth_kernel(a_ref, b_ref, out_a, out_b, x_ref, gram_ref, mix_ref):
    rows, half = a_ref.shape
    part = 256
    chunk = 512
    blocks = rows // part
    total = jnp.zeros((1, 1), f32)
    for ref in (a_ref, b_ref):
        for i in range(blocks):
            v = ref[i * part : (i + 1) * part, :].astype(f32)
            total = total + jnp.sum(v * v).reshape(1, 1)
    inverse = 1.0 / (jnp.sqrt(total) + 1e-07)
    for i in range(blocks):
        at = slice(i * part, (i + 1) * part)
        x_ref[at, :half] = (a_ref[at, :].astype(f32) * inverse).astype(bf16)
        x_ref[at, half:] = (b_ref[at, :].astype(f32) * inverse).astype(bf16)

    def sweep(_, carry):
        for i in range(blocks):
            for j in range(i, blocks):
                g = lax.dot_general(
                    x_ref[i * part : (i + 1) * part, :],
                    x_ref[j * part : (j + 1) * part, :],
                    (((1,), (1,)), ((), ())),
                    preferred_element_type=f32,
                )
                gram_ref[i * part : (i + 1) * part, j * part : (j + 1) * part] = g.astype(bf16)
                if j > i:
                    gram_ref[j * part : (j + 1) * part, i * part : (i + 1) * part] = jnp.transpose(
                        g
                    ).astype(bf16)
        for i in range(blocks):
            for j in range(i, blocks):
                square = lax.dot_general(
                    gram_ref[i * part : (i + 1) * part, :],
                    gram_ref[:, j * part : (j + 1) * part],
                    (((1,), (0,)), ((), ())),
                    preferred_element_type=f32,
                )
                g = gram_ref[i * part : (i + 1) * part, j * part : (j + 1) * part].astype(f32)
                m = NS_B * g + NS_C * square
                mix_ref[i * part : (i + 1) * part, j * part : (j + 1) * part] = m.astype(bf16)
                if j > i:
                    mix_ref[j * part : (j + 1) * part, i * part : (i + 1) * part] = jnp.transpose(
                        m
                    ).astype(bf16)
        for c in range(2 * half // chunk):
            cols = slice(c * chunk, (c + 1) * chunk)
            x = x_ref[:, cols]
            y = NS_A * x.astype(f32) + jnp.dot(mix_ref[...], x, preferred_element_type=f32)
            x_ref[:, cols] = y.astype(bf16)
        return carry

    lax.fori_loop(0, 5, sweep, 0)
    out_a[...] = x_ref[:, :half]
    out_b[...] = x_ref[:, half:]


def orthogonalize(a, b):
    rows, half = a.shape
    spec = pl.BlockSpec(memory_space=pltpu.VMEM)
    return pl.pallas_call(
        orth_kernel,
        in_specs=[spec, spec],
        out_specs=[spec, spec],
        out_shape=[jax.ShapeDtypeStruct((rows, half), bf16)] * 2,
        scratch_shapes=[
            pltpu.VMEM((rows, 2 * half), bf16),
            pltpu.VMEM((rows, rows), bf16),
            pltpu.VMEM((rows, rows), bf16),
        ],
        compiler_params=pltpu.CompilerParams(vmem_limit_bytes=VMEM_CAP),
        cost_estimate=pl.CostEstimate(
            flops=5 * 4 * rows * rows * 2 * half, bytes_accessed=rows * half * 8, transcendentals=0
        ),
        name="orthogonalize",
    )(a, b)


def shards(
    tokens,
    cotangent,
    w_qkv,
    w_out,
    w_up,
    w_down,
    mom_qkv,
    mom_out,
    mom_up,
    mom_down,
    vectors,
    vec_first,
    vec_second,
    lengths,
):
    tok_rows = tokens.shape[0]
    row_part = w_qkv.shape[1]
    head_part = w_qkv.shape[-1]
    hidden_part = w_up.shape[-1]
    pairs = head_part // PAIR
    fsdp_count = lax.axis_size("fsdp")
    tp_count = lax.axis_size("tp")
    fsdp_index = lax.axis_index("fsdp")
    tp_index = lax.axis_index("tp")
    longest = SEQ_DEV * fsdp_count
    window_span = (tok_rows + longest - 2) // tok_rows
    base = fsdp_index * tok_rows
    token_index = base + jnp.arange(tok_rows, dtype=jnp.int32)
    starts = sequence_starts(lengths, token_index).astype(jnp.int32)
    tables = rope_tables(token_index - starts)
    tp_first = (tp_index == 0).astype(f32)
    start_cols = jnp.broadcast_to(starts[:, None], (tok_rows, PAIR))
    start_rows = jnp.broadcast_to(starts[None, :], (8, tok_rows))
    scalars = jnp.concatenate([base[None].astype(jnp.int32), starts[::BLK]])
    offsets = [-step * tok_rows for step in range(window_span, 0, -1)]

    widths = (3 * head_part, head_part, hidden_part, hidden_part)
    ends = (widths[0], widths[0] + widths[1], widths[0] + widths[1] + widths[2], sum(widths))

    def by_rows(qkv, out, up, down, layer):
        return [
            qkv[layer].reshape(row_part, 3 * head_part),
            out[layer].T,
            up[layer],
            down[layer].T,
        ]

    def read_vectors(layer):
        row_vec = vectors[layer]
        qkv_bias = lax.dynamic_slice_in_dim(
            row_vec[6 * D : 9 * D].reshape(3, D), tp_index * head_part, head_part, 1
        ).reshape(1, 3 * head_part)
        up_bias = lax.dynamic_slice_in_dim(row_vec[9 * D :], tp_index * hidden_part, hidden_part, 0)
        parts = [row_vec[i * D : (i + 1) * D] for i in range(6)]
        return parts + [qkv_bias, up_bias]

    weights = []
    for layer in range(LAYERS):
        mats = [m.astype(bf16) for m in by_rows(w_qkv, w_out, w_up, w_down, layer)]
        rest = jnp.concatenate(mats[1:], axis=1)
        if layer == 0:
            first = gather_streams(mats[0])
            others = lax.all_gather(rest, "fsdp", axis=0, tiled=True)
        else:
            both = lax.all_gather(
                jnp.concatenate([mats[0], rest], axis=1), "fsdp", axis=0, tiled=True
            )
            first, others = both[:, : widths[0]], both[:, widths[0] :]
        weights.append(
            (
                first,
                others[:, : widths[1]],
                others[:, widths[1] : widths[1] + widths[2]],
                others[:, widths[1] + widths[2] :],
            )
        )

    hidden_x = tokens.astype(f32)
    kept = []
    for layer in range(LAYERS):
        gain_one, shift_one, gain_two, shift_two, bias_out, bias_down, qkv_bias, up_bias = (
            read_vectors(layer)
        )
        full_qkv, full_out, full_up, full_down = weights[layer]
        unit, inverse = normalize(hidden_x)
        normed = (unit * gain_one + shift_one).astype(bf16)
        normed_two = (unit * gain_two + shift_two).astype(bf16)
        pre = jnp.dot(normed, full_qkv, preferred_element_type=f32) + qkv_bias
        query, own_kv = rope_forward(pre, tables)
        kvs = [from_behind(own_kv, step) for step in range(window_span, 0, -1)] + [own_kv]
        hidden_pre = jnp.dot(normed_two, full_up, preferred_element_type=f32) + up_bias
        hidden_low = jax.nn.gelu(hidden_pre, approximate=False).astype(bf16)
        mixed, lse = attend(scalars, query, start_cols, kvs)
        partial = jnp.einsum("tf,df->td", hidden_low, full_down, preferred_element_type=f32)
        partial = partial + jnp.einsum("tn,dn->td", mixed, full_out, preferred_element_type=f32)
        partial = partial.astype(bf16)
        branch = partial.astype(f32) + core_swap(partial).astype(f32)
        kept.append(
            (unit, inverse, normed, normed_two, query, kvs, mixed, lse, hidden_pre, hidden_low)
        )
        hidden_x = hidden_x + branch + bias_out + bias_down

    moments = [by_rows(mom_qkv, mom_out, mom_up, mom_down, layer) for layer in range(LAYERS)]
    grad_x = cotangent.astype(f32)
    grads = [None] * LAYERS
    vector_rows = [None] * LAYERS
    head_of = (jnp.arange(head_part) // HEAD)[:, None] == jnp.arange(head_part // HEAD)[None, :]
    for layer in range(LAYERS - 1, -1, -1):
        gain_one, shift_one, gain_two, shift_two, bias_out, bias_down, qkv_bias, up_bias = (
            read_vectors(layer)
        )
        full_qkv, full_out, full_up, full_down = weights[layer]
        unit, inverse, normed, normed_two, query, kvs, mixed, lse, hidden_pre, hidden_low = kept[layer]
        grad_low = grad_x.astype(bf16)
        grad_mixed = jnp.dot(grad_low, full_out, preferred_element_type=f32).astype(bf16)
        product = (grad_mixed.astype(f32) * mixed.astype(f32)).reshape(tok_rows, head_part // HEAD, HEAD)
        delta = jnp.sum(product, axis=-1).T.reshape(pairs, 2, tok_rows)
        delta = jnp.pad(delta, ((0, 0), (0, 6), (0, 0)))
        dq_far, *far = attend_back(
            scalars, query, grad_mixed, lse, delta, start_rows, kvs[:-1], offsets, bf16
        )
        back = [from_behind(far[i], -(window_span - i)) for i in range(window_span)]
        dq_own, own = attend_back(
            scalars, query, grad_mixed, lse, delta, start_rows, kvs[-1:], [0], f32
        )
        grad_hidden = jnp.dot(grad_low, full_down, preferred_element_type=f32)
        grad_hidden = (grad_hidden * gelu_slope(hidden_pre)).astype(bf16)
        grad_up = jnp.einsum("td,tf->df", normed_two, grad_hidden, preferred_element_type=f32)
        grad_out = jnp.einsum("td,tn->dn", grad_low, mixed, preferred_element_type=f32)
        grad_down = jnp.einsum("td,tf->df", grad_low, hidden_low, preferred_element_type=f32)
        grad_two = jnp.einsum("tf,df->td", grad_hidden, full_up, preferred_element_type=f32)
        grad_pre, pre_sum = rope_backward(dq_far, dq_own, own, back, tables)
        grad_qkv = jnp.einsum("td,tn->dn", normed, grad_pre, preferred_element_type=f32)
        grad_one = jnp.einsum("tn,dn->td", grad_pre, full_qkv, preferred_element_type=f32)
        joint = (grad_one * gain_one + grad_two * gain_two).astype(bf16)
        joint = joint.astype(f32) + core_swap(joint).astype(f32)
        full_grad = jnp.concatenate(
            [m.astype(bf16) for m in (grad_qkv, grad_out, grad_up, grad_down)], axis=1
        )
        if layer == 0:
            reduced = scatter_streams(full_grad)
        else:
            reduced = lax.psum_scatter(full_grad, "fsdp", scatter_dimension=0, tiled=True)
        reduced = reduced.astype(f32)
        grads[layer] = [
            reduced[:, : ends[0]],
            reduced[:, ends[0] : ends[1]],
            reduced[:, ends[1] : ends[2]],
            reduced[:, ends[2] :],
        ]
        bias_sum = jnp.sum(grad_x, axis=0) * tp_first
        qkv_column = lax.dynamic_update_slice_in_dim(
            jnp.zeros((3, D), f32), pre_sum.reshape(3, head_part), tp_index * head_part, 1
        )
        up_column = lax.dynamic_update_slice_in_dim(
            jnp.zeros((FF,), f32),
            jnp.sum(grad_hidden.astype(f32), axis=0),
            tp_index * hidden_part,
            0,
        )
        vector_rows[layer] = jnp.concatenate(
            [
                jnp.sum(grad_one * unit, axis=0),
                jnp.sum(grad_one, axis=0),
                jnp.sum(grad_two * unit, axis=0),
                jnp.sum(grad_two, axis=0),
                bias_sum,
                bias_sum,
                qkv_column.reshape(3 * D),
                up_column,
            ]
        )
        centered = joint - jnp.mean(joint, axis=-1, keepdims=True)
        grad_x = grad_x + inverse * (
            centered - unit * jnp.mean(joint * unit, axis=-1, keepdims=True)
        )
    grad_vectors = sum_everywhere(jnp.stack(vector_rows))

    widest = max(widths)
    chip = fsdp_index % KINDS
    planes = fsdp_count // KINDS
    new_moms = [
        [MOMENTUM * moments[layer][k] + grads[layer][k] for k in range(KINDS)]
        for layer in range(LAYERS)
    ]
    halves = []
    for layer in range(LAYERS):
        low = jnp.concatenate([m.astype(bf16) for m in new_moms[layer]], axis=1)[None]
        step = KINDS
        while step < fsdp_count:
            low = jnp.concatenate([low, permute(low, xor_pairs(fsdp_count, step))], axis=0)
            step *= 2
        blocks = jnp.stack(
            [
                jnp.pad(
                    low[:, :, ends[k] - widths[k] : ends[k]],
                    ((0, 0), (0, 0), (0, widest - widths[k])),
                )
                for k in range(KINDS)
            ]
        )
        own = [take(blocks, chip, 0)]
        for by in range(1, KINDS):
            own.append(permute(take(blocks, chip ^ by, 0), xor_pairs(fsdp_count, by)))
        halves.append(jnp.concatenate(own, axis=0).reshape(D, widest))
    mine = jnp.where(tp_index == 0, halves[0], halves[1])
    other = core_swap(jnp.where(tp_index == 0, halves[1], halves[0]))
    made = orthogonalize(mine, other)
    made = [m.reshape(KINDS, planes, row_part, widest)[:, 0] for m in made]
    made = jnp.stack(made, axis=1)
    back = [made[0]] + [permute(made[by], xor_pairs(fsdp_count, by)) for by in range(1, KINDS)]
    back = jnp.stack(back)
    kept_half = back[:, 0]
    swapped = core_swap(back[:, 1])
    by_layer = [
        jnp.where(tp_index == 0, kept_half, swapped),
        jnp.where(tp_index == 0, swapped, kept_half),
    ]
    masters = [by_rows(w_qkv, w_out, w_up, w_down, layer) for layer in range(LAYERS)]
    new_weights = []
    for layer in range(LAYERS):
        made_layer = []
        for k in range(KINDS):
            factor = RATE_MAT * math.sqrt((3 * D, D, FF, FF)[k])
            update = take(by_layer[layer], chip ^ k, 0)[0, :, : widths[k]].astype(f32)
            made_layer.append(masters[layer][k] * SHRINK - factor * update)
        new_weights.append(made_layer)

    def as_stored(per_layer):
        return [
            jnp.stack([m[0].reshape(row_part, 3, head_part) for m in per_layer]),
            jnp.stack([m[1].T for m in per_layer]),
            jnp.stack([m[2] for m in per_layer]),
            jnp.stack([m[3].T for m in per_layer]),
        ]

    first_new = BETA_ONE * vec_first + (1.0 - BETA_ONE) * grad_vectors
    second_new = BETA_TWO * vec_second + (1.0 - BETA_TWO) * grad_vectors * grad_vectors
    first_hat = first_new / (1.0 - BETA_ONE**STEP)
    second_hat = second_new / (1.0 - BETA_TWO**STEP)
    vectors_new = vectors - RATE_VEC * first_hat / (jnp.sqrt(second_hat) + ADAM_EPS)
    return (
        hidden_x,
        grad_x,
        *as_stored(grads),
        *as_stored(new_moms),
        *as_stored(new_weights),
        first_new,
        second_new,
        vectors_new,
        grad_vectors[:, 9 * D :],
    )


def solution(mesh):
    weights = (
        P(None, "fsdp", None, "tp"),
        P(None, "tp", "fsdp"),
        P(None, "fsdp", "tp"),
        P(None, "tp", "fsdp"),
    )
    rows = (P("fsdp", None), P("fsdp", None))
    return jax.shard_map(
        shards,
        mesh=mesh,
        in_specs=rows + weights + weights + (P(), P(), P(), P()),
        out_specs=rows + weights + weights + weights + (P(), P(), P(), P()),
        check_vma=False,
    )
```

```python
import functools
import math

import jax
import jax.numpy as jnp
from jax import lax
from jax.experimental.layout import Layout, with_layout_constraint
from jax.experimental import pallas as pl
from jax.experimental.pallas import tpu as pltpu
from jax.sharding import PartitionSpec as P

D = 768
HEAD = 64
ROT = 16
FF = 3072
LAYERS = 2
SEQ_DEV = 64
STEP = 10
PAIR = 2 * HEAD
BLK = 256
KINDS = 4

MASKED = -1000000000.0
EPS_NORM = 1e-05
NS_A = 3.4445
NS_B = -4.775
NS_C = 2.0315
MOMENTUM = 0.95
RATE_MAT = 0.02
SHRINK = 0.99
RATE_VEC = 0.25
BETA_ONE = 0.9
BETA_TWO = 0.95
ADAM_EPS = 1e-08
VMEM_CAP = 56 * 1024 * 1024

bf16 = jnp.bfloat16
f32 = jnp.float32


def permute(x, pairs):
    return lax.ppermute(x, "fsdp", pairs)


def xor_pairs(count, by):
    return [(i, i ^ by) for i in range(count)]


def core_swap(x):
    count = lax.axis_size("tp")
    return lax.ppermute(x, "tp", [(i, i ^ 1) for i in range(count)])


def shifted(x, by):
    devices = lax.axis_size("fsdp")
    return lax.ppermute(
        x, "fsdp", [(i, i + by) for i in range(devices) if 0 <= i + by < devices]
    )


def bit_pos(stride):
    return (lax.axis_index("fsdp") // stride) % 2


def take(block, index, axis):
    return lax.dynamic_slice_in_dim(block, index, 1, axis)


class Task:
    def __init__(self, steps):
        self.steps = steps
        self.result = None
        self.flying = None
        self.resume(None)

    def resume(self, arrived):
        try:
            self.flying = self.steps.send(arrived)
        except StopIteration as stop:
            self.result = stop.value
            self.flying = None


def advance(tasks, *arrays):
    tasks = [t for t in tasks if t.flying is not None]
    arrived, arrays = lax.optimization_barrier(([t.flying for t in tasks], arrays))
    for task, got in zip(tasks, arrived):
        task.resume(got)
    return arrays if len(arrays) != 1 else arrays[0]


def finish(task, *arrays):
    while task.flying is not None:
        arrays = advance([task], *arrays)
        arrays = arrays if isinstance(arrays, tuple) else (arrays,)
    return task.result


def join_bit(block, other, axis, stride):
    first = bit_pos(stride) == 0
    joined = jnp.where(
        first,
        jnp.concatenate([block, other], axis),
        jnp.concatenate([other, block], axis),
    )
    return with_layout_constraint(joined, Layout(tuple(range(joined.ndim))))


def gather_steps(piece, cut, apart=False):
    count = lax.axis_size("fsdp")
    rows, cols = piece.shape
    if count != 16:
        whole = lax.all_gather(piece, "fsdp", axis=0, tiled=True)
        return whole[:, :cut], whole[:, cut:]
        yield
    pos = lax.axis_index("fsdp") // 4
    got = [piece]
    for group in ((1, 2), (3,)) if apart else ((1, 2, 3),):
        got += yield [permute(piece, xor_pairs(16, 4 * by)) for by in group]

    def placed(at):
        found = [m[:, at] for m in got]

        def pick(plane):
            out = found[plane ^ 3]
            for k in (2, 1, 0):
                out = jnp.where(pos == k, found[plane ^ k], out)
            return out

        return jnp.stack([pick(plane) for plane in range(4)]).reshape(4, 1, 1, rows, -1)

    part_a, part_b = placed(slice(0, cut)), placed(slice(cut, cols))
    got_a, got_b = yield [permute(part_a, xor_pairs(16, 1)), permute(part_b, xor_pairs(16, 2))]
    part_a, part_b = join_bit(part_a, got_a, 2, 1), join_bit(part_b, got_b, 1, 2)
    got_a, got_b = yield [permute(part_a, xor_pairs(16, 2)), permute(part_b, xor_pairs(16, 1))]
    part_a, part_b = join_bit(part_a, got_a, 1, 2), join_bit(part_b, got_b, 2, 1)
    return part_a.reshape(16 * rows, -1), part_b.reshape(16 * rows, -1)


def scatter_steps(full_a, full_b, apart=False):
    count = lax.axis_size("fsdp")
    rows = full_a.shape[0] // count
    if count != 16:
        whole = jnp.concatenate([full_a, full_b], axis=1)
        return lax.psum_scatter(whole, "fsdp", scatter_dimension=0, tiled=True).astype(f32)
        yield

    def parts(block, axis, stride):
        pos = bit_pos(stride)
        return take(block, 1 - pos, axis), take(block, pos, axis)

    def added(own, got):
        return (own.astype(f32) + got.astype(f32)).astype(bf16)

    full_a, full_b = [m.reshape(4, 2, 2, rows, -1) for m in (full_a, full_b)]
    send_a, keep_a = parts(full_a, 1, 2)
    send_b, keep_b = parts(full_b, 2, 1)
    got_a, got_b = yield [permute(send_a, xor_pairs(16, 2)), permute(send_b, xor_pairs(16, 1))]
    send_a, keep_a = parts(added(keep_a, got_a), 2, 1)
    send_b, keep_b = parts(added(keep_b, got_b), 1, 2)
    got_a, got_b = yield [permute(send_a, xor_pairs(16, 1)), permute(send_b, xor_pairs(16, 2))]
    block = jnp.concatenate([added(keep_a, got_a), added(keep_b, got_b)], axis=-1)
    block = block.reshape(4, rows, -1)
    pos = lax.axis_index("fsdp") // 4
    got = []
    for group in ((1, 2), (3,)) if apart else ((1, 2, 3),):
        got += yield [permute(take(block, pos ^ by, 0)[0], xor_pairs(16, 4 * by)) for by in group]
    return take(block, pos, 0)[0].astype(f32) + sum(g.astype(f32) for g in got)


def half_of(x, index):
    width = x.shape[-1] // 2
    return jnp.where(index == 0, x[..., :width], x[..., width:])


def both_halves(own, other, index):
    return jnp.where(
        index == 0, jnp.concatenate([own, other], -1), jnp.concatenate([other, own], -1)
    )


def window_steps(rows_low, span):
    core = lax.axis_index("tp")
    half = half_of(rows_low, core)
    got = yield [shifted(half, step) for step in range(span, 0, -1)]
    got = jnp.concatenate(got, axis=0)
    (other,) = yield [core_swap(got)]
    return jnp.concatenate([both_halves(got, other, core), rows_low], axis=0)


def window_back_steps(rows_low, span):
    core = lax.axis_index("tp")
    (got,) = yield [core_swap(half_of(rows_low, 1 - core))]
    half = (half_of(rows_low, core).astype(f32) + got.astype(f32)).astype(bf16)
    half = half.reshape(span, -1, half.shape[-1])
    back = yield [shifted(half[span - step], -step) for step in range(span, 0, -1)]
    total = sum(b.astype(f32) for b in back)
    zero = jnp.zeros_like(total)
    return jnp.concatenate(
        [jnp.where(core == 0, total, zero), jnp.where(core == 0, zero, total)], axis=-1
    )


def sum_steps(x):
    count = lax.axis_size("fsdp")
    (got,) = yield [core_swap(x)]
    x = x + got
    step = 1
    while step < count:
        (got,) = yield [permute(x, xor_pairs(count, step))]
        x = x + got
        step *= 2
    return x


def owner_steps(blocks):
    count = lax.axis_size("fsdp")
    inner = count // KINDS
    quarter = lax.axis_index("fsdp") // inner
    layers, rows = blocks[0].shape[:2]
    widest = max(b.shape[2] for b in blocks)
    padded = [jnp.pad(b, ((0, 0), (0, 0), (0, widest - b.shape[2]))) for b in blocks]

    def block_for(owner):
        out = padded[KINDS - 1]
        for k in range(KINDS - 1):
            out = jnp.where(owner == k, padded[k], out)
        return out

    got = yield [
        permute(block_for(quarter ^ by), xor_pairs(count, by * inner)) for by in range(1, KINDS)
    ]
    block = jnp.stack([block_for(quarter)] + list(got), axis=1)
    bits = inner.bit_length() - 1
    block = block.reshape((layers, KINDS) + (1,) * bits + (rows, widest))
    cut = widest // 256 * 128
    part_a, part_b = block[..., :cut], block[..., cut:]
    for step in range(bits):
        bit_a, bit_b = step, bits - 1 - step
        got_a, got_b = yield [
            permute(part_a, xor_pairs(count, 1 << bit_a)),
            permute(part_b, xor_pairs(count, 1 << bit_b)),
        ]
        part_a = jnp.concatenate([part_a, got_a], axis=2 + bit_a)
        part_b = jnp.concatenate([part_b, got_b], axis=2 + bit_b)
    return jnp.concatenate([part_a, part_b], axis=-1).reshape(layers, count * rows, widest)


def normalize(inputs):
    average = jnp.mean(inputs, axis=-1, keepdims=True)
    centered = inputs - average
    variance = jnp.mean(centered * centered, axis=-1, keepdims=True)
    inverse = lax.rsqrt(variance + EPS_NORM)
    return centered * inverse, inverse


def sequence_starts(lengths, token_index):
    ends_at = jnp.cumsum(lengths)
    picked = jnp.where(ends_at[None, :] <= token_index[:, None], lengths[None, :], 0)
    return jnp.sum(picked, axis=1)


def rope_tables(positions):
    lane = jnp.arange(PAIR, dtype=jnp.int32) % HEAD
    half = ROT // 2
    freqs = jnp.exp((lane % half).astype(f32) * (-2.0 * math.log(10000.0) / ROT))
    freqs = jnp.where(lane < ROT, freqs, 0.0)
    phase = positions.astype(f32)[:, None] * freqs[None, :]
    sine = jnp.sin(phase)
    front = jnp.where(lane < half, -sine, 0.0)
    back = jnp.where((lane >= half) & (lane < ROT), sine, 0.0)
    return jnp.stack([jnp.cos(phase), front, back])


PARAMS = pltpu.CompilerParams(vmem_limit_bytes=VMEM_CAP)
NT = (((1,), (1,)), ((), ()))
TN = (((0,), (0,)), ((), ()))


def dot(a, b, how=(((1,), (0,)), ((), ()))):
    return lax.dot_general(a, b, how, preferred_element_type=f32)


SMALL = pl.CostEstimate(flops=1, bytes_accessed=1, transcendentals=0)


def rope(u, tables, sign):
    half = ROT // 2
    return u * tables[0] + sign * (
        pltpu.roll(u, PAIR - half, 1) * tables[1] + pltpu.roll(u, half, 1) * tables[2]
    )


def qkv_kernel(before, a_ref, w_ref, bias_ref, table_ref, q_ref, k_ref, v_ref, vt_ref):
    width = q_ref.shape[1]
    a = a_ref[...]
    tables = [table_ref[i] for i in range(3)]

    @pl.when(pl.program_id(0) >= before)
    def _():
        pre = dot(a, w_ref[:, :width]) + bias_ref[:, :width]
        for p in range(width // PAIR):
            at = slice(p * PAIR, (p + 1) * PAIR)
            q_ref[:, at] = (rope(pre[:, at], tables, 1.0) * HEAD ** (-0.5)).astype(bf16)

    pre = dot(a, w_ref[:, width:]) + bias_ref[:, width:]
    values = pre[:, width:].astype(bf16)
    v_ref[...] = values
    vt_ref[...] = jnp.transpose(values)
    for p in range(width // PAIR):
        at = slice(p * PAIR, (p + 1) * PAIR)
        k_ref[:, at] = rope(pre[:, at], tables, 1.0).astype(bf16)


def qkv_forward(window, weight, bias, tables, rows):
    total, width = window.shape[0], weight.shape[1] // 3
    before = total // rows - 1
    flat = pl.BlockSpec((rows, width), lambda i: (i, 0))
    return pl.pallas_call(
        functools.partial(qkv_kernel, before),
        grid=(total // rows,),
        in_specs=[
            pl.BlockSpec((rows, D), lambda i: (i, 0)),
            pl.BlockSpec((D, 3 * width), lambda i: (0, 0)),
            pl.BlockSpec((1, 3 * width), lambda i: (0, 0)),
            pl.BlockSpec((3, rows, PAIR), lambda i: (0, i, 0)),
        ],
        out_specs=[
            pl.BlockSpec((rows, width), lambda i: (0, 0)),
            flat,
            flat,
            pl.BlockSpec((width, rows), lambda i: (0, i)),
        ],
        out_shape=[
            jax.ShapeDtypeStruct((rows, width), bf16),
            jax.ShapeDtypeStruct((total, width), bf16),
            jax.ShapeDtypeStruct((total, width), bf16),
            jax.ShapeDtypeStruct((width, total), bf16),
        ],
        compiler_params=PARAMS,
        cost_estimate=SMALL,
        name="qkv_forward",
    )(window, weight, bias, tables)


def qkv_back_kernel(
    before, cut, dq_ref, dk_ref, dv_ref, a_ref, w_ref, table_ref,
    ga_ref, gb_ref, own_ref, prev_ref, sum_ref, pre_ref, acc_ref,
):
    width = dq_ref.shape[1]
    step = pl.program_id(0)
    tables = [table_ref[i] for i in range(3)]

    @pl.when(step == 0)
    def _():
        acc_ref[...] = jnp.zeros_like(acc_ref)
        sum_ref[...] = jnp.zeros_like(sum_ref)

    def put(at, value):
        pre_ref[:, at] = value
        sum_ref[:, at] += jnp.sum(value.astype(f32), axis=0, keepdims=True)

    a_turned = jnp.transpose(a_ref[...])
    for p in range(width // PAIR):
        at = slice(p * PAIR, (p + 1) * PAIR)
        put(
            slice(width + p * PAIR, width + (p + 1) * PAIR),
            rope(dk_ref[:, at].astype(f32), tables, -1.0).astype(bf16),
        )
    put(slice(2 * width, 3 * width), dv_ref[...])

    @pl.when(step < before)
    def _():
        pre = pre_ref[:, width:]
        acc_ref[:, width:] += dot(a_turned, pre)
        prev_ref[...] = dot(pre, w_ref[:, width:], NT).astype(bf16)

    @pl.when(step == before)
    def _():
        for p in range(width // PAIR):
            at = slice(p * PAIR, (p + 1) * PAIR)
            query = rope(dq_ref[:, at].astype(f32), tables, -1.0) * HEAD ** (-0.5)
            put(at, query.astype(bf16))
        pre = pre_ref[...]
        ga_ref[...] = (acc_ref[:, :cut] + dot(a_turned, pre[:, :cut])).astype(bf16)
        gb_ref[...] = (acc_ref[:, cut:] + dot(a_turned, pre[:, cut:])).astype(bf16)
        own_ref[...] = dot(pre, w_ref[...], NT)


def qkv_backward(dq, dk, dv, window, weight, tables, cut):
    rows, width = dq.shape
    total = window.shape[0]
    before = total // rows - 1
    fixed = lambda i: (0, 0)
    each = lambda i: (i, 0)
    return pl.pallas_call(
        functools.partial(qkv_back_kernel, before, cut),
        grid=(total // rows,),
        in_specs=[
            pl.BlockSpec((rows, width), fixed),
            pl.BlockSpec((rows, width), each),
            pl.BlockSpec((rows, width), each),
            pl.BlockSpec((rows, D), each),
            pl.BlockSpec((D, 3 * width), fixed),
            pl.BlockSpec((3, rows, PAIR), lambda i: (0, i, 0)),
        ],
        out_specs=[
            pl.BlockSpec((D, cut), fixed),
            pl.BlockSpec((D, 3 * width - cut), fixed),
            pl.BlockSpec((rows, D), fixed),
            pl.BlockSpec((rows, D), lambda i: (jnp.minimum(i, before - 1), 0)),
            pl.BlockSpec((1, 3 * width), fixed),
        ],
        out_shape=[
            jax.ShapeDtypeStruct((D, cut), bf16),
            jax.ShapeDtypeStruct((D, 3 * width - cut), bf16),
            jax.ShapeDtypeStruct((rows, D), f32),
            jax.ShapeDtypeStruct((total - rows, D), bf16),
            jax.ShapeDtypeStruct((1, 3 * width), f32),
        ],
        scratch_shapes=[pltpu.VMEM((rows, 3 * width), bf16), pltpu.VMEM((D, 3 * width), f32)],
        compiler_params=PARAMS,
        cost_estimate=SMALL,
        name="qkv_backward",
    )(dq, dk, dv, window, weight, tables)


def low_lanes():
    return lax.broadcasted_iota(jnp.int32, (1, PAIR), 1) < HEAD


def both_heads(x):
    low = low_lanes()
    zero = jnp.zeros_like(x[:BLK])
    parts = []
    for at in range(0, x.shape[0], BLK):
        block = x[at : at + BLK]
        parts += [jnp.where(low, block, zero), jnp.where(low, zero, block)]
    return jnp.concatenate(parts, axis=0)


def both_columns(first, second):
    parts = []
    for at in range(0, first.shape[1], BLK):
        parts += [first[:, at : at + BLK], second[:, at : at + BLK]]
    return jnp.concatenate(parts, axis=1)


def key_loops(scal_ref, blocks, own, work):
    work(own + 1, slice(2 * BLK, 4 * BLK))
    low_all, low_first = scal_ref[1], scal_ref[2]

    def full(i, carry):
        work(own - i, slice(0, 4 * BLK))
        return carry

    def first_only(i, carry):
        work(low_all - 1 - i, slice(0, 2 * BLK))
        return carry

    lax.fori_loop(0, own - low_all + 1, full, 0)
    lax.fori_loop(0, low_all - low_first, first_only, 0)


def attend_kernel(scal_ref, q_ref, start_ref, k_ref, vt_ref, o_ref, lse_ref, q2_ref, m_ref, l_ref, acc_ref):
    rows, total = q_ref.shape[0], k_ref.shape[0]
    pairs = q_ref.shape[1] // PAIR
    base = scal_ref[0]
    m_ref[...] = jnp.full_like(m_ref, -1e30)
    l_ref[...] = jnp.zeros_like(l_ref)
    acc_ref[...] = jnp.zeros_like(acc_ref)
    for p in range(pairs):
        q2_ref[p] = both_heads(q_ref[:, p * PAIR : (p + 1) * PAIR])
    starts = both_columns(start_ref[0:1, :], start_ref[0:1, :])
    index = base + lax.broadcasted_iota(jnp.int32, (1, rows), 1)
    index = both_columns(index, index)

    def work(kb, cols):
        at = pl.ds(pl.multiple_of(kb * BLK, BLK), BLK)
        key_index = base - (total - rows) + kb * BLK + lax.broadcasted_iota(jnp.int32, (BLK, 1), 0)
        seen = (key_index >= starts[:, cols]) & (key_index <= index[:, cols])
        for p in range(pairs):
            lanes = slice(p * PAIR, (p + 1) * PAIR)
            s = jnp.where(seen, dot(k_ref[at, lanes], q2_ref[p, cols, :], NT), MASKED)
            m_old = m_ref[p, 0:1, cols]
            m_new = jnp.maximum(m_old, jnp.max(s, axis=0, keepdims=True))
            scale = jnp.exp(m_old - m_new)
            e = jnp.exp(s - m_new)
            m_ref[p, 0:1, cols] = m_new
            l_ref[p, 0:1, cols] = l_ref[p, 0:1, cols] * scale + jnp.sum(e, axis=0, keepdims=True)
            acc_ref[p, :, cols] = acc_ref[p, :, cols] * scale + dot(vt_ref[lanes, at], e.astype(bf16))

    key_loops(scal_ref, total // BLK, (total - rows) // BLK, work)
    for p in range(pairs):
        total_p = l_ref[p, 0:1, :]
        acc = acc_ref[p] / total_p
        lse_ref[p, 0:1, :] = m_ref[p, 0:1, :] + jnp.log(total_p)
        for qb in range(rows // BLK):
            first = acc[:HEAD, 2 * qb * BLK : (2 * qb + 1) * BLK]
            second = acc[HEAD:, (2 * qb + 1) * BLK : (2 * qb + 2) * BLK]
            o_ref[qb * BLK : (qb + 1) * BLK, p * PAIR : (p + 1) * PAIR] = jnp.transpose(
                jnp.concatenate([first, second], axis=0)
            ).astype(bf16)


def whole(*shape):
    return pl.BlockSpec(shape, lambda *_: (0,) * len(shape))


def attend(scalars, q, start_rows, k, vt):
    rows, width = q.shape
    total = k.shape[0]
    pairs = width // PAIR
    return pl.pallas_call(
        attend_kernel,
        grid=(1,),
        in_specs=[
            pl.BlockSpec(memory_space=pltpu.SMEM),
            whole(rows, width),
            whole(8, rows),
            whole(total, width),
            whole(width, total),
        ],
        out_specs=[whole(rows, width), whole(pairs, 8, 2 * rows)],
        out_shape=[
            jax.ShapeDtypeStruct((rows, width), bf16),
            jax.ShapeDtypeStruct((pairs, 8, 2 * rows), f32),
        ],
        scratch_shapes=[
            pltpu.VMEM((pairs, 2 * rows, PAIR), bf16),
            pltpu.VMEM((pairs, 8, 2 * rows), f32),
            pltpu.VMEM((pairs, 8, 2 * rows), f32),
            pltpu.VMEM((pairs, PAIR, 2 * rows), f32),
        ],
        compiler_params=PARAMS,
        cost_estimate=SMALL,
        name="attend",
    )(scalars, q, start_rows, k, vt)


def attend_back_kernel(
    scal_ref, q_ref, g_ref, o_ref, lse_ref, start_ref, k_ref, v_ref,
    dq_ref, dk_ref, dv_ref, q2_ref, g2_ref, delta_ref, acc_ref,
):
    rows, total = q_ref.shape[0], k_ref.shape[0]
    pairs = q_ref.shape[1] // PAIR
    base = scal_ref[0]
    dk_ref[...] = jnp.zeros_like(dk_ref)
    dv_ref[...] = jnp.zeros_like(dv_ref)
    acc_ref[...] = jnp.zeros_like(acc_ref)
    which = lax.broadcasted_iota(jnp.int32, (8, PAIR), 0)
    lane = lax.broadcasted_iota(jnp.int32, (8, PAIR), 1)
    chosen = (which == lane // HEAD).astype(f32)
    for p in range(pairs):
        lanes = slice(p * PAIR, (p + 1) * PAIR)
        g = g_ref[:, lanes]
        q2_ref[p] = both_heads(q_ref[:, lanes])
        g2_ref[p] = both_heads(g)
        delta = lax.dot_general(
            chosen,
            g.astype(f32) * o_ref[:, lanes].astype(f32),
            NT,
            precision=lax.Precision.HIGHEST,
            preferred_element_type=f32,
        )
        delta_ref[p, 0:1, :] = both_columns(delta[0:1, :], delta[1:2, :])
    starts = both_columns(start_ref[0:1, :], start_ref[0:1, :])
    index = base + lax.broadcasted_iota(jnp.int32, (1, rows), 1)
    index = both_columns(index, index)

    def work(kb, cols):
        at = pl.ds(pl.multiple_of(kb * BLK, BLK), BLK)
        key_index = base - (total - rows) + kb * BLK + lax.broadcasted_iota(jnp.int32, (BLK, 1), 0)
        seen = (key_index >= starts[:, cols]) & (key_index <= index[:, cols])
        for p in range(pairs):
            lanes = slice(p * PAIR, (p + 1) * PAIR)
            keys, q2, g2 = k_ref[at, lanes], q2_ref[p, cols, :], g2_ref[p, cols, :]
            s = jnp.where(seen, dot(keys, q2, NT), MASKED)
            prob = jnp.exp(s - lse_ref[p, 0:1, cols])
            d_prob = dot(v_ref[at, lanes], g2, NT)
            d_score = (prob * (d_prob - delta_ref[p, 0:1, cols])).astype(bf16)
            dv_ref[at, lanes] = dot(prob.astype(bf16), g2).astype(bf16)
            dk_ref[at, lanes] = dot(d_score, q2).astype(bf16)
            acc_ref[p, cols, :] += dot(d_score, keys, TN)

    key_loops(scal_ref, total // BLK, (total - rows) // BLK, work)
    low = low_lanes()
    for p in range(pairs):
        for qb in range(rows // BLK):
            first = acc_ref[p, 2 * qb * BLK : (2 * qb + 1) * BLK, :]
            second = acc_ref[p, (2 * qb + 1) * BLK : (2 * qb + 2) * BLK, :]
            dq_ref[qb * BLK : (qb + 1) * BLK, p * PAIR : (p + 1) * PAIR] = jnp.where(
                low, first, second
            ).astype(bf16)


def attend_back(scalars, q, g, o, lse, start_rows, k, v):
    rows, width = q.shape
    total = k.shape[0]
    pairs = width // PAIR
    return pl.pallas_call(
        attend_back_kernel,
        grid=(1,),
        in_specs=[
            pl.BlockSpec(memory_space=pltpu.SMEM),
            whole(rows, width),
            whole(rows, width),
            whole(rows, width),
            whole(pairs, 8, 2 * rows),
            whole(8, rows),
            whole(total, width),
            whole(total, width),
        ],
        out_specs=[whole(rows, width), whole(total, width), whole(total, width)],
        out_shape=[
            jax.ShapeDtypeStruct((rows, width), bf16),
            jax.ShapeDtypeStruct((total, width), bf16),
            jax.ShapeDtypeStruct((total, width), bf16),
        ],
        scratch_shapes=[
            pltpu.VMEM((pairs, 2 * rows, PAIR), bf16),
            pltpu.VMEM((pairs, 2 * rows, PAIR), bf16),
            pltpu.VMEM((pairs, 8, 2 * rows), f32),
            pltpu.VMEM((pairs, 2 * rows, PAIR), f32),
        ],
        compiler_params=PARAMS,
        cost_estimate=SMALL,
        name="attend_back",
    )(scalars, q, g, o, lse, start_rows, k, v)


def ffn_kernel(
    a_ref, up0_ref, up1_ref, dn0_ref, dn1_ref, outa_ref, outb_ref, bias_ref, mix_ref,
    hid_ref, slope_ref, out_ref, acc_ref,
):
    step = pl.program_id(0)
    over_a = outa_ref.shape[1]
    over_b = mix_ref.shape[1] - over_a

    @pl.when(step == 0)
    def _():
        acc_ref[...] = dot(mix_ref[:, :over_a], outa_ref[...], NT) + dot(
            mix_ref[:, over_a:], outb_ref[:, :over_b], NT
        )

    a = a_ref[...]
    total = acc_ref[...]
    for i, (up, down) in enumerate(((up0_ref, dn0_ref), (up1_ref, dn1_ref))):
        at = slice(i * BLK, (i + 1) * BLK)
        u = dot(a, up[...]) + bias_ref[:, at]
        phi = 0.5 * (1.0 + lax.erf(u * (1.0 / math.sqrt(2.0))))
        slope = phi + u * jnp.exp(-0.5 * u * u) * (1.0 / math.sqrt(2.0 * math.pi))
        slope_ref[:, at] = slope.astype(bf16)
        low = (u * phi).astype(bf16)
        hid_ref[:, at] = low
        total = total + dot(low, down[...], NT)
    acc_ref[...] = total

    @pl.when(step == pl.num_programs(0) - 1)
    def _():
        out_ref[...] = acc_ref[...].astype(bf16)


def ffn_weights(hidden, skip):
    steps = hidden // BLK
    return [
        pl.BlockSpec((D, BLK), lambda i: (0, 2 * i)),
        pl.BlockSpec((D, BLK), lambda i: (0, 2 * i + 1)),
        pl.BlockSpec((D, BLK), lambda i: (0, skip + 2 * i)),
        pl.BlockSpec((D, BLK), lambda i: (0, skip + 2 * i + 1)),
        pl.BlockSpec((D, BLK), lambda i: (0, steps)),
        pl.BlockSpec((D, BLK), lambda i: (0, skip + steps)),
    ]


def ffn_forward(a, wa, wb, skip, bias, mixed, hidden):
    rows, width = a.shape[0], mixed.shape[1]
    wide = pl.BlockSpec((rows, 2 * BLK), lambda i: (0, i))
    return pl.pallas_call(
        ffn_kernel,
        grid=(hidden // (2 * BLK),),
        in_specs=[whole(rows, D)]
        + ffn_weights(hidden, skip)
        + [pl.BlockSpec((1, 2 * BLK), lambda i: (0, i)), whole(rows, width)],
        out_specs=[wide, wide, whole(rows, D)],
        out_shape=[
            jax.ShapeDtypeStruct((rows, hidden), bf16),
            jax.ShapeDtypeStruct((rows, hidden), bf16),
            jax.ShapeDtypeStruct((rows, D), bf16),
        ],
        scratch_shapes=[pltpu.VMEM((rows, D), f32)],
        compiler_params=PARAMS,
        cost_estimate=SMALL,
        name="ffn_forward",
    )(a, wa, wa, wb, wb, wa, wb, bias, mixed)


def ffn_back_kernel(
    g_ref, a_ref, up0_ref, up1_ref, dn0_ref, dn1_ref, outa_ref, outb_ref, slope_ref, hid_ref, mix_ref,
    ga_ref, gb_ref, da_ref, gmix_ref, sum_ref, at_ref, gt_ref,
):
    step = pl.program_id(0)
    last = pl.num_programs(0) - 1
    over_a = outa_ref.shape[1]
    over_b = mix_ref.shape[1] - over_a

    @pl.when(step == 0)
    def _():
        at_ref[...] = jnp.transpose(a_ref[...])
        gt_ref[...] = jnp.transpose(g_ref[...])
        da_ref[...] = jnp.zeros_like(da_ref)

    @pl.when(step < last)
    def _():
        g = g_ref[...]
        total = da_ref[...]
        gb_ref[...] = dot(gt_ref[...], hid_ref[...]).astype(bf16)
        for i, (up, down) in enumerate(((up0_ref, dn0_ref), (up1_ref, dn1_ref))):
            at = slice(i * BLK, (i + 1) * BLK)
            d_pre = (dot(g, down[...]) * slope_ref[:, at].astype(f32)).astype(bf16)
            sum_ref[:, at] = jnp.sum(d_pre.astype(f32), axis=0, keepdims=True)
            ga_ref[:, at] = dot(at_ref[...], d_pre).astype(bf16)
            total = total + dot(d_pre, up[...], NT)
        da_ref[...] = total

    @pl.when(step == last)
    def _():
        g = g_ref[...]
        gmix_ref[:, :over_a] = dot(g, outa_ref[...]).astype(bf16)
        gmix_ref[:, over_a:] = dot(g, outb_ref[:, :over_b]).astype(bf16)
        ga_ref[:, :over_a] = dot(gt_ref[...], mix_ref[:, :over_a]).astype(bf16)
        gb_ref[:, :over_b] = dot(gt_ref[...], mix_ref[:, over_a:]).astype(bf16)


def ffn_backward(g, a, wa, wb, skip, slope, hid, mixed):
    rows, width = mixed.shape
    hidden = hid.shape[1]
    steps = hidden // (2 * BLK)
    upto = lambda i: (0, jnp.minimum(i, steps - 1))
    weights = []
    for spec in ffn_weights(hidden, skip):
        weights.append(
            pl.BlockSpec(spec.block_shape, lambda i, f=spec.index_map: f(jnp.minimum(i, steps - 1)))
        )
    wide = pl.BlockSpec((rows, 2 * BLK), upto)
    return pl.pallas_call(
        ffn_back_kernel,
        grid=(steps + 1,),
        in_specs=[whole(rows, D), whole(rows, D)] + weights + [wide, wide, whole(rows, width)],
        out_specs=[
            pl.BlockSpec((D, 2 * BLK), lambda i: (0, i)),
            pl.BlockSpec((D, 2 * BLK), lambda i: (0, i)),
            whole(rows, D),
            whole(rows, width),
            pl.BlockSpec((1, 2 * BLK), upto),
        ],
        out_shape=[
            jax.ShapeDtypeStruct((D, hidden + BLK), bf16),
            jax.ShapeDtypeStruct((D, hidden + width - BLK), bf16),
            jax.ShapeDtypeStruct((rows, D), f32),
            jax.ShapeDtypeStruct((rows, width), bf16),
            jax.ShapeDtypeStruct((1, hidden), f32),
        ],
        scratch_shapes=[pltpu.VMEM((D, rows), bf16), pltpu.VMEM((D, rows), bf16)],
        compiler_params=PARAMS,
        cost_estimate=SMALL,
        name="ffn_backward",
    )(g, a, wa, wa, wb, wb, wa, wb, slope, hid, mixed)


def orth_kernel(a_ref, b_ref, out_a, out_b, x_ref, gram_ref, mix_ref):
    rows, half = a_ref.shape
    part = 256
    chunk = 512
    blocks = rows // part
    total = jnp.zeros((1, 1), f32)
    for ref in (a_ref, b_ref):
        for i in range(blocks):
            v = ref[i * part : (i + 1) * part, :].astype(f32)
            total = total + jnp.sum(v * v).reshape(1, 1)
    inverse = 1.0 / (jnp.sqrt(total) + 1e-07)
    for i in range(blocks):
        at = slice(i * part, (i + 1) * part)
        x_ref[at, :half] = (a_ref[at, :].astype(f32) * inverse).astype(bf16)
        x_ref[at, half:] = (b_ref[at, :].astype(f32) * inverse).astype(bf16)

    def sweep(_, carry):
        for i in range(blocks):
            for j in range(i, blocks):
                g = lax.dot_general(
                    x_ref[i * part : (i + 1) * part, :],
                    x_ref[j * part : (j + 1) * part, :],
                    (((1,), (1,)), ((), ())),
                    preferred_element_type=f32,
                )
                gram_ref[i * part : (i + 1) * part, j * part : (j + 1) * part] = g.astype(bf16)
                if j > i:
                    gram_ref[j * part : (j + 1) * part, i * part : (i + 1) * part] = jnp.transpose(
                        g
                    ).astype(bf16)
        for i in range(blocks):
            for j in range(i, blocks):
                square = lax.dot_general(
                    gram_ref[i * part : (i + 1) * part, :],
                    gram_ref[:, j * part : (j + 1) * part],
                    (((1,), (0,)), ((), ())),
                    preferred_element_type=f32,
                )
                g = gram_ref[i * part : (i + 1) * part, j * part : (j + 1) * part].astype(f32)
                m = NS_B * g + NS_C * square
                mix_ref[i * part : (i + 1) * part, j * part : (j + 1) * part] = m.astype(bf16)
                if j > i:
                    mix_ref[j * part : (j + 1) * part, i * part : (i + 1) * part] = jnp.transpose(
                        m
                    ).astype(bf16)
        for c in range(2 * half // chunk):
            cols = slice(c * chunk, (c + 1) * chunk)
            x = x_ref[:, cols]
            y = NS_A * x.astype(f32) + jnp.dot(mix_ref[...], x, preferred_element_type=f32)
            x_ref[:, cols] = y.astype(bf16)
        return carry

    lax.fori_loop(0, 5, sweep, 0)
    out_a[...] = x_ref[:, :half]
    out_b[...] = x_ref[:, half:]


def orthogonalize(a, b):
    rows, half = a.shape
    spec = pl.BlockSpec(memory_space=pltpu.VMEM)
    return pl.pallas_call(
        orth_kernel,
        in_specs=[spec, spec],
        out_specs=[spec, spec],
        out_shape=[jax.ShapeDtypeStruct((rows, half), bf16)] * 2,
        scratch_shapes=[
            pltpu.VMEM((rows, 2 * half), bf16),
            pltpu.VMEM((rows, rows), bf16),
            pltpu.VMEM((rows, rows), bf16),
        ],
        compiler_params=pltpu.CompilerParams(vmem_limit_bytes=VMEM_CAP),
        cost_estimate=SMALL,
        name="orthogonalize",
    )(a, b)


def shards(
    tokens,
    cotangent,
    w_qkv,
    w_out,
    w_up,
    w_down,
    mom_qkv,
    mom_out,
    mom_up,
    mom_down,
    vectors,
    vec_first,
    vec_second,
    lengths,
):
    tok_rows = tokens.shape[0]
    row_part = w_qkv.shape[1]
    head_part = w_qkv.shape[-1]
    hidden_part = w_up.shape[-1]
    widths = (3 * head_part, head_part, hidden_part, hidden_part)
    over = BLK
    cut_qkv = widths[0] // 256 * 128 + 128
    cut_rest = hidden_part + over

    def qkv_piece(layer):
        return w_qkv[layer].reshape(row_part, 3 * head_part).astype(bf16)

    def rest_of(mats):
        return jnp.concatenate([mats[2], mats[1][:, :over], mats[3], mats[1][:, over:]], axis=1)

    qkv_0 = Task(gather_steps(qkv_piece(0), cut_qkv))
    piece = rest_of([None, w_out[0].T, w_up[0], w_down[0].T]).astype(bf16)
    whole_0 = lax.all_gather(piece, "fsdp", axis=0, tiled=True)
    tokens, lengths, vectors, w_qkv, w_out, w_up, w_down = advance(
        [qkv_0], tokens, lengths, vectors, w_qkv, w_out, w_up, w_down
    )
    fsdp_count = lax.axis_size("fsdp")
    fsdp_index = lax.axis_index("fsdp")
    core = lax.axis_index("tp")
    longest = SEQ_DEV * fsdp_count
    span = (tok_rows + longest - 2) // tok_rows
    total = (span + 1) * tok_rows
    base = fsdp_index * tok_rows
    window_index = base - span * tok_rows + jnp.arange(total, dtype=jnp.int32)
    window_starts = sequence_starts(lengths, window_index).astype(jnp.int32)
    starts = window_starts[span * tok_rows :]
    tables = rope_tables(window_index - window_starts)
    tp_first = (core == 0).astype(f32)
    start_rows = jnp.broadcast_to(starts[None, :], (8, tok_rows))
    window_base = base - span * tok_rows
    low_all = jnp.minimum((starts[BLK] - window_base) // BLK, span * tok_rows // BLK)
    low_first = (starts[0] - window_base) // BLK
    scalars = jnp.stack([base, low_all, low_first]).astype(jnp.int32)

    def by_rows(qkv, out, up, down, layer):
        return [
            qkv[layer].reshape(row_part, 3 * head_part),
            out[layer].T,
            up[layer],
            down[layer].T,
        ]

    def read_vectors(layer):
        row_vec = vectors[layer]
        qkv_bias = lax.dynamic_slice_in_dim(
            row_vec[6 * D : 9 * D].reshape(3, D), core * head_part, head_part, 1
        ).reshape(1, 3 * head_part)
        up_bias = lax.dynamic_slice_in_dim(row_vec[9 * D :], core * hidden_part, hidden_part, 0)
        parts = [row_vec[i * D : (i + 1) * D] for i in range(6)]
        return parts + [qkv_bias, up_bias.reshape(1, hidden_part)]

    masters = [by_rows(w_qkv, w_out, w_up, w_down, layer) for layer in range(LAYERS)]

    params = [read_vectors(layer) for layer in range(LAYERS)]

    def normed(x, layer):
        unit, inverse = normalize(x)
        first = (unit * params[layer][0] + params[layer][1]).astype(bf16)
        second = (unit * params[layer][2] + params[layer][3]).astype(bf16)
        return unit, inverse, first, second

    def block_output(x, partial, layer):
        return (
            x
            + (partial.astype(f32) + core_swap(partial).astype(f32))
            + params[layer][4]
            + params[layer][5]
        )

    hidden_x = tokens.astype(f32)
    unit0, inverse0, a0, b0 = normed(hidden_x, 0)
    win_0 = Task(window_steps(a0, span))
    w_next = advance([qkv_0, win_0], w_qkv[1], w_out[1], w_up[1], w_down[1])
    qkv_1 = Task(gather_steps(w_next[0].reshape(row_part, -1).astype(bf16), cut_qkv))
    tables, start_rows, scalars, *w_next = advance(
        [qkv_0, qkv_1, win_0], tables, start_rows, scalars, *w_next
    )
    rest_1 = Task(
        gather_steps(
            rest_of(
                [None, w_next[1].T.astype(bf16), w_next[2].astype(bf16), w_next[3].T.astype(bf16)]
            ),
            cut_rest,
            True,
        )
    )
    wq = jnp.concatenate(qkv_0.result, axis=1)
    win0 = win_0.result
    q, k, v, vt = qkv_forward(win0, wq, params[0][6], tables, tok_rows)
    q, k, v, vt = advance([rest_1, qkv_1], q, k, v, vt)
    mixed, lse = attend(scalars, q, start_rows, k, vt)
    mixed, lse, b0 = advance([rest_1, qkv_1], mixed, lse, b0)
    whole_0, mixed, b0 = advance([], whole_0, mixed, b0)
    skip = cut_rest // BLK
    hid, slope, partial = ffn_forward(b0, whole_0, whole_0, skip, params[0][7], mixed, hidden_part)
    kept = [(unit0, inverse0, win0, b0, q, k, v, mixed, lse, hid, slope)]
    weights = [(wq, whole_0, whole_0, skip)]
    partial = advance([rest_1], partial)

    hidden_x = block_output(hidden_x, partial, 0)
    unit1, inverse1, a1, b1 = normed(hidden_x, 1)
    win_1 = Task(window_steps(a1, span))
    b1, unit1, inverse1 = advance([win_1], b1, unit1, inverse1)
    wq = jnp.concatenate(qkv_1.result, axis=1)
    b1, unit1, inverse1, wq = advance([win_1], b1, unit1, inverse1, wq)
    win1 = win_1.result
    q, k, v, vt = qkv_forward(win1, wq, params[1][6], tables, tok_rows)
    mixed, lse = attend(scalars, q, start_rows, k, vt)
    mixed, lse, b1, q, k, v = advance([rest_1], mixed, lse, b1, q, k, v)
    wa, wb = rest_1.result
    hid, slope, partial = ffn_forward(b1, wa, wb, 0, params[1][7], mixed, hidden_part)
    kept.append((unit1, inverse1, win1, b1, q, k, v, mixed, lse, hid, slope))
    weights.append((wq, wa, wb, 0))

    def own_gradients(grad_x, layer):
        _, _, _, b, _, _, _, mixed, _, hid, slope = kept[layer]
        grad_low = grad_x.astype(bf16)
        _, wa, wb, skip = weights[layer]
        return ffn_backward(grad_low, b, wa, wb, skip, slope, hid, mixed)

    def attention_gradients(g_mixed, layer):
        _, _, win, _, q, k, v, mixed, lse, _, _ = kept[layer]
        dq, dk, dv = attend_back(scalars, q, g_mixed, mixed, lse, start_rows, k, v)
        return qkv_backward(dq, dk, dv, win, weights[layer][0], tables, cut_qkv)

    def vector_row(grad_x, da, db, pre_sum, up_sum, layer):
        unit = kept[layer][0]
        bias_sum = jnp.sum(grad_x, axis=0) * tp_first
        qkv_column = lax.dynamic_update_slice_in_dim(
            jnp.zeros((3, D), f32), pre_sum.reshape(3, head_part), core * head_part, 1
        )
        up_column = lax.dynamic_update_slice_in_dim(
            jnp.zeros((FF,), f32), up_sum[0], core * hidden_part, 0
        )
        return jnp.concatenate(
            [
                jnp.sum(da * unit, axis=0),
                jnp.sum(da, axis=0),
                jnp.sum(db * unit, axis=0),
                jnp.sum(db, axis=0),
                bias_sum,
                bias_sum,
                qkv_column.reshape(3 * D),
                up_column,
            ]
        )

    def joint_of(da, db, layer):
        return (da * params[layer][0] + db * params[layer][2]).astype(bf16)

    def next_grad(grad_x, joint, other, layer):
        unit, inverse = kept[layer][:2]
        joint = joint.astype(f32) + other.astype(f32)
        centered = joint - jnp.mean(joint, axis=-1, keepdims=True)
        return grad_x + inverse * (
            centered - unit * jnp.mean(joint * unit, axis=-1, keepdims=True)
        )

    def shares(reduced_qkv, reduced_rest):
        ends = (hidden_part, hidden_part + over, 2 * hidden_part + over)
        up, out_a, down, out_b = (
            reduced_rest[:, : ends[0]],
            reduced_rest[:, ends[0] : ends[1]],
            reduced_rest[:, ends[1] : ends[2]],
            reduced_rest[:, ends[2] :],
        )
        return [reduced_qkv, jnp.concatenate([out_a, out_b], axis=1), up, down]

    moments = [by_rows(mom_qkv, mom_out, mom_up, mom_down, layer) for layer in range(LAYERS)]

    def moved(grad, layer, kind):
        return MOMENTUM * moments[layer][kind] + grad

    grad_x1 = cotangent.astype(f32)
    ga, gb, db1, g_mixed, up_sum1 = own_gradients(grad_x1, 1)
    ga, gb, g_mixed, partial, db1 = advance([], ga, gb, g_mixed, partial, db1)
    rest_1 = Task(scatter_steps(ga, gb, True))
    gqa1, gqb1, da1, da1_prev, pre_sum1 = attention_gradients(g_mixed, 1)
    gqa1, gqb1, da1, da1_prev, partial = advance([rest_1], gqa1, gqb1, da1, da1_prev, partial)
    back_1 = Task(window_back_steps(da1_prev, span))
    da1, partial = advance([back_1], da1, partial)
    block_out = block_output(hidden_x, partial, 1)
    da1 = advance([back_1], da1)
    da1 = da1 + back_1.result
    joint = joint_of(da1, db1, 1)
    grad_x0 = next_grad(grad_x1, joint, core_swap(joint), 1)
    ga, gb, db0, g_mixed, up_sum0 = own_gradients(grad_x0, 0)
    ga, gb, g_mixed, da1, db0 = advance([rest_1], ga, gb, g_mixed, da1, db0)
    rest_0 = Task(scatter_steps(ga, gb, True))
    gqa, gqb, da0, da0_prev, pre_sum0 = attention_gradients(g_mixed, 0)
    gqa, gqb, da0, da0_prev = advance([rest_0, rest_1], gqa, gqb, da0, da0_prev)
    back_0 = Task(window_back_steps(da0_prev, span))
    gqa, gqb, da0 = advance([rest_0, rest_1, back_0], gqa, gqb, da0)
    both_qkv = Task(
        scatter_steps(
            jnp.concatenate([gqa, gqa1], axis=1), jnp.concatenate([gqb, gqb1], axis=1)
        )
    )
    da0, da1 = advance([both_qkv, back_0, rest_0], da0, da1)
    da0 = da0 + back_0.result
    joint = joint_of(da0, db0, 0)
    grad_in = next_grad(grad_x0, joint, core_swap(joint), 0)
    advance([both_qkv, rest_0])
    rows_both = jnp.stack(
        [
            vector_row(grad_x0, da0, db0, pre_sum0, up_sum0, 0),
            vector_row(grad_x1, da1, db1, pre_sum1, up_sum1, 1),
        ]
    )
    grad_in, rows_both = advance([both_qkv], grad_in, rows_both)
    vec_sum = Task(sum_steps(rows_both))
    finish(both_qkv)
    got = both_qkv.result
    both = jnp.split(got, [cut_qkv, 2 * cut_qkv, widths[0] + cut_qkv], axis=1)
    grads = [
        shares(jnp.concatenate([both[0], both[2]], axis=1), rest_0.result),
        shares(jnp.concatenate([both[1], both[3]], axis=1), rest_1.result),
    ]
    new_moms = [[moved(grads[layer][kind], layer, kind) for kind in range(KINDS)] for layer in (0, 1)]
    owned = Task(
        owner_steps(
            [
                jnp.stack([new_moms[layer][kind].astype(bf16) for layer in (0, 1)])
                for kind in range(KINDS)
            ]
        )
    )
    while owned.flying is not None or vec_sum.flying is not None:
        advance([owned, vec_sum])
    grad_vectors = vec_sum.result

    widest = max(widths)
    inner = fsdp_count // KINDS
    quarter = fsdp_index // inner
    owned0, owned1 = owned.result[0], owned.result[1]
    mine = jnp.where(core == 0, owned0, owned1)
    other = core_swap(jnp.where(core == 0, owned1, owned0))
    made = orthogonalize(mine, other)
    made = [m.reshape(KINDS, inner, row_part, widest)[:, 0] for m in made]
    made = jnp.stack(made, axis=1)
    back = [made[0]] + [
        permute(made[by], xor_pairs(fsdp_count, by * inner)) for by in range(1, KINDS)
    ]
    back = jnp.stack(back)
    kept_half = back[:, 0]
    swapped = core_swap(back[:, 1])
    by_layer = [
        jnp.where(core == 0, kept_half, swapped),
        jnp.where(core == 0, swapped, kept_half),
    ]
    new_weights = []
    for layer in range(LAYERS):
        made_layer = []
        for kind in range(KINDS):
            factor = RATE_MAT * math.sqrt((3 * D, D, FF, FF)[kind])
            update = take(by_layer[layer], quarter ^ kind, 0)[0, :, : widths[kind]].astype(f32)
            made_layer.append(masters[layer][kind] * SHRINK - factor * update)
        new_weights.append(made_layer)

    def as_stored(per_layer):
        return [
            jnp.stack([m[0].reshape(row_part, 3, head_part) for m in per_layer]),
            jnp.stack([m[1].T for m in per_layer]),
            jnp.stack([m[2] for m in per_layer]),
            jnp.stack([m[3].T for m in per_layer]),
        ]

    first_new = BETA_ONE * vec_first + (1.0 - BETA_ONE) * grad_vectors
    second_new = BETA_TWO * vec_second + (1.0 - BETA_TWO) * grad_vectors * grad_vectors
    first_hat = first_new / (1.0 - BETA_ONE**STEP)
    second_hat = second_new / (1.0 - BETA_TWO**STEP)
    vectors_new = vectors - RATE_VEC * first_hat / (jnp.sqrt(second_hat) + ADAM_EPS)
    return (
        block_out,
        grad_in,
        *as_stored(grads),
        *as_stored(new_moms),
        *as_stored(new_weights),
        first_new,
        second_new,
        vectors_new,
        grad_vectors[:, 9 * D :],
    )


def solution(mesh):
    weights = (
        P(None, "fsdp", None, "tp"),
        P(None, "tp", "fsdp"),
        P(None, "fsdp", "tp"),
        P(None, "tp", "fsdp"),
    )
    rows = (P("fsdp", None), P("fsdp", None))
    return jax.shard_map(
        shards,
        mesh=mesh,
        in_specs=rows + weights + weights + (P(), P(), P(), P()),
        out_specs=rows + weights + weights + weights + (P(), P(), P(), P()),
        check_vma=False,
    )
```

```python
import functools
import math

import jax
import jax.numpy as jnp
import numpy as np
from jax import lax
from jax.experimental import pallas as pl
from jax.experimental.pallas import tpu as pltpu
from jax.sharding import PartitionSpec as P

D = 768
HEAD = 64
ROT = 16
FF = 3072
LAYERS = 2
SEQ_DEV = 64
STEP = 10
PAIR = 2 * HEAD
BLK = 256
KINDS = 4

MASKED = -1000000000.0
EPS_NORM = 1e-05
NS_A = 3.4445
NS_B = -4.775
NS_C = 2.0315
MOMENTUM = 0.95
RATE_MAT = 0.02
SHRINK = 0.99
RATE_VEC = 0.25
BETA_ONE = 0.9
BETA_TWO = 0.95
ADAM_EPS = 1e-08
ROOM_ATTEND = 28

bf16 = jnp.bfloat16
f32 = jnp.float32


def permute(x, pairs):
    return lax.ppermute(x, "fsdp", pairs)


def xor_pairs(count, by):
    return [(i, i ^ by) for i in range(count)]


def core_swap(x):
    count = lax.axis_size("tp")
    return lax.ppermute(x, "tp", [(i, i ^ 1) for i in range(count)])


def shifted(x, by):
    devices = lax.axis_size("fsdp")
    return lax.ppermute(
        x, "fsdp", [(i, i + by) for i in range(devices) if 0 <= i + by < devices]
    )


def on_grid():
    return lax.axis_size("fsdp") == 16


def place():
    index = lax.axis_index("fsdp")
    inner = lax.axis_size("fsdp") // KINDS
    bits = [(index // 2) % 2, index % 2] if on_grid() else [index * 0, index * 0]
    parts = [lax.axis_index("tp"), index // inner, *bits, index]
    return jnp.stack([p.astype(jnp.int32) for p in parts])


class Task:
    def __init__(self, steps):
        self.steps = steps
        self.result = None
        self.flying = None
        self.resume(None)

    def resume(self, arrived):
        try:
            self.flying = self.steps.send(arrived)
        except StopIteration as stop:
            self.result = stop.value
            self.flying = None


def advance(tasks, *arrays):
    tasks = [t for t in tasks if t.flying is not None]
    arrived, arrays = lax.optimization_barrier(([t.flying for t in tasks], arrays))
    for task, got in zip(tasks, arrived):
        task.resume(got)
    return arrays if len(arrays) != 1 else arrays[0]


def gather_steps(where, piece, cut, apart=False, pause=False):
    rows, cols = piece.shape
    if not on_grid():
        full = lax.all_gather(piece, "fsdp", axis=0, tiled=True)
        return full[:, :cut], full[:, cut:]
        yield
    got = []
    for group in ((1, 2), (3,)) if apart else ((1, 2, 3),):
        got += yield [permute(piece, xor_pairs(16, 4 * by)) for by in group]
    part_a, part_b = join_planes(where, [piece] + got, cut)
    if pause:
        part_a, part_b = yield [part_a, part_b]
    got_a, got_b = yield [permute(part_a, xor_pairs(16, 1)), permute(part_b, xor_pairs(16, 2))]
    part_a, part_b = join_chips(where, part_a, got_a, part_b, got_b, False)
    got_a, got_b = yield [permute(part_a, xor_pairs(16, 2)), permute(part_b, xor_pairs(16, 1))]
    part_a, part_b = join_chips(where, part_a, got_a, part_b, got_b, True)
    return part_a.reshape(16 * rows, -1), part_b.reshape(16 * rows, -1)


def natural(keep, send, axis):
    shape = (4, 1, 2, -1) if axis == 1 else (4, 2, 1, -1)
    parts = [m.reshape(shape + (m.shape[-1],)) for m in (keep, send)]
    full = jnp.concatenate(parts, axis=axis)
    return full.reshape(-1, keep.shape[-1])


def scatter_steps(where, keep_a, send_a, keep_b, send_b, pause=False, apart=False):
    if not on_grid():
        full = jnp.concatenate([natural(keep_a, send_a, 1), natural(keep_b, send_b, 2)], axis=1)
        return [lax.psum_scatter(full, "fsdp", scatter_dimension=0, tiled=True)]
        yield
    got_a, got_b = yield [permute(send_a, xor_pairs(16, 2)), permute(send_b, xor_pairs(16, 1))]
    keep_a, send_a, keep_b, send_b = add_split(where, keep_a, got_a, keep_b, got_b)
    if pause:
        keep_a, send_a, keep_b, send_b = yield [keep_a, send_a, keep_b, send_b]
    got_a, got_b = yield [permute(send_a, xor_pairs(16, 1)), permute(send_b, xor_pairs(16, 2))]
    own, *sends = add_planes(where, keep_a, got_a, keep_b, got_b)
    if pause:
        own, *sends = yield [own, *sends]
    got = [own]
    for group in ((0, 1), (2,)) if apart else ((0, 1, 2),):
        got += yield [permute(sends[i], xor_pairs(16, 4 * (i + 1))) for i in group]
    return got


def window_steps(half, span):
    got = yield [shifted(half, step) for step in range(span, 0, -1)]
    got = jnp.concatenate(got, axis=0)
    (other,) = yield [core_swap(got)]
    return got, other


def window_back_steps(keep, give, span):
    (got,) = yield [core_swap(give)]
    half = (keep.astype(f32) + got.astype(f32)).astype(bf16).reshape(span, -1, keep.shape[-1])
    back = yield [shifted(half[span - step], -step) for step in range(span, 0, -1)]
    return back


def sum_steps(x):
    count = lax.axis_size("fsdp")
    (got,) = yield [core_swap(x)]
    x = x + got
    step = 1
    while step < count:
        got = yield [permute(x, xor_pairs(count, step * by)) for by in (1, 2, 3)]
        x = (x + got[0]) + (got[1] + got[2])
        step *= 4
    return x


def owner_steps(own, sends):
    count = lax.axis_size("fsdp")
    inner = count // KINDS
    core = lax.axis_index("tp")
    rows, width = own.shape[1:]
    got = yield [permute(sends[by - 1], xor_pairs(count, by * inner)) for by in range(1, KINDS)]
    terms = [own] + list(got)
    give = jnp.stack([jnp.where(core == 0, m[1], m[0]) for m in terms])
    part_a = jnp.stack([jnp.where(core == 0, m[0], m[1]) for m in terms])
    part_a, part_b = yield [part_a, core_swap(give)]
    bits = inner.bit_length() - 1
    shape = (KINDS,) + (1,) * bits + (rows, width)
    part_a, part_b = part_a.reshape(shape), part_b.reshape(shape)
    for step in range(bits):
        bit_a, bit_b = step, bits - 1 - step
        got_a, got_b = yield [
            permute(part_a, xor_pairs(count, 1 << bit_a)),
            permute(part_b, xor_pairs(count, 1 << bit_b)),
        ]
        part_a = jnp.concatenate([part_a, got_a], axis=1 + bit_a)
        part_b = jnp.concatenate([part_b, got_b], axis=1 + bit_b)
    return [m.reshape(count * rows, width) for m in (part_a, part_b)]


SMALL = pl.CostEstimate(flops=1, bytes_accessed=1, transcendentals=0)
SCALARS = pl.BlockSpec(memory_space=pltpu.SMEM)
NT = (((1,), (1,)), ((), ()))
TN = (((0,), (0,)), ((), ()))


def dot(a, b, how=(((1,), (0,)), ((), ()))):
    return lax.dot_general(a, b, how, preferred_element_type=f32)


def whole(*shape):
    return pl.BlockSpec(shape, lambda *_: (0,) * len(shape))


def shaped(*shapes_and_kinds):
    return [jax.ShapeDtypeStruct(shape, kind) for shape, kind in shapes_and_kinds]


def call(kernel, name, grid, in_specs, out_specs, out_shape, scratch=(), room=16):
    return pl.pallas_call(
        kernel,
        grid=grid,
        in_specs=in_specs,
        out_specs=out_specs,
        out_shape=out_shape,
        scratch_shapes=list(scratch),
        compiler_params=pltpu.CompilerParams(vmem_limit_bytes=room << 20),
        cost_estimate=SMALL,
        name=name,
    )


def join_planes_kernel(cut, where_ref, *refs):
    *pieces, out_a, out_b = refs
    quarter = where_ref[1]
    for by, piece in enumerate(pieces):
        plane = quarter ^ by
        out_a[plane] = piece[:, :cut]
        out_b[plane] = piece[:, cut:]


def join_planes(where, pieces, cut):
    rows, cols = pieces[0].shape
    shapes = [(4, rows, cut), (4, rows, cols - cut)]
    return call(
        functools.partial(join_planes_kernel, cut),
        "join_planes",
        (1,),
        [SCALARS] + [whole(rows, cols)] * 4,
        [whole(*shape) for shape in shapes],
        shaped(*[(shape, bf16) for shape in shapes]),
    )(where, *pieces)


def join_chips_kernel(last, where_ref, own_a, got_a, own_b, got_b, out_a, out_b):
    y, x = where_ref[2], where_ref[3]
    if not last:
        out_a[0, x], out_a[0, 1 - x] = own_a[0], got_a[0]
        out_b[0, y], out_b[0, 1 - y] = own_b[0], got_b[0]
    else:
        out_a[0, y], out_a[0, 1 - y] = own_a[0], got_a[0]
        for side in range(2):
            out_b[0, side, x], out_b[0, side, 1 - x] = own_b[0, side], got_b[0, side]


def join_chips(where, own_a, got_a, own_b, got_b, last):
    rows = own_a.shape[-2]
    ins, outs = ((2, rows), (2, 2, rows)) if last else ((rows,), (2, rows))

    def spec(shape, width):
        return pl.BlockSpec((1,) + shape + (width,), lambda i: (i,) + (0,) * (len(shape) + 1))

    wide_a, wide_b = own_a.shape[-1], own_b.shape[-1]
    return call(
        functools.partial(join_chips_kernel, last),
        "join_chips",
        (4,),
        [SCALARS, spec(ins, wide_a), spec(ins, wide_a), spec(ins, wide_b), spec(ins, wide_b)],
        [spec(outs, wide_a), spec(outs, wide_b)],
        shaped(((4,) + outs + (wide_a,), bf16), ((4,) + outs + (wide_b,), bf16)),
    )(where, own_a, got_a, own_b, got_b)


def add_split_kernel(where_ref, keep_a, got_a, keep_b, got_b, out_ka, out_sa, out_kb, out_sb):
    rows = keep_a.shape[0] // 8
    for bit, keep, got, out_k, out_s in (
        (where_ref[3], keep_a, got_a, out_ka, out_sa),
        (where_ref[2], keep_b, got_b, out_kb, out_sb),
    ):
        for z in range(4):
            for flip, out in ((0, out_k), (1, out_s)):
                at = pl.ds(pl.multiple_of((2 * z + (bit ^ flip)) * rows, 16), rows)
                total = keep[at, :].astype(f32) + got[at, :].astype(f32)
                out[z * rows : (z + 1) * rows, :] = total.astype(bf16)


def add_split(where, keep_a, got_a, keep_b, got_b):
    rows, wide_a = keep_a.shape
    wide_b = keep_b.shape[1]
    outs = [(rows // 2, wide_a)] * 2 + [(rows // 2, wide_b)] * 2
    return call(
        add_split_kernel,
        "add_split",
        (1,),
        [SCALARS] + [whole(rows, wide_a)] * 2 + [whole(rows, wide_b)] * 2,
        [whole(*shape) for shape in outs],
        shaped(*[(shape, bf16) for shape in outs]),
        room=24,
    )(where, keep_a, got_a, keep_b, got_b)


def add_planes_kernel(where_ref, keep_a, got_a, keep_b, got_b, *outs):
    rows = keep_a.shape[0] // 4
    cut = keep_a.shape[1]
    for by, out in enumerate(outs):
        at = pl.ds(pl.multiple_of((where_ref[1] ^ by) * rows, 16), rows)
        out[:, :cut] = (keep_a[at, :].astype(f32) + got_a[at, :].astype(f32)).astype(bf16)
        out[:, cut:] = (keep_b[at, :].astype(f32) + got_b[at, :].astype(f32)).astype(bf16)


def add_planes(where, keep_a, got_a, keep_b, got_b):
    rows, wide_a = keep_a.shape
    wide_b = keep_b.shape[1]
    shape = (rows // 4, wide_a + wide_b)
    return call(
        add_planes_kernel,
        "add_planes",
        (1,),
        [SCALARS] + [whole(rows, wide_a)] * 2 + [whole(rows, wide_b)] * 2,
        [whole(*shape)] * 4,
        shaped(*[(shape, bf16)] * 4),
    )(where, keep_a, got_a, keep_b, got_b)


def setup_kernel(len_ref, where_ref, freq_ref, table_ref, start_ref, scal_ref):
    rows, total = start_ref.shape[1], table_ref.shape[1]
    base = where_ref[4] * rows
    first = base - (total - rows)
    half = ROT // 2

    def starts_of(index):
        end, out = jnp.int32(0), jnp.zeros_like(index)
        for i in range(len_ref.shape[0]):
            end = end + len_ref[i]
            out = jnp.where(index >= end, end, out)
        return out

    lane = lax.broadcasted_iota(jnp.int32, (BLK, PAIR), 1) % HEAD
    for c in range(total // BLK):
        at = slice(c * BLK, (c + 1) * BLK)
        index = first + c * BLK + lax.broadcasted_iota(jnp.int32, (BLK, PAIR), 0)
        phase = (index - starts_of(index)).astype(f32) * freq_ref[...]
        sine = jnp.sin(phase)
        table_ref[0, at, :] = jnp.cos(phase)
        table_ref[1, at, :] = jnp.where(lane < half, -sine, 0.0)
        table_ref[2, at, :] = jnp.where((lane >= half) & (lane < ROT), sine, 0.0)
    start_ref[...] = starts_of(base + lax.broadcasted_iota(jnp.int32, start_ref.shape, 1))
    own = (total - rows) // BLK
    scal_ref[0] = base
    scal_ref[1] = jnp.minimum((starts_of(base + BLK) - first) // BLK, own)
    scal_ref[2] = (starts_of(base) - first) // BLK


def setup(lengths, where, rows, total):
    lane = np.arange(PAIR) % HEAD
    freqs = np.exp((lane % (ROT // 2)) * (-2.0 * math.log(10000.0) / ROT))
    freqs = np.where(lane < ROT, freqs, 0.0).astype(np.float32)[None]
    return call(
        setup_kernel,
        "setup",
        (1,),
        [SCALARS, SCALARS, whole(1, PAIR)],
        [whole(3, total, PAIR), whole(8, rows), SCALARS],
        shaped(((3, total, PAIR), f32), ((8, rows), jnp.int32), ((3,), jnp.int32)),
        room=24,
    )(lengths, where, jnp.asarray(freqs))


def unit_rows(x):
    centered = x - jnp.mean(x, axis=-1, keepdims=True)
    inverse = lax.rsqrt(jnp.mean(centered * centered, axis=-1, keepdims=True) + EPS_NORM)
    return centered * inverse, inverse


def norm_kernel(where_ref, vec_ref, x_ref, a_ref, b_ref, half_ref):
    unit, _ = unit_rows(x_ref[...].astype(f32))
    a = (unit * vec_ref[:, :D] + vec_ref[:, D : 2 * D]).astype(bf16)
    a_ref[...] = a
    b_ref[...] = (unit * vec_ref[:, 2 * D : 3 * D] + vec_ref[:, 3 * D : 4 * D]).astype(bf16)
    half_ref[...] = jnp.where(where_ref[0] == 0, a[:, : D // 2], a[:, D // 2 :])


def add_norm_kernel(where_ref, old_ref, vec_ref, x_ref, part_ref, got_ref, new_ref, *outs):
    x = x_ref[...].astype(f32) + part_ref[...].astype(f32) + got_ref[...].astype(f32)
    x = x + old_ref[:, 4 * D : 5 * D] + old_ref[:, 5 * D : 6 * D]
    new_ref[...] = x
    if outs:
        norm_kernel(where_ref, vec_ref, new_ref, *outs)


def norm_rows(where, vec, x, old_vec=None, part=None, got=None, normed=True):
    rows = x.shape[0]
    step = rows // 4
    block = lambda width: pl.BlockSpec((step, width), lambda i: (i, 0))
    flat = whole(1, vec.shape[1])
    out = [((rows, D), bf16), ((rows, D), bf16), ((rows, D // 2), bf16)] if normed else []
    if part is None:
        specs, kernel, args = [flat, block(D)], norm_kernel, (vec, x)
    else:
        specs, kernel = [flat, flat] + [block(D)] * 3, add_norm_kernel
        args, out = (old_vec, vec, x, part, got), [((rows, D), f32)] + out
    return call(
        kernel,
        "norm_rows",
        (4,),
        [SCALARS] + specs,
        [block(shape[1]) for shape, _ in out],
        shaped(*out),
    )(where, *args)


def rope(u, tables, sign):
    half = ROT // 2
    return u * tables[0] + sign * (
        pltpu.roll(u, PAIR - half, 1) * tables[1] + pltpu.roll(u, half, 1) * tables[2]
    )


def window_block(before, where_ref, own_ref, half_ref, other_ref):
    half, other = half_ref[...], other_ref[...]
    first = jnp.where(where_ref[0] == 0, half, other)
    second = jnp.where(where_ref[0] == 0, other, half)
    earlier = jnp.concatenate([first, second], axis=1)
    return jnp.where(pl.program_id(0) < before, earlier, own_ref[...])


def qkv_kernel(
    before, where_ref, own_ref, half_ref, other_ref, wa_ref, wb_ref, vec_ref, table_ref,
    q_ref, k_ref, v_ref, vt_ref,
):
    width = q_ref.shape[1]
    over = wa_ref.shape[1] - width
    a = window_block(before, where_ref, own_ref, half_ref, other_ref)
    tables = [table_ref[i] for i in range(3)]
    bias = [
        vec_ref[:, pl.ds(pl.multiple_of((6 + c) * D + where_ref[0] * width, PAIR), width)]
        for c in range(3)
    ]

    @pl.when(pl.program_id(0) == before)
    def _():
        pre = dot(a, wa_ref[:, :width]) + bias[0]
        for p in range(width // PAIR):
            at = slice(p * PAIR, (p + 1) * PAIR)
            q_ref[:, at] = (rope(pre[:, at], tables, 1.0) * HEAD ** (-0.5)).astype(bf16)

    front, rest = dot(a, wa_ref[:, width:]), dot(a, wb_ref[...])
    values = (rest[:, width - over :] + bias[2]).astype(bf16)
    v_ref[...] = values
    vt_ref[...] = jnp.transpose(values)
    pre = jnp.concatenate([front, rest[:, : width - over]], axis=1) + bias[1]
    for p in range(width // PAIR):
        at = slice(p * PAIR, (p + 1) * PAIR)
        k_ref[:, at] = rope(pre[:, at], tables, 1.0).astype(bf16)


def window_specs(rows, before):
    earlier = pl.BlockSpec((rows, D // 2), lambda i: (jnp.minimum(i, before - 1), 0))
    return [whole(rows, D), earlier, earlier]


def qkv_forward(where, own, half, other, weights, vec, tables):
    rows, total = own.shape[0], tables.shape[1]
    width = (weights[0].shape[1] + weights[1].shape[1]) // 3
    before = total // rows - 1
    flat = pl.BlockSpec((rows, width), lambda i: (i, 0))
    return call(
        functools.partial(qkv_kernel, before),
        "qkv_forward",
        (total // rows,),
        [SCALARS]
        + window_specs(rows, before)
        + [whole(*weights[0].shape), whole(*weights[1].shape), whole(*vec.shape)]
        + [pl.BlockSpec((3, rows, PAIR), lambda i: (0, i, 0))],
        [whole(rows, width), flat, flat, pl.BlockSpec((width, rows), lambda i: (0, i))],
        shaped(
            ((rows, width), bf16),
            ((total, width), bf16),
            ((total, width), bf16),
            ((width, total), bf16),
        ),
        room=24,
    )(where, own, half, other, *weights, vec, tables)


def qkv_back_kernel(
    before, more, where_ref, dq_ref, dk_ref, dv_ref, own_ref, half_ref, other_ref, wa_ref, wb_ref, table_ref,
    *refs,
):
    more_refs, refs = refs[:more], refs[more:]
    ka_ref, sa_ref, kb_ref, sb_ref, da_ref, keep_ref, give_ref, sum_ref, pre_ref, acc_ref = refs
    width = dq_ref.shape[1]
    cut = wa_ref.shape[1]
    step = pl.program_id(0)
    tables = [table_ref[i] for i in range(3)]

    @pl.when(step == 0)
    def _():
        acc_ref[...] = jnp.zeros_like(acc_ref)
        sum_ref[...] = jnp.zeros_like(sum_ref)

    def put(at, value):
        pre_ref[:, at] = value
        sum_ref[:, at] += jnp.sum(value.astype(f32), axis=0, keepdims=True)

    turned = jnp.transpose(window_block(before, where_ref, own_ref, half_ref, other_ref))
    for p in range(width // PAIR):
        at = slice(p * PAIR, (p + 1) * PAIR)
        put(
            slice(width + p * PAIR, width + (p + 1) * PAIR),
            rope(dk_ref[:, at].astype(f32), tables, -1.0).astype(bf16),
        )
    put(slice(2 * width, 3 * width), dv_ref[...])

    @pl.when(step < before)
    def _():
        acc_ref[:, width:] += dot(turned, pre_ref[:, width:])
        da = dot(pre_ref[:, width:cut], wa_ref[:, width:], NT) + dot(pre_ref[:, cut:], wb_ref[...], NT)
        low, high = da[:, : D // 2].astype(bf16), da[:, D // 2 :].astype(bf16)
        keep_ref[...] = jnp.where(where_ref[0] == 0, low, high)
        give_ref[...] = jnp.where(where_ref[0] == 0, high, low)

    @pl.when(step == before)
    def _():
        for p in range(width // PAIR):
            at = slice(p * PAIR, (p + 1) * PAIR)
            query = rope(dq_ref[:, at].astype(f32), tables, -1.0) * HEAD ** (-0.5)
            put(at, query.astype(bf16))
        acc_ref[...] += dot(turned, pre_ref[...])
        da_ref[...] = dot(pre_ref[:, :cut], wa_ref[...], NT) + dot(pre_ref[:, cut:], wb_ref[...], NT)
        part = acc_ref.shape[0] // 16
        for flip, out_a, out_b in ((0, ka_ref, kb_ref), (1, sa_ref, sb_ref)):
            for z in range(4):
                at = pl.ds(pl.multiple_of((2 * z + (where_ref[2] ^ flip)) * 2 * part, 16), 2 * part)
                out_a[2 * z * part : (2 * z + 2) * part, :cut] = acc_ref[at, :cut].astype(bf16)
                for y in range(2):
                    row = (2 * z + y) * part
                    at = pl.ds(pl.multiple_of(2 * row + (where_ref[3] ^ flip) * part, 16), part)
                    out_b[row : row + part, : 3 * width - cut] = acc_ref[at, cut:].astype(bf16)
        for ref, out in zip(more_refs, (ka_ref, sa_ref, kb_ref, sb_ref)):
            out[:, ref.shape[1] :] = ref[...]


def qkv_backward(where, dq, dk, dv, own, half, other, weights, tables, more=()):
    rows, width = dq.shape
    total = tables.shape[1]
    before = total // rows - 1
    cut = weights[0].shape[1]
    each = pl.BlockSpec((rows, width), lambda i: (i, 0))
    earlier = pl.BlockSpec((rows, D // 2), lambda i: (jnp.minimum(i, before - 1), 0))
    times = 2 if more else 1
    splits = [(D // 2, times * cut)] * 2 + [(D // 2, times * (3 * width - cut))] * 2
    return call(
        functools.partial(qkv_back_kernel, before, len(more)),
        "qkv_backward",
        (total // rows,),
        [SCALARS, whole(rows, width), each, each]
        + window_specs(rows, before)
        + [whole(*weights[0].shape), whole(*weights[1].shape)]
        + [pl.BlockSpec((3, rows, PAIR), lambda i: (0, i, 0))]
        + [whole(*m.shape) for m in more],
        [whole(*shape) for shape in splits]
        + [whole(rows, D), earlier, earlier, whole(1, 3 * width)],
        shaped(
            *[(shape, bf16) for shape in splits],
            ((rows, D), f32),
            ((total - rows, D // 2), bf16),
            ((total - rows, D // 2), bf16),
            ((1, 3 * width), f32),
        ),
        [pltpu.VMEM((rows, 3 * width), bf16), pltpu.VMEM((D, 3 * width), f32)],
        room=32,
    )(where, dq, dk, dv, own, half, other, *weights, tables, *more)


def low_lanes():
    return lax.broadcasted_iota(jnp.int32, (1, PAIR), 1) < HEAD


def both_heads(x):
    low = low_lanes()
    zero = jnp.zeros_like(x[:BLK])
    parts = []
    for at in range(0, x.shape[0], BLK):
        block = x[at : at + BLK]
        parts += [jnp.where(low, block, zero), jnp.where(low, zero, block)]
    return jnp.concatenate(parts, axis=0)


def both_columns(first, second):
    parts = []
    for at in range(0, first.shape[1], BLK):
        parts += [first[:, at : at + BLK], second[:, at : at + BLK]]
    return jnp.concatenate(parts, axis=1)


def key_loops(scal_ref, blocks, own, work):
    work(own + 1, slice(2 * BLK, 4 * BLK))
    low_all, low_first = scal_ref[1], scal_ref[2]

    def full(i, carry):
        work(own - i, slice(0, 4 * BLK))
        return carry

    def first_only(i, carry):
        work(low_all - 1 - i, slice(0, 2 * BLK))
        return carry

    lax.fori_loop(0, own - low_all + 1, full, 0)
    lax.fori_loop(0, low_all - low_first, first_only, 0)


def attend_kernel(scal_ref, q_ref, start_ref, k_ref, vt_ref, o_ref, lse_ref, q2_ref, m_ref, l_ref, acc_ref):
    rows, total = q_ref.shape[0], k_ref.shape[0]
    pairs = q_ref.shape[1] // PAIR
    base = scal_ref[0]
    m_ref[...] = jnp.full_like(m_ref, -1e30)
    l_ref[...] = jnp.zeros_like(l_ref)
    acc_ref[...] = jnp.zeros_like(acc_ref)
    for p in range(pairs):
        q2_ref[p] = both_heads(q_ref[:, p * PAIR : (p + 1) * PAIR])
    starts = both_columns(start_ref[0:1, :], start_ref[0:1, :])
    index = base + lax.broadcasted_iota(jnp.int32, (1, rows), 1)
    index = both_columns(index, index)

    def work(kb, cols):
        at = pl.ds(pl.multiple_of(kb * BLK, BLK), BLK)
        key_index = base - (total - rows) + kb * BLK + lax.broadcasted_iota(jnp.int32, (BLK, 1), 0)
        seen = (key_index >= starts[:, cols]) & (key_index <= index[:, cols])
        for p in range(pairs):
            lanes = slice(p * PAIR, (p + 1) * PAIR)
            s = jnp.where(seen, dot(k_ref[at, lanes], q2_ref[p, cols, :], NT), MASKED)
            m_old = m_ref[p, 0:1, cols]
            m_new = jnp.maximum(m_old, jnp.max(s, axis=0, keepdims=True))
            scale = jnp.exp(m_old - m_new)
            e = jnp.exp(s - m_new)
            m_ref[p, 0:1, cols] = m_new
            l_ref[p, 0:1, cols] = l_ref[p, 0:1, cols] * scale + jnp.sum(e, axis=0, keepdims=True)
            acc_ref[p, :, cols] = acc_ref[p, :, cols] * scale + dot(vt_ref[lanes, at], e.astype(bf16))

    key_loops(scal_ref, total // BLK, (total - rows) // BLK, work)
    for p in range(pairs):
        total_p = l_ref[p, 0:1, :]
        acc = acc_ref[p] / total_p
        lse_ref[p, 0:1, :] = m_ref[p, 0:1, :] + jnp.log(total_p)
        for qb in range(rows // BLK):
            first = acc[:HEAD, 2 * qb * BLK : (2 * qb + 1) * BLK]
            second = acc[HEAD:, (2 * qb + 1) * BLK : (2 * qb + 2) * BLK]
            o_ref[qb * BLK : (qb + 1) * BLK, p * PAIR : (p + 1) * PAIR] = jnp.transpose(
                jnp.concatenate([first, second], axis=0)
            ).astype(bf16)


def attend(scalars, q, start_rows, k, vt):
    rows, width = q.shape
    total = k.shape[0]
    pairs = width // PAIR
    return pl.pallas_call(
        attend_kernel,
        grid=(1,),
        in_specs=[
            pl.BlockSpec(memory_space=pltpu.SMEM),
            whole(rows, width),
            whole(8, rows),
            whole(total, width),
            whole(width, total),
        ],
        out_specs=[whole(rows, width), whole(pairs, 8, 2 * rows)],
        out_shape=[
            jax.ShapeDtypeStruct((rows, width), bf16),
            jax.ShapeDtypeStruct((pairs, 8, 2 * rows), f32),
        ],
        scratch_shapes=[
            pltpu.VMEM((pairs, 2 * rows, PAIR), bf16),
            pltpu.VMEM((pairs, 8, 2 * rows), f32),
            pltpu.VMEM((pairs, 8, 2 * rows), f32),
            pltpu.VMEM((pairs, PAIR, 2 * rows), f32),
        ],
        compiler_params=pltpu.CompilerParams(vmem_limit_bytes=ROOM_ATTEND << 20),
        cost_estimate=SMALL,
        name="attend",
    )(scalars, q, start_rows, k, vt)


def attend_back_kernel(
    scal_ref, q_ref, g_ref, o_ref, lse_ref, start_ref, k_ref, v_ref,
    dq_ref, dk_ref, dv_ref, q2_ref, g2_ref, delta_ref, acc_ref,
):
    rows, total = q_ref.shape[0], k_ref.shape[0]
    pairs = q_ref.shape[1] // PAIR
    base = scal_ref[0]
    dk_ref[...] = jnp.zeros_like(dk_ref)
    dv_ref[...] = jnp.zeros_like(dv_ref)
    acc_ref[...] = jnp.zeros_like(acc_ref)
    which = lax.broadcasted_iota(jnp.int32, (8, PAIR), 0)
    lane = lax.broadcasted_iota(jnp.int32, (8, PAIR), 1)
    chosen = (which == lane // HEAD).astype(f32)
    for p in range(pairs):
        lanes = slice(p * PAIR, (p + 1) * PAIR)
        g = g_ref[:, lanes]
        q2_ref[p] = both_heads(q_ref[:, lanes])
        g2_ref[p] = both_heads(g)
        delta = lax.dot_general(
            chosen,
            g.astype(f32) * o_ref[:, lanes].astype(f32),
            NT,
            precision=lax.Precision.HIGHEST,
            preferred_element_type=f32,
        )
        delta_ref[p, 0:1, :] = both_columns(delta[0:1, :], delta[1:2, :])
    starts = both_columns(start_ref[0:1, :], start_ref[0:1, :])
    index = base + lax.broadcasted_iota(jnp.int32, (1, rows), 1)
    index = both_columns(index, index)

    def work(kb, cols):
        at = pl.ds(pl.multiple_of(kb * BLK, BLK), BLK)
        key_index = base - (total - rows) + kb * BLK + lax.broadcasted_iota(jnp.int32, (BLK, 1), 0)
        seen = (key_index >= starts[:, cols]) & (key_index <= index[:, cols])
        for p in range(pairs):
            lanes = slice(p * PAIR, (p + 1) * PAIR)
            keys, q2, g2 = k_ref[at, lanes], q2_ref[p, cols, :], g2_ref[p, cols, :]
            s = jnp.where(seen, dot(keys, q2, NT), MASKED)
            prob = jnp.exp(s - lse_ref[p, 0:1, cols])
            d_prob = dot(v_ref[at, lanes], g2, NT)
            d_score = (prob * (d_prob - delta_ref[p, 0:1, cols])).astype(bf16)
            dv_ref[at, lanes] = dot(prob.astype(bf16), g2).astype(bf16)
            dk_ref[at, lanes] = dot(d_score, q2).astype(bf16)
            acc_ref[p, cols, :] += dot(d_score, keys, TN)

    key_loops(scal_ref, total // BLK, (total - rows) // BLK, work)
    low = low_lanes()
    for p in range(pairs):
        for qb in range(rows // BLK):
            first = acc_ref[p, 2 * qb * BLK : (2 * qb + 1) * BLK, :]
            second = acc_ref[p, (2 * qb + 1) * BLK : (2 * qb + 2) * BLK, :]
            dq_ref[qb * BLK : (qb + 1) * BLK, p * PAIR : (p + 1) * PAIR] = jnp.where(
                low, first, second
            ).astype(bf16)


def attend_back(scalars, q, g, o, lse, start_rows, k, v):
    rows, width = q.shape
    total = k.shape[0]
    pairs = width // PAIR
    return pl.pallas_call(
        attend_back_kernel,
        grid=(1,),
        in_specs=[
            pl.BlockSpec(memory_space=pltpu.SMEM),
            whole(rows, width),
            whole(rows, width),
            whole(rows, width),
            whole(pairs, 8, 2 * rows),
            whole(8, rows),
            whole(total, width),
            whole(total, width),
        ],
        out_specs=[whole(rows, width), whole(total, width), whole(total, width)],
        out_shape=[
            jax.ShapeDtypeStruct((rows, width), bf16),
            jax.ShapeDtypeStruct((total, width), bf16),
            jax.ShapeDtypeStruct((total, width), bf16),
        ],
        scratch_shapes=[
            pltpu.VMEM((pairs, 2 * rows, PAIR), bf16),
            pltpu.VMEM((pairs, 2 * rows, PAIR), bf16),
            pltpu.VMEM((pairs, 8, 2 * rows), f32),
            pltpu.VMEM((pairs, 2 * rows, PAIR), f32),
        ],
        compiler_params=pltpu.CompilerParams(vmem_limit_bytes=ROOM_ATTEND << 20),
        cost_estimate=SMALL,
        name="attend_back",
    )(scalars, q, g, o, lse, start_rows, k, v)


def ffn_kernel(
    where_ref, a_ref, up0_ref, up1_ref, dn0_ref, dn1_ref, outa_ref, outb_ref, vec_ref, mix_ref,
    hid_ref, slope_ref, out_ref, acc_ref,
):
    step = pl.program_id(0)
    over_a = outa_ref.shape[1]
    over_b = mix_ref.shape[1] - over_a
    hidden = pl.num_programs(0) * 2 * BLK

    @pl.when(step == 0)
    def _():
        acc_ref[...] = dot(mix_ref[:, :over_a], outa_ref[...], NT) + dot(
            mix_ref[:, over_a:], outb_ref[:, :over_b], NT
        )

    a = a_ref[...]
    total = acc_ref[...]
    for i, (up, down) in enumerate(((up0_ref, dn0_ref), (up1_ref, dn1_ref))):
        at = slice(i * BLK, (i + 1) * BLK)
        first = 9 * D + where_ref[0] * hidden + (2 * step + i) * BLK
        u = dot(a, up[...]) + vec_ref[:, pl.ds(pl.multiple_of(first, BLK), BLK)]
        phi = 0.5 * (1.0 + lax.erf(u * (1.0 / math.sqrt(2.0))))
        slope = phi + u * jnp.exp(-0.5 * u * u) * (1.0 / math.sqrt(2.0 * math.pi))
        slope_ref[:, at] = slope.astype(bf16)
        low = (u * phi).astype(bf16)
        hid_ref[:, at] = low
        total = total + dot(low, down[...], NT)
    acc_ref[...] = total

    @pl.when(step == pl.num_programs(0) - 1)
    def _():
        out_ref[...] = acc_ref[...].astype(bf16)


def ffn_weights(hidden, skip):
    steps = hidden // BLK
    return [
        pl.BlockSpec((D, BLK), lambda i: (0, 2 * i)),
        pl.BlockSpec((D, BLK), lambda i: (0, 2 * i + 1)),
        pl.BlockSpec((D, BLK), lambda i: (0, skip + 2 * i)),
        pl.BlockSpec((D, BLK), lambda i: (0, skip + 2 * i + 1)),
        pl.BlockSpec((D, BLK), lambda i: (0, steps)),
        pl.BlockSpec((D, BLK), lambda i: (0, skip + steps)),
    ]


def ffn_forward(where, a, wa, wb, skip, vec, mixed, hidden):
    rows, width = a.shape[0], mixed.shape[1]
    wide = pl.BlockSpec((rows, 2 * BLK), lambda i: (0, i))
    return call(
        ffn_kernel,
        "ffn_forward",
        (hidden // (2 * BLK),),
        [SCALARS, whole(rows, D)]
        + ffn_weights(hidden, skip)
        + [whole(*vec.shape), whole(rows, width)],
        [wide, wide, whole(rows, D)],
        shaped(((rows, hidden), bf16), ((rows, hidden), bf16), ((rows, D), bf16)),
        [pltpu.VMEM((rows, D), f32)],
        room=24,
    )(where, a, wa, wa, wb, wb, wa, wb, vec, mixed)


def ffn_back_kernel(
    where_ref, g_ref, a_ref, up0_ref, up1_ref, dn0_ref, dn1_ref, outa_ref, outb_ref,
    slope_ref, hid_ref, mix_ref,
    ka_ref, sa_ref, kb_ref, sb_ref, da_ref, gmix_ref, sum_ref, ay_ref, gy_ref, gx_ref,
):
    step = pl.program_id(0)
    last = pl.num_programs(0) - 1
    over_a = outa_ref.shape[1]
    over_b = mix_ref.shape[1] - over_a
    half = ka_ref.shape[0]
    part = half // 8

    @pl.when(step == 0)
    def _():
        da_ref[...] = jnp.zeros_like(da_ref)
        for turned, split_y, split_x in (
            (jnp.transpose(a_ref[...]), ay_ref, None),
            (jnp.transpose(g_ref[...]), gy_ref, gx_ref),
        ):
            for z in range(4):
                for y in range(2):
                    row = (2 * z + y) * 2 * part
                    to = pl.multiple_of((where_ref[2] ^ y) * half + 2 * z * part, 16)
                    split_y[pl.ds(to, 2 * part), :] = turned[row : row + 2 * part]
                    for x in range(2) if split_x is not None else ():
                        to = pl.multiple_of((where_ref[3] ^ x) * half + (2 * z + y) * part, 16)
                        split_x[pl.ds(to, part), :] = turned[row + x * part : row + (x + 1) * part]

    @pl.when(step < last)
    def _():
        g = g_ref[...]
        total = da_ref[...]
        grad = dot(gx_ref[...], hid_ref[...]).astype(bf16)
        kb_ref[...], sb_ref[...] = grad[:half], grad[half:]
        for i, (up, down) in enumerate(((up0_ref, dn0_ref), (up1_ref, dn1_ref))):
            at = slice(i * BLK, (i + 1) * BLK)
            d_pre = (dot(g, down[...]) * slope_ref[:, at].astype(f32)).astype(bf16)
            sum_ref[:, at] = jnp.sum(d_pre.astype(f32), axis=0, keepdims=True)
            grad = dot(ay_ref[...], d_pre).astype(bf16)
            ka_ref[:, at], sa_ref[:, at] = grad[:half], grad[half:]
            total = total + dot(d_pre, up[...], NT)
        da_ref[...] = total

    @pl.when(step == last)
    def _():
        g = g_ref[...]
        gmix_ref[:, :over_a] = dot(g, outa_ref[...]).astype(bf16)
        gmix_ref[:, over_a:] = dot(g, outb_ref[:, :over_b]).astype(bf16)
        grad = dot(gy_ref[...], mix_ref[:, :over_a]).astype(bf16)
        ka_ref[:, :over_a], sa_ref[:, :over_a] = grad[:half], grad[half:]
        grad = dot(gx_ref[...], mix_ref[:, over_a:]).astype(bf16)
        kb_ref[:, :over_b], sb_ref[:, :over_b] = grad[:half], grad[half:]


def ffn_backward(where, g, a, wa, wb, skip, slope, hid, mixed):
    rows, width = mixed.shape
    hidden = hid.shape[1]
    steps = hidden // (2 * BLK)
    upto = lambda i: (0, jnp.minimum(i, steps - 1))
    weights = []
    for spec in ffn_weights(hidden, skip):
        weights.append(
            pl.BlockSpec(spec.block_shape, lambda i, f=spec.index_map: f(jnp.minimum(i, steps - 1)))
        )
    wide = pl.BlockSpec((rows, 2 * BLK), upto)
    split = pl.BlockSpec((D // 2, 2 * BLK), lambda i: (0, i))
    wide_a, wide_b = hidden + BLK, hidden + width - BLK
    return call(
        ffn_back_kernel,
        "ffn_backward",
        (steps + 1,),
        [SCALARS, whole(rows, D), whole(rows, D)] + weights + [wide, wide, whole(rows, width)],
        [split] * 4
        + [whole(rows, D), whole(rows, width), pl.BlockSpec((1, 2 * BLK), upto)],
        shaped(
            *[((D // 2, wide_a), bf16)] * 2,
            *[((D // 2, wide_b), bf16)] * 2,
            ((rows, D), f32),
            ((rows, width), bf16),
            ((1, hidden), f32),
        ),
        [pltpu.VMEM((D, rows), bf16)] * 3,
        room=32,
    )(where, g, a, wa, wa, wb, wb, wa, wb, slope, hid, mixed)


def with_half(where_ref, da_ref, back_refs):
    half = sum(ref[...].astype(f32) for ref in back_refs)
    zero = jnp.zeros_like(half)
    first = jnp.where(where_ref[0] == 0, half, zero)
    return da_ref[...] + jnp.concatenate([first, half - first], axis=1)


def joint_kernel(where_ref, vec_ref, da_ref, db_ref, *refs):
    *back_refs, out_ref = refs
    da = with_half(where_ref, da_ref, back_refs)
    out_ref[...] = (da * vec_ref[:, :D] + db_ref[...] * vec_ref[:, 2 * D : 3 * D]).astype(bf16)


def row_call(kernel, name, where, vec, rows_in, outs, steps=4):
    rows = rows_in[0].shape[0]
    block = lambda width: pl.BlockSpec((rows // steps, width), lambda i: (i, 0))
    return call(
        kernel,
        name,
        (steps,),
        [SCALARS, whole(*vec.shape)] + [block(m.shape[1]) for m in rows_in],
        [block(shape[1]) for shape, _ in outs],
        shaped(*outs),
    )(where, vec, *rows_in)


def next_kernel(where_ref, vec_ref, grad_ref, own_ref, got_ref, x_ref, out_ref, low_ref):
    unit, inverse = unit_rows(x_ref[...].astype(f32))
    joint = own_ref[...].astype(f32) + got_ref[...].astype(f32)
    centered = joint - jnp.mean(joint, axis=-1, keepdims=True)
    grad = grad_ref[...].astype(f32) + inverse * (
        centered - unit * jnp.mean(joint * unit, axis=-1, keepdims=True)
    )
    out_ref[...] = grad
    low_ref[...] = grad.astype(bf16)


def vector_kernel(where_ref, qkv_ref, up_ref, grad_ref, x_ref, da_ref, db_ref, *refs):
    *back_refs, out_ref = refs
    core = where_ref[0]
    width, hidden = qkv_ref.shape[1] // 3, up_ref.shape[1]

    @pl.when(pl.program_id(0) == 0)
    def _():
        out_ref[...] = jnp.zeros_like(out_ref)
        for c in range(3):
            to = pl.multiple_of((6 + c) * D + core * width, PAIR)
            out_ref[:, pl.ds(to, width)] = qkv_ref[:, c * width : (c + 1) * width]
        out_ref[:, pl.ds(pl.multiple_of(9 * D + core * hidden, PAIR), hidden)] = up_ref[...]

    unit, _ = unit_rows(x_ref[...].astype(f32))
    da, db = with_half(where_ref, da_ref, back_refs), db_ref[...]
    first = (core == 0).astype(f32)
    bias = jnp.sum(grad_ref[...].astype(f32), axis=0, keepdims=True) * first
    for i, term in enumerate((da * unit, da, db * unit, db)):
        out_ref[:, i * D : (i + 1) * D] += jnp.sum(term, axis=0, keepdims=True)
    out_ref[:, 4 * D : 5 * D] += bias
    out_ref[:, 5 * D : 6 * D] += bias


def vector_row(where, qkv_sum, up_sum, grad, x, da, db, back):
    rows, steps = grad.shape[0], 4
    block = lambda width: pl.BlockSpec((rows // steps, width), lambda i: (i, 0))
    rows_in = [grad, x, da, db] + list(back)
    size = 9 * D + FF
    return call(
        vector_kernel,
        "vector_row",
        (steps,),
        [SCALARS, whole(*qkv_sum.shape), whole(*up_sum.shape)] + [block(m.shape[1]) for m in rows_in],
        [whole(1, size)],
        shaped(((1, size), f32)),
    )(where, qkv_sum, up_sum, *rows_in)[0]


def settle_kernel(counts, where_ref, *refs):
    refs = list(refs)
    terms = [[refs.pop(0) for _ in range(n)] for n in counts]
    moms, refs = refs[:KINDS], refs[KINDS:]
    grads, refs = refs[:KINDS], refs[KINDS:]
    news, refs = refs[:KINDS], refs[KINDS:]
    *sends, pad_ref = refs
    layers, _, rows, width = moms[0].shape
    hidden = moms[2].shape[2]
    cut = 3 * width // 256 * 128 + 128
    pad_ref[...] = jnp.zeros_like(pad_ref)

    def total(parts, at):
        return sum(part[:, at].astype(f32) for part in parts)

    for layer in range(layers):
        first = total(terms[2], slice(layer * cut, (layer + 1) * cut))
        skip, rest = layers * cut, 3 * width - cut
        second = total(terms[2], slice(skip + layer * rest, skip + (layer + 1) * rest))
        qkv = jnp.concatenate([first, second], axis=1)
        up = total(terms[layer], slice(0, hidden))
        out_a = total(terms[layer], slice(hidden, hidden + BLK))
        down = total(terms[layer], slice(hidden + BLK, 2 * hidden + BLK))
        out_b = total(terms[layer], slice(2 * hidden + BLK, 2 * hidden + width))
        out = jnp.concatenate([out_a, out_b], axis=1)
        for c in range(3):
            grad = qkv[:, c * width : (c + 1) * width]
            new = MOMENTUM * moms[0][layer, c] + grad
            grads[0][layer, c], news[0][layer, c] = grad, new
            pad_ref[layer, :, c * width : (c + 1) * width] = new.astype(bf16)
        for kind, grad in ((1, out), (2, up), (3, down)):
            new = MOMENTUM * moms[kind][layer] + grad
            grads[kind][layer], news[kind][layer] = grad, new
            pad_ref[layer, :, kind * hidden : kind * hidden + grad.shape[1]] = new.astype(bf16)
    for by, send in enumerate(sends):
        at = pl.ds(pl.multiple_of((where_ref[1] ^ by) * hidden, PAIR), hidden)
        for layer in range(layers):
            send[layer] = pad_ref[layer, :, at]


def settle(where, terms, moms):
    rows, hidden = moms[2].shape[1:]
    flat = [m for group in terms for m in group]
    send = (LAYERS, rows, hidden)
    outs = [(m.shape, f32) for m in moms] * 2 + [(send, bf16)] * KINDS
    got = call(
        functools.partial(settle_kernel, [len(group) for group in terms]),
        "settle",
        (1,),
        [SCALARS] + [whole(*m.shape) for m in flat] + [whole(*m.shape) for m in moms],
        [whole(*shape) for shape, _ in outs],
        shaped(*outs),
        [pltpu.VMEM((LAYERS, rows, KINDS * hidden), bf16)],
        room=24,
    )(where, *flat, *moms)
    return got[:KINDS], got[KINDS : 2 * KINDS], got[2 * KINDS :]


def update_kernel(where_ref, *refs):
    backs, swapped = refs[:KINDS], refs[KINDS]
    masters, outs = refs[KINDS + 1 : 2 * KINDS + 1], refs[2 * KINDS + 1 : 3 * KINDS + 1]
    kept_ref = refs[-1]
    layers, _, rows, width = masters[0].shape
    for slot in range(KINDS):
        kept_ref[slot] = backs[slot][0]
    for layer in range(layers):
        mine = where_ref[0] == layer
        for kind in range(KINDS):
            slot = where_ref[1] ^ kind
            made = jnp.where(mine, kept_ref[slot], swapped[slot]).astype(f32)
            made = made * (-RATE_MAT * math.sqrt((3 * D, D, FF, FF)[kind]))
            if kind == 0:
                for c in range(3):
                    step = made[:, c * width : (c + 1) * width]
                    outs[0][layer, c] = masters[0][layer, c] * SHRINK + step
            else:
                outs[kind][layer] = masters[kind][layer] * SHRINK + made[:, : outs[kind].shape[2]]


def update(where, backs, swapped, masters):
    return call(
        update_kernel,
        "update",
        (1,),
        [SCALARS] + [whole(*m.shape) for m in (*backs, swapped, *masters)],
        [whole(*m.shape) for m in masters],
        shaped(*[(m.shape, f32) for m in masters]),
        [pltpu.VMEM(swapped.shape, bf16)],
    )(where, *backs, swapped, *masters)


def orth_kernel(inner, *refs):
    ins, outs = refs[:2], refs[2 : 2 + KINDS]
    x_ref, gram_ref, mix_ref = refs[2 + KINDS :]
    rows, width = ins[0].shape
    part, chunk = 256, 512
    blocks = rows // part
    total = jnp.zeros((1, 1), f32)
    for ref in ins:
        for i in range(blocks):
            v = ref[i * part : (i + 1) * part, :].astype(f32)
            total = total + jnp.sum(v * v).reshape(1, 1)
    inverse = 1.0 / (jnp.sqrt(total) + 1e-07)
    for i, ref in enumerate(ins):
        x_ref[:, i * width : (i + 1) * width] = (ref[...].astype(f32) * inverse).astype(bf16)

    def spread(ref, i, j, value):
        low = value.astype(bf16)
        ref[i * part : (i + 1) * part, j * part : (j + 1) * part] = low
        if j > i:
            ref[j * part : (j + 1) * part, i * part : (i + 1) * part] = jnp.transpose(low)

    def mixer():
        for i in range(blocks):
            at = slice(i * part, (i + 1) * part)
            gram = dot(x_ref[at, :], x_ref[i * part :, :], NT)
            for j in range(i, blocks):
                spread(gram_ref, i, j, gram[:, (j - i) * part : (j - i + 1) * part])
        for i in range(blocks):
            at = slice(i * part, (i + 1) * part)
            square = dot(gram_ref[at, :], gram_ref[:, i * part :])
            mixed = NS_B * gram_ref[at, i * part :].astype(f32) + NS_C * square
            for j in range(i, blocks):
                spread(mix_ref, i, j, mixed[:, (j - i) * part : (j - i + 1) * part])

    def sweep(_, carry):
        mixer()
        for c in range(2 * width // chunk):
            cols = slice(c * chunk, (c + 1) * chunk)
            x = x_ref[:, cols]
            y = NS_A * x.astype(f32) + dot(mix_ref[...], x)
            x_ref[:, cols] = y.astype(bf16)
        return carry

    lax.fori_loop(0, 4, sweep, 0)
    mixer()
    size = outs[0].shape[1]
    firsts = [by * inner * size for by in range(KINDS)]
    mine = jnp.concatenate([mix_ref[first : first + size, :] for first in firsts], axis=0)
    for half in range(2):
        cols = slice(half * width, (half + 1) * width)
        made = dot(mine, x_ref[:, cols])
        for by, out in enumerate(outs):
            x = x_ref[firsts[by] : firsts[by] + size, cols].astype(f32)
            out[half] = (NS_A * x + made[by * size : (by + 1) * size]).astype(bf16)


def orthogonalize(parts, inner):
    rows, width = parts[0].shape
    shape = (2, rows // (KINDS * inner), width)
    return call(
        functools.partial(orth_kernel, inner),
        "orthogonalize",
        (1,),
        [whole(rows, width)] * 2,
        [whole(*shape)] * KINDS,
        shaped(*[(shape, bf16)] * KINDS),
        [
            pltpu.VMEM((rows, 2 * width), bf16),
            pltpu.VMEM((rows, rows), bf16),
            pltpu.VMEM((rows, rows), bf16),
        ],
        room=32,
    )(*parts)


def shards(
    tokens,
    cotangent,
    w_qkv,
    w_out,
    w_up,
    w_down,
    mom_qkv,
    mom_out,
    mom_up,
    mom_down,
    vectors,
    vec_first,
    vec_second,
    lengths,
):
    tok_rows = tokens.shape[0]
    row_part = w_qkv.shape[1]
    head_part = w_qkv.shape[-1]
    hidden_part = w_up.shape[-1]
    widths = (3 * head_part, head_part, hidden_part, hidden_part)
    over = BLK
    cut_qkv = widths[0] // 256 * 128 + 128
    cut_rest = hidden_part + over
    skip = cut_rest // BLK
    fsdp_count = lax.axis_size("fsdp")
    core = lax.axis_index("tp")
    longest = SEQ_DEV * fsdp_count
    span = (tok_rows + longest - 2) // tok_rows
    where = place()

    def stored(qkv, out, up, down):
        return [qkv.transpose(0, 2, 1, 3), out.transpose(0, 2, 1), up, down.transpose(0, 2, 1)]

    def unstored(qkv, out, up, down):
        return [qkv.transpose(0, 2, 1, 3), out.transpose(0, 2, 1), up, down.transpose(0, 2, 1)]

    def qkv_piece(mats, layer):
        low = mats[0][layer].astype(bf16)
        return jnp.concatenate([low[c] for c in range(3)], axis=1)

    def rest_piece(mats, layer):
        out, up, down = [m[layer].astype(bf16) for m in mats[1:]]
        return jnp.concatenate([up, out[:, :over], down, out[:, over:]], axis=1)

    masters = stored(w_qkv, w_out, w_up, w_down)
    moments = stored(mom_qkv, mom_out, mom_up, mom_down)

    qkv_0 = Task(gather_steps(where, qkv_piece(masters, 0), cut_qkv))
    vecs = [vectors[layer : layer + 1] for layer in range(LAYERS)]
    a0, b0, half = norm_rows(where, vecs[0], tokens)
    rest, half, lengths, *later = advance(
        [qkv_0], rest_piece(masters, 0), half, lengths, *masters
    )
    rest_0 = Task(gather_steps(where, rest, cut_rest, True))
    half, lengths, *later = advance([qkv_0, rest_0], half, lengths, *later)
    win_0 = Task(window_steps(half, span))
    tables, start_rows, scalars = setup(lengths, where, tok_rows, (span + 1) * tok_rows)
    tables, start_rows, scalars, *later = advance(
        [qkv_0, rest_0, win_0], tables, start_rows, scalars, *later
    )
    qkv_1 = Task(gather_steps(where, qkv_piece(later, 1), cut_qkv))
    wq0 = qkv_0.result
    tables, *later = advance([win_0], tables, *later)
    q, k, v, vt = qkv_forward(where, a0, *win_0.result, wq0, vecs[0], tables)
    q, k, v, vt, *later = advance([rest_0], q, k, v, vt, *later)
    rest_1 = Task(gather_steps(where, rest_piece(later, 1), cut_rest, False, True))
    mixed, lse = attend(scalars, q, start_rows, k, vt)
    mixed, lse, b0 = advance([rest_0, rest_1], mixed, lse, b0)
    mixed, b0, wa, wb = advance([rest_1], mixed, b0, *rest_0.result)
    hid, slope, partial = ffn_forward(where, b0, wa, wb, 0, vecs[0], mixed, hidden_part)
    partial = advance([qkv_1], partial)
    kept = [(tokens, a0, win_0.result, b0, q, k, v, mixed, lse, hid, slope)]
    weights = [(wq0, wa, wb, 0)]
    got = core_swap(partial)
    partial, got = advance([rest_1, qkv_1], partial, got)
    x1, a1, b1, half = norm_rows(where, vecs[1], tokens, vecs[0], partial, got)
    win_1 = Task(window_steps(half, span))
    a1, b1 = advance([win_1, qkv_1], a1, b1)
    a1, b1 = advance([win_1], a1, b1)
    wq1 = qkv_1.result
    q, k, v, vt = qkv_forward(where, a1, *win_1.result, wq1, vecs[1], tables)
    mixed, lse = attend(scalars, q, start_rows, k, vt)
    mixed, lse, b1, q, k, v = advance([rest_1], mixed, lse, b1, q, k, v)
    wa, wb = rest_1.result
    hid, slope, partial = ffn_forward(where, b1, wa, wb, 0, vecs[1], mixed, hidden_part)
    kept.append((x1, a1, win_1.result, b1, q, k, v, mixed, lse, hid, slope))
    weights.append((wq1, wa, wb, 0))

    def own_gradients(grad_low, layer):
        _, _, _, b, _, _, _, mixed, _, hid, slope = kept[layer]
        _, wa, wb, skip = weights[layer]
        return ffn_backward(where, grad_low, b, wa, wb, skip, slope, hid, mixed)

    def attention_gradients(g_mixed, layer, more=()):
        _, a, win, _, q, k, v, mixed, lse, _, _ = kept[layer]
        dq, dk, dv = attend_back(scalars, q, g_mixed, mixed, lse, start_rows, k, v)
        return qkv_backward(where, dq, dk, dv, a, *win, weights[layer][0], tables, more)

    def joint_of(da, db, back, layer):
        rows_in = [da, db] + list(back)
        return row_call(joint_kernel, "joint", where, vecs[layer], rows_in, [(da.shape, bf16)])[0]

    def next_grad(grad, joint, got, layer):
        outs = [(joint.shape, f32), (joint.shape, bf16)]
        rows_in = [grad, joint, got, kept[layer][0]]
        return row_call(next_kernel, "next_grad", where, vecs[layer], rows_in, outs)

    *split, db1, g_mixed, up_sum1 = own_gradients(cotangent, 1)
    *split, g_mixed, partial, db1 = advance([], *split, g_mixed, partial, db1)
    rest_1 = Task(scatter_steps(where, *split, True))
    *split1, da1, keep, give, pre_sum1 = attention_gradients(g_mixed, 1)
    *split1, da1, keep, give, partial = advance([], *split1, da1, keep, give, partial)
    back_1 = Task(window_back_steps(keep, give, span))
    da1, partial = advance([back_1, rest_1], da1, partial)
    da1, partial = advance([back_1, rest_1], da1, partial)
    joint = joint_of(da1, db1, back_1.result, 1)
    got = core_swap(joint)
    grad_x0, grad_low = next_grad(cotangent, joint, got, 1)
    *split, db0, g_mixed, up_sum0 = own_gradients(grad_low, 0)
    *split, g_mixed, da1, db0, partial = advance([rest_1], *split, g_mixed, da1, db0, partial)
    *split, g_mixed = advance([rest_1], *split, g_mixed)
    rest_0 = Task(scatter_steps(where, *split, False, True))
    *split, da0, keep, give, pre_sum0 = attention_gradients(g_mixed, 0, split1)
    *split, da0, keep, give, da1, db1, partial = advance(
        [rest_0, rest_1], *split, da0, keep, give, da1, db1, partial
    )
    both_qkv = Task(scatter_steps(where, *split, True))
    back_0 = Task(window_back_steps(keep, give, span))
    da0, da1, db1, partial = advance([rest_0, back_0, both_qkv], da0, da1, db1, partial)
    da0, da1, db1, partial = advance([both_qkv], da0, da1, db1, partial)
    row_1 = vector_row(where, pre_sum1, up_sum1, cotangent, kept[1][0], da1, db1, back_1.result)
    da0, row_1, partial = advance([both_qkv, back_0, rest_0], da0, row_1, partial)
    da0, row_1, partial = advance([both_qkv], da0, row_1, partial)
    joint = joint_of(da0, db0, back_0.result, 0)
    got = core_swap(joint)
    row_0 = vector_row(where, pre_sum0, up_sum0, grad_x0, kept[0][0], da0, db0, back_0.result)
    grad_in, _ = next_grad(grad_x0, joint, got, 0)
    got = core_swap(partial)
    block_out = norm_rows(where, vecs[1], kept[1][0], vecs[1], partial, got, False)[0]
    grad_in, block_out, row_0, row_1 = advance(
        [both_qkv, rest_0], grad_in, block_out, row_0, row_1
    )
    vec_sum = Task(sum_steps(jnp.concatenate([row_0, row_1], axis=0)))
    terms = [rest_0.result, rest_1.result, both_qkv.result]
    grads, new_moms, blocks = settle(where, terms, moments)
    owned = Task(owner_steps(blocks[0], blocks[1:]))
    advance([owned, vec_sum])
    advance([owned])
    while owned.flying is not None or vec_sum.flying is not None:
        advance([owned, vec_sum])

    inner = fsdp_count // KINDS
    made = orthogonalize(owned.result, inner)
    backs = [made[0]] + [
        permute(made[by], xor_pairs(fsdp_count, by * inner)) for by in range(1, KINDS)
    ]
    swapped = core_swap(jnp.stack([m[1] for m in backs]))
    new_weights = update(where, backs, swapped, masters)

    grad_vectors = vec_sum.result
    first_new = BETA_ONE * vec_first + (1.0 - BETA_ONE) * grad_vectors
    second_new = BETA_TWO * vec_second + (1.0 - BETA_TWO) * grad_vectors * grad_vectors
    first_hat = first_new / (1.0 - BETA_ONE**STEP)
    second_hat = second_new / (1.0 - BETA_TWO**STEP)
    vectors_new = vectors - RATE_VEC * first_hat / (jnp.sqrt(second_hat) + ADAM_EPS)
    return (
        block_out,
        grad_in,
        *unstored(*grads),
        *unstored(*new_moms),
        *unstored(*new_weights),
        first_new,
        second_new,
        vectors_new,
        grad_vectors[:, 9 * D :],
    )


def solution(mesh):
    weights = (
        P(None, "fsdp", None, "tp"),
        P(None, "tp", "fsdp"),
        P(None, "fsdp", "tp"),
        P(None, "tp", "fsdp"),
    )
    rows = (P("fsdp", None), P("fsdp", None))
    return jax.shard_map(
        shards,
        mesh=mesh,
        in_specs=rows + weights + weights + (P(), P(), P(), P()),
        out_specs=rows + weights + weights + weights + (P(), P(), P(), P()),
        check_vma=False,
    )
```

```python
import functools
import math

import jax
import jax.numpy as jnp
import numpy as np
from jax import lax
from jax.experimental import pallas as pl
from jax.experimental.pallas import tpu as pltpu
from jax.sharding import PartitionSpec as P

D = 768
HEAD = 64
ROT = 16
FF = 3072
LAYERS = 2
SEQ_DEV = 64
STEP = 10
PAIR = 2 * HEAD
BLK = 256
KINDS = 4

MASKED = -1000000000.0
EPS_NORM = 1e-05
NS_A = 3.4445
NS_B = -4.775
NS_C = 2.0315
MOMENTUM = 0.95
RATE_MAT = 0.02
SHRINK = 0.99
RATE_VEC = 0.25
BETA_ONE = 0.9
BETA_TWO = 0.95
ADAM_EPS = 1e-08
ROOM_ATTEND = 16

bf16 = jnp.bfloat16
f32 = jnp.float32


def permute(x, pairs):
    return lax.ppermute(x, "fsdp", pairs)


def xor_pairs(count, by):
    return [(i, i ^ by) for i in range(count)]


def core_swap(x):
    count = lax.axis_size("tp")
    return lax.ppermute(x, "tp", [(i, i ^ 1) for i in range(count)])


def shifted(x, by):
    devices = lax.axis_size("fsdp")
    return lax.ppermute(
        x, "fsdp", [(i, i + by) for i in range(devices) if 0 <= i + by < devices]
    )


def on_grid():
    return lax.axis_size("fsdp") == 16


def place():
    index = lax.axis_index("fsdp")
    inner = lax.axis_size("fsdp") // KINDS
    bits = [(index // 2) % 2, index % 2] if on_grid() else [index * 0, index * 0]
    parts = [lax.axis_index("tp"), index // inner, *bits, index]
    return jnp.stack([p.astype(jnp.int32) for p in parts])


class Task:
    def __init__(self, steps):
        self.steps = steps
        self.result = None
        self.flying = None
        self.resume(None)

    def resume(self, arrived):
        try:
            self.flying = self.steps.send(arrived)
        except StopIteration as stop:
            self.result = stop.value
            self.flying = None


def advance(tasks, *arrays):
    tasks = [t for t in tasks if t.flying is not None]
    arrived, arrays = lax.optimization_barrier(([t.flying for t in tasks], arrays))
    for task, got in zip(tasks, arrived):
        task.resume(got)
    return arrays if len(arrays) != 1 else arrays[0]


def gather_steps(where, piece, cut, apart=False, pause=False):
    rows, cols = piece.shape
    if not on_grid():
        full = lax.all_gather(piece, "fsdp", axis=0, tiled=True)
        return full[:, :cut], full[:, cut:]
        yield
    got = []
    for group in ((1, 2), (3,)) if apart else ((1, 2, 3),):
        got += yield [permute(piece, xor_pairs(16, 4 * by)) for by in group]
    part_a, part_b = join_planes(where, [piece] + got, cut)
    if pause:
        part_a, part_b = yield [part_a, part_b]
    got_a, got_b = yield [permute(part_a, xor_pairs(16, 1)), permute(part_b, xor_pairs(16, 2))]
    part_a, part_b = join_chips(where, part_a, got_a, part_b, got_b, False)
    got_a, got_b = yield [permute(part_a, xor_pairs(16, 2)), permute(part_b, xor_pairs(16, 1))]
    part_a, part_b = join_chips(where, part_a, got_a, part_b, got_b, True)
    return part_a.reshape(16 * rows, -1), part_b.reshape(16 * rows, -1)


def natural(keep, send, axis):
    shape = (4, 1, 2, -1) if axis == 1 else (4, 2, 1, -1)
    parts = [m.reshape(shape + (m.shape[-1],)) for m in (keep, send)]
    full = jnp.concatenate(parts, axis=axis)
    return full.reshape(-1, keep.shape[-1])


def scatter_steps(where, keep_a, send_a, keep_b, send_b, pause=False, apart=False):
    if not on_grid():
        full = jnp.concatenate([natural(keep_a, send_a, 1), natural(keep_b, send_b, 2)], axis=1)
        return [lax.psum_scatter(full, "fsdp", scatter_dimension=0, tiled=True)]
        yield
    got_a, got_b = yield [permute(send_a, xor_pairs(16, 2)), permute(send_b, xor_pairs(16, 1))]
    keep_a, send_a, keep_b, send_b = add_split(where, keep_a, got_a, keep_b, got_b)
    if pause:
        keep_a, send_a, keep_b, send_b = yield [keep_a, send_a, keep_b, send_b]
    got_a, got_b = yield [permute(send_a, xor_pairs(16, 1)), permute(send_b, xor_pairs(16, 2))]
    own, *sends = add_planes(where, keep_a, got_a, keep_b, got_b)
    if pause:
        own, *sends = yield [own, *sends]
    got = [own]
    for group in ((0, 1), (2,)) if apart else ((0, 1, 2),):
        got += yield [permute(sends[i], xor_pairs(16, 4 * (i + 1))) for i in group]
    return got


def window_steps(half, span):
    got = yield [shifted(half, step) for step in range(span, 0, -1)]
    got = jnp.concatenate(got, axis=0)
    (other,) = yield [core_swap(got)]
    return got, other


def window_back_steps(keep, give, span, pause=False):
    (got,) = yield [core_swap(give)]
    half = (keep.astype(f32) + got.astype(f32)).astype(bf16).reshape(span, -1, keep.shape[-1])
    if pause:
        (half,) = yield [half]
    back = yield [shifted(half[span - step], -step) for step in range(span, 0, -1)]
    return back


def sum_steps(x):
    count = lax.axis_size("fsdp")
    step = 1
    while step < count:
        got = yield [permute(x, xor_pairs(count, step * by)) for by in (1, 2, 3)]
        x = (x + got[0]) + (got[1] + got[2])
        step *= 4
    (got,) = yield [core_swap(x)]
    return x + got


def owner_steps(own, sends):
    count = lax.axis_size("fsdp")
    inner = count // KINDS
    core = lax.axis_index("tp")
    rows, width = own.shape[1:]
    got = yield [permute(sends[by - 1], xor_pairs(count, by * inner)) for by in range(1, KINDS)]
    terms = [own] + list(got)
    give = jnp.stack([jnp.where(core == 0, m[1], m[0]) for m in terms])
    part_a = jnp.stack([jnp.where(core == 0, m[0], m[1]) for m in terms])
    part_a, part_b = yield [part_a, core_swap(give)]
    bits = inner.bit_length() - 1
    shape = (KINDS,) + (1,) * bits + (rows, width)
    part_a, part_b = part_a.reshape(shape), part_b.reshape(shape)
    for step in range(bits):
        bit_a, bit_b = step, bits - 1 - step
        got_a, got_b = yield [
            permute(part_a, xor_pairs(count, 1 << bit_a)),
            permute(part_b, xor_pairs(count, 1 << bit_b)),
        ]
        part_a = jnp.concatenate([part_a, got_a], axis=1 + bit_a)
        part_b = jnp.concatenate([part_b, got_b], axis=1 + bit_b)
    return [m.reshape(count * rows, width) for m in (part_a, part_b)]


SMALL = pl.CostEstimate(flops=1, bytes_accessed=1, transcendentals=0)
SCALARS = pl.BlockSpec(memory_space=pltpu.SMEM)
NT = (((1,), (1,)), ((), ()))
TN = (((0,), (0,)), ((), ()))


def dot(a, b, how=(((1,), (0,)), ((), ()))):
    return lax.dot_general(a, b, how, preferred_element_type=f32)


def whole(*shape):
    return pl.BlockSpec(shape, lambda *_: (0,) * len(shape))


def shaped(*shapes_and_kinds):
    return [jax.ShapeDtypeStruct(shape, kind) for shape, kind in shapes_and_kinds]


def call(kernel, name, grid, in_specs, out_specs, out_shape, scratch=(), room=8):
    return pl.pallas_call(
        kernel,
        grid=grid,
        in_specs=in_specs,
        out_specs=out_specs,
        out_shape=out_shape,
        scratch_shapes=list(scratch),
        compiler_params=pltpu.CompilerParams(vmem_limit_bytes=room << 20),
        cost_estimate=SMALL,
        name=name,
    )


def join_planes_kernel(cut, where_ref, *refs):
    *pieces, out_a, out_b = refs
    quarter = where_ref[1]
    for by, piece in enumerate(pieces):
        plane = quarter ^ by
        out_a[plane] = piece[:, :cut]
        out_b[plane] = piece[:, cut:]


def join_planes(where, pieces, cut):
    rows, cols = pieces[0].shape
    shapes = [(4, rows, cut), (4, rows, cols - cut)]
    return call(
        functools.partial(join_planes_kernel, cut),
        "join_planes",
        (1,),
        [SCALARS] + [whole(rows, cols)] * 4,
        [whole(*shape) for shape in shapes],
        shaped(*[(shape, bf16) for shape in shapes]),
    )(where, *pieces)


def join_chips_kernel(last, where_ref, own_a, got_a, own_b, got_b, out_a, out_b):
    y, x = where_ref[2], where_ref[3]
    if not last:
        out_a[0, x], out_a[0, 1 - x] = own_a[0], got_a[0]
        out_b[0, y], out_b[0, 1 - y] = own_b[0], got_b[0]
    else:
        out_a[0, y], out_a[0, 1 - y] = own_a[0], got_a[0]
        for side in range(2):
            out_b[0, side, x], out_b[0, side, 1 - x] = own_b[0, side], got_b[0, side]


def join_chips(where, own_a, got_a, own_b, got_b, last):
    rows = own_a.shape[-2]
    ins, outs = ((2, rows), (2, 2, rows)) if last else ((rows,), (2, rows))

    def spec(shape, width):
        return pl.BlockSpec((1,) + shape + (width,), lambda i: (i,) + (0,) * (len(shape) + 1))

    wide_a, wide_b = own_a.shape[-1], own_b.shape[-1]
    return call(
        functools.partial(join_chips_kernel, last),
        "join_chips",
        (4,),
        [SCALARS, spec(ins, wide_a), spec(ins, wide_a), spec(ins, wide_b), spec(ins, wide_b)],
        [spec(outs, wide_a), spec(outs, wide_b)],
        shaped(((4,) + outs + (wide_a,), bf16), ((4,) + outs + (wide_b,), bf16)),
    )(where, own_a, got_a, own_b, got_b)


def add_split_kernel(where_ref, keep_a, got_a, keep_b, got_b, out_ka, out_sa, out_kb, out_sb):
    rows = keep_a.shape[0] // 8
    for bit, keep, got, out_k, out_s in (
        (where_ref[3], keep_a, got_a, out_ka, out_sa),
        (where_ref[2], keep_b, got_b, out_kb, out_sb),
    ):
        for z in range(4):
            for flip, out in ((0, out_k), (1, out_s)):
                at = pl.ds(pl.multiple_of((2 * z + (bit ^ flip)) * rows, 16), rows)
                total = keep[at, :].astype(f32) + got[at, :].astype(f32)
                out[z * rows : (z + 1) * rows, :] = total.astype(bf16)


def add_split(where, keep_a, got_a, keep_b, got_b):
    rows, wide_a = keep_a.shape
    wide_b = keep_b.shape[1]
    outs = [(rows // 2, wide_a)] * 2 + [(rows // 2, wide_b)] * 2
    return call(
        add_split_kernel,
        "add_split",
        (1,),
        [SCALARS] + [whole(rows, wide_a)] * 2 + [whole(rows, wide_b)] * 2,
        [whole(*shape) for shape in outs],
        shaped(*[(shape, bf16) for shape in outs]),
        room=12,
    )(where, keep_a, got_a, keep_b, got_b)


def add_planes_kernel(where_ref, keep_a, got_a, keep_b, got_b, *outs):
    rows = keep_a.shape[0] // 4
    cut = keep_a.shape[1]
    for by, out in enumerate(outs):
        at = pl.ds(pl.multiple_of((where_ref[1] ^ by) * rows, 16), rows)
        out[:, :cut] = (keep_a[at, :].astype(f32) + got_a[at, :].astype(f32)).astype(bf16)
        out[:, cut:] = (keep_b[at, :].astype(f32) + got_b[at, :].astype(f32)).astype(bf16)


def add_planes(where, keep_a, got_a, keep_b, got_b):
    rows, wide_a = keep_a.shape
    wide_b = keep_b.shape[1]
    shape = (rows // 4, wide_a + wide_b)
    return call(
        add_planes_kernel,
        "add_planes",
        (1,),
        [SCALARS] + [whole(rows, wide_a)] * 2 + [whole(rows, wide_b)] * 2,
        [whole(*shape)] * 4,
        shaped(*[(shape, bf16)] * 4),
    )(where, keep_a, got_a, keep_b, got_b)


def setup_kernel(len_ref, where_ref, freq_ref, table_ref, start_ref, scal_ref):
    rows, total = start_ref.shape[1], table_ref.shape[1]
    base = where_ref[4] * rows
    first = base - (total - rows)
    half = ROT // 2

    def starts_of(index):
        end, out = jnp.int32(0), jnp.zeros_like(index)
        for i in range(len_ref.shape[0]):
            end = end + len_ref[i]
            out = jnp.where(index >= end, end, out)
        return out

    lane = lax.broadcasted_iota(jnp.int32, (BLK, PAIR), 1) % HEAD
    for c in range(total // BLK):
        at = slice(c * BLK, (c + 1) * BLK)
        index = first + c * BLK + lax.broadcasted_iota(jnp.int32, (BLK, PAIR), 0)
        phase = (index - starts_of(index)).astype(f32) * freq_ref[...]
        sine = jnp.sin(phase)
        table_ref[0, at, :] = jnp.cos(phase)
        table_ref[1, at, :] = jnp.where(lane < half, -sine, 0.0)
        table_ref[2, at, :] = jnp.where((lane >= half) & (lane < ROT), sine, 0.0)
    start_ref[...] = starts_of(base + lax.broadcasted_iota(jnp.int32, start_ref.shape, 1))
    own = (total - rows) // BLK
    scal_ref[0] = base
    scal_ref[1] = jnp.minimum((starts_of(base + BLK) - first) // BLK, own)
    scal_ref[2] = (starts_of(base) - first) // BLK


def setup(lengths, where, rows, total):
    lane = np.arange(PAIR) % HEAD
    freqs = np.exp((lane % (ROT // 2)) * (-2.0 * math.log(10000.0) / ROT))
    freqs = np.where(lane < ROT, freqs, 0.0).astype(np.float32)[None]
    return call(
        setup_kernel,
        "setup",
        (1,),
        [SCALARS, SCALARS, whole(1, PAIR)],
        [whole(3, total, PAIR), whole(8, rows), SCALARS],
        shaped(((3, total, PAIR), f32), ((8, rows), jnp.int32), ((3,), jnp.int32)),
        room=8,
    )(lengths, where, jnp.asarray(freqs))


def unit_rows(x):
    centered = x - jnp.mean(x, axis=-1, keepdims=True)
    inverse = lax.rsqrt(jnp.mean(centered * centered, axis=-1, keepdims=True) + EPS_NORM)
    return centered * inverse, inverse


def norm_kernel(where_ref, vec_ref, x_ref, a_ref, b_ref, half_ref):
    unit, _ = unit_rows(x_ref[...].astype(f32))
    a = (unit * vec_ref[:, :D] + vec_ref[:, D : 2 * D]).astype(bf16)
    a_ref[...] = a
    b_ref[...] = (unit * vec_ref[:, 2 * D : 3 * D] + vec_ref[:, 3 * D : 4 * D]).astype(bf16)
    half_ref[...] = jnp.where(where_ref[0] == 0, a[:, : D // 2], a[:, D // 2 :])


def add_norm_kernel(where_ref, old_ref, vec_ref, x_ref, part_ref, got_ref, new_ref, *outs):
    x = x_ref[...].astype(f32) + part_ref[...].astype(f32) + got_ref[...].astype(f32)
    x = x + old_ref[:, 4 * D : 5 * D] + old_ref[:, 5 * D : 6 * D]
    new_ref[...] = x
    if outs:
        norm_kernel(where_ref, vec_ref, new_ref, *outs)


def norm_rows(where, vec, x, old_vec=None, part=None, got=None, normed=True):
    rows = x.shape[0]
    step = rows // 4
    block = lambda width: pl.BlockSpec((step, width), lambda i: (i, 0))
    flat = whole(1, vec.shape[1])
    out = [((rows, D), bf16), ((rows, D), bf16), ((rows, D // 2), bf16)] if normed else []
    if part is None:
        specs, kernel, args = [flat, block(D)], norm_kernel, (vec, x)
    else:
        specs, kernel = [flat, flat] + [block(D)] * 3, add_norm_kernel
        args, out = (old_vec, vec, x, part, got), [((rows, D), f32)] + out
    return call(
        kernel,
        "norm_rows",
        (4,),
        [SCALARS] + specs,
        [block(shape[1]) for shape, _ in out],
        shaped(*out),
    )(where, *args)


def rope(u, tables, sign):
    half = ROT // 2
    return u * tables[0] + sign * (
        pltpu.roll(u, PAIR - half, 1) * tables[1] + pltpu.roll(u, half, 1) * tables[2]
    )


def window_block(before, where_ref, own_ref, half_ref, other_ref):
    half, other = half_ref[...], other_ref[...]
    first = jnp.where(where_ref[0] == 0, half, other)
    second = jnp.where(where_ref[0] == 0, other, half)
    earlier = jnp.concatenate([first, second], axis=1)
    return jnp.where(pl.program_id(0) < before, earlier, own_ref[...])


def qkv_kernel(
    before, where_ref, own_ref, half_ref, other_ref, wa_ref, wb_ref, vec_ref, table_ref,
    q_ref, k_ref, v_ref, vt_ref,
):
    width = q_ref.shape[1]
    over = wa_ref.shape[1] - width
    a = window_block(before, where_ref, own_ref, half_ref, other_ref)
    tables = [table_ref[i] for i in range(3)]
    bias = [
        vec_ref[:, pl.ds(pl.multiple_of((6 + c) * D + where_ref[0] * width, PAIR), width)]
        for c in range(3)
    ]

    @pl.when(pl.program_id(0) == before)
    def _():
        pre = dot(a, wa_ref[:, :width]) + bias[0]
        for p in range(width // PAIR):
            at = slice(p * PAIR, (p + 1) * PAIR)
            q_ref[:, at] = (rope(pre[:, at], tables, 1.0) * HEAD ** (-0.5)).astype(bf16)

    front, rest = dot(a, wa_ref[:, width:]), dot(a, wb_ref[...])
    values = (rest[:, width - over :] + bias[2]).astype(bf16)
    v_ref[...] = values
    vt_ref[...] = jnp.transpose(values)
    pre = jnp.concatenate([front, rest[:, : width - over]], axis=1) + bias[1]
    for p in range(width // PAIR):
        at = slice(p * PAIR, (p + 1) * PAIR)
        k_ref[:, at] = rope(pre[:, at], tables, 1.0).astype(bf16)


def window_specs(rows, before):
    earlier = pl.BlockSpec((rows, D // 2), lambda i: (jnp.minimum(i, before - 1), 0))
    return [whole(rows, D), earlier, earlier]


def qkv_forward(where, own, half, other, weights, vec, tables):
    rows, total = own.shape[0], tables.shape[1]
    width = (weights[0].shape[1] + weights[1].shape[1]) // 3
    before = total // rows - 1
    flat = pl.BlockSpec((rows, width), lambda i: (i, 0))
    return call(
        functools.partial(qkv_kernel, before),
        "qkv_forward",
        (total // rows,),
        [SCALARS]
        + window_specs(rows, before)
        + [whole(*weights[0].shape), whole(*weights[1].shape), whole(*vec.shape)]
        + [pl.BlockSpec((3, rows, PAIR), lambda i: (0, i, 0))],
        [whole(rows, width), flat, flat, pl.BlockSpec((width, rows), lambda i: (0, i))],
        shaped(
            ((rows, width), bf16),
            ((total, width), bf16),
            ((total, width), bf16),
            ((width, total), bf16),
        ),
        room=14,
    )(where, own, half, other, *weights, vec, tables)


def qkv_back_kernel(
    before, more, where_ref, dq_ref, dk_ref, dv_ref, own_ref, half_ref, other_ref, wa_ref, wb_ref, table_ref,
    *refs,
):
    more_refs, refs = refs[:more], refs[more:]
    ka_ref, sa_ref, kb_ref, sb_ref, da_ref, keep_ref, give_ref, sum_ref, pre_ref, acc_ref = refs
    width = dq_ref.shape[1]
    cut = wa_ref.shape[1]
    step = pl.program_id(0)
    tables = [table_ref[i] for i in range(3)]

    @pl.when(step == 0)
    def _():
        acc_ref[...] = jnp.zeros_like(acc_ref)
        sum_ref[...] = jnp.zeros_like(sum_ref)

    def put(at, value):
        pre_ref[:, at] = value
        sum_ref[:, at] += jnp.sum(value.astype(f32), axis=0, keepdims=True)

    turned = jnp.transpose(window_block(before, where_ref, own_ref, half_ref, other_ref))
    for p in range(width // PAIR):
        at = slice(p * PAIR, (p + 1) * PAIR)
        put(
            slice(width + p * PAIR, width + (p + 1) * PAIR),
            rope(dk_ref[:, at].astype(f32), tables, -1.0).astype(bf16),
        )
    put(slice(2 * width, 3 * width), dv_ref[...])

    @pl.when(step < before)
    def _():
        acc_ref[:, width:] += dot(turned, pre_ref[:, width:])
        da = dot(pre_ref[:, width:cut], wa_ref[:, width:], NT) + dot(pre_ref[:, cut:], wb_ref[...], NT)
        low, high = da[:, : D // 2].astype(bf16), da[:, D // 2 :].astype(bf16)
        keep_ref[...] = jnp.where(where_ref[0] == 0, low, high)
        give_ref[...] = jnp.where(where_ref[0] == 0, high, low)

    @pl.when(step == before)
    def _():
        for p in range(width // PAIR):
            at = slice(p * PAIR, (p + 1) * PAIR)
            query = rope(dq_ref[:, at].astype(f32), tables, -1.0) * HEAD ** (-0.5)
            put(at, query.astype(bf16))
        acc_ref[...] += dot(turned, pre_ref[...])
        da_ref[...] = dot(pre_ref[:, :cut], wa_ref[...], NT) + dot(pre_ref[:, cut:], wb_ref[...], NT)
        part = acc_ref.shape[0] // 16
        for flip, out_a, out_b in ((0, ka_ref, kb_ref), (1, sa_ref, sb_ref)):
            for z in range(4):
                at = pl.ds(pl.multiple_of((2 * z + (where_ref[2] ^ flip)) * 2 * part, 16), 2 * part)
                out_a[2 * z * part : (2 * z + 2) * part, :cut] = acc_ref[at, :cut].astype(bf16)
                for y in range(2):
                    row = (2 * z + y) * part
                    at = pl.ds(pl.multiple_of(2 * row + (where_ref[3] ^ flip) * part, 16), part)
                    out_b[row : row + part, : 3 * width - cut] = acc_ref[at, cut:].astype(bf16)
        for ref, out in zip(more_refs, (ka_ref, sa_ref, kb_ref, sb_ref)):
            out[:, ref.shape[1] :] = ref[...]


def qkv_backward(where, dq, dk, dv, own, half, other, weights, tables, more=()):
    rows, width = dq.shape
    total = tables.shape[1]
    before = total // rows - 1
    cut = weights[0].shape[1]
    each = pl.BlockSpec((rows, width), lambda i: (i, 0))
    earlier = pl.BlockSpec((rows, D // 2), lambda i: (jnp.minimum(i, before - 1), 0))
    times = 2 if more else 1
    splits = [(D // 2, times * cut)] * 2 + [(D // 2, times * (3 * width - cut))] * 2
    return call(
        functools.partial(qkv_back_kernel, before, len(more)),
        "qkv_backward",
        (total // rows,),
        [SCALARS, whole(rows, width), each, each]
        + window_specs(rows, before)
        + [whole(*weights[0].shape), whole(*weights[1].shape)]
        + [pl.BlockSpec((3, rows, PAIR), lambda i: (0, i, 0))]
        + [whole(*m.shape) for m in more],
        [whole(*shape) for shape in splits]
        + [whole(rows, D), earlier, earlier, whole(1, 3 * width)],
        shaped(
            *[(shape, bf16) for shape in splits],
            ((rows, D), f32),
            ((total - rows, D // 2), bf16),
            ((total - rows, D // 2), bf16),
            ((1, 3 * width), f32),
        ),
        [pltpu.VMEM((rows, 3 * width), bf16), pltpu.VMEM((D, 3 * width), f32)],
        room=18,
    )(where, dq, dk, dv, own, half, other, *weights, tables, *more)


def low_lanes():
    return lax.broadcasted_iota(jnp.int32, (1, PAIR), 1) < HEAD


def both_heads(x):
    low = low_lanes()
    zero = jnp.zeros_like(x[:BLK])
    parts = []
    for at in range(0, x.shape[0], BLK):
        block = x[at : at + BLK]
        parts += [jnp.where(low, block, zero), jnp.where(low, zero, block)]
    return jnp.concatenate(parts, axis=0)


def both_columns(first, second):
    parts = []
    for at in range(0, first.shape[1], BLK):
        parts += [first[:, at : at + BLK], second[:, at : at + BLK]]
    return jnp.concatenate(parts, axis=1)


def key_loops(scal_ref, blocks, own, work):
    work(own + 1, slice(2 * BLK, 4 * BLK))
    low_all, low_first = scal_ref[1], scal_ref[2]

    def full(i, carry):
        work(own - i, slice(0, 4 * BLK))
        return carry

    def first_only(i, carry):
        work(low_all - 1 - i, slice(0, 2 * BLK))
        return carry

    lax.fori_loop(0, own - low_all + 1, full, 0)
    lax.fori_loop(0, low_all - low_first, first_only, 0)


def attend_kernel(scal_ref, q_ref, start_ref, k_ref, vt_ref, o_ref, lse_ref, q2_ref, m_ref, l_ref, acc_ref):
    rows, total = q_ref.shape[0], k_ref.shape[0]
    pairs = q_ref.shape[1] // PAIR
    base = scal_ref[0]
    m_ref[...] = jnp.full_like(m_ref, -1e30)
    l_ref[...] = jnp.zeros_like(l_ref)
    acc_ref[...] = jnp.zeros_like(acc_ref)
    for p in range(pairs):
        q2_ref[p] = both_heads(q_ref[:, p * PAIR : (p + 1) * PAIR])
    starts = both_columns(start_ref[0:1, :], start_ref[0:1, :])
    index = base + lax.broadcasted_iota(jnp.int32, (1, rows), 1)
    index = both_columns(index, index)

    def work(kb, cols):
        at = pl.ds(pl.multiple_of(kb * BLK, BLK), BLK)
        key_index = base - (total - rows) + kb * BLK + lax.broadcasted_iota(jnp.int32, (BLK, 1), 0)
        seen = (key_index >= starts[:, cols]) & (key_index <= index[:, cols])
        for p in range(pairs):
            lanes = slice(p * PAIR, (p + 1) * PAIR)
            s = jnp.where(seen, dot(k_ref[at, lanes], q2_ref[p, cols, :], NT), MASKED)
            m_old = m_ref[p, 0:1, cols]
            m_new = jnp.maximum(m_old, jnp.max(s, axis=0, keepdims=True))
            scale = jnp.exp(m_old - m_new)
            e = jnp.exp(s - m_new)
            m_ref[p, 0:1, cols] = m_new
            l_ref[p, 0:1, cols] = l_ref[p, 0:1, cols] * scale + jnp.sum(e, axis=0, keepdims=True)
            acc_ref[p, :, cols] = acc_ref[p, :, cols] * scale + dot(vt_ref[lanes, at], e.astype(bf16))

    key_loops(scal_ref, total // BLK, (total - rows) // BLK, work)
    for p in range(pairs):
        total_p = l_ref[p, 0:1, :]
        acc = acc_ref[p] / total_p
        lse_ref[p, 0:1, :] = m_ref[p, 0:1, :] + jnp.log(total_p)
        for qb in range(rows // BLK):
            first = acc[:HEAD, 2 * qb * BLK : (2 * qb + 1) * BLK]
            second = acc[HEAD:, (2 * qb + 1) * BLK : (2 * qb + 2) * BLK]
            o_ref[qb * BLK : (qb + 1) * BLK, p * PAIR : (p + 1) * PAIR] = jnp.transpose(
                jnp.concatenate([first, second], axis=0)
            ).astype(bf16)


def attend(scalars, q, start_rows, k, vt):
    rows, width = q.shape
    total = k.shape[0]
    pairs = width // PAIR
    return pl.pallas_call(
        attend_kernel,
        grid=(1,),
        in_specs=[
            pl.BlockSpec(memory_space=pltpu.SMEM),
            whole(rows, width),
            whole(8, rows),
            whole(total, width),
            whole(width, total),
        ],
        out_specs=[whole(rows, width), whole(pairs, 8, 2 * rows)],
        out_shape=[
            jax.ShapeDtypeStruct((rows, width), bf16),
            jax.ShapeDtypeStruct((pairs, 8, 2 * rows), f32),
        ],
        scratch_shapes=[
            pltpu.VMEM((pairs, 2 * rows, PAIR), bf16),
            pltpu.VMEM((pairs, 8, 2 * rows), f32),
            pltpu.VMEM((pairs, 8, 2 * rows), f32),
            pltpu.VMEM((pairs, PAIR, 2 * rows), f32),
        ],
        compiler_params=pltpu.CompilerParams(vmem_limit_bytes=ROOM_ATTEND << 20),
        cost_estimate=SMALL,
        name="attend",
    )(scalars, q, start_rows, k, vt)


def attend_back_kernel(
    scal_ref, q_ref, g_ref, o_ref, lse_ref, start_ref, k_ref, v_ref,
    dq_ref, dk_ref, dv_ref, q2_ref, g2_ref, delta_ref, acc_ref,
):
    rows, total = q_ref.shape[0], k_ref.shape[0]
    pairs = q_ref.shape[1] // PAIR
    base = scal_ref[0]
    dk_ref[...] = jnp.zeros_like(dk_ref)
    dv_ref[...] = jnp.zeros_like(dv_ref)
    acc_ref[...] = jnp.zeros_like(acc_ref)
    which = lax.broadcasted_iota(jnp.int32, (8, PAIR), 0)
    lane = lax.broadcasted_iota(jnp.int32, (8, PAIR), 1)
    chosen = (which == lane // HEAD).astype(f32)
    for p in range(pairs):
        lanes = slice(p * PAIR, (p + 1) * PAIR)
        g = g_ref[:, lanes]
        q2_ref[p] = both_heads(q_ref[:, lanes])
        g2_ref[p] = both_heads(g)
        delta = lax.dot_general(
            chosen,
            g.astype(f32) * o_ref[:, lanes].astype(f32),
            NT,
            precision=lax.Precision.HIGHEST,
            preferred_element_type=f32,
        )
        delta_ref[p, 0:1, :] = both_columns(delta[0:1, :], delta[1:2, :])
    starts = both_columns(start_ref[0:1, :], start_ref[0:1, :])
    index = base + lax.broadcasted_iota(jnp.int32, (1, rows), 1)
    index = both_columns(index, index)

    def work(kb, cols):
        at = pl.ds(pl.multiple_of(kb * BLK, BLK), BLK)
        key_index = base - (total - rows) + kb * BLK + lax.broadcasted_iota(jnp.int32, (BLK, 1), 0)
        seen = (key_index >= starts[:, cols]) & (key_index <= index[:, cols])
        for p in range(pairs):
            lanes = slice(p * PAIR, (p + 1) * PAIR)
            keys, q2, g2 = k_ref[at, lanes], q2_ref[p, cols, :], g2_ref[p, cols, :]
            s = jnp.where(seen, dot(keys, q2, NT), MASKED)
            prob = jnp.exp(s - lse_ref[p, 0:1, cols])
            d_prob = dot(v_ref[at, lanes], g2, NT)
            d_score = (prob * (d_prob - delta_ref[p, 0:1, cols])).astype(bf16)
            dv_ref[at, lanes] = dot(prob.astype(bf16), g2).astype(bf16)
            dk_ref[at, lanes] = dot(d_score, q2).astype(bf16)
            acc_ref[p, cols, :] += dot(d_score, keys, TN)

    key_loops(scal_ref, total // BLK, (total - rows) // BLK, work)
    low = low_lanes()
    for p in range(pairs):
        for qb in range(rows // BLK):
            first = acc_ref[p, 2 * qb * BLK : (2 * qb + 1) * BLK, :]
            second = acc_ref[p, (2 * qb + 1) * BLK : (2 * qb + 2) * BLK, :]
            dq_ref[qb * BLK : (qb + 1) * BLK, p * PAIR : (p + 1) * PAIR] = jnp.where(
                low, first, second
            ).astype(bf16)


def attend_back(scalars, q, g, o, lse, start_rows, k, v):
    rows, width = q.shape
    total = k.shape[0]
    pairs = width // PAIR
    return pl.pallas_call(
        attend_back_kernel,
        grid=(1,),
        in_specs=[
            pl.BlockSpec(memory_space=pltpu.SMEM),
            whole(rows, width),
            whole(rows, width),
            whole(rows, width),
            whole(pairs, 8, 2 * rows),
            whole(8, rows),
            whole(total, width),
            whole(total, width),
        ],
        out_specs=[whole(rows, width), whole(total, width), whole(total, width)],
        out_shape=[
            jax.ShapeDtypeStruct((rows, width), bf16),
            jax.ShapeDtypeStruct((total, width), bf16),
            jax.ShapeDtypeStruct((total, width), bf16),
        ],
        scratch_shapes=[
            pltpu.VMEM((pairs, 2 * rows, PAIR), bf16),
            pltpu.VMEM((pairs, 2 * rows, PAIR), bf16),
            pltpu.VMEM((pairs, 8, 2 * rows), f32),
            pltpu.VMEM((pairs, 2 * rows, PAIR), f32),
        ],
        compiler_params=pltpu.CompilerParams(vmem_limit_bytes=ROOM_ATTEND << 20),
        cost_estimate=SMALL,
        name="attend_back",
    )(scalars, q, g, o, lse, start_rows, k, v)


def ffn_kernel(
    where_ref, a_ref, up0_ref, up1_ref, dn0_ref, dn1_ref, outa_ref, outb_ref, vec_ref, mix_ref,
    hid_ref, slope_ref, out_ref, acc_ref,
):
    step = pl.program_id(0)
    over_a = outa_ref.shape[1]
    over_b = mix_ref.shape[1] - over_a
    hidden = pl.num_programs(0) * 2 * BLK

    @pl.when(step == 0)
    def _():
        acc_ref[...] = dot(mix_ref[:, :over_a], outa_ref[...], NT) + dot(
            mix_ref[:, over_a:], outb_ref[:, :over_b], NT
        )

    a = a_ref[...]
    total = acc_ref[...]
    for i, (up, down) in enumerate(((up0_ref, dn0_ref), (up1_ref, dn1_ref))):
        at = slice(i * BLK, (i + 1) * BLK)
        first = 9 * D + where_ref[0] * hidden + (2 * step + i) * BLK
        u = dot(a, up[...]) + vec_ref[:, pl.ds(pl.multiple_of(first, BLK), BLK)]
        phi = 0.5 * (1.0 + lax.erf(u * (1.0 / math.sqrt(2.0))))
        slope = phi + u * jnp.exp(-0.5 * u * u) * (1.0 / math.sqrt(2.0 * math.pi))
        slope_ref[:, at] = slope.astype(bf16)
        low = (u * phi).astype(bf16)
        hid_ref[:, at] = low
        total = total + dot(low, down[...], NT)
    acc_ref[...] = total

    @pl.when(step == pl.num_programs(0) - 1)
    def _():
        out_ref[...] = acc_ref[...].astype(bf16)


def ffn_weights(hidden, skip):
    steps = hidden // BLK
    return [
        pl.BlockSpec((D, BLK), lambda i: (0, 2 * i)),
        pl.BlockSpec((D, BLK), lambda i: (0, 2 * i + 1)),
        pl.BlockSpec((D, BLK), lambda i: (0, skip + 2 * i)),
        pl.BlockSpec((D, BLK), lambda i: (0, skip + 2 * i + 1)),
        pl.BlockSpec((D, BLK), lambda i: (0, steps)),
        pl.BlockSpec((D, BLK), lambda i: (0, skip + steps)),
    ]


def ffn_forward(where, a, wa, wb, skip, vec, mixed, hidden):
    rows, width = a.shape[0], mixed.shape[1]
    wide = pl.BlockSpec((rows, 2 * BLK), lambda i: (0, i))
    return call(
        ffn_kernel,
        "ffn_forward",
        (hidden // (2 * BLK),),
        [SCALARS, whole(rows, D)]
        + ffn_weights(hidden, skip)
        + [whole(*vec.shape), whole(rows, width)],
        [wide, wide, whole(rows, D)],
        shaped(((rows, hidden), bf16), ((rows, hidden), bf16), ((rows, D), bf16)),
        [pltpu.VMEM((rows, D), f32)],
        room=12,
    )(where, a, wa, wa, wb, wb, wa, wb, vec, mixed)


def ffn_back_kernel(
    where_ref, g_ref, a_ref, up0_ref, up1_ref, dn0_ref, dn1_ref, outa_ref, outb_ref,
    slope_ref, hid_ref, mix_ref,
    ka_ref, sa_ref, kb_ref, sb_ref, da_ref, gmix_ref, sum_ref, ay_ref, gy_ref, gx_ref,
):
    step = pl.program_id(0)
    last = pl.num_programs(0) - 1
    over_a = outa_ref.shape[1]
    over_b = mix_ref.shape[1] - over_a
    half = ka_ref.shape[0]
    part = half // 8

    @pl.when(step == 0)
    def _():
        da_ref[...] = jnp.zeros_like(da_ref)
        for turned, split_y, split_x in (
            (jnp.transpose(a_ref[...]), ay_ref, None),
            (jnp.transpose(g_ref[...]), gy_ref, gx_ref),
        ):
            for z in range(4):
                for y in range(2):
                    row = (2 * z + y) * 2 * part
                    to = pl.multiple_of((where_ref[2] ^ y) * half + 2 * z * part, 16)
                    split_y[pl.ds(to, 2 * part), :] = turned[row : row + 2 * part]
                    for x in range(2) if split_x is not None else ():
                        to = pl.multiple_of((where_ref[3] ^ x) * half + (2 * z + y) * part, 16)
                        split_x[pl.ds(to, part), :] = turned[row + x * part : row + (x + 1) * part]

    @pl.when(step < last)
    def _():
        g = g_ref[...]
        total = da_ref[...]
        grad = dot(gx_ref[...], hid_ref[...]).astype(bf16)
        kb_ref[...], sb_ref[...] = grad[:half], grad[half:]
        for i, (up, down) in enumerate(((up0_ref, dn0_ref), (up1_ref, dn1_ref))):
            at = slice(i * BLK, (i + 1) * BLK)
            d_pre = (dot(g, down[...]) * slope_ref[:, at].astype(f32)).astype(bf16)
            sum_ref[:, at] = jnp.sum(d_pre.astype(f32), axis=0, keepdims=True)
            grad = dot(ay_ref[...], d_pre).astype(bf16)
            ka_ref[:, at], sa_ref[:, at] = grad[:half], grad[half:]
            total = total + dot(d_pre, up[...], NT)
        da_ref[...] = total

    @pl.when(step == last)
    def _():
        g = g_ref[...]
        gmix_ref[:, :over_a] = dot(g, outa_ref[...]).astype(bf16)
        gmix_ref[:, over_a:] = dot(g, outb_ref[:, :over_b]).astype(bf16)
        grad = dot(gy_ref[...], mix_ref[:, :over_a]).astype(bf16)
        ka_ref[:, :over_a], sa_ref[:, :over_a] = grad[:half], grad[half:]
        grad = dot(gx_ref[...], mix_ref[:, over_a:]).astype(bf16)
        kb_ref[:, :over_b], sb_ref[:, :over_b] = grad[:half], grad[half:]


def ffn_backward(where, g, a, wa, wb, skip, slope, hid, mixed):
    rows, width = mixed.shape
    hidden = hid.shape[1]
    steps = hidden // (2 * BLK)
    upto = lambda i: (0, jnp.minimum(i, steps - 1))
    weights = []
    for spec in ffn_weights(hidden, skip):
        weights.append(
            pl.BlockSpec(spec.block_shape, lambda i, f=spec.index_map: f(jnp.minimum(i, steps - 1)))
        )
    wide = pl.BlockSpec((rows, 2 * BLK), upto)
    split = pl.BlockSpec((D // 2, 2 * BLK), lambda i: (0, i))
    wide_a, wide_b = hidden + BLK, hidden + width - BLK
    return call(
        ffn_back_kernel,
        "ffn_backward",
        (steps + 1,),
        [SCALARS, whole(rows, D), whole(rows, D)] + weights + [wide, wide, whole(rows, width)],
        [split] * 4
        + [whole(rows, D), whole(rows, width), pl.BlockSpec((1, 2 * BLK), upto)],
        shaped(
            *[((D // 2, wide_a), bf16)] * 2,
            *[((D // 2, wide_b), bf16)] * 2,
            ((rows, D), f32),
            ((rows, width), bf16),
            ((1, hidden), f32),
        ),
        [pltpu.VMEM((D, rows), bf16)] * 3,
        room=18,
    )(where, g, a, wa, wa, wb, wb, wa, wb, slope, hid, mixed)


def with_half(where_ref, da_ref, back_refs):
    half = sum(ref[...].astype(f32) for ref in back_refs)
    zero = jnp.zeros_like(half)
    first = jnp.where(where_ref[0] == 0, half, zero)
    return da_ref[...] + jnp.concatenate([first, half - first], axis=1)


def joint_kernel(where_ref, vec_ref, da_ref, db_ref, *refs):
    *back_refs, out_ref = refs
    da = with_half(where_ref, da_ref, back_refs)
    out_ref[...] = (da * vec_ref[:, :D] + db_ref[...] * vec_ref[:, 2 * D : 3 * D]).astype(bf16)


def row_call(kernel, name, where, vec, rows_in, outs, steps=4):
    rows = rows_in[0].shape[0]
    block = lambda width: pl.BlockSpec((rows // steps, width), lambda i: (i, 0))
    return call(
        kernel,
        name,
        (steps,),
        [SCALARS, whole(*vec.shape)] + [block(m.shape[1]) for m in rows_in],
        [block(shape[1]) for shape, _ in outs],
        shaped(*outs),
    )(where, vec, *rows_in)


def next_kernel(where_ref, vec_ref, grad_ref, own_ref, got_ref, x_ref, out_ref, low_ref):
    unit, inverse = unit_rows(x_ref[...].astype(f32))
    joint = own_ref[...].astype(f32) + got_ref[...].astype(f32)
    centered = joint - jnp.mean(joint, axis=-1, keepdims=True)
    grad = grad_ref[...].astype(f32) + inverse * (
        centered - unit * jnp.mean(joint * unit, axis=-1, keepdims=True)
    )
    out_ref[...] = grad
    low_ref[...] = grad.astype(bf16)


def vector_kernel(where_ref, qkv_ref, up_ref, grad_ref, x_ref, da_ref, db_ref, *refs):
    *back_refs, out_ref = refs
    core = where_ref[0]
    width, hidden = qkv_ref.shape[1] // 3, up_ref.shape[1]

    @pl.when(pl.program_id(0) == 0)
    def _():
        out_ref[...] = jnp.zeros_like(out_ref)
        for c in range(3):
            to = pl.multiple_of((6 + c) * D + core * width, PAIR)
            out_ref[:, pl.ds(to, width)] = qkv_ref[:, c * width : (c + 1) * width]
        out_ref[:, pl.ds(pl.multiple_of(9 * D + core * hidden, PAIR), hidden)] = up_ref[...]

    unit, _ = unit_rows(x_ref[...].astype(f32))
    da, db = with_half(where_ref, da_ref, back_refs), db_ref[...]
    first = (core == 0).astype(f32)
    bias = jnp.sum(grad_ref[...].astype(f32), axis=0, keepdims=True) * first
    for i, term in enumerate((da * unit, da, db * unit, db)):
        out_ref[:, i * D : (i + 1) * D] += jnp.sum(term, axis=0, keepdims=True)
    out_ref[:, 4 * D : 5 * D] += bias
    out_ref[:, 5 * D : 6 * D] += bias


def vector_row(where, qkv_sum, up_sum, grad, x, da, db, back):
    rows, steps = grad.shape[0], 4
    block = lambda width: pl.BlockSpec((rows // steps, width), lambda i: (i, 0))
    rows_in = [grad, x, da, db] + list(back)
    size = 9 * D + FF
    return call(
        vector_kernel,
        "vector_row",
        (steps,),
        [SCALARS, whole(*qkv_sum.shape), whole(*up_sum.shape)] + [block(m.shape[1]) for m in rows_in],
        [whole(1, size)],
        shaped(((1, size), f32)),
    )(where, qkv_sum, up_sum, *rows_in)[0]


def settle_kernel(counts, where_ref, *refs):
    refs = list(refs)
    terms = [[refs.pop(0) for _ in range(n)] for n in counts]
    moms, refs = refs[:KINDS], refs[KINDS:]
    grads, refs = refs[:KINDS], refs[KINDS:]
    news, refs = refs[:KINDS], refs[KINDS:]
    *sends, pad_ref = refs
    layers, _, rows, width = moms[0].shape
    hidden = moms[2].shape[2]
    cut = 3 * width // 256 * 128 + 128
    pad_ref[...] = jnp.zeros_like(pad_ref)

    def total(parts, at):
        return sum(part[:, at].astype(f32) for part in parts)

    for layer in range(layers):
        first = total(terms[2], slice(layer * cut, (layer + 1) * cut))
        skip, rest = layers * cut, 3 * width - cut
        second = total(terms[2], slice(skip + layer * rest, skip + (layer + 1) * rest))
        qkv = jnp.concatenate([first, second], axis=1)
        up = total(terms[layer], slice(0, hidden))
        out_a = total(terms[layer], slice(hidden, hidden + BLK))
        down = total(terms[layer], slice(hidden + BLK, 2 * hidden + BLK))
        out_b = total(terms[layer], slice(2 * hidden + BLK, 2 * hidden + width))
        out = jnp.concatenate([out_a, out_b], axis=1)
        for c in range(3):
            grad = qkv[:, c * width : (c + 1) * width]
            new = MOMENTUM * moms[0][layer, c] + grad
            grads[0][layer, c], news[0][layer, c] = grad, new
            pad_ref[layer, :, c * width : (c + 1) * width] = new.astype(bf16)
        for kind, grad in ((1, out), (2, up), (3, down)):
            new = MOMENTUM * moms[kind][layer] + grad
            grads[kind][layer], news[kind][layer] = grad, new
            pad_ref[layer, :, kind * hidden : kind * hidden + grad.shape[1]] = new.astype(bf16)
    for by, send in enumerate(sends):
        at = pl.ds(pl.multiple_of((where_ref[1] ^ by) * hidden, PAIR), hidden)
        for layer in range(layers):
            send[layer] = pad_ref[layer, :, at]


def settle(where, terms, moms):
    rows, hidden = moms[2].shape[1:]
    flat = [m for group in terms for m in group]
    send = (LAYERS, rows, hidden)
    outs = [(m.shape, f32) for m in moms] * 2 + [(send, bf16)] * KINDS
    got = call(
        functools.partial(settle_kernel, [len(group) for group in terms]),
        "settle",
        (1,),
        [SCALARS] + [whole(*m.shape) for m in flat] + [whole(*m.shape) for m in moms],
        [whole(*shape) for shape, _ in outs],
        shaped(*outs),
        [pltpu.VMEM((LAYERS, rows, KINDS * hidden), bf16)],
        room=12,
    )(where, *flat, *moms)
    return got[:KINDS], got[KINDS : 2 * KINDS], got[2 * KINDS :]


def update_kernel(where_ref, *refs):
    backs, swapped = refs[:KINDS], refs[KINDS]
    masters, outs = refs[KINDS + 1 : 2 * KINDS + 1], refs[2 * KINDS + 1 : 3 * KINDS + 1]
    kept_ref = refs[-1]
    layers, _, rows, width = masters[0].shape
    for slot in range(KINDS):
        kept_ref[slot] = backs[slot][0]
    for layer in range(layers):
        mine = where_ref[0] == layer
        for kind in range(KINDS):
            slot = where_ref[1] ^ kind
            made = jnp.where(mine, kept_ref[slot], swapped[slot]).astype(f32)
            made = made * (-RATE_MAT * math.sqrt((3 * D, D, FF, FF)[kind]))
            if kind == 0:
                for c in range(3):
                    step = made[:, c * width : (c + 1) * width]
                    outs[0][layer, c] = masters[0][layer, c] * SHRINK + step
            else:
                outs[kind][layer] = masters[kind][layer] * SHRINK + made[:, : outs[kind].shape[2]]


def update(where, backs, swapped, masters):
    return call(
        update_kernel,
        "update",
        (1,),
        [SCALARS] + [whole(*m.shape) for m in (*backs, swapped, *masters)],
        [whole(*m.shape) for m in masters],
        shaped(*[(m.shape, f32) for m in masters]),
        [pltpu.VMEM(swapped.shape, bf16)],
    )(where, *backs, swapped, *masters)


def orth_kernel(inner, *refs):
    ins, outs = refs[:2], refs[2 : 2 + KINDS]
    x_ref, gram_ref, mix_ref = refs[2 + KINDS :]
    rows, width = ins[0].shape
    part, chunk = 256, 512
    blocks = rows // part
    total = jnp.zeros((1, 1), f32)
    for ref in ins:
        for i in range(blocks):
            v = ref[i * part : (i + 1) * part, :].astype(f32)
            total = total + jnp.sum(v * v).reshape(1, 1)
    inverse = 1.0 / (jnp.sqrt(total) + 1e-07)
    for i, ref in enumerate(ins):
        x_ref[:, i * width : (i + 1) * width] = (ref[...].astype(f32) * inverse).astype(bf16)

    def spread(ref, i, j, value):
        low = value.astype(bf16)
        ref[i * part : (i + 1) * part, j * part : (j + 1) * part] = low
        if j > i:
            ref[j * part : (j + 1) * part, i * part : (i + 1) * part] = jnp.transpose(low)

    def mixer():
        for i in range(blocks):
            at = slice(i * part, (i + 1) * part)
            gram = dot(x_ref[at, :], x_ref[i * part :, :], NT)
            for j in range(i, blocks):
                spread(gram_ref, i, j, gram[:, (j - i) * part : (j - i + 1) * part])
        for i in range(blocks):
            at = slice(i * part, (i + 1) * part)
            square = dot(gram_ref[at, :], gram_ref[:, i * part :])
            mixed = NS_B * gram_ref[at, i * part :].astype(f32) + NS_C * square
            for j in range(i, blocks):
                spread(mix_ref, i, j, mixed[:, (j - i) * part : (j - i + 1) * part])

    def sweep(_, carry):
        mixer()
        for c in range(2 * width // chunk):
            cols = slice(c * chunk, (c + 1) * chunk)
            x = x_ref[:, cols]
            y = NS_A * x.astype(f32) + dot(mix_ref[...], x)
            x_ref[:, cols] = y.astype(bf16)
        return carry

    lax.fori_loop(0, 4, sweep, 0)
    mixer()
    size = outs[0].shape[1]
    firsts = [by * inner * size for by in range(KINDS)]
    mine = jnp.concatenate([mix_ref[first : first + size, :] for first in firsts], axis=0)
    for half in range(2):
        cols = slice(half * width, (half + 1) * width)
        made = dot(mine, x_ref[:, cols])
        for by, out in enumerate(outs):
            x = x_ref[firsts[by] : firsts[by] + size, cols].astype(f32)
            out[half] = (NS_A * x + made[by * size : (by + 1) * size]).astype(bf16)


def orthogonalize(parts, inner):
    rows, width = parts[0].shape
    shape = (2, rows // (KINDS * inner), width)
    return call(
        functools.partial(orth_kernel, inner),
        "orthogonalize",
        (1,),
        [whole(rows, width)] * 2,
        [whole(*shape)] * KINDS,
        shaped(*[(shape, bf16)] * KINDS),
        [
            pltpu.VMEM((rows, 2 * width), bf16),
            pltpu.VMEM((rows, rows), bf16),
            pltpu.VMEM((rows, rows), bf16),
        ],
        room=20,
    )(*parts)


def shards(
    tokens,
    cotangent,
    w_qkv,
    w_out,
    w_up,
    w_down,
    mom_qkv,
    mom_out,
    mom_up,
    mom_down,
    vectors,
    vec_first,
    vec_second,
    lengths,
):
    tok_rows = tokens.shape[0]
    row_part = w_qkv.shape[1]
    head_part = w_qkv.shape[-1]
    hidden_part = w_up.shape[-1]
    widths = (3 * head_part, head_part, hidden_part, hidden_part)
    over = BLK
    cut_qkv = widths[0] // 256 * 128 + 128
    cut_rest = hidden_part + over
    skip = cut_rest // BLK
    fsdp_count = lax.axis_size("fsdp")
    core = lax.axis_index("tp")
    longest = SEQ_DEV * fsdp_count
    span = (tok_rows + longest - 2) // tok_rows
    where = place()

    def stored(qkv, out, up, down):
        return [qkv.transpose(0, 2, 1, 3), out.transpose(0, 2, 1), up, down.transpose(0, 2, 1)]

    def unstored(qkv, out, up, down):
        return [qkv.transpose(0, 2, 1, 3), out.transpose(0, 2, 1), up, down.transpose(0, 2, 1)]

    def qkv_piece(mats, layer):
        low = mats[0][layer].astype(bf16)
        return jnp.concatenate([low[c] for c in range(3)], axis=1)

    def rest_piece(mats, layer):
        out, up, down = [m[layer].astype(bf16) for m in mats[1:]]
        return jnp.concatenate([up, out[:, :over], down, out[:, over:]], axis=1)

    masters = stored(w_qkv, w_out, w_up, w_down)
    moments = stored(mom_qkv, mom_out, mom_up, mom_down)

    qkv_0 = Task(gather_steps(where, qkv_piece(masters, 0), cut_qkv))
    vecs = [vectors[layer : layer + 1] for layer in range(LAYERS)]
    a0, b0, half = norm_rows(where, vecs[0], tokens)
    rest, half, lengths, *later = advance(
        [qkv_0], rest_piece(masters, 0), half, lengths, *masters
    )
    rest_0 = Task(gather_steps(where, rest, cut_rest, True))
    half, lengths, *later = advance([qkv_0, rest_0], half, lengths, *later)
    win_0 = Task(window_steps(half, span))
    tables, start_rows, scalars = setup(lengths, where, tok_rows, (span + 1) * tok_rows)
    tables, start_rows, scalars, *later = advance(
        [qkv_0, rest_0, win_0], tables, start_rows, scalars, *later
    )
    qkv_1 = Task(gather_steps(where, qkv_piece(later, 1), cut_qkv, False, True))
    wq0 = qkv_0.result
    tables, *later = advance([win_0], tables, *later)
    q, k, v, vt = qkv_forward(where, a0, *win_0.result, wq0, vecs[0], tables)
    q, k, v, vt, *later = advance([rest_0, qkv_1], q, k, v, vt, *later)
    rest_1 = Task(gather_steps(where, rest_piece(later, 1), cut_rest, False, True))
    mixed, lse = attend(scalars, q, start_rows, k, vt)
    mixed, lse, b0 = advance([rest_0, rest_1], mixed, lse, b0)
    mixed, b0, wa, wb = advance([rest_1, qkv_1], mixed, b0, *rest_0.result)
    hid, slope, partial = ffn_forward(where, b0, wa, wb, 0, vecs[0], mixed, hidden_part)
    partial = advance([rest_1, qkv_1], partial)
    kept = [(tokens, a0, win_0.result, b0, q, k, v, mixed, lse, hid, slope)]
    weights = [(wq0, wa, wb, 0)]
    got = core_swap(partial)
    x1, a1, b1, half = norm_rows(where, vecs[1], tokens, vecs[0], partial, got)
    win_1 = Task(window_steps(half, span))
    a1, b1 = advance([win_1, qkv_1], a1, b1)
    a1, b1 = advance([win_1], a1, b1)
    wq1 = qkv_1.result
    q, k, v, vt = qkv_forward(where, a1, *win_1.result, wq1, vecs[1], tables)
    mixed, lse = attend(scalars, q, start_rows, k, vt)
    mixed, lse, b1, q, k, v = advance([rest_1], mixed, lse, b1, q, k, v)
    wa, wb = rest_1.result
    hid, slope, partial = ffn_forward(where, b1, wa, wb, 0, vecs[1], mixed, hidden_part)
    kept.append((x1, a1, win_1.result, b1, q, k, v, mixed, lse, hid, slope))
    weights.append((wq1, wa, wb, 0))

    def own_gradients(grad_low, layer):
        _, _, _, b, _, _, _, mixed, _, hid, slope = kept[layer]
        _, wa, wb, skip = weights[layer]
        return ffn_backward(where, grad_low, b, wa, wb, skip, slope, hid, mixed)

    def attention_gradients(g_mixed, layer, more=()):
        _, a, win, _, q, k, v, mixed, lse, _, _ = kept[layer]
        dq, dk, dv = attend_back(scalars, q, g_mixed, mixed, lse, start_rows, k, v)
        return qkv_backward(where, dq, dk, dv, a, *win, weights[layer][0], tables, more)

    def joint_of(da, db, back, layer):
        rows_in = [da, db] + list(back)
        return row_call(joint_kernel, "joint", where, vecs[layer], rows_in, [(da.shape, bf16)])[0]

    def next_grad(grad, joint, got, layer):
        outs = [(joint.shape, f32), (joint.shape, bf16)]
        rows_in = [grad, joint, got, kept[layer][0]]
        return row_call(next_kernel, "next_grad", where, vecs[layer], rows_in, outs)

    *split, db1, g_mixed, up_sum1 = own_gradients(cotangent, 1)
    *split, g_mixed, partial, db1 = advance([], *split, g_mixed, partial, db1)
    rest_1 = Task(scatter_steps(where, *split, True))
    *split1, da1, keep, give, pre_sum1 = attention_gradients(g_mixed, 1)
    *split1, da1, keep, give, partial = advance([], *split1, da1, keep, give, partial)
    back_1 = Task(window_back_steps(keep, give, span))
    da1, partial = advance([back_1, rest_1], da1, partial)
    da1, partial = advance([back_1, rest_1], da1, partial)
    joint = joint_of(da1, db1, back_1.result, 1)
    got = core_swap(joint)
    grad_x0, grad_low = next_grad(cotangent, joint, got, 1)
    *split, db0, g_mixed, up_sum0 = own_gradients(grad_low, 0)
    *split, g_mixed, da1, db0, partial = advance([rest_1], *split, g_mixed, da1, db0, partial)
    *split, g_mixed = advance([rest_1], *split, g_mixed)
    rest_0 = Task(scatter_steps(where, *split, False, True))
    *split, da0, keep, give, pre_sum0 = attention_gradients(g_mixed, 0, split1)
    *split, da0, keep, give, da1, db1, partial = advance(
        [rest_0, rest_1], *split, da0, keep, give, da1, db1, partial
    )
    both_qkv = Task(scatter_steps(where, *split, True))
    back_0 = Task(window_back_steps(keep, give, span, True))
    da1, db1, partial = advance([rest_0, both_qkv], da1, db1, partial)
    da1, db1, partial = advance([both_qkv], da1, db1, partial)
    row_1 = vector_row(where, pre_sum1, up_sum1, cotangent, kept[1][0], da1, db1, back_1.result)
    row_1, partial = advance([both_qkv, rest_0, back_0], row_1, partial)
    row_1, partial = advance([both_qkv], row_1, partial)
    got = core_swap(partial)
    block_out = norm_rows(where, vecs[1], kept[1][0], vecs[1], partial, got, False)[0]
    row_1, block_out = advance([both_qkv, rest_0], row_1, block_out)
    terms = [rest_0.result, rest_1.result, both_qkv.result]
    grads, new_moms, blocks = settle(where, terms, moments)
    owned = Task(owner_steps(blocks[0], blocks[1:]))
    while owned.flying is not None:
        advance([owned])

    inner = fsdp_count // KINDS
    parts = advance([back_0], *owned.result)
    made = orthogonalize(parts, inner)
    *made, da0, row_1 = advance([back_0], *made, da0, row_1)
    first, second = [
        permute(made[by], xor_pairs(fsdp_count, by * inner)) for by in (1, 2)
    ]
    joint = joint_of(da0, db0, back_0.result, 0)
    row_0 = vector_row(where, pre_sum0, up_sum0, grad_x0, kept[0][0], da0, db0, back_0.result)
    vec_sum = Task(sum_steps(jnp.concatenate([row_0, row_1], axis=0)))
    got = core_swap(joint)
    grad_in, _ = next_grad(grad_x0, joint, got, 0)
    first, second, third = advance([vec_sum], first, second, made[3])
    third = permute(third, xor_pairs(fsdp_count, 3 * inner))
    third = advance([vec_sum], third)
    backs = [made[0], first, second, third]
    swapped = core_swap(jnp.stack([m[1] for m in backs]))
    while vec_sum.flying is not None:
        advance([vec_sum])
    new_weights = update(where, backs, swapped, masters)

    grad_vectors = vec_sum.result
    first_new = BETA_ONE * vec_first + (1.0 - BETA_ONE) * grad_vectors
    second_new = BETA_TWO * vec_second + (1.0 - BETA_TWO) * grad_vectors * grad_vectors
    first_hat = first_new / (1.0 - BETA_ONE**STEP)
    second_hat = second_new / (1.0 - BETA_TWO**STEP)
    vectors_new = vectors - RATE_VEC * first_hat / (jnp.sqrt(second_hat) + ADAM_EPS)
    return (
        block_out,
        grad_in,
        *unstored(*grads),
        *unstored(*new_moms),
        *unstored(*new_weights),
        first_new,
        second_new,
        vectors_new,
        grad_vectors[:, 9 * D :],
    )


def solution(mesh):
    weights = (
        P(None, "fsdp", None, "tp"),
        P(None, "tp", "fsdp"),
        P(None, "fsdp", "tp"),
        P(None, "tp", "fsdp"),
    )
    rows = (P("fsdp", None), P("fsdp", None))
    return jax.shard_map(
        shards,
        mesh=mesh,
        in_specs=rows + weights + weights + (P(), P(), P(), P()),
        out_specs=rows + weights + weights + weights + (P(), P(), P(), P()),
        check_vma=False,
    )
```

```python
import functools
import math

import jax
import jax.numpy as jnp
import numpy as np
from jax import lax
from jax.experimental import pallas as pl
from jax.experimental.pallas import tpu as pltpu
from jax.sharding import PartitionSpec as P

D = 768
HEAD = 64
ROT = 16
FF = 3072
LAYERS = 2
SEQ_DEV = 64
STEP = 10
PAIR = 2 * HEAD
BLK = 256
KINDS = 4

MASKED = -1000000000.0
EPS_NORM = 1e-05
NS_A = 3.4445
NS_B = -4.775
NS_C = 2.0315
MOMENTUM = 0.95
RATE_MAT = 0.02
SHRINK = 0.99
RATE_VEC = 0.25
BETA_ONE = 0.9
BETA_TWO = 0.95
ADAM_EPS = 1e-08
ROOM_ATTEND = 16

bf16 = jnp.bfloat16
f32 = jnp.float32


def permute(x, pairs):
    return lax.ppermute(x, "fsdp", pairs)


def xor_pairs(count, by):
    return [(i, i ^ by) for i in range(count)]


def core_swap(x):
    count = lax.axis_size("tp")
    return lax.ppermute(x, "tp", [(i, i ^ 1) for i in range(count)])


def shifted(x, by):
    devices = lax.axis_size("fsdp")
    return lax.ppermute(
        x, "fsdp", [(i, i + by) for i in range(devices) if 0 <= i + by < devices]
    )


def on_grid():
    return lax.axis_size("fsdp") == 16


def place():
    index = lax.axis_index("fsdp")
    inner = lax.axis_size("fsdp") // KINDS
    bits = [(index // 2) % 2, index % 2] if on_grid() else [index * 0, index * 0]
    parts = [lax.axis_index("tp"), index // inner, *bits, index]
    return jnp.stack([p.astype(jnp.int32) for p in parts])


class Task:
    def __init__(self, steps):
        self.steps = steps
        self.result = None
        self.flying = None
        self.resume(None)

    def resume(self, arrived):
        try:
            self.flying = self.steps.send(arrived)
        except StopIteration as stop:
            self.result = stop.value
            self.flying = None


def advance(tasks, *arrays):
    tasks = [t for t in tasks if t.flying is not None]
    arrived, arrays = lax.optimization_barrier(([t.flying for t in tasks], arrays))
    for task, got in zip(tasks, arrived):
        task.resume(got)
    return arrays if len(arrays) != 1 else arrays[0]


def gather_steps(where, piece, cut, apart=False, pause=False):
    rows, cols = piece.shape
    if not on_grid():
        full = lax.all_gather(piece, "fsdp", axis=0, tiled=True)
        return full[:, :cut], full[:, cut:]
        yield
    got = []
    for group in ((1, 2), (3,)) if apart else ((1, 2, 3),):
        got += yield [permute(piece, xor_pairs(16, 4 * by)) for by in group]
    part_a, part_b = join_planes(where, [piece] + got, cut)
    if pause:
        part_a, part_b = yield [part_a, part_b]
    got_a, got_b = yield [permute(part_a, xor_pairs(16, 1)), permute(part_b, xor_pairs(16, 2))]
    part_a, part_b = join_chips(where, part_a, got_a, part_b, got_b, False)
    got_a, got_b = yield [permute(part_a, xor_pairs(16, 2)), permute(part_b, xor_pairs(16, 1))]
    part_a, part_b = join_chips(where, part_a, got_a, part_b, got_b, True)
    return part_a.reshape(16 * rows, -1), part_b.reshape(16 * rows, -1)


def natural(keep, send, axis):
    shape = (4, 1, 2, -1) if axis == 1 else (4, 2, 1, -1)
    parts = [m.reshape(shape + (m.shape[-1],)) for m in (keep, send)]
    full = jnp.concatenate(parts, axis=axis)
    return full.reshape(-1, keep.shape[-1])


def scatter_steps(where, keep_a, send_a, keep_b, send_b, pause=False, apart=False):
    if not on_grid():
        full = jnp.concatenate([natural(keep_a, send_a, 1), natural(keep_b, send_b, 2)], axis=1)
        return [lax.psum_scatter(full, "fsdp", scatter_dimension=0, tiled=True)]
        yield
    got_a, got_b = yield [permute(send_a, xor_pairs(16, 2)), permute(send_b, xor_pairs(16, 1))]
    keep_a, send_a, keep_b, send_b = add_split(where, keep_a, got_a, keep_b, got_b)
    if pause:
        keep_a, send_a, keep_b, send_b = yield [keep_a, send_a, keep_b, send_b]
    got_a, got_b = yield [permute(send_a, xor_pairs(16, 1)), permute(send_b, xor_pairs(16, 2))]
    own, *sends = add_planes(where, keep_a, got_a, keep_b, got_b)
    if pause:
        own, *sends = yield [own, *sends]
    got = [own]
    for group in ((0, 1), (2,)) if apart else ((0, 1, 2),):
        got += yield [permute(sends[i], xor_pairs(16, 4 * (i + 1))) for i in group]
    return got


def window_steps(half, span):
    got = yield [shifted(half, step) for step in range(span, 0, -1)]
    got = jnp.concatenate(got, axis=0)
    (other,) = yield [core_swap(got)]
    return got, other


def window_back_steps(keep, give, span, pause=False):
    (got,) = yield [core_swap(give)]
    half = (keep.astype(f32) + got.astype(f32)).astype(bf16).reshape(span, -1, keep.shape[-1])
    if pause:
        (half,) = yield [half]
    back = yield [shifted(half[span - step], -step) for step in range(span, 0, -1)]
    return back


def sum_steps(x):
    count = lax.axis_size("fsdp")
    step = 1
    while step < count:
        (got,) = yield [permute(x, xor_pairs(count, step))]
        x = x + got
        step *= 2
    (got,) = yield [core_swap(x)]
    return x + got


def owner_steps(own, sends):
    count = lax.axis_size("fsdp")
    inner = count // KINDS
    core = lax.axis_index("tp")
    rows, width = own.shape[1:]
    got = yield [permute(sends[by - 1], xor_pairs(count, by * inner)) for by in range(1, KINDS)]
    terms = [own] + list(got)
    give = jnp.stack([jnp.where(core == 0, m[1], m[0]) for m in terms])
    part_a = jnp.stack([jnp.where(core == 0, m[0], m[1]) for m in terms])
    part_a, part_b = yield [part_a, core_swap(give)]
    bits = inner.bit_length() - 1
    shape = (KINDS,) + (1,) * bits + (rows, width)
    part_a, part_b = part_a.reshape(shape), part_b.reshape(shape)
    for step in range(bits):
        bit_a, bit_b = step, bits - 1 - step
        got_a, got_b = yield [
            permute(part_a, xor_pairs(count, 1 << bit_a)),
            permute(part_b, xor_pairs(count, 1 << bit_b)),
        ]
        part_a = jnp.concatenate([part_a, got_a], axis=1 + bit_a)
        part_b = jnp.concatenate([part_b, got_b], axis=1 + bit_b)
    return [m.reshape(count * rows, width) for m in (part_a, part_b)]


SMALL = pl.CostEstimate(flops=1, bytes_accessed=1, transcendentals=0)
SCALARS = pl.BlockSpec(memory_space=pltpu.SMEM)
NT = (((1,), (1,)), ((), ()))
TN = (((0,), (0,)), ((), ()))


def dot(a, b, how=(((1,), (0,)), ((), ()))):
    return lax.dot_general(a, b, how, preferred_element_type=f32)


def whole(*shape):
    return pl.BlockSpec(shape, lambda *_: (0,) * len(shape))


def shaped(*shapes_and_kinds):
    return [jax.ShapeDtypeStruct(shape, kind) for shape, kind in shapes_and_kinds]


def call(kernel, name, grid, in_specs, out_specs, out_shape, scratch=(), room=8):
    return pl.pallas_call(
        kernel,
        grid=grid,
        in_specs=in_specs,
        out_specs=out_specs,
        out_shape=out_shape,
        scratch_shapes=list(scratch),
        compiler_params=pltpu.CompilerParams(vmem_limit_bytes=room << 20),
        cost_estimate=SMALL,
        name=name,
    )


def join_planes_kernel(cut, where_ref, *refs):
    *pieces, out_a, out_b = refs
    quarter = where_ref[1]
    for by, piece in enumerate(pieces):
        plane = quarter ^ by
        out_a[plane] = piece[:, :cut]
        out_b[plane] = piece[:, cut:]


def join_planes(where, pieces, cut):
    rows, cols = pieces[0].shape
    shapes = [(4, rows, cut), (4, rows, cols - cut)]
    return call(
        functools.partial(join_planes_kernel, cut),
        "join_planes",
        (1,),
        [SCALARS] + [whole(rows, cols)] * 4,
        [whole(*shape) for shape in shapes],
        shaped(*[(shape, bf16) for shape in shapes]),
    )(where, *pieces)


def join_chips_kernel(last, where_ref, own_a, got_a, own_b, got_b, out_a, out_b):
    y, x = where_ref[2], where_ref[3]
    if not last:
        out_a[0, x], out_a[0, 1 - x] = own_a[0], got_a[0]
        out_b[0, y], out_b[0, 1 - y] = own_b[0], got_b[0]
    else:
        out_a[0, y], out_a[0, 1 - y] = own_a[0], got_a[0]
        for side in range(2):
            out_b[0, side, x], out_b[0, side, 1 - x] = own_b[0, side], got_b[0, side]


def join_chips(where, own_a, got_a, own_b, got_b, last):
    rows = own_a.shape[-2]
    ins, outs = ((2, rows), (2, 2, rows)) if last else ((rows,), (2, rows))

    def spec(shape, width):
        return pl.BlockSpec((1,) + shape + (width,), lambda i: (i,) + (0,) * (len(shape) + 1))

    wide_a, wide_b = own_a.shape[-1], own_b.shape[-1]
    return call(
        functools.partial(join_chips_kernel, last),
        "join_chips",
        (4,),
        [SCALARS, spec(ins, wide_a), spec(ins, wide_a), spec(ins, wide_b), spec(ins, wide_b)],
        [spec(outs, wide_a), spec(outs, wide_b)],
        shaped(((4,) + outs + (wide_a,), bf16), ((4,) + outs + (wide_b,), bf16)),
    )(where, own_a, got_a, own_b, got_b)


def add_split_kernel(where_ref, keep_a, got_a, keep_b, got_b, out_ka, out_sa, out_kb, out_sb):
    rows = keep_a.shape[0] // 8
    for bit, keep, got, out_k, out_s in (
        (where_ref[3], keep_a, got_a, out_ka, out_sa),
        (where_ref[2], keep_b, got_b, out_kb, out_sb),
    ):
        for z in range(4):
            for flip, out in ((0, out_k), (1, out_s)):
                at = pl.ds(pl.multiple_of((2 * z + (bit ^ flip)) * rows, 16), rows)
                total = keep[at, :].astype(f32) + got[at, :].astype(f32)
                out[z * rows : (z + 1) * rows, :] = total.astype(bf16)


def add_split(where, keep_a, got_a, keep_b, got_b):
    rows, wide_a = keep_a.shape
    wide_b = keep_b.shape[1]
    outs = [(rows // 2, wide_a)] * 2 + [(rows // 2, wide_b)] * 2
    return call(
        add_split_kernel,
        "add_split",
        (1,),
        [SCALARS] + [whole(rows, wide_a)] * 2 + [whole(rows, wide_b)] * 2,
        [whole(*shape) for shape in outs],
        shaped(*[(shape, bf16) for shape in outs]),
        room=12,
    )(where, keep_a, got_a, keep_b, got_b)


def add_planes_kernel(where_ref, keep_a, got_a, keep_b, got_b, *outs):
    rows = keep_a.shape[0] // 4
    cut = keep_a.shape[1]
    for by, out in enumerate(outs):
        at = pl.ds(pl.multiple_of((where_ref[1] ^ by) * rows, 16), rows)
        out[:, :cut] = (keep_a[at, :].astype(f32) + got_a[at, :].astype(f32)).astype(bf16)
        out[:, cut:] = (keep_b[at, :].astype(f32) + got_b[at, :].astype(f32)).astype(bf16)


def add_planes(where, keep_a, got_a, keep_b, got_b):
    rows, wide_a = keep_a.shape
    wide_b = keep_b.shape[1]
    shape = (rows // 4, wide_a + wide_b)
    return call(
        add_planes_kernel,
        "add_planes",
        (1,),
        [SCALARS] + [whole(rows, wide_a)] * 2 + [whole(rows, wide_b)] * 2,
        [whole(*shape)] * 4,
        shaped(*[(shape, bf16)] * 4),
    )(where, keep_a, got_a, keep_b, got_b)


def setup_kernel(len_ref, where_ref, freq_ref, table_ref, start_ref, scal_ref):
    rows, total = start_ref.shape[1], table_ref.shape[1]
    base = where_ref[4] * rows
    first = base - (total - rows)
    half = ROT // 2

    def starts_of(index):
        end, out = jnp.int32(0), jnp.zeros_like(index)
        for i in range(len_ref.shape[0]):
            end = end + len_ref[i]
            out = jnp.where(index >= end, end, out)
        return out

    lane = lax.broadcasted_iota(jnp.int32, (BLK, PAIR), 1) % HEAD
    for c in range(total // BLK):
        at = slice(c * BLK, (c + 1) * BLK)
        index = first + c * BLK + lax.broadcasted_iota(jnp.int32, (BLK, PAIR), 0)
        phase = (index - starts_of(index)).astype(f32) * freq_ref[...]
        sine = jnp.sin(phase)
        table_ref[0, at, :] = jnp.cos(phase)
        table_ref[1, at, :] = jnp.where(lane < half, -sine, 0.0)
        table_ref[2, at, :] = jnp.where((lane >= half) & (lane < ROT), sine, 0.0)
    start_ref[...] = starts_of(base + lax.broadcasted_iota(jnp.int32, start_ref.shape, 1))
    own = (total - rows) // BLK
    scal_ref[0] = base
    scal_ref[1] = jnp.minimum((starts_of(base + BLK) - first) // BLK, own)
    scal_ref[2] = (starts_of(base) - first) // BLK


def setup(lengths, where, rows, total):
    lane = np.arange(PAIR) % HEAD
    freqs = np.exp((lane % (ROT // 2)) * (-2.0 * math.log(10000.0) / ROT))
    freqs = np.where(lane < ROT, freqs, 0.0).astype(np.float32)[None]
    return call(
        setup_kernel,
        "setup",
        (1,),
        [SCALARS, SCALARS, whole(1, PAIR)],
        [whole(3, total, PAIR), whole(8, rows), SCALARS],
        shaped(((3, total, PAIR), f32), ((8, rows), jnp.int32), ((3,), jnp.int32)),
        room=8,
    )(lengths, where, jnp.asarray(freqs))


def unit_rows(x):
    centered = x - jnp.mean(x, axis=-1, keepdims=True)
    inverse = lax.rsqrt(jnp.mean(centered * centered, axis=-1, keepdims=True) + EPS_NORM)
    return centered * inverse, inverse


def norm_kernel(where_ref, vec_ref, x_ref, a_ref, b_ref, half_ref):
    unit, _ = unit_rows(x_ref[...].astype(f32))
    a = (unit * vec_ref[:, :D] + vec_ref[:, D : 2 * D]).astype(bf16)
    a_ref[...] = a
    b_ref[...] = (unit * vec_ref[:, 2 * D : 3 * D] + vec_ref[:, 3 * D : 4 * D]).astype(bf16)
    half_ref[...] = jnp.where(where_ref[0] == 0, unit[:, : D // 2], unit[:, D // 2 :]).astype(bf16)


def add_norm_kernel(where_ref, old_ref, vec_ref, x_ref, part_ref, got_ref, new_ref, *outs):
    x = x_ref[...].astype(f32) + part_ref[...].astype(f32) + got_ref[...].astype(f32)
    x = x + old_ref[:, 4 * D : 5 * D] + old_ref[:, 5 * D : 6 * D]
    new_ref[...] = x
    if outs:
        norm_kernel(where_ref, vec_ref, new_ref, *outs)


def norm_rows(where, vec, x, old_vec=None, part=None, got=None, normed=True):
    rows = x.shape[0]
    step = rows // 4
    block = lambda width: pl.BlockSpec((step, width), lambda i: (i, 0))
    flat = whole(1, vec.shape[1])
    out = [((rows, D), bf16), ((rows, D), bf16), ((rows, D // 2), bf16)] if normed else []
    if part is None:
        specs, kernel, args = [flat, block(D)], norm_kernel, (vec, x)
    else:
        specs, kernel = [flat, flat] + [block(D)] * 3, add_norm_kernel
        args, out = (old_vec, vec, x, part, got), [((rows, D), f32)] + out
    return call(
        kernel,
        "norm_rows",
        (4,),
        [SCALARS] + specs,
        [block(shape[1]) for shape, _ in out],
        shaped(*out),
    )(where, *args)


def rope(u, tables, sign):
    half = ROT // 2
    return u * tables[0] + sign * (
        pltpu.roll(u, PAIR - half, 1) * tables[1] + pltpu.roll(u, half, 1) * tables[2]
    )


def window_block(before, where_ref, vec_ref, own_ref, half_ref, other_ref):
    half, other = half_ref[...], other_ref[...]
    first = jnp.where(where_ref[0] == 0, half, other)
    second = jnp.where(where_ref[0] == 0, other, half)
    unit = jnp.concatenate([first, second], axis=1).astype(f32)
    earlier = (unit * vec_ref[:, :D] + vec_ref[:, D : 2 * D]).astype(bf16)
    return jnp.where(pl.program_id(0) < before, earlier, own_ref[...]), unit


def qkv_kernel(
    before, where_ref, own_ref, half_ref, other_ref, wa_ref, wb_ref, vec_ref, table_ref,
    q_ref, k_ref, v_ref, vt_ref,
):
    width = q_ref.shape[1]
    over = wa_ref.shape[1] - width
    a, _ = window_block(before, where_ref, vec_ref, own_ref, half_ref, other_ref)
    tables = [table_ref[i] for i in range(3)]
    bias = [
        vec_ref[:, pl.ds(pl.multiple_of((6 + c) * D + where_ref[0] * width, PAIR), width)]
        for c in range(3)
    ]

    @pl.when(pl.program_id(0) == before)
    def _():
        pre = dot(a, wa_ref[:, :width]) + bias[0]
        for p in range(width // PAIR):
            at = slice(p * PAIR, (p + 1) * PAIR)
            q_ref[:, at] = (rope(pre[:, at], tables, 1.0) * HEAD ** (-0.5)).astype(bf16)

    front, rest = dot(a, wa_ref[:, width:]), dot(a, wb_ref[...])
    values = (rest[:, width - over :] + bias[2]).astype(bf16)
    v_ref[...] = values
    vt_ref[...] = jnp.transpose(values)
    pre = jnp.concatenate([front, rest[:, : width - over]], axis=1) + bias[1]
    for p in range(width // PAIR):
        at = slice(p * PAIR, (p + 1) * PAIR)
        k_ref[:, at] = rope(pre[:, at], tables, 1.0).astype(bf16)


def window_specs(rows, before):
    earlier = pl.BlockSpec((rows, D // 2), lambda i: (jnp.minimum(i, before - 1), 0))
    return [whole(rows, D), earlier, earlier]


def qkv_forward(where, own, half, other, weights, vec, tables):
    rows, total = own.shape[0], tables.shape[1]
    width = (weights[0].shape[1] + weights[1].shape[1]) // 3
    before = total // rows - 1
    flat = pl.BlockSpec((rows, width), lambda i: (i, 0))
    return call(
        functools.partial(qkv_kernel, before),
        "qkv_forward",
        (total // rows,),
        [SCALARS]
        + window_specs(rows, before)
        + [whole(*weights[0].shape), whole(*weights[1].shape), whole(*vec.shape)]
        + [pl.BlockSpec((3, rows, PAIR), lambda i: (0, i, 0))],
        [whole(rows, width), flat, flat, pl.BlockSpec((width, rows), lambda i: (0, i))],
        shaped(
            ((rows, width), bf16),
            ((total, width), bf16),
            ((total, width), bf16),
            ((width, total), bf16),
        ),
        room=14,
    )(where, own, half, other, *weights, vec, tables)


def qkv_back_kernel(
    before, more, where_ref, dq_ref, dk_ref, dv_ref, own_ref, half_ref, other_ref, wa_ref, wb_ref, table_ref,
    vec_ref, *refs,
):
    more_refs, refs = refs[:more], refs[more:]
    ka_ref, sa_ref, kb_ref, sb_ref, da_ref, keep_ref, give_ref, sum_ref, far_ref, pre_ref, acc_ref = refs
    width = dq_ref.shape[1]
    cut = wa_ref.shape[1]
    step = pl.program_id(0)
    tables = [table_ref[i] for i in range(3)]

    @pl.when(step == 0)
    def _():
        acc_ref[...] = jnp.zeros_like(acc_ref)
        sum_ref[...] = jnp.zeros_like(sum_ref)
        far_ref[...] = jnp.zeros_like(far_ref)

    def put(at, value):
        pre_ref[:, at] = value
        sum_ref[:, at] += jnp.sum(value.astype(f32), axis=0, keepdims=True)

    a, unit = window_block(before, where_ref, vec_ref, own_ref, half_ref, other_ref)
    turned = jnp.transpose(a)
    for p in range(width // PAIR):
        at = slice(p * PAIR, (p + 1) * PAIR)
        put(
            slice(width + p * PAIR, width + (p + 1) * PAIR),
            rope(dk_ref[:, at].astype(f32), tables, -1.0).astype(bf16),
        )
    put(slice(2 * width, 3 * width), dv_ref[...])

    @pl.when(step < before)
    def _():
        acc_ref[:, width:] += dot(turned, pre_ref[:, width:])
        da = dot(pre_ref[:, width:cut], wa_ref[:, width:], NT) + dot(pre_ref[:, cut:], wb_ref[...], NT)
        far_ref[0:1, :] += jnp.sum(da * unit, axis=0, keepdims=True)
        far_ref[1:2, :] += jnp.sum(da, axis=0, keepdims=True)
        low, high = da[:, : D // 2].astype(bf16), da[:, D // 2 :].astype(bf16)
        keep_ref[...] = jnp.where(where_ref[0] == 0, low, high)
        give_ref[...] = jnp.where(where_ref[0] == 0, high, low)

    @pl.when(step == before)
    def _():
        for p in range(width // PAIR):
            at = slice(p * PAIR, (p + 1) * PAIR)
            query = rope(dq_ref[:, at].astype(f32), tables, -1.0) * HEAD ** (-0.5)
            put(at, query.astype(bf16))
        acc_ref[...] += dot(turned, pre_ref[...])
        da_ref[...] = dot(pre_ref[:, :cut], wa_ref[...], NT) + dot(pre_ref[:, cut:], wb_ref[...], NT)
        part = acc_ref.shape[0] // 16
        for flip, out_a, out_b in ((0, ka_ref, kb_ref), (1, sa_ref, sb_ref)):
            for z in range(4):
                at = pl.ds(pl.multiple_of((2 * z + (where_ref[2] ^ flip)) * 2 * part, 16), 2 * part)
                out_a[2 * z * part : (2 * z + 2) * part, :cut] = acc_ref[at, :cut].astype(bf16)
                for y in range(2):
                    row = (2 * z + y) * part
                    at = pl.ds(pl.multiple_of(2 * row + (where_ref[3] ^ flip) * part, 16), part)
                    out_b[row : row + part, : 3 * width - cut] = acc_ref[at, cut:].astype(bf16)
        for ref, out in zip(more_refs, (ka_ref, sa_ref, kb_ref, sb_ref)):
            out[:, ref.shape[1] :] = ref[...]


def qkv_backward(where, dq, dk, dv, own, half, other, weights, tables, vec, more=()):
    rows, width = dq.shape
    total = tables.shape[1]
    before = total // rows - 1
    cut = weights[0].shape[1]
    each = pl.BlockSpec((rows, width), lambda i: (i, 0))
    earlier = pl.BlockSpec((rows, D // 2), lambda i: (jnp.minimum(i, before - 1), 0))
    times = 2 if more else 1
    splits = [(D // 2, times * cut)] * 2 + [(D // 2, times * (3 * width - cut))] * 2
    return call(
        functools.partial(qkv_back_kernel, before, len(more)),
        "qkv_backward",
        (total // rows,),
        [SCALARS, whole(rows, width), each, each]
        + window_specs(rows, before)
        + [whole(*weights[0].shape), whole(*weights[1].shape)]
        + [pl.BlockSpec((3, rows, PAIR), lambda i: (0, i, 0)), whole(*vec.shape)]
        + [whole(*m.shape) for m in more],
        [whole(*shape) for shape in splits]
        + [whole(rows, D), earlier, earlier, whole(1, 3 * width), whole(8, D)],
        shaped(
            *[(shape, bf16) for shape in splits],
            ((rows, D), f32),
            ((total - rows, D // 2), bf16),
            ((total - rows, D // 2), bf16),
            ((1, 3 * width), f32),
            ((8, D), f32),
        ),
        [pltpu.VMEM((rows, 3 * width), bf16), pltpu.VMEM((D, 3 * width), f32)],
        room=18,
    )(where, dq, dk, dv, own, half, other, *weights, tables, vec, *more)


def low_lanes():
    return lax.broadcasted_iota(jnp.int32, (1, PAIR), 1) < HEAD


def both_heads(x):
    low = low_lanes()
    zero = jnp.zeros_like(x[:BLK])
    parts = []
    for at in range(0, x.shape[0], BLK):
        block = x[at : at + BLK]
        parts += [jnp.where(low, block, zero), jnp.where(low, zero, block)]
    return jnp.concatenate(parts, axis=0)


def both_columns(first, second):
    parts = []
    for at in range(0, first.shape[1], BLK):
        parts += [first[:, at : at + BLK], second[:, at : at + BLK]]
    return jnp.concatenate(parts, axis=1)


def key_loops(scal_ref, blocks, own, work):
    work(own + 1, slice(2 * BLK, 4 * BLK))
    low_all, low_first = scal_ref[1], scal_ref[2]

    def full(i, carry):
        work(own - i, slice(0, 4 * BLK))
        return carry

    def first_only(i, carry):
        work(low_all - 1 - i, slice(0, 2 * BLK))
        return carry

    lax.fori_loop(0, own - low_all + 1, full, 0)
    lax.fori_loop(0, low_all - low_first, first_only, 0)


def attend_kernel(scal_ref, q_ref, start_ref, k_ref, vt_ref, o_ref, lse_ref, q2_ref, m_ref, l_ref, acc_ref):
    rows, total = q_ref.shape[0], k_ref.shape[0]
    pairs = q_ref.shape[1] // PAIR
    base = scal_ref[0]
    m_ref[...] = jnp.full_like(m_ref, -1e30)
    l_ref[...] = jnp.zeros_like(l_ref)
    acc_ref[...] = jnp.zeros_like(acc_ref)
    for p in range(pairs):
        q2_ref[p] = both_heads(q_ref[:, p * PAIR : (p + 1) * PAIR])
    starts = both_columns(start_ref[0:1, :], start_ref[0:1, :])
    index = base + lax.broadcasted_iota(jnp.int32, (1, rows), 1)
    index = both_columns(index, index)

    def work(kb, cols):
        at = pl.ds(pl.multiple_of(kb * BLK, BLK), BLK)
        key_index = base - (total - rows) + kb * BLK + lax.broadcasted_iota(jnp.int32, (BLK, 1), 0)
        seen = (key_index >= starts[:, cols]) & (key_index <= index[:, cols])
        for p in range(pairs):
            lanes = slice(p * PAIR, (p + 1) * PAIR)
            s = jnp.where(seen, dot(k_ref[at, lanes], q2_ref[p, cols, :], NT), MASKED)
            m_old = m_ref[p, 0:1, cols]
            m_new = jnp.maximum(m_old, jnp.max(s, axis=0, keepdims=True))
            scale = jnp.exp(m_old - m_new)
            e = jnp.exp(s - m_new)
            m_ref[p, 0:1, cols] = m_new
            l_ref[p, 0:1, cols] = l_ref[p, 0:1, cols] * scale + jnp.sum(e, axis=0, keepdims=True)
            acc_ref[p, :, cols] = acc_ref[p, :, cols] * scale + dot(vt_ref[lanes, at], e.astype(bf16))

    key_loops(scal_ref, total // BLK, (total - rows) // BLK, work)
    for p in range(pairs):
        total_p = l_ref[p, 0:1, :]
        acc = acc_ref[p] / total_p
        lse_ref[p, 0:1, :] = m_ref[p, 0:1, :] + jnp.log(total_p)
        for qb in range(rows // BLK):
            first = acc[:HEAD, 2 * qb * BLK : (2 * qb + 1) * BLK]
            second = acc[HEAD:, (2 * qb + 1) * BLK : (2 * qb + 2) * BLK]
            o_ref[qb * BLK : (qb + 1) * BLK, p * PAIR : (p + 1) * PAIR] = jnp.transpose(
                jnp.concatenate([first, second], axis=0)
            ).astype(bf16)


def attend(scalars, q, start_rows, k, vt):
    rows, width = q.shape
    total = k.shape[0]
    pairs = width // PAIR
    return pl.pallas_call(
        attend_kernel,
        grid=(1,),
        in_specs=[
            pl.BlockSpec(memory_space=pltpu.SMEM),
            whole(rows, width),
            whole(8, rows),
            whole(total, width),
            whole(width, total),
        ],
        out_specs=[whole(rows, width), whole(pairs, 8, 2 * rows)],
        out_shape=[
            jax.ShapeDtypeStruct((rows, width), bf16),
            jax.ShapeDtypeStruct((pairs, 8, 2 * rows), f32),
        ],
        scratch_shapes=[
            pltpu.VMEM((pairs, 2 * rows, PAIR), bf16),
            pltpu.VMEM((pairs, 8, 2 * rows), f32),
            pltpu.VMEM((pairs, 8, 2 * rows), f32),
            pltpu.VMEM((pairs, PAIR, 2 * rows), f32),
        ],
        compiler_params=pltpu.CompilerParams(vmem_limit_bytes=ROOM_ATTEND << 20),
        cost_estimate=SMALL,
        name="attend",
    )(scalars, q, start_rows, k, vt)


def attend_back_kernel(
    scal_ref, q_ref, g_ref, o_ref, lse_ref, start_ref, k_ref, v_ref,
    dq_ref, dk_ref, dv_ref, q2_ref, g2_ref, delta_ref, acc_ref,
):
    rows, total = q_ref.shape[0], k_ref.shape[0]
    pairs = q_ref.shape[1] // PAIR
    base = scal_ref[0]
    dk_ref[...] = jnp.zeros_like(dk_ref)
    dv_ref[...] = jnp.zeros_like(dv_ref)
    acc_ref[...] = jnp.zeros_like(acc_ref)
    which = lax.broadcasted_iota(jnp.int32, (8, PAIR), 0)
    lane = lax.broadcasted_iota(jnp.int32, (8, PAIR), 1)
    chosen = (which == lane // HEAD).astype(f32)
    for p in range(pairs):
        lanes = slice(p * PAIR, (p + 1) * PAIR)
        g = g_ref[:, lanes]
        q2_ref[p] = both_heads(q_ref[:, lanes])
        g2_ref[p] = both_heads(g)
        delta = lax.dot_general(
            chosen,
            g.astype(f32) * o_ref[:, lanes].astype(f32),
            NT,
            precision=lax.Precision.HIGHEST,
            preferred_element_type=f32,
        )
        delta_ref[p, 0:1, :] = both_columns(delta[0:1, :], delta[1:2, :])
    starts = both_columns(start_ref[0:1, :], start_ref[0:1, :])
    index = base + lax.broadcasted_iota(jnp.int32, (1, rows), 1)
    index = both_columns(index, index)

    def work(kb, cols):
        at = pl.ds(pl.multiple_of(kb * BLK, BLK), BLK)
        key_index = base - (total - rows) + kb * BLK + lax.broadcasted_iota(jnp.int32, (BLK, 1), 0)
        seen = (key_index >= starts[:, cols]) & (key_index <= index[:, cols])
        for p in range(pairs):
            lanes = slice(p * PAIR, (p + 1) * PAIR)
            keys, q2, g2 = k_ref[at, lanes], q2_ref[p, cols, :], g2_ref[p, cols, :]
            s = jnp.where(seen, dot(keys, q2, NT), MASKED)
            prob = jnp.exp(s - lse_ref[p, 0:1, cols])
            d_prob = dot(v_ref[at, lanes], g2, NT)
            d_score = (prob * (d_prob - delta_ref[p, 0:1, cols])).astype(bf16)
            dv_ref[at, lanes] = dot(prob.astype(bf16), g2).astype(bf16)
            dk_ref[at, lanes] = dot(d_score, q2).astype(bf16)
            acc_ref[p, cols, :] += dot(d_score, keys, TN)

    key_loops(scal_ref, total // BLK, (total - rows) // BLK, work)
    low = low_lanes()
    for p in range(pairs):
        for qb in range(rows // BLK):
            first = acc_ref[p, 2 * qb * BLK : (2 * qb + 1) * BLK, :]
            second = acc_ref[p, (2 * qb + 1) * BLK : (2 * qb + 2) * BLK, :]
            dq_ref[qb * BLK : (qb + 1) * BLK, p * PAIR : (p + 1) * PAIR] = jnp.where(
                low, first, second
            ).astype(bf16)


def attend_back(scalars, q, g, o, lse, start_rows, k, v):
    rows, width = q.shape
    total = k.shape[0]
    pairs = width // PAIR
    return pl.pallas_call(
        attend_back_kernel,
        grid=(1,),
        in_specs=[
            pl.BlockSpec(memory_space=pltpu.SMEM),
            whole(rows, width),
            whole(rows, width),
            whole(rows, width),
            whole(pairs, 8, 2 * rows),
            whole(8, rows),
            whole(total, width),
            whole(total, width),
        ],
        out_specs=[whole(rows, width), whole(total, width), whole(total, width)],
        out_shape=[
            jax.ShapeDtypeStruct((rows, width), bf16),
            jax.ShapeDtypeStruct((total, width), bf16),
            jax.ShapeDtypeStruct((total, width), bf16),
        ],
        scratch_shapes=[
            pltpu.VMEM((pairs, 2 * rows, PAIR), bf16),
            pltpu.VMEM((pairs, 2 * rows, PAIR), bf16),
            pltpu.VMEM((pairs, 8, 2 * rows), f32),
            pltpu.VMEM((pairs, 2 * rows, PAIR), f32),
        ],
        compiler_params=pltpu.CompilerParams(vmem_limit_bytes=ROOM_ATTEND << 20),
        cost_estimate=SMALL,
        name="attend_back",
    )(scalars, q, g, o, lse, start_rows, k, v)


def ffn_kernel(
    where_ref, a_ref, up0_ref, up1_ref, dn0_ref, dn1_ref, outa_ref, outb_ref, vec_ref, mix_ref,
    hid_ref, slope_ref, out_ref, acc_ref,
):
    step = pl.program_id(0)
    over_a = outa_ref.shape[1]
    over_b = mix_ref.shape[1] - over_a
    hidden = pl.num_programs(0) * 2 * BLK

    @pl.when(step == 0)
    def _():
        acc_ref[...] = dot(mix_ref[:, :over_a], outa_ref[...], NT) + dot(
            mix_ref[:, over_a:], outb_ref[:, :over_b], NT
        )

    a = a_ref[...]
    total = acc_ref[...]
    for i, (up, down) in enumerate(((up0_ref, dn0_ref), (up1_ref, dn1_ref))):
        at = slice(i * BLK, (i + 1) * BLK)
        first = 9 * D + where_ref[0] * hidden + (2 * step + i) * BLK
        u = dot(a, up[...]) + vec_ref[:, pl.ds(pl.multiple_of(first, BLK), BLK)]
        phi = 0.5 * (1.0 + lax.erf(u * (1.0 / math.sqrt(2.0))))
        slope = phi + u * jnp.exp(-0.5 * u * u) * (1.0 / math.sqrt(2.0 * math.pi))
        slope_ref[:, at] = slope.astype(bf16)
        low = (u * phi).astype(bf16)
        hid_ref[:, at] = low
        total = total + dot(low, down[...], NT)
    acc_ref[...] = total

    @pl.when(step == pl.num_programs(0) - 1)
    def _():
        out_ref[...] = acc_ref[...].astype(bf16)


def ffn_weights(hidden, skip):
    steps = hidden // BLK
    return [
        pl.BlockSpec((D, BLK), lambda i: (0, 2 * i)),
        pl.BlockSpec((D, BLK), lambda i: (0, 2 * i + 1)),
        pl.BlockSpec((D, BLK), lambda i: (0, skip + 2 * i)),
        pl.BlockSpec((D, BLK), lambda i: (0, skip + 2 * i + 1)),
        pl.BlockSpec((D, BLK), lambda i: (0, steps)),
        pl.BlockSpec((D, BLK), lambda i: (0, skip + steps)),
    ]


def ffn_forward(where, a, wa, wb, skip, vec, mixed, hidden):
    rows, width = a.shape[0], mixed.shape[1]
    wide = pl.BlockSpec((rows, 2 * BLK), lambda i: (0, i))
    return call(
        ffn_kernel,
        "ffn_forward",
        (hidden // (2 * BLK),),
        [SCALARS, whole(rows, D)]
        + ffn_weights(hidden, skip)
        + [whole(*vec.shape), whole(rows, width)],
        [wide, wide, whole(rows, D)],
        shaped(((rows, hidden), bf16), ((rows, hidden), bf16), ((rows, D), bf16)),
        [pltpu.VMEM((rows, D), f32)],
        room=12,
    )(where, a, wa, wa, wb, wb, wa, wb, vec, mixed)


def ffn_back_kernel(
    where_ref, g_ref, a_ref, up0_ref, up1_ref, dn0_ref, dn1_ref, outa_ref, outb_ref,
    slope_ref, hid_ref, mix_ref,
    ka_ref, sa_ref, kb_ref, sb_ref, da_ref, gmix_ref, sum_ref, ay_ref, gy_ref, gx_ref,
):
    step = pl.program_id(0)
    last = pl.num_programs(0) - 1
    over_a = outa_ref.shape[1]
    over_b = mix_ref.shape[1] - over_a
    half = ka_ref.shape[0]
    part = half // 8

    @pl.when(step == 0)
    def _():
        da_ref[...] = jnp.zeros_like(da_ref)
        for turned, split_y, split_x in (
            (jnp.transpose(a_ref[...]), ay_ref, None),
            (jnp.transpose(g_ref[...]), gy_ref, gx_ref),
        ):
            for z in range(4):
                for y in range(2):
                    row = (2 * z + y) * 2 * part
                    to = pl.multiple_of((where_ref[2] ^ y) * half + 2 * z * part, 16)
                    split_y[pl.ds(to, 2 * part), :] = turned[row : row + 2 * part]
                    for x in range(2) if split_x is not None else ():
                        to = pl.multiple_of((where_ref[3] ^ x) * half + (2 * z + y) * part, 16)
                        split_x[pl.ds(to, part), :] = turned[row + x * part : row + (x + 1) * part]

    @pl.when(step < last)
    def _():
        g = g_ref[...]
        total = da_ref[...]
        grad = dot(gx_ref[...], hid_ref[...]).astype(bf16)
        kb_ref[...], sb_ref[...] = grad[:half], grad[half:]
        for i, (up, down) in enumerate(((up0_ref, dn0_ref), (up1_ref, dn1_ref))):
            at = slice(i * BLK, (i + 1) * BLK)
            d_pre = (dot(g, down[...]) * slope_ref[:, at].astype(f32)).astype(bf16)
            sum_ref[:, at] = jnp.sum(d_pre.astype(f32), axis=0, keepdims=True)
            grad = dot(ay_ref[...], d_pre).astype(bf16)
            ka_ref[:, at], sa_ref[:, at] = grad[:half], grad[half:]
            total = total + dot(d_pre, up[...], NT)
        da_ref[...] = total

    @pl.when(step == last)
    def _():
        g = g_ref[...]
        gmix_ref[:, :over_a] = dot(g, outa_ref[...]).astype(bf16)
        gmix_ref[:, over_a:] = dot(g, outb_ref[:, :over_b]).astype(bf16)
        grad = dot(gy_ref[...], mix_ref[:, :over_a]).astype(bf16)
        ka_ref[:, :over_a], sa_ref[:, :over_a] = grad[:half], grad[half:]
        grad = dot(gx_ref[...], mix_ref[:, over_a:]).astype(bf16)
        kb_ref[:, :over_b], sb_ref[:, :over_b] = grad[:half], grad[half:]


def ffn_backward(where, g, a, wa, wb, skip, slope, hid, mixed):
    rows, width = mixed.shape
    hidden = hid.shape[1]
    steps = hidden // (2 * BLK)
    upto = lambda i: (0, jnp.minimum(i, steps - 1))
    weights = []
    for spec in ffn_weights(hidden, skip):
        weights.append(
            pl.BlockSpec(spec.block_shape, lambda i, f=spec.index_map: f(jnp.minimum(i, steps - 1)))
        )
    wide = pl.BlockSpec((rows, 2 * BLK), upto)
    split = pl.BlockSpec((D // 2, 2 * BLK), lambda i: (0, i))
    wide_a, wide_b = hidden + BLK, hidden + width - BLK
    return call(
        ffn_back_kernel,
        "ffn_backward",
        (steps + 1,),
        [SCALARS, whole(rows, D), whole(rows, D)] + weights + [wide, wide, whole(rows, width)],
        [split] * 4
        + [whole(rows, D), whole(rows, width), pl.BlockSpec((1, 2 * BLK), upto)],
        shaped(
            *[((D // 2, wide_a), bf16)] * 2,
            *[((D // 2, wide_b), bf16)] * 2,
            ((rows, D), f32),
            ((rows, width), bf16),
            ((1, hidden), f32),
        ),
        [pltpu.VMEM((D, rows), bf16)] * 3,
        room=18,
    )(where, g, a, wa, wa, wb, wb, wa, wb, slope, hid, mixed)


def with_half(where_ref, da_ref, back_refs):
    half = sum(ref[...].astype(f32) for ref in back_refs)
    zero = jnp.zeros_like(half)
    first = jnp.where(where_ref[0] == 0, half, zero)
    return da_ref[...] + jnp.concatenate([first, half - first], axis=1)


def joint_kernel(where_ref, vec_ref, da_ref, db_ref, *refs):
    *back_refs, out_ref = refs
    da = with_half(where_ref, da_ref, back_refs)
    out_ref[...] = (da * vec_ref[:, :D] + db_ref[...] * vec_ref[:, 2 * D : 3 * D]).astype(bf16)


def row_call(kernel, name, where, vec, rows_in, outs, steps=4):
    rows = rows_in[0].shape[0]
    block = lambda width: pl.BlockSpec((rows // steps, width), lambda i: (i, 0))
    return call(
        kernel,
        name,
        (steps,),
        [SCALARS, whole(*vec.shape)] + [block(m.shape[1]) for m in rows_in],
        [block(shape[1]) for shape, _ in outs],
        shaped(*outs),
    )(where, vec, *rows_in)


def next_kernel(where_ref, vec_ref, grad_ref, own_ref, got_ref, x_ref, out_ref, low_ref):
    unit, inverse = unit_rows(x_ref[...].astype(f32))
    joint = own_ref[...].astype(f32) + got_ref[...].astype(f32)
    centered = joint - jnp.mean(joint, axis=-1, keepdims=True)
    grad = grad_ref[...].astype(f32) + inverse * (
        centered - unit * jnp.mean(joint * unit, axis=-1, keepdims=True)
    )
    out_ref[...] = grad
    low_ref[...] = grad.astype(bf16)


def vector_kernel(where_ref, qkv_ref, up_ref, far_ref, grad_ref, x_ref, da_ref, db_ref, out_ref):
    core = where_ref[0]
    width, hidden = qkv_ref.shape[1] // 3, up_ref.shape[1]

    @pl.when(pl.program_id(0) == 0)
    def _():
        out_ref[...] = jnp.zeros_like(out_ref)
        for c in range(3):
            to = pl.multiple_of((6 + c) * D + core * width, PAIR)
            out_ref[:, pl.ds(to, width)] = qkv_ref[:, c * width : (c + 1) * width]
        out_ref[:, pl.ds(pl.multiple_of(9 * D + core * hidden, PAIR), hidden)] = up_ref[...]
        for i in range(2):
            out_ref[:, i * D : (i + 1) * D] = far_ref[i : i + 1, :]

    unit, _ = unit_rows(x_ref[...].astype(f32))
    da, db = da_ref[...], db_ref[...]
    first = (core == 0).astype(f32)
    bias = jnp.sum(grad_ref[...].astype(f32), axis=0, keepdims=True) * first
    for i, term in enumerate((da * unit, da, db * unit, db)):
        out_ref[:, i * D : (i + 1) * D] += jnp.sum(term, axis=0, keepdims=True)
    out_ref[:, 4 * D : 5 * D] += bias
    out_ref[:, 5 * D : 6 * D] += bias


def vector_row(where, qkv_sum, up_sum, far, grad, x, da, db):
    rows, steps = grad.shape[0], 4
    block = lambda width: pl.BlockSpec((rows // steps, width), lambda i: (i, 0))
    rows_in = [grad, x, da, db]
    size = 9 * D + FF
    return call(
        vector_kernel,
        "vector_row",
        (steps,),
        [SCALARS, whole(*qkv_sum.shape), whole(*up_sum.shape), whole(*far.shape)] + [block(m.shape[1]) for m in rows_in],
        [whole(1, size)],
        shaped(((1, size), f32)),
    )(where, qkv_sum, up_sum, far, *rows_in)[0]


def settle_kernel(counts, where_ref, *refs):
    refs = list(refs)
    terms = [[refs.pop(0) for _ in range(n)] for n in counts]
    moms, refs = refs[:KINDS], refs[KINDS:]
    grads, refs = refs[:KINDS], refs[KINDS:]
    news, refs = refs[:KINDS], refs[KINDS:]
    *sends, pad_ref = refs
    layers, _, rows, width = moms[0].shape
    hidden = moms[2].shape[2]
    cut = 3 * width // 256 * 128 + 128
    pad_ref[...] = jnp.zeros_like(pad_ref)

    def total(parts, at):
        return sum(part[:, at].astype(f32) for part in parts)

    for layer in range(layers):
        first = total(terms[2], slice(layer * cut, (layer + 1) * cut))
        skip, rest = layers * cut, 3 * width - cut
        second = total(terms[2], slice(skip + layer * rest, skip + (layer + 1) * rest))
        qkv = jnp.concatenate([first, second], axis=1)
        up = total(terms[layer], slice(0, hidden))
        out_a = total(terms[layer], slice(hidden, hidden + BLK))
        down = total(terms[layer], slice(hidden + BLK, 2 * hidden + BLK))
        out_b = total(terms[layer], slice(2 * hidden + BLK, 2 * hidden + width))
        out = jnp.concatenate([out_a, out_b], axis=1)
        for c in range(3):
            grad = qkv[:, c * width : (c + 1) * width]
            new = MOMENTUM * moms[0][layer, c] + grad
            grads[0][layer, c], news[0][layer, c] = grad, new
            pad_ref[layer, :, c * width : (c + 1) * width] = new.astype(bf16)
        for kind, grad in ((1, out), (2, up), (3, down)):
            new = MOMENTUM * moms[kind][layer] + grad
            grads[kind][layer], news[kind][layer] = grad, new
            pad_ref[layer, :, kind * hidden : kind * hidden + grad.shape[1]] = new.astype(bf16)
    for by, send in enumerate(sends):
        at = pl.ds(pl.multiple_of((where_ref[1] ^ by) * hidden, PAIR), hidden)
        for layer in range(layers):
            send[layer] = pad_ref[layer, :, at]


def settle(where, terms, moms):
    rows, hidden = moms[2].shape[1:]
    flat = [m for group in terms for m in group]
    send = (LAYERS, rows, hidden)
    outs = [(m.shape, f32) for m in moms] * 2 + [(send, bf16)] * KINDS
    got = call(
        functools.partial(settle_kernel, [len(group) for group in terms]),
        "settle",
        (1,),
        [SCALARS] + [whole(*m.shape) for m in flat] + [whole(*m.shape) for m in moms],
        [whole(*shape) for shape, _ in outs],
        shaped(*outs),
        [pltpu.VMEM((LAYERS, rows, KINDS * hidden), bf16)],
        room=12,
    )(where, *flat, *moms)
    return got[:KINDS], got[KINDS : 2 * KINDS], got[2 * KINDS :]


def update_kernel(where_ref, *refs):
    backs, swapped = refs[:KINDS], refs[KINDS]
    masters, outs = refs[KINDS + 1 : 2 * KINDS + 1], refs[2 * KINDS + 1 : 3 * KINDS + 1]
    kept_ref = refs[-1]
    layers, _, rows, width = masters[0].shape
    for slot in range(KINDS):
        kept_ref[slot] = backs[slot][0]
    for layer in range(layers):
        mine = where_ref[0] == layer
        for kind in range(KINDS):
            slot = where_ref[1] ^ kind
            made = jnp.where(mine, kept_ref[slot], swapped[slot]).astype(f32)
            made = made * (-RATE_MAT * math.sqrt((3 * D, D, FF, FF)[kind]))
            if kind == 0:
                for c in range(3):
                    step = made[:, c * width : (c + 1) * width]
                    outs[0][layer, c] = masters[0][layer, c] * SHRINK + step
            else:
                outs[kind][layer] = masters[kind][layer] * SHRINK + made[:, : outs[kind].shape[2]]


def update(where, backs, swapped, masters):
    return call(
        update_kernel,
        "update",
        (1,),
        [SCALARS] + [whole(*m.shape) for m in (*backs, swapped, *masters)],
        [whole(*m.shape) for m in masters],
        shaped(*[(m.shape, f32) for m in masters]),
        [pltpu.VMEM(swapped.shape, bf16)],
    )(where, *backs, swapped, *masters)


def orth_kernel(inner, *refs):
    ins, outs = refs[:2], refs[2 : 2 + KINDS]
    x_ref, gram_ref, mix_ref = refs[2 + KINDS :]
    rows, width = ins[0].shape
    part, chunk = 256, 512
    blocks = rows // part
    total = jnp.zeros((1, 1), f32)
    for ref in ins:
        for i in range(blocks):
            v = ref[i * part : (i + 1) * part, :].astype(f32)
            total = total + jnp.sum(v * v).reshape(1, 1)
    inverse = 1.0 / (jnp.sqrt(total) + 1e-07)
    for i, ref in enumerate(ins):
        x_ref[:, i * width : (i + 1) * width] = (ref[...].astype(f32) * inverse).astype(bf16)

    def spread(ref, i, j, value):
        low = value.astype(bf16)
        ref[i * part : (i + 1) * part, j * part : (j + 1) * part] = low
        if j > i:
            ref[j * part : (j + 1) * part, i * part : (i + 1) * part] = jnp.transpose(low)

    def mixer():
        for i in range(blocks):
            at = slice(i * part, (i + 1) * part)
            gram = dot(x_ref[at, :], x_ref[i * part :, :], NT)
            for j in range(i, blocks):
                spread(gram_ref, i, j, gram[:, (j - i) * part : (j - i + 1) * part])
        for i in range(blocks):
            at = slice(i * part, (i + 1) * part)
            square = dot(gram_ref[at, :], gram_ref[:, i * part :])
            mixed = NS_B * gram_ref[at, i * part :].astype(f32) + NS_C * square
            for j in range(i, blocks):
                spread(mix_ref, i, j, mixed[:, (j - i) * part : (j - i + 1) * part])

    def sweep(_, carry):
        mixer()
        for c in range(2 * width // chunk):
            cols = slice(c * chunk, (c + 1) * chunk)
            x = x_ref[:, cols]
            y = NS_A * x.astype(f32) + dot(mix_ref[...], x)
            x_ref[:, cols] = y.astype(bf16)
        return carry

    lax.fori_loop(0, 4, sweep, 0)
    mixer()
    size = outs[0].shape[1]
    firsts = [by * inner * size for by in range(KINDS)]
    mine = jnp.concatenate([mix_ref[first : first + size, :] for first in firsts], axis=0)
    for half in range(2):
        cols = slice(half * width, (half + 1) * width)
        made = dot(mine, x_ref[:, cols])
        for by, out in enumerate(outs):
            x = x_ref[firsts[by] : firsts[by] + size, cols].astype(f32)
            out[half] = (NS_A * x + made[by * size : (by + 1) * size]).astype(bf16)


def orthogonalize(parts, inner):
    rows, width = parts[0].shape
    shape = (2, rows // (KINDS * inner), width)
    return call(
        functools.partial(orth_kernel, inner),
        "orthogonalize",
        (1,),
        [whole(rows, width)] * 2,
        [whole(*shape)] * KINDS,
        shaped(*[(shape, bf16)] * KINDS),
        [
            pltpu.VMEM((rows, 2 * width), bf16),
            pltpu.VMEM((rows, rows), bf16),
            pltpu.VMEM((rows, rows), bf16),
        ],
        room=20,
    )(*parts)


def shards(
    tokens,
    cotangent,
    w_qkv,
    w_out,
    w_up,
    w_down,
    mom_qkv,
    mom_out,
    mom_up,
    mom_down,
    vectors,
    vec_first,
    vec_second,
    lengths,
):
    tok_rows = tokens.shape[0]
    row_part = w_qkv.shape[1]
    head_part = w_qkv.shape[-1]
    hidden_part = w_up.shape[-1]
    widths = (3 * head_part, head_part, hidden_part, hidden_part)
    over = BLK
    cut_qkv = widths[0] // 256 * 128 + 128
    cut_rest = hidden_part + over
    skip = cut_rest // BLK
    fsdp_count = lax.axis_size("fsdp")
    core = lax.axis_index("tp")
    longest = SEQ_DEV * fsdp_count
    span = (tok_rows + longest - 2) // tok_rows
    where = place()

    def stored(qkv, out, up, down):
        return [qkv.transpose(0, 2, 1, 3), out.transpose(0, 2, 1), up, down.transpose(0, 2, 1)]

    def unstored(qkv, out, up, down):
        return [qkv.transpose(0, 2, 1, 3), out.transpose(0, 2, 1), up, down.transpose(0, 2, 1)]

    def qkv_piece(mats, layer):
        low = mats[0][layer].astype(bf16)
        return jnp.concatenate([low[c] for c in range(3)], axis=1)

    def rest_piece(mats, layer):
        out, up, down = [m[layer].astype(bf16) for m in mats[1:]]
        return jnp.concatenate([up, out[:, :over], down, out[:, over:]], axis=1)

    masters = stored(w_qkv, w_out, w_up, w_down)
    moments = stored(mom_qkv, mom_out, mom_up, mom_down)

    qkv_0 = Task(gather_steps(where, qkv_piece(masters, 0), cut_qkv))
    vecs = [vectors[layer : layer + 1] for layer in range(LAYERS)]
    a0, b0, half = norm_rows(where, vecs[0], tokens)
    rest, half, lengths, *later = advance(
        [qkv_0], rest_piece(masters, 0), half, lengths, *masters
    )
    rest_0 = Task(gather_steps(where, rest, cut_rest, True))
    half, lengths, *later = advance([qkv_0, rest_0], half, lengths, *later)
    win_0 = Task(window_steps(half, span))
    tables, start_rows, scalars = setup(lengths, where, tok_rows, (span + 1) * tok_rows)
    tables, start_rows, scalars, *later = advance(
        [qkv_0, rest_0, win_0], tables, start_rows, scalars, *later
    )
    qkv_1 = Task(gather_steps(where, qkv_piece(later, 1), cut_qkv, False, True))
    wq0 = qkv_0.result
    tables, *later = advance([win_0], tables, *later)
    q, k, v, vt = qkv_forward(where, a0, *win_0.result, wq0, vecs[0], tables)
    q, k, v, vt, *later = advance([rest_0, qkv_1], q, k, v, vt, *later)
    rest_1 = Task(gather_steps(where, rest_piece(later, 1), cut_rest, False, True))
    mixed, lse = attend(scalars, q, start_rows, k, vt)
    mixed, lse, b0 = advance([rest_0, rest_1], mixed, lse, b0)
    mixed, b0, wa, wb = advance([rest_1, qkv_1], mixed, b0, *rest_0.result)
    hid, slope, partial = ffn_forward(where, b0, wa, wb, 0, vecs[0], mixed, hidden_part)
    partial = advance([rest_1, qkv_1], partial)
    kept = [(tokens, a0, win_0.result, b0, q, k, v, mixed, lse, hid, slope)]
    weights = [(wq0, wa, wb, 0)]
    got = core_swap(partial)
    x1, a1, b1, half = norm_rows(where, vecs[1], tokens, vecs[0], partial, got)
    win_1 = Task(window_steps(half, span))
    a1, b1 = advance([win_1, qkv_1], a1, b1)
    a1, b1 = advance([win_1], a1, b1)
    wq1 = qkv_1.result
    q, k, v, vt = qkv_forward(where, a1, *win_1.result, wq1, vecs[1], tables)
    mixed, lse = attend(scalars, q, start_rows, k, vt)
    mixed, lse, b1, q, k, v = advance([rest_1], mixed, lse, b1, q, k, v)
    wa, wb = rest_1.result
    hid, slope, partial = ffn_forward(where, b1, wa, wb, 0, vecs[1], mixed, hidden_part)
    kept.append((x1, a1, win_1.result, b1, q, k, v, mixed, lse, hid, slope))
    weights.append((wq1, wa, wb, 0))

    def own_gradients(grad_low, layer):
        _, _, _, b, _, _, _, mixed, _, hid, slope = kept[layer]
        _, wa, wb, skip = weights[layer]
        return ffn_backward(where, grad_low, b, wa, wb, skip, slope, hid, mixed)

    def attention_gradients(g_mixed, layer, more=()):
        _, a, win, _, q, k, v, mixed, lse, _, _ = kept[layer]
        dq, dk, dv = attend_back(scalars, q, g_mixed, mixed, lse, start_rows, k, v)
        return qkv_backward(where, dq, dk, dv, a, *win, weights[layer][0], tables, vecs[layer], more)

    def joint_of(da, db, back, layer):
        rows_in = [da, db] + list(back)
        return row_call(joint_kernel, "joint", where, vecs[layer], rows_in, [(da.shape, bf16)])[0]

    def next_grad(grad, joint, got, layer):
        outs = [(joint.shape, f32), (joint.shape, bf16)]
        rows_in = [grad, joint, got, kept[layer][0]]
        return row_call(next_kernel, "next_grad", where, vecs[layer], rows_in, outs)

    *split, db1, g_mixed, up_sum1 = own_gradients(cotangent, 1)
    *split, g_mixed, partial, db1 = advance([], *split, g_mixed, partial, db1)
    rest_1 = Task(scatter_steps(where, *split, True))
    *split1, da1, keep, give, pre_sum1, far1 = attention_gradients(g_mixed, 1)
    *split1, da1, keep, give, partial = advance([], *split1, da1, keep, give, partial)
    back_1 = Task(window_back_steps(keep, give, span))
    da1, partial = advance([back_1, rest_1], da1, partial)
    da1, partial = advance([back_1, rest_1], da1, partial)
    joint = joint_of(da1, db1, back_1.result, 1)
    got = core_swap(joint)
    grad_x0, grad_low = next_grad(cotangent, joint, got, 1)
    *split, db0, g_mixed, up_sum0 = own_gradients(grad_low, 0)
    *split, g_mixed, da1, db0, partial = advance([rest_1], *split, g_mixed, da1, db0, partial)
    *split, g_mixed = advance([rest_1], *split, g_mixed)
    rest_0 = Task(scatter_steps(where, *split, False, True))
    *split, da0, keep, give, pre_sum0, far0 = attention_gradients(g_mixed, 0, split1)
    *split, da0, keep, give, da1, db1, partial = advance(
        [rest_0, rest_1], *split, da0, keep, give, da1, db1, partial
    )
    both_qkv = Task(scatter_steps(where, *split, True))
    back_0 = Task(window_back_steps(keep, give, span, True))
    row_0 = vector_row(where, pre_sum0, up_sum0, far0, grad_x0, kept[0][0], da0, db0)
    row_1 = vector_row(where, pre_sum1, up_sum1, far1, cotangent, kept[1][0], da1, db1)
    rows_both, partial = advance(
        [rest_0, both_qkv], jnp.concatenate([row_0, row_1], axis=0), partial
    )
    rows_both, partial = advance([both_qkv], rows_both, partial)
    vec_sum = Task(sum_steps(rows_both))
    partial = advance([both_qkv, rest_0, back_0, vec_sum], partial)
    partial = advance([both_qkv], partial)
    got = core_swap(partial)
    block_out = norm_rows(where, vecs[1], kept[1][0], vecs[1], partial, got, False)[0]
    block_out = advance([both_qkv, rest_0], block_out)
    terms = [rest_0.result, rest_1.result, both_qkv.result]
    grads, new_moms, blocks = settle(where, terms, moments)
    owned = Task(owner_steps(blocks[0], blocks[1:]))
    advance([owned, vec_sum])
    advance([owned])
    while owned.flying is not None:
        advance([owned, vec_sum])

    inner = fsdp_count // KINDS
    parts = advance([back_0], *owned.result)
    made = orthogonalize(parts, inner)
    *made, da0 = advance([back_0], *made, da0)
    backs = [made[0]] + [
        permute(made[by], xor_pairs(fsdp_count, by * inner)) for by in range(1, KINDS)
    ]
    joint = joint_of(da0, db0, back_0.result, 0)
    got = core_swap(joint)
    grad_in, _ = next_grad(grad_x0, joint, got, 0)
    while vec_sum.flying is not None:
        grad_in = advance([vec_sum], grad_in)
    swapped = core_swap(jnp.stack([m[1] for m in backs]))
    new_weights = update(where, backs, swapped, masters)

    grad_vectors = vec_sum.result
    first_new = BETA_ONE * vec_first + (1.0 - BETA_ONE) * grad_vectors
    second_new = BETA_TWO * vec_second + (1.0 - BETA_TWO) * grad_vectors * grad_vectors
    first_hat = first_new / (1.0 - BETA_ONE**STEP)
    second_hat = second_new / (1.0 - BETA_TWO**STEP)
    vectors_new = vectors - RATE_VEC * first_hat / (jnp.sqrt(second_hat) + ADAM_EPS)
    return (
        block_out,
        grad_in,
        *unstored(*grads),
        *unstored(*new_moms),
        *unstored(*new_weights),
        first_new,
        second_new,
        vectors_new,
        grad_vectors[:, 9 * D :],
    )


def solution(mesh):
    weights = (
        P(None, "fsdp", None, "tp"),
        P(None, "tp", "fsdp"),
        P(None, "fsdp", "tp"),
        P(None, "tp", "fsdp"),
    )
    rows = (P("fsdp", None), P("fsdp", None))
    return jax.shard_map(
        shards,
        mesh=mesh,
        in_specs=rows + weights + weights + (P(), P(), P(), P()),
        out_specs=rows + weights + weights + weights + (P(), P(), P(), P()),
        check_vma=False,
    )
```

```python
import functools
import math

import jax
import jax.numpy as jnp
import numpy as np
from jax import lax
from jax.experimental import pallas as pl
from jax.experimental.pallas import tpu as pltpu
from jax.sharding import PartitionSpec as P

D = 768
HEAD = 64
ROT = 16
FF = 3072
LAYERS = 2
SEQ_DEV = 64
STEP = 10
PAIR = 2 * HEAD
BLK = 256
KINDS = 4

MASKED = -1000000000.0
EPS_NORM = 1e-05
NS_A = 3.4445
NS_B = -4.775
NS_C = 2.0315
MOMENTUM = 0.95
RATE_MAT = 0.02
SHRINK = 0.99
RATE_VEC = 0.25
BETA_ONE = 0.9
BETA_TWO = 0.95
ADAM_EPS = 1e-08
ROOM_ATTEND = 16

bf16 = jnp.bfloat16
f32 = jnp.float32


def permute(x, pairs):
    return lax.ppermute(x, "fsdp", pairs)


def xor_pairs(count, by):
    return [(i, i ^ by) for i in range(count)]


def core_swap(x):
    count = lax.axis_size("tp")
    return lax.ppermute(x, "tp", [(i, i ^ 1) for i in range(count)])


def shifted(x, by):
    devices = lax.axis_size("fsdp")
    return lax.ppermute(
        x, "fsdp", [(i, i + by) for i in range(devices) if 0 <= i + by < devices]
    )


def on_grid():
    return lax.axis_size("fsdp") == 16


def place():
    index = lax.axis_index("fsdp")
    inner = lax.axis_size("fsdp") // KINDS
    bits = [(index // 2) % 2, index % 2] if on_grid() else [index * 0, index * 0]
    parts = [lax.axis_index("tp"), index // inner, *bits, index]
    return jnp.stack([p.astype(jnp.int32) for p in parts])


class Task:
    def __init__(self, steps):
        self.steps = steps
        self.result = None
        self.flying = None
        self.resume(None)

    def resume(self, arrived):
        try:
            self.flying = self.steps.send(arrived)
        except StopIteration as stop:
            self.result = stop.value
            self.flying = None


def advance(tasks, *arrays):
    tasks = [t for t in tasks if t.flying is not None]
    arrived, arrays = lax.optimization_barrier(([t.flying for t in tasks], arrays))
    for task, got in zip(tasks, arrived):
        task.resume(got)
    return arrays if len(arrays) != 1 else arrays[0]


def gather_steps(where, piece, cut, apart=False, pause=False):
    rows, cols = piece.shape
    if not on_grid():
        full = lax.all_gather(piece, "fsdp", axis=0, tiled=True)
        return full[:, :cut], full[:, cut:]
        yield
    got = []
    for group in ((1, 2), (3,)) if apart else ((1, 2, 3),):
        got += yield [permute(piece, xor_pairs(16, 4 * by)) for by in group]
    part_a, part_b = join_planes(where, [piece] + got, cut)
    if pause:
        part_a, part_b = yield [part_a, part_b]
    got_a, got_b = yield [permute(part_a, xor_pairs(16, 1)), permute(part_b, xor_pairs(16, 2))]
    part_a, part_b = join_chips(where, part_a, got_a, part_b, got_b, False)
    got_a, got_b = yield [permute(part_a, xor_pairs(16, 2)), permute(part_b, xor_pairs(16, 1))]
    part_a, part_b = join_chips(where, part_a, got_a, part_b, got_b, True)
    return part_a.reshape(16 * rows, -1), part_b.reshape(16 * rows, -1)


def natural(keep, send, axis):
    shape = (4, 1, 2, -1) if axis == 1 else (4, 2, 1, -1)
    parts = [m.reshape(shape + (m.shape[-1],)) for m in (keep, send)]
    full = jnp.concatenate(parts, axis=axis)
    return full.reshape(-1, keep.shape[-1])


def scatter_steps(where, keep_a, send_a, keep_b, send_b, pause=False, apart=False):
    if not on_grid():
        full = jnp.concatenate([natural(keep_a, send_a, 1), natural(keep_b, send_b, 2)], axis=1)
        return [lax.psum_scatter(full, "fsdp", scatter_dimension=0, tiled=True)]
        yield
    got_a, got_b = yield [permute(send_a, xor_pairs(16, 2)), permute(send_b, xor_pairs(16, 1))]
    keep_a, send_a, keep_b, send_b = add_split(where, keep_a, got_a, keep_b, got_b)
    if pause:
        keep_a, send_a, keep_b, send_b = yield [keep_a, send_a, keep_b, send_b]
    got_a, got_b = yield [permute(send_a, xor_pairs(16, 1)), permute(send_b, xor_pairs(16, 2))]
    own, *sends = add_planes(where, keep_a, got_a, keep_b, got_b)
    if pause:
        own, *sends = yield [own, *sends]
    got = [own]
    for group in ((0, 1), (2,)) if apart else ((0, 1, 2),):
        got += yield [permute(sends[i], xor_pairs(16, 4 * (i + 1))) for i in group]
    return got


def window_steps(half, span):
    got = yield [shifted(half, step) for step in range(span, 0, -1)]
    got = jnp.concatenate(got, axis=0)
    (other,) = yield [core_swap(got)]
    return got, other


def window_back_steps(keep, give, span, pause=False):
    (got,) = yield [core_swap(give)]
    half = (keep.astype(f32) + got.astype(f32)).astype(bf16).reshape(span, -1, keep.shape[-1])
    if pause:
        (half,) = yield [half]
    back = yield [shifted(half[span - step], -step) for step in range(span, 0, -1)]
    return back


def sum_steps(x):
    count = lax.axis_size("fsdp")
    step = 1
    while step < count:
        (got,) = yield [permute(x, xor_pairs(count, step))]
        x = x + got
        step *= 2
    (got,) = yield [core_swap(x)]
    return x + got


def owner_steps(own, sends):
    count = lax.axis_size("fsdp")
    inner = count // KINDS
    core = lax.axis_index("tp")
    rows, width = own.shape[1:]
    got = yield [permute(sends[by - 1], xor_pairs(count, by * inner)) for by in range(1, KINDS)]
    terms = [own] + list(got)
    give = jnp.stack([jnp.where(core == 0, m[1], m[0]) for m in terms])
    part_a = jnp.stack([jnp.where(core == 0, m[0], m[1]) for m in terms])
    part_a, part_b = yield [part_a, core_swap(give)]
    bits = inner.bit_length() - 1
    shape = (KINDS,) + (1,) * bits + (rows, width)
    part_a, part_b = part_a.reshape(shape), part_b.reshape(shape)
    for step in range(bits):
        bit_a, bit_b = step, bits - 1 - step
        got_a, got_b = yield [
            permute(part_a, xor_pairs(count, 1 << bit_a)),
            permute(part_b, xor_pairs(count, 1 << bit_b)),
        ]
        part_a = jnp.concatenate([part_a, got_a], axis=1 + bit_a)
        part_b = jnp.concatenate([part_b, got_b], axis=1 + bit_b)
    return [m.reshape(count * rows, width) for m in (part_a, part_b)]


SMALL = pl.CostEstimate(flops=1, bytes_accessed=1, transcendentals=0)
SCALARS = pl.BlockSpec(memory_space=pltpu.SMEM)
NT = (((1,), (1,)), ((), ()))
TN = (((0,), (0,)), ((), ()))


def dot(a, b, how=(((1,), (0,)), ((), ()))):
    return lax.dot_general(a, b, how, preferred_element_type=f32)


def whole(*shape):
    return pl.BlockSpec(shape, lambda *_: (0,) * len(shape))


def shaped(*shapes_and_kinds):
    return [jax.ShapeDtypeStruct(shape, kind) for shape, kind in shapes_and_kinds]


def call(kernel, name, grid, in_specs, out_specs, out_shape, scratch=(), room=8):
    return pl.pallas_call(
        kernel,
        grid=grid,
        in_specs=in_specs,
        out_specs=out_specs,
        out_shape=out_shape,
        scratch_shapes=list(scratch),
        compiler_params=pltpu.CompilerParams(vmem_limit_bytes=room << 20),
        cost_estimate=SMALL,
        name=name,
    )


def join_planes_kernel(cut, where_ref, *refs):
    *pieces, out_a, out_b = refs
    quarter = where_ref[1]
    for by, piece in enumerate(pieces):
        plane = quarter ^ by
        out_a[plane] = piece[:, :cut]
        out_b[plane] = piece[:, cut:]


def join_planes(where, pieces, cut):
    rows, cols = pieces[0].shape
    shapes = [(4, rows, cut), (4, rows, cols - cut)]
    return call(
        functools.partial(join_planes_kernel, cut),
        "join_planes",
        (1,),
        [SCALARS] + [whole(rows, cols)] * 4,
        [whole(*shape) for shape in shapes],
        shaped(*[(shape, bf16) for shape in shapes]),
    )(where, *pieces)


def join_chips_kernel(last, where_ref, own_a, got_a, own_b, got_b, out_a, out_b):
    y, x = where_ref[2], where_ref[3]
    if not last:
        out_a[0, x], out_a[0, 1 - x] = own_a[0], got_a[0]
        out_b[0, y], out_b[0, 1 - y] = own_b[0], got_b[0]
    else:
        out_a[0, y], out_a[0, 1 - y] = own_a[0], got_a[0]
        for side in range(2):
            out_b[0, side, x], out_b[0, side, 1 - x] = own_b[0, side], got_b[0, side]


def join_chips(where, own_a, got_a, own_b, got_b, last):
    rows = own_a.shape[-2]
    ins, outs = ((2, rows), (2, 2, rows)) if last else ((rows,), (2, rows))

    def spec(shape, width):
        return pl.BlockSpec((1,) + shape + (width,), lambda i: (i,) + (0,) * (len(shape) + 1))

    wide_a, wide_b = own_a.shape[-1], own_b.shape[-1]
    return call(
        functools.partial(join_chips_kernel, last),
        "join_chips",
        (4,),
        [SCALARS, spec(ins, wide_a), spec(ins, wide_a), spec(ins, wide_b), spec(ins, wide_b)],
        [spec(outs, wide_a), spec(outs, wide_b)],
        shaped(((4,) + outs + (wide_a,), bf16), ((4,) + outs + (wide_b,), bf16)),
    )(where, own_a, got_a, own_b, got_b)


def add_split_kernel(where_ref, keep_a, got_a, keep_b, got_b, out_ka, out_sa, out_kb, out_sb):
    rows = keep_a.shape[0] // 8
    for bit, keep, got, out_k, out_s in (
        (where_ref[3], keep_a, got_a, out_ka, out_sa),
        (where_ref[2], keep_b, got_b, out_kb, out_sb),
    ):
        for z in range(4):
            for flip, out in ((0, out_k), (1, out_s)):
                at = pl.ds(pl.multiple_of((2 * z + (bit ^ flip)) * rows, 16), rows)
                total = keep[at, :].astype(f32) + got[at, :].astype(f32)
                out[z * rows : (z + 1) * rows, :] = total.astype(bf16)


def add_split(where, keep_a, got_a, keep_b, got_b):
    rows, wide_a = keep_a.shape
    wide_b = keep_b.shape[1]
    outs = [(rows // 2, wide_a)] * 2 + [(rows // 2, wide_b)] * 2
    return call(
        add_split_kernel,
        "add_split",
        (1,),
        [SCALARS] + [whole(rows, wide_a)] * 2 + [whole(rows, wide_b)] * 2,
        [whole(*shape) for shape in outs],
        shaped(*[(shape, bf16) for shape in outs]),
        room=12,
    )(where, keep_a, got_a, keep_b, got_b)


def add_planes_kernel(where_ref, keep_a, got_a, keep_b, got_b, *outs):
    rows = keep_a.shape[0] // 4
    cut = keep_a.shape[1]
    for by, out in enumerate(outs):
        at = pl.ds(pl.multiple_of((where_ref[1] ^ by) * rows, 16), rows)
        out[:, :cut] = (keep_a[at, :].astype(f32) + got_a[at, :].astype(f32)).astype(bf16)
        out[:, cut:] = (keep_b[at, :].astype(f32) + got_b[at, :].astype(f32)).astype(bf16)


def add_planes(where, keep_a, got_a, keep_b, got_b):
    rows, wide_a = keep_a.shape
    wide_b = keep_b.shape[1]
    shape = (rows // 4, wide_a + wide_b)
    return call(
        add_planes_kernel,
        "add_planes",
        (1,),
        [SCALARS] + [whole(rows, wide_a)] * 2 + [whole(rows, wide_b)] * 2,
        [whole(*shape)] * 4,
        shaped(*[(shape, bf16)] * 4),
    )(where, keep_a, got_a, keep_b, got_b)


def setup_kernel(len_ref, where_ref, freq_ref, table_ref, start_ref, scal_ref):
    rows, total = start_ref.shape[1], table_ref.shape[1]
    base = where_ref[4] * rows
    first = base - (total - rows)
    half = ROT // 2

    def starts_of(index):
        end, out = jnp.int32(0), jnp.zeros_like(index)
        for i in range(len_ref.shape[0]):
            end = end + len_ref[i]
            out = jnp.where(index >= end, end, out)
        return out

    lane = lax.broadcasted_iota(jnp.int32, (BLK, PAIR), 1) % HEAD
    for c in range(total // BLK):
        at = slice(c * BLK, (c + 1) * BLK)
        index = first + c * BLK + lax.broadcasted_iota(jnp.int32, (BLK, PAIR), 0)
        phase = (index - starts_of(index)).astype(f32) * freq_ref[...]
        sine = jnp.sin(phase)
        table_ref[0, at, :] = jnp.cos(phase)
        table_ref[1, at, :] = jnp.where(lane < half, -sine, 0.0)
        table_ref[2, at, :] = jnp.where((lane >= half) & (lane < ROT), sine, 0.0)
    start_ref[...] = starts_of(base + lax.broadcasted_iota(jnp.int32, start_ref.shape, 1))
    own = (total - rows) // BLK
    scal_ref[0] = base
    scal_ref[1] = jnp.minimum((starts_of(base + BLK) - first) // BLK, own)
    scal_ref[2] = (starts_of(base) - first) // BLK


def setup(lengths, where, rows, total):
    lane = np.arange(PAIR) % HEAD
    freqs = np.exp((lane % (ROT // 2)) * (-2.0 * math.log(10000.0) / ROT))
    freqs = np.where(lane < ROT, freqs, 0.0).astype(np.float32)[None]
    return call(
        setup_kernel,
        "setup",
        (1,),
        [SCALARS, SCALARS, whole(1, PAIR)],
        [whole(3, total, PAIR), whole(8, rows), SCALARS],
        shaped(((3, total, PAIR), f32), ((8, rows), jnp.int32), ((3,), jnp.int32)),
        room=8,
    )(lengths, where, jnp.asarray(freqs))


def unit_rows(x):
    centered = x - jnp.mean(x, axis=-1, keepdims=True)
    inverse = lax.rsqrt(jnp.mean(centered * centered, axis=-1, keepdims=True) + EPS_NORM)
    return centered * inverse, inverse


def norm_kernel(where_ref, vec_ref, x_ref, a_ref, b_ref, half_ref):
    unit, _ = unit_rows(x_ref[...].astype(f32))
    a = (unit * vec_ref[:, :D] + vec_ref[:, D : 2 * D]).astype(bf16)
    a_ref[...] = a
    b_ref[...] = (unit * vec_ref[:, 2 * D : 3 * D] + vec_ref[:, 3 * D : 4 * D]).astype(bf16)
    half_ref[...] = jnp.where(where_ref[0] == 0, unit[:, : D // 2], unit[:, D // 2 :]).astype(bf16)


def add_norm_kernel(where_ref, old_ref, vec_ref, x_ref, part_ref, got_ref, new_ref, *outs):
    x = x_ref[...].astype(f32) + part_ref[...].astype(f32) + got_ref[...].astype(f32)
    x = x + old_ref[:, 4 * D : 5 * D] + old_ref[:, 5 * D : 6 * D]
    new_ref[...] = x
    if outs:
        norm_kernel(where_ref, vec_ref, new_ref, *outs)


def norm_rows(where, vec, x, old_vec=None, part=None, got=None, normed=True):
    rows = x.shape[0]
    step = rows // 4
    block = lambda width: pl.BlockSpec((step, width), lambda i: (i, 0))
    flat = whole(1, vec.shape[1])
    out = [((rows, D), bf16), ((rows, D), bf16), ((rows, D // 2), bf16)] if normed else []
    if part is None:
        specs, kernel, args = [flat, block(D)], norm_kernel, (vec, x)
    else:
        specs, kernel = [flat, flat] + [block(D)] * 3, add_norm_kernel
        args, out = (old_vec, vec, x, part, got), [((rows, D), f32)] + out
    return call(
        kernel,
        "norm_rows",
        (4,),
        [SCALARS] + specs,
        [block(shape[1]) for shape, _ in out],
        shaped(*out),
    )(where, *args)


def rope(u, tables, sign):
    half = ROT // 2
    return u * tables[0] + sign * (
        pltpu.roll(u, PAIR - half, 1) * tables[1] + pltpu.roll(u, half, 1) * tables[2]
    )


def window_block(before, where_ref, vec_ref, own_ref, half_ref, other_ref):
    half, other = half_ref[...], other_ref[...]
    first = jnp.where(where_ref[0] == 0, half, other)
    second = jnp.where(where_ref[0] == 0, other, half)
    unit = jnp.concatenate([first, second], axis=1).astype(f32)
    earlier = (unit * vec_ref[:, :D] + vec_ref[:, D : 2 * D]).astype(bf16)
    return jnp.where(pl.program_id(0) < before, earlier, own_ref[...]), unit


def qkv_kernel(
    before, where_ref, own_ref, half_ref, other_ref, wa_ref, wb_ref, vec_ref, table_ref,
    q_ref, k_ref, v_ref, vt_ref,
):
    width = q_ref.shape[1]
    over = wa_ref.shape[1] - width
    a, _ = window_block(before, where_ref, vec_ref, own_ref, half_ref, other_ref)
    tables = [table_ref[i] for i in range(3)]
    bias = [
        vec_ref[:, pl.ds(pl.multiple_of((6 + c) * D + where_ref[0] * width, PAIR), width)]
        for c in range(3)
    ]

    @pl.when(pl.program_id(0) == before)
    def _():
        pre = dot(a, wa_ref[:, :width]) + bias[0]
        for p in range(width // PAIR):
            at = slice(p * PAIR, (p + 1) * PAIR)
            q_ref[:, at] = (rope(pre[:, at], tables, 1.0) * HEAD ** (-0.5)).astype(bf16)

    front, rest = dot(a, wa_ref[:, width:]), dot(a, wb_ref[...])
    values = (rest[:, width - over :] + bias[2]).astype(bf16)
    v_ref[...] = values
    vt_ref[...] = jnp.transpose(values)
    pre = jnp.concatenate([front, rest[:, : width - over]], axis=1) + bias[1]
    for p in range(width // PAIR):
        at = slice(p * PAIR, (p + 1) * PAIR)
        k_ref[:, at] = rope(pre[:, at], tables, 1.0).astype(bf16)


def window_specs(rows, before):
    earlier = pl.BlockSpec((rows, D // 2), lambda i: (jnp.minimum(i, before - 1), 0))
    return [whole(rows, D), earlier, earlier]


def qkv_forward(where, own, half, other, weights, vec, tables):
    rows, total = own.shape[0], tables.shape[1]
    width = (weights[0].shape[1] + weights[1].shape[1]) // 3
    before = total // rows - 1
    flat = pl.BlockSpec((rows, width), lambda i: (i, 0))
    return call(
        functools.partial(qkv_kernel, before),
        "qkv_forward",
        (total // rows,),
        [SCALARS]
        + window_specs(rows, before)
        + [whole(*weights[0].shape), whole(*weights[1].shape), whole(*vec.shape)]
        + [pl.BlockSpec((3, rows, PAIR), lambda i: (0, i, 0))],
        [whole(rows, width), flat, flat, pl.BlockSpec((width, rows), lambda i: (0, i))],
        shaped(
            ((rows, width), bf16),
            ((total, width), bf16),
            ((total, width), bf16),
            ((width, total), bf16),
        ),
        room=14,
    )(where, own, half, other, *weights, vec, tables)


def qkv_back_kernel(
    before, more, where_ref, dq_ref, dk_ref, dv_ref, own_ref, half_ref, other_ref, wa_ref, wb_ref, table_ref,
    vec_ref, *refs,
):
    more_refs, refs = refs[:more], refs[more:]
    ka_ref, sa_ref, kb_ref, sb_ref, da_ref, keep_ref, give_ref, sum_ref, far_ref, pre_ref, acc_ref = refs
    width = dq_ref.shape[1]
    cut = wa_ref.shape[1]
    step = pl.program_id(0)
    tables = [table_ref[i] for i in range(3)]

    @pl.when(step == 0)
    def _():
        acc_ref[...] = jnp.zeros_like(acc_ref)
        sum_ref[...] = jnp.zeros_like(sum_ref)
        far_ref[...] = jnp.zeros_like(far_ref)

    def put(at, value):
        pre_ref[:, at] = value
        sum_ref[:, at] += jnp.sum(value.astype(f32), axis=0, keepdims=True)

    a, unit = window_block(before, where_ref, vec_ref, own_ref, half_ref, other_ref)
    turned = jnp.transpose(a)
    for p in range(width // PAIR):
        at = slice(p * PAIR, (p + 1) * PAIR)
        put(
            slice(width + p * PAIR, width + (p + 1) * PAIR),
            rope(dk_ref[:, at].astype(f32), tables, -1.0).astype(bf16),
        )
    put(slice(2 * width, 3 * width), dv_ref[...])

    @pl.when(step < before)
    def _():
        acc_ref[:, width:] += dot(turned, pre_ref[:, width:])
        da = dot(pre_ref[:, width:cut], wa_ref[:, width:], NT) + dot(pre_ref[:, cut:], wb_ref[...], NT)
        far_ref[0:1, :] += jnp.sum(da * unit, axis=0, keepdims=True)
        far_ref[1:2, :] += jnp.sum(da, axis=0, keepdims=True)
        low, high = da[:, : D // 2].astype(bf16), da[:, D // 2 :].astype(bf16)
        keep_ref[...] = jnp.where(where_ref[0] == 0, low, high)
        give_ref[...] = jnp.where(where_ref[0] == 0, high, low)

    @pl.when(step == before)
    def _():
        for p in range(width // PAIR):
            at = slice(p * PAIR, (p + 1) * PAIR)
            query = rope(dq_ref[:, at].astype(f32), tables, -1.0) * HEAD ** (-0.5)
            put(at, query.astype(bf16))
        acc_ref[...] += dot(turned, pre_ref[...])
        da_ref[...] = dot(pre_ref[:, :cut], wa_ref[...], NT) + dot(pre_ref[:, cut:], wb_ref[...], NT)
        part = acc_ref.shape[0] // 16
        for flip, out_a, out_b in ((0, ka_ref, kb_ref), (1, sa_ref, sb_ref)):
            for z in range(4):
                at = pl.ds(pl.multiple_of((2 * z + (where_ref[2] ^ flip)) * 2 * part, 16), 2 * part)
                out_a[2 * z * part : (2 * z + 2) * part, :cut] = acc_ref[at, :cut].astype(bf16)
                for y in range(2):
                    row = (2 * z + y) * part
                    at = pl.ds(pl.multiple_of(2 * row + (where_ref[3] ^ flip) * part, 16), part)
                    out_b[row : row + part, : 3 * width - cut] = acc_ref[at, cut:].astype(bf16)
        for ref, out in zip(more_refs, (ka_ref, sa_ref, kb_ref, sb_ref)):
            out[:, ref.shape[1] :] = ref[...]


def qkv_backward(where, dq, dk, dv, own, half, other, weights, tables, vec, more=()):
    rows, width = dq.shape
    total = tables.shape[1]
    before = total // rows - 1
    cut = weights[0].shape[1]
    each = pl.BlockSpec((rows, width), lambda i: (i, 0))
    earlier = pl.BlockSpec((rows, D // 2), lambda i: (jnp.minimum(i, before - 1), 0))
    times = 2 if more else 1
    splits = [(D // 2, times * cut)] * 2 + [(D // 2, times * (3 * width - cut))] * 2
    return call(
        functools.partial(qkv_back_kernel, before, len(more)),
        "qkv_backward",
        (total // rows,),
        [SCALARS, whole(rows, width), each, each]
        + window_specs(rows, before)
        + [whole(*weights[0].shape), whole(*weights[1].shape)]
        + [pl.BlockSpec((3, rows, PAIR), lambda i: (0, i, 0)), whole(*vec.shape)]
        + [whole(*m.shape) for m in more],
        [whole(*shape) for shape in splits]
        + [whole(rows, D), earlier, earlier, whole(1, 3 * width), whole(8, D)],
        shaped(
            *[(shape, bf16) for shape in splits],
            ((rows, D), f32),
            ((total - rows, D // 2), bf16),
            ((total - rows, D // 2), bf16),
            ((1, 3 * width), f32),
            ((8, D), f32),
        ),
        [pltpu.VMEM((rows, 3 * width), bf16), pltpu.VMEM((D, 3 * width), f32)],
        room=18,
    )(where, dq, dk, dv, own, half, other, *weights, tables, vec, *more)


def low_lanes():
    return lax.broadcasted_iota(jnp.int32, (1, PAIR), 1) < HEAD


def both_heads(x):
    low = low_lanes()
    zero = jnp.zeros_like(x[:BLK])
    parts = []
    for at in range(0, x.shape[0], BLK):
        block = x[at : at + BLK]
        parts += [jnp.where(low, block, zero), jnp.where(low, zero, block)]
    return jnp.concatenate(parts, axis=0)


def both_columns(first, second):
    parts = []
    for at in range(0, first.shape[1], BLK):
        parts += [first[:, at : at + BLK], second[:, at : at + BLK]]
    return jnp.concatenate(parts, axis=1)


def key_loops(scal_ref, blocks, own, work):
    work(own + 1, slice(2 * BLK, 4 * BLK))
    low_all, low_first = scal_ref[1], scal_ref[2]

    def full(i, carry):
        work(own - i, slice(0, 4 * BLK))
        return carry

    def first_only(i, carry):
        work(low_all - 1 - i, slice(0, 2 * BLK))
        return carry

    lax.fori_loop(0, own - low_all + 1, full, 0)
    lax.fori_loop(0, low_all - low_first, first_only, 0)


def attend_kernel(scal_ref, q_ref, start_ref, k_ref, vt_ref, o_ref, lse_ref, q2_ref, m_ref, l_ref, acc_ref):
    rows, total = q_ref.shape[0], k_ref.shape[0]
    pairs = q_ref.shape[1] // PAIR
    base = scal_ref[0]
    m_ref[...] = jnp.full_like(m_ref, -1e30)
    l_ref[...] = jnp.zeros_like(l_ref)
    acc_ref[...] = jnp.zeros_like(acc_ref)
    for p in range(pairs):
        q2_ref[p] = both_heads(q_ref[:, p * PAIR : (p + 1) * PAIR])
    starts = both_columns(start_ref[0:1, :], start_ref[0:1, :])
    index = base + lax.broadcasted_iota(jnp.int32, (1, rows), 1)
    index = both_columns(index, index)

    def work(kb, cols):
        at = pl.ds(pl.multiple_of(kb * BLK, BLK), BLK)
        key_index = base - (total - rows) + kb * BLK + lax.broadcasted_iota(jnp.int32, (BLK, 1), 0)
        seen = (key_index >= starts[:, cols]) & (key_index <= index[:, cols])
        for p in range(pairs):
            lanes = slice(p * PAIR, (p + 1) * PAIR)
            s = jnp.where(seen, dot(k_ref[at, lanes], q2_ref[p, cols, :], NT), MASKED)
            m_old = m_ref[p, 0:1, cols]
            m_new = jnp.maximum(m_old, jnp.max(s, axis=0, keepdims=True))
            scale = jnp.exp(m_old - m_new)
            e = jnp.exp(s - m_new)
            m_ref[p, 0:1, cols] = m_new
            l_ref[p, 0:1, cols] = l_ref[p, 0:1, cols] * scale + jnp.sum(e, axis=0, keepdims=True)
            acc_ref[p, :, cols] = acc_ref[p, :, cols] * scale + dot(vt_ref[lanes, at], e.astype(bf16))

    key_loops(scal_ref, total // BLK, (total - rows) // BLK, work)
    for p in range(pairs):
        total_p = l_ref[p, 0:1, :]
        acc = acc_ref[p] / total_p
        lse_ref[p, 0:1, :] = m_ref[p, 0:1, :] + jnp.log(total_p)
        for qb in range(rows // BLK):
            first = acc[:HEAD, 2 * qb * BLK : (2 * qb + 1) * BLK]
            second = acc[HEAD:, (2 * qb + 1) * BLK : (2 * qb + 2) * BLK]
            o_ref[qb * BLK : (qb + 1) * BLK, p * PAIR : (p + 1) * PAIR] = jnp.transpose(
                jnp.concatenate([first, second], axis=0)
            ).astype(bf16)


def attend(scalars, q, start_rows, k, vt):
    rows, width = q.shape
    total = k.shape[0]
    pairs = width // PAIR
    return pl.pallas_call(
        attend_kernel,
        grid=(1,),
        in_specs=[
            pl.BlockSpec(memory_space=pltpu.SMEM),
            whole(rows, width),
            whole(8, rows),
            whole(total, width),
            whole(width, total),
        ],
        out_specs=[whole(rows, width), whole(pairs, 8, 2 * rows)],
        out_shape=[
            jax.ShapeDtypeStruct((rows, width), bf16),
            jax.ShapeDtypeStruct((pairs, 8, 2 * rows), f32),
        ],
        scratch_shapes=[
            pltpu.VMEM((pairs, 2 * rows, PAIR), bf16),
            pltpu.VMEM((pairs, 8, 2 * rows), f32),
            pltpu.VMEM((pairs, 8, 2 * rows), f32),
            pltpu.VMEM((pairs, PAIR, 2 * rows), f32),
        ],
        compiler_params=pltpu.CompilerParams(vmem_limit_bytes=ROOM_ATTEND << 20),
        cost_estimate=SMALL,
        name="attend",
    )(scalars, q, start_rows, k, vt)


def attend_back_kernel(
    scal_ref, q_ref, g_ref, o_ref, lse_ref, start_ref, k_ref, v_ref,
    dq_ref, dk_ref, dv_ref, q2_ref, g2_ref, delta_ref, acc_ref,
):
    rows, total = q_ref.shape[0], k_ref.shape[0]
    pairs = q_ref.shape[1] // PAIR
    base = scal_ref[0]
    dk_ref[...] = jnp.zeros_like(dk_ref)
    dv_ref[...] = jnp.zeros_like(dv_ref)
    acc_ref[...] = jnp.zeros_like(acc_ref)
    which = lax.broadcasted_iota(jnp.int32, (8, PAIR), 0)
    lane = lax.broadcasted_iota(jnp.int32, (8, PAIR), 1)
    chosen = (which == lane // HEAD).astype(f32)
    for p in range(pairs):
        lanes = slice(p * PAIR, (p + 1) * PAIR)
        g = g_ref[:, lanes]
        q2_ref[p] = both_heads(q_ref[:, lanes])
        g2_ref[p] = both_heads(g)
        delta = lax.dot_general(
            chosen,
            g.astype(f32) * o_ref[:, lanes].astype(f32),
            NT,
            precision=lax.Precision.HIGHEST,
            preferred_element_type=f32,
        )
        delta_ref[p, 0:1, :] = both_columns(delta[0:1, :], delta[1:2, :])
    starts = both_columns(start_ref[0:1, :], start_ref[0:1, :])
    index = base + lax.broadcasted_iota(jnp.int32, (1, rows), 1)
    index = both_columns(index, index)

    def work(kb, cols):
        at = pl.ds(pl.multiple_of(kb * BLK, BLK), BLK)
        key_index = base - (total - rows) + kb * BLK + lax.broadcasted_iota(jnp.int32, (BLK, 1), 0)
        seen = (key_index >= starts[:, cols]) & (key_index <= index[:, cols])
        for p in range(pairs):
            lanes = slice(p * PAIR, (p + 1) * PAIR)
            keys, q2, g2 = k_ref[at, lanes], q2_ref[p, cols, :], g2_ref[p, cols, :]
            s = jnp.where(seen, dot(keys, q2, NT), MASKED)
            prob = jnp.exp(s - lse_ref[p, 0:1, cols])
            d_prob = dot(v_ref[at, lanes], g2, NT)
            d_score = (prob * (d_prob - delta_ref[p, 0:1, cols])).astype(bf16)
            dv_ref[at, lanes] = dot(prob.astype(bf16), g2).astype(bf16)
            dk_ref[at, lanes] = dot(d_score, q2).astype(bf16)
            acc_ref[p, cols, :] += dot(d_score, keys, TN)

    key_loops(scal_ref, total // BLK, (total - rows) // BLK, work)
    low = low_lanes()
    for p in range(pairs):
        for qb in range(rows // BLK):
            first = acc_ref[p, 2 * qb * BLK : (2 * qb + 1) * BLK, :]
            second = acc_ref[p, (2 * qb + 1) * BLK : (2 * qb + 2) * BLK, :]
            dq_ref[qb * BLK : (qb + 1) * BLK, p * PAIR : (p + 1) * PAIR] = jnp.where(
                low, first, second
            ).astype(bf16)


def attend_back(scalars, q, g, o, lse, start_rows, k, v):
    rows, width = q.shape
    total = k.shape[0]
    pairs = width // PAIR
    return pl.pallas_call(
        attend_back_kernel,
        grid=(1,),
        in_specs=[
            pl.BlockSpec(memory_space=pltpu.SMEM),
            whole(rows, width),
            whole(rows, width),
            whole(rows, width),
            whole(pairs, 8, 2 * rows),
            whole(8, rows),
            whole(total, width),
            whole(total, width),
        ],
        out_specs=[whole(rows, width), whole(total, width), whole(total, width)],
        out_shape=[
            jax.ShapeDtypeStruct((rows, width), bf16),
            jax.ShapeDtypeStruct((total, width), bf16),
            jax.ShapeDtypeStruct((total, width), bf16),
        ],
        scratch_shapes=[
            pltpu.VMEM((pairs, 2 * rows, PAIR), bf16),
            pltpu.VMEM((pairs, 2 * rows, PAIR), bf16),
            pltpu.VMEM((pairs, 8, 2 * rows), f32),
            pltpu.VMEM((pairs, 2 * rows, PAIR), f32),
        ],
        compiler_params=pltpu.CompilerParams(vmem_limit_bytes=ROOM_ATTEND << 20),
        cost_estimate=SMALL,
        name="attend_back",
    )(scalars, q, g, o, lse, start_rows, k, v)


def ffn_kernel(
    where_ref, a_ref, up0_ref, up1_ref, dn0_ref, dn1_ref, outa_ref, outb_ref, vec_ref, mix_ref,
    hid_ref, slope_ref, out_ref, acc_ref,
):
    step = pl.program_id(0)
    over_a = outa_ref.shape[1]
    over_b = mix_ref.shape[1] - over_a
    hidden = pl.num_programs(0) * 2 * BLK

    @pl.when(step == 0)
    def _():
        acc_ref[...] = dot(mix_ref[:, :over_a], outa_ref[...], NT) + dot(
            mix_ref[:, over_a:], outb_ref[:, :over_b], NT
        )

    a = a_ref[...]
    total = acc_ref[...]
    for i, (up, down) in enumerate(((up0_ref, dn0_ref), (up1_ref, dn1_ref))):
        at = slice(i * BLK, (i + 1) * BLK)
        first = 9 * D + where_ref[0] * hidden + (2 * step + i) * BLK
        u = dot(a, up[...]) + vec_ref[:, pl.ds(pl.multiple_of(first, BLK), BLK)]
        phi = 0.5 * (1.0 + lax.erf(u * (1.0 / math.sqrt(2.0))))
        slope = phi + u * jnp.exp(-0.5 * u * u) * (1.0 / math.sqrt(2.0 * math.pi))
        slope_ref[:, at] = slope.astype(bf16)
        low = (u * phi).astype(bf16)
        hid_ref[:, at] = low
        total = total + dot(low, down[...], NT)
    acc_ref[...] = total

    @pl.when(step == pl.num_programs(0) - 1)
    def _():
        out_ref[...] = acc_ref[...].astype(bf16)


def ffn_weights(hidden, skip):
    steps = hidden // BLK
    return [
        pl.BlockSpec((D, BLK), lambda i: (0, 2 * i)),
        pl.BlockSpec((D, BLK), lambda i: (0, 2 * i + 1)),
        pl.BlockSpec((D, BLK), lambda i: (0, skip + 2 * i)),
        pl.BlockSpec((D, BLK), lambda i: (0, skip + 2 * i + 1)),
        pl.BlockSpec((D, BLK), lambda i: (0, steps)),
        pl.BlockSpec((D, BLK), lambda i: (0, skip + steps)),
    ]


def ffn_forward(where, a, wa, wb, skip, vec, mixed, hidden):
    rows, width = a.shape[0], mixed.shape[1]
    wide = pl.BlockSpec((rows, 2 * BLK), lambda i: (0, i))
    return call(
        ffn_kernel,
        "ffn_forward",
        (hidden // (2 * BLK),),
        [SCALARS, whole(rows, D)]
        + ffn_weights(hidden, skip)
        + [whole(*vec.shape), whole(rows, width)],
        [wide, wide, whole(rows, D)],
        shaped(((rows, hidden), bf16), ((rows, hidden), bf16), ((rows, D), bf16)),
        [pltpu.VMEM((rows, D), f32)],
        room=12,
    )(where, a, wa, wa, wb, wb, wa, wb, vec, mixed)


def ffn_back_kernel(
    where_ref, g_ref, a_ref, up0_ref, up1_ref, dn0_ref, dn1_ref, outa_ref, outb_ref,
    slope_ref, hid_ref, mix_ref,
    ka_ref, sa_ref, kb_ref, sb_ref, da_ref, gmix_ref, sum_ref, ay_ref, gy_ref, gx_ref,
):
    step = pl.program_id(0)
    last = pl.num_programs(0) - 1
    over_a = outa_ref.shape[1]
    over_b = mix_ref.shape[1] - over_a
    half = ka_ref.shape[0]
    part = half // 8

    @pl.when(step == 0)
    def _():
        da_ref[...] = jnp.zeros_like(da_ref)
        for turned, split_y, split_x in (
            (jnp.transpose(a_ref[...]), ay_ref, None),
            (jnp.transpose(g_ref[...]), gy_ref, gx_ref),
        ):
            for z in range(4):
                for y in range(2):
                    row = (2 * z + y) * 2 * part
                    to = pl.multiple_of((where_ref[2] ^ y) * half + 2 * z * part, 16)
                    split_y[pl.ds(to, 2 * part), :] = turned[row : row + 2 * part]
                    for x in range(2) if split_x is not None else ():
                        to = pl.multiple_of((where_ref[3] ^ x) * half + (2 * z + y) * part, 16)
                        split_x[pl.ds(to, part), :] = turned[row + x * part : row + (x + 1) * part]

    @pl.when(step < last)
    def _():
        g = g_ref[...]
        total = da_ref[...]
        grad = dot(gx_ref[...], hid_ref[...]).astype(bf16)
        kb_ref[...], sb_ref[...] = grad[:half], grad[half:]
        for i, (up, down) in enumerate(((up0_ref, dn0_ref), (up1_ref, dn1_ref))):
            at = slice(i * BLK, (i + 1) * BLK)
            d_pre = (dot(g, down[...]) * slope_ref[:, at].astype(f32)).astype(bf16)
            sum_ref[:, at] = jnp.sum(d_pre.astype(f32), axis=0, keepdims=True)
            grad = dot(ay_ref[...], d_pre).astype(bf16)
            ka_ref[:, at], sa_ref[:, at] = grad[:half], grad[half:]
            total = total + dot(d_pre, up[...], NT)
        da_ref[...] = total

    @pl.when(step == last)
    def _():
        g = g_ref[...]
        gmix_ref[:, :over_a] = dot(g, outa_ref[...]).astype(bf16)
        gmix_ref[:, over_a:] = dot(g, outb_ref[:, :over_b]).astype(bf16)
        grad = dot(gy_ref[...], mix_ref[:, :over_a]).astype(bf16)
        ka_ref[:, :over_a], sa_ref[:, :over_a] = grad[:half], grad[half:]
        grad = dot(gx_ref[...], mix_ref[:, over_a:]).astype(bf16)
        kb_ref[:, :over_b], sb_ref[:, :over_b] = grad[:half], grad[half:]


def ffn_backward(where, g, a, wa, wb, skip, slope, hid, mixed):
    rows, width = mixed.shape
    hidden = hid.shape[1]
    steps = hidden // (2 * BLK)
    upto = lambda i: (0, jnp.minimum(i, steps - 1))
    weights = []
    for spec in ffn_weights(hidden, skip):
        weights.append(
            pl.BlockSpec(spec.block_shape, lambda i, f=spec.index_map: f(jnp.minimum(i, steps - 1)))
        )
    wide = pl.BlockSpec((rows, 2 * BLK), upto)
    split = pl.BlockSpec((D // 2, 2 * BLK), lambda i: (0, i))
    wide_a, wide_b = hidden + BLK, hidden + width - BLK
    return call(
        ffn_back_kernel,
        "ffn_backward",
        (steps + 1,),
        [SCALARS, whole(rows, D), whole(rows, D)] + weights + [wide, wide, whole(rows, width)],
        [split] * 4
        + [whole(rows, D), whole(rows, width), pl.BlockSpec((1, 2 * BLK), upto)],
        shaped(
            *[((D // 2, wide_a), bf16)] * 2,
            *[((D // 2, wide_b), bf16)] * 2,
            ((rows, D), f32),
            ((rows, width), bf16),
            ((1, hidden), f32),
        ),
        [pltpu.VMEM((D, rows), bf16)] * 3,
        room=18,
    )(where, g, a, wa, wa, wb, wb, wa, wb, slope, hid, mixed)


def with_half(where_ref, da_ref, back_refs):
    half = sum(ref[...].astype(f32) for ref in back_refs)
    zero = jnp.zeros_like(half)
    first = jnp.where(where_ref[0] == 0, half, zero)
    return da_ref[...] + jnp.concatenate([first, half - first], axis=1)


def joint_kernel(where_ref, vec_ref, da_ref, db_ref, *refs):
    *back_refs, out_ref = refs
    da = with_half(where_ref, da_ref, back_refs)
    out_ref[...] = (da * vec_ref[:, :D] + db_ref[...] * vec_ref[:, 2 * D : 3 * D]).astype(bf16)


def row_call(kernel, name, where, vec, rows_in, outs, steps=4):
    rows = rows_in[0].shape[0]
    block = lambda width: pl.BlockSpec((rows // steps, width), lambda i: (i, 0))
    return call(
        kernel,
        name,
        (steps,),
        [SCALARS, whole(*vec.shape)] + [block(m.shape[1]) for m in rows_in],
        [block(shape[1]) for shape, _ in outs],
        shaped(*outs),
    )(where, vec, *rows_in)


def next_kernel(where_ref, vec_ref, grad_ref, own_ref, got_ref, x_ref, out_ref, low_ref):
    unit, inverse = unit_rows(x_ref[...].astype(f32))
    joint = own_ref[...].astype(f32) + got_ref[...].astype(f32)
    centered = joint - jnp.mean(joint, axis=-1, keepdims=True)
    grad = grad_ref[...].astype(f32) + inverse * (
        centered - unit * jnp.mean(joint * unit, axis=-1, keepdims=True)
    )
    out_ref[...] = grad
    low_ref[...] = grad.astype(bf16)


def vector_kernel(where_ref, qkv_ref, up_ref, far_ref, grad_ref, x_ref, da_ref, db_ref, out_ref):
    core = where_ref[0]
    width, hidden = qkv_ref.shape[1] // 3, up_ref.shape[1]

    @pl.when(pl.program_id(0) == 0)
    def _():
        out_ref[...] = jnp.zeros_like(out_ref)
        for c in range(3):
            to = pl.multiple_of((6 + c) * D + core * width, PAIR)
            out_ref[:, pl.ds(to, width)] = qkv_ref[:, c * width : (c + 1) * width]
        out_ref[:, pl.ds(pl.multiple_of(9 * D + core * hidden, PAIR), hidden)] = up_ref[...]
        for i in range(2):
            out_ref[:, i * D : (i + 1) * D] = far_ref[i : i + 1, :]

    unit, _ = unit_rows(x_ref[...].astype(f32))
    da, db = da_ref[...], db_ref[...]
    first = (core == 0).astype(f32)
    bias = jnp.sum(grad_ref[...].astype(f32), axis=0, keepdims=True) * first
    for i, term in enumerate((da * unit, da, db * unit, db)):
        out_ref[:, i * D : (i + 1) * D] += jnp.sum(term, axis=0, keepdims=True)
    out_ref[:, 4 * D : 5 * D] += bias
    out_ref[:, 5 * D : 6 * D] += bias


def vector_row(where, qkv_sum, up_sum, far, grad, x, da, db):
    rows, steps = grad.shape[0], 4
    block = lambda width: pl.BlockSpec((rows // steps, width), lambda i: (i, 0))
    rows_in = [grad, x, da, db]
    size = 9 * D + FF
    return call(
        vector_kernel,
        "vector_row",
        (steps,),
        [SCALARS, whole(*qkv_sum.shape), whole(*up_sum.shape), whole(*far.shape)] + [block(m.shape[1]) for m in rows_in],
        [whole(1, size)],
        shaped(((1, size), f32)),
    )(where, qkv_sum, up_sum, far, *rows_in)[0]


def settle_kernel(counts, where_ref, *refs):
    refs = list(refs)
    terms = [[refs.pop(0) for _ in range(n)] for n in counts]
    moms, refs = refs[:KINDS], refs[KINDS:]
    grads, refs = refs[:KINDS], refs[KINDS:]
    news, refs = refs[:KINDS], refs[KINDS:]
    *sends, pad_ref = refs
    layers, _, rows, width = moms[0].shape
    hidden = moms[2].shape[2]
    cut = 3 * width // 256 * 128 + 128
    pad_ref[...] = jnp.zeros_like(pad_ref)

    def total(parts, at):
        return sum(part[:, at].astype(f32) for part in parts)

    for layer in range(layers):
        first = total(terms[2], slice(layer * cut, (layer + 1) * cut))
        skip, rest = layers * cut, 3 * width - cut
        second = total(terms[2], slice(skip + layer * rest, skip + (layer + 1) * rest))
        qkv = jnp.concatenate([first, second], axis=1)
        up = total(terms[layer], slice(0, hidden))
        out_a = total(terms[layer], slice(hidden, hidden + BLK))
        down = total(terms[layer], slice(hidden + BLK, 2 * hidden + BLK))
        out_b = total(terms[layer], slice(2 * hidden + BLK, 2 * hidden + width))
        out = jnp.concatenate([out_a, out_b], axis=1)
        for c in range(3):
            grad = qkv[:, c * width : (c + 1) * width]
            new = MOMENTUM * moms[0][layer, c] + grad
            grads[0][layer, c], news[0][layer, c] = grad, new
            pad_ref[layer, :, c * width : (c + 1) * width] = new.astype(bf16)
        for kind, grad in ((1, out), (2, up), (3, down)):
            new = MOMENTUM * moms[kind][layer] + grad
            grads[kind][layer], news[kind][layer] = grad, new
            pad_ref[layer, :, kind * hidden : kind * hidden + grad.shape[1]] = new.astype(bf16)
    for by, send in enumerate(sends):
        at = pl.ds(pl.multiple_of((where_ref[1] ^ by) * hidden, PAIR), hidden)
        for layer in range(layers):
            send[layer] = pad_ref[layer, :, at]


def settle(where, terms, moms):
    rows, hidden = moms[2].shape[1:]
    flat = [m for group in terms for m in group]
    send = (LAYERS, rows, hidden)
    outs = [(m.shape, f32) for m in moms] * 2 + [(send, bf16)] * KINDS
    got = call(
        functools.partial(settle_kernel, [len(group) for group in terms]),
        "settle",
        (1,),
        [SCALARS] + [whole(*m.shape) for m in flat] + [whole(*m.shape) for m in moms],
        [whole(*shape) for shape, _ in outs],
        shaped(*outs),
        [pltpu.VMEM((LAYERS, rows, KINDS * hidden), bf16)],
        room=12,
    )(where, *flat, *moms)
    return got[:KINDS], got[KINDS : 2 * KINDS], got[2 * KINDS :]


def update_kernel(where_ref, *refs):
    backs, swapped = refs[:KINDS], refs[KINDS]
    masters, outs = refs[KINDS + 1 : 2 * KINDS + 1], refs[2 * KINDS + 1 : 3 * KINDS + 1]
    kept_ref = refs[-1]
    layers, _, rows, width = masters[0].shape
    for slot in range(KINDS):
        kept_ref[slot] = backs[slot][0]
    for layer in range(layers):
        mine = where_ref[0] == layer
        for kind in range(KINDS):
            slot = where_ref[1] ^ kind
            made = jnp.where(mine, kept_ref[slot], swapped[slot]).astype(f32)
            made = made * (-RATE_MAT * math.sqrt((3 * D, D, FF, FF)[kind]))
            if kind == 0:
                for c in range(3):
                    step = made[:, c * width : (c + 1) * width]
                    outs[0][layer, c] = masters[0][layer, c] * SHRINK + step
            else:
                outs[kind][layer] = masters[kind][layer] * SHRINK + made[:, : outs[kind].shape[2]]


def update(where, backs, swapped, masters):
    return call(
        update_kernel,
        "update",
        (1,),
        [SCALARS] + [whole(*m.shape) for m in (*backs, swapped, *masters)],
        [whole(*m.shape) for m in masters],
        shaped(*[(m.shape, f32) for m in masters]),
        [pltpu.VMEM(swapped.shape, bf16)],
    )(where, *backs, swapped, *masters)


def orth_kernel(inner, *refs):
    ins, outs = refs[:2], refs[2 : 2 + KINDS]
    x_ref, gram_ref, mix_ref = refs[2 + KINDS :]
    rows, width = ins[0].shape
    part, chunk = 256, 512
    blocks = rows // part
    total = jnp.zeros((1, 1), f32)
    for ref in ins:
        for i in range(blocks):
            v = ref[i * part : (i + 1) * part, :].astype(f32)
            total = total + jnp.sum(v * v).reshape(1, 1)
    inverse = 1.0 / (jnp.sqrt(total) + 1e-07)
    for i, ref in enumerate(ins):
        x_ref[:, i * width : (i + 1) * width] = (ref[...].astype(f32) * inverse).astype(bf16)

    def spread(ref, i, j, value):
        low = value.astype(bf16)
        ref[i * part : (i + 1) * part, j * part : (j + 1) * part] = low
        if j > i:
            ref[j * part : (j + 1) * part, i * part : (i + 1) * part] = jnp.transpose(low)

    def mixer():
        for i in range(blocks):
            at = slice(i * part, (i + 1) * part)
            gram = dot(x_ref[at, :], x_ref[i * part :, :], NT)
            for j in range(i, blocks):
                spread(gram_ref, i, j, gram[:, (j - i) * part : (j - i + 1) * part])
        for i in range(blocks):
            at = slice(i * part, (i + 1) * part)
            square = dot(gram_ref[at, :], gram_ref[:, i * part :])
            mixed = NS_B * gram_ref[at, i * part :].astype(f32) + NS_C * square
            for j in range(i, blocks):
                spread(mix_ref, i, j, mixed[:, (j - i) * part : (j - i + 1) * part])

    def sweep(_, carry):
        mixer()
        for c in range(2 * width // chunk):
            cols = slice(c * chunk, (c + 1) * chunk)
            x = x_ref[:, cols]
            y = NS_A * x.astype(f32) + dot(mix_ref[...], x)
            x_ref[:, cols] = y.astype(bf16)
        return carry

    lax.fori_loop(0, 4, sweep, 0)
    mixer()
    size = outs[0].shape[1]
    firsts = [by * inner * size for by in range(KINDS)]
    mine = jnp.concatenate([mix_ref[first : first + size, :] for first in firsts], axis=0)
    for half in range(2):
        cols = slice(half * width, (half + 1) * width)
        made = dot(mine, x_ref[:, cols])
        for by, out in enumerate(outs):
            x = x_ref[firsts[by] : firsts[by] + size, cols].astype(f32)
            out[half] = (NS_A * x + made[by * size : (by + 1) * size]).astype(bf16)


def orthogonalize(parts, inner):
    rows, width = parts[0].shape
    shape = (2, rows // (KINDS * inner), width)
    return call(
        functools.partial(orth_kernel, inner),
        "orthogonalize",
        (1,),
        [whole(rows, width)] * 2,
        [whole(*shape)] * KINDS,
        shaped(*[(shape, bf16)] * KINDS),
        [
            pltpu.VMEM((rows, 2 * width), bf16),
            pltpu.VMEM((rows, rows), bf16),
            pltpu.VMEM((rows, rows), bf16),
        ],
        room=20,
    )(*parts)


def shards(
    tokens,
    cotangent,
    w_qkv,
    w_out,
    w_up,
    w_down,
    mom_qkv,
    mom_out,
    mom_up,
    mom_down,
    vectors,
    vec_first,
    vec_second,
    lengths,
):
    tok_rows = tokens.shape[0]
    row_part = w_qkv.shape[1]
    head_part = w_qkv.shape[-1]
    hidden_part = w_up.shape[-1]
    widths = (3 * head_part, head_part, hidden_part, hidden_part)
    over = BLK
    cut_qkv = widths[0] // 256 * 128 + 128
    cut_rest = hidden_part + over
    skip = cut_rest // BLK
    fsdp_count = lax.axis_size("fsdp")
    core = lax.axis_index("tp")
    longest = SEQ_DEV * fsdp_count
    span = (tok_rows + longest - 2) // tok_rows
    where = place()

    def stored(qkv, out, up, down):
        return [qkv.transpose(0, 2, 1, 3), out.transpose(0, 2, 1), up, down.transpose(0, 2, 1)]

    def unstored(qkv, out, up, down):
        return [qkv.transpose(0, 2, 1, 3), out.transpose(0, 2, 1), up, down.transpose(0, 2, 1)]

    def qkv_piece(mats, layer):
        low = mats[0][layer].astype(bf16)
        return jnp.concatenate([low[c] for c in range(3)], axis=1)

    def rest_piece(mats, layer):
        out, up, down = [m[layer].astype(bf16) for m in mats[1:]]
        return jnp.concatenate([up, out[:, :over], down, out[:, over:]], axis=1)

    masters = stored(w_qkv, w_out, w_up, w_down)
    moments = stored(mom_qkv, mom_out, mom_up, mom_down)

    qkv_0 = Task(gather_steps(where, qkv_piece(masters, 0), cut_qkv))
    vecs = [vectors[layer : layer + 1] for layer in range(LAYERS)]
    a0, b0, half = norm_rows(where, vecs[0], tokens)
    rest, half, lengths, *later = advance(
        [qkv_0], rest_piece(masters, 0), half, lengths, *masters
    )
    rest_0 = Task(gather_steps(where, rest, cut_rest, True))
    half, lengths, *later = advance([qkv_0, rest_0], half, lengths, *later)
    win_0 = Task(window_steps(half, span))
    tables, start_rows, scalars = setup(lengths, where, tok_rows, (span + 1) * tok_rows)
    tables, start_rows, scalars, *later = advance(
        [qkv_0, rest_0, win_0], tables, start_rows, scalars, *later
    )
    qkv_1 = Task(gather_steps(where, qkv_piece(later, 1), cut_qkv, False, True))
    wq0 = qkv_0.result
    tables, *later = advance([win_0], tables, *later)
    q, k, v, vt = qkv_forward(where, a0, *win_0.result, wq0, vecs[0], tables)
    q, k, v, vt, *later = advance([rest_0, qkv_1], q, k, v, vt, *later)
    rest_1 = Task(gather_steps(where, rest_piece(later, 1), cut_rest, False, True))
    mixed, lse = attend(scalars, q, start_rows, k, vt)
    mixed, lse, b0 = advance([rest_0, rest_1], mixed, lse, b0)
    mixed, b0, wa, wb = advance([rest_1, qkv_1], mixed, b0, *rest_0.result)
    hid, slope, partial = ffn_forward(where, b0, wa, wb, 0, vecs[0], mixed, hidden_part)
    partial = advance([rest_1, qkv_1], partial)
    kept = [(tokens, a0, win_0.result, b0, q, k, v, mixed, lse, hid, slope)]
    weights = [(wq0, wa, wb, 0)]
    got = core_swap(partial)
    x1, a1, b1, half = norm_rows(where, vecs[1], tokens, vecs[0], partial, got)
    win_1 = Task(window_steps(half, span))
    a1, b1 = advance([win_1, qkv_1], a1, b1)
    a1, b1 = advance([win_1], a1, b1)
    wq1 = qkv_1.result
    q, k, v, vt = qkv_forward(where, a1, *win_1.result, wq1, vecs[1], tables)
    mixed, lse = attend(scalars, q, start_rows, k, vt)
    mixed, lse, b1, q, k, v = advance([rest_1], mixed, lse, b1, q, k, v)
    wa, wb = rest_1.result
    hid, slope, partial = ffn_forward(where, b1, wa, wb, 0, vecs[1], mixed, hidden_part)
    kept.append((x1, a1, win_1.result, b1, q, k, v, mixed, lse, hid, slope))
    weights.append((wq1, wa, wb, 0))

    def own_gradients(grad_low, layer):
        _, _, _, b, _, _, _, mixed, _, hid, slope = kept[layer]
        _, wa, wb, skip = weights[layer]
        return ffn_backward(where, grad_low, b, wa, wb, skip, slope, hid, mixed)

    def attention_gradients(g_mixed, layer, more=()):
        _, a, win, _, q, k, v, mixed, lse, _, _ = kept[layer]
        dq, dk, dv = attend_back(scalars, q, g_mixed, mixed, lse, start_rows, k, v)
        return qkv_backward(where, dq, dk, dv, a, *win, weights[layer][0], tables, vecs[layer], more)

    def joint_of(da, db, back, layer):
        rows_in = [da, db] + list(back)
        return row_call(joint_kernel, "joint", where, vecs[layer], rows_in, [(da.shape, bf16)])[0]

    def next_grad(grad, joint, got, layer):
        outs = [(joint.shape, f32), (joint.shape, bf16)]
        rows_in = [grad, joint, got, kept[layer][0]]
        return row_call(next_kernel, "next_grad", where, vecs[layer], rows_in, outs)

    *split, db1, g_mixed, up_sum1 = own_gradients(cotangent, 1)
    *split, g_mixed, partial, db1 = advance([], *split, g_mixed, partial, db1)
    rest_1 = Task(scatter_steps(where, *split, True))
    *split1, da1, keep, give, pre_sum1, far1 = attention_gradients(g_mixed, 1)
    *split1, da1, keep, give, partial = advance([], *split1, da1, keep, give, partial)
    back_1 = Task(window_back_steps(keep, give, span))
    da1, partial = advance([back_1, rest_1], da1, partial)
    da1, partial = advance([back_1, rest_1], da1, partial)
    joint = joint_of(da1, db1, back_1.result, 1)
    got = core_swap(joint)
    grad_x0, grad_low = next_grad(cotangent, joint, got, 1)
    *split, db0, g_mixed, up_sum0 = own_gradients(grad_low, 0)
    *split, g_mixed, da1, db0, partial = advance([rest_1], *split, g_mixed, da1, db0, partial)
    *split, g_mixed = advance([rest_1], *split, g_mixed)
    rest_0 = Task(scatter_steps(where, *split, False, True))
    *split, da0, keep, give, pre_sum0, far0 = attention_gradients(g_mixed, 0, split1)
    *split, da0, keep, give, da1, db1, partial = advance(
        [rest_0, rest_1], *split, da0, keep, give, da1, db1, partial
    )
    both_qkv = Task(scatter_steps(where, *split, True))
    back_0 = Task(window_back_steps(keep, give, span, True))
    row_0 = vector_row(where, pre_sum0, up_sum0, far0, grad_x0, kept[0][0], da0, db0)
    row_1 = vector_row(where, pre_sum1, up_sum1, far1, cotangent, kept[1][0], da1, db1)
    rows_both, partial = advance(
        [rest_0, both_qkv], jnp.concatenate([row_0, row_1], axis=0), partial
    )
    rows_both, partial = advance([both_qkv], rows_both, partial)
    vec_sum = Task(sum_steps(rows_both))
    partial = advance([both_qkv, rest_0, back_0, vec_sum], partial)
    partial = advance([both_qkv], partial)
    got = core_swap(partial)
    block_out = norm_rows(where, vecs[1], kept[1][0], vecs[1], partial, got, False)[0]
    block_out = advance([both_qkv, rest_0], block_out)
    terms = [rest_0.result, rest_1.result, both_qkv.result]
    grads, new_moms, blocks = settle(where, terms, moments)
    owned = Task(owner_steps(blocks[0], blocks[1:]))
    advance([owned, vec_sum])
    advance([owned])
    while owned.flying is not None:
        advance([owned, vec_sum])

    inner = fsdp_count // KINDS
    parts = advance([back_0], *owned.result)
    made = orthogonalize(parts, inner)
    *made, da0 = advance([back_0], *made, da0)
    backs = [made[0]] + [
        permute(made[by], xor_pairs(fsdp_count, by * inner)) for by in range(1, KINDS)
    ]
    joint = joint_of(da0, db0, back_0.result, 0)
    got = core_swap(joint)
    grad_in, _ = next_grad(grad_x0, joint, got, 0)
    grad_in = advance([vec_sum], grad_in)
    while vec_sum.flying is not None:
        grad_in = advance([vec_sum], grad_in)
    grad_vectors = vec_sum.result
    grad_in, grad_vectors, *backs = advance([], grad_in, grad_vectors, *backs)
    swapped = core_swap(jnp.stack([m[1] for m in backs]))
    new_weights = update(where, backs, swapped, masters)

    first_new = BETA_ONE * vec_first + (1.0 - BETA_ONE) * grad_vectors
    second_new = BETA_TWO * vec_second + (1.0 - BETA_TWO) * grad_vectors * grad_vectors
    first_hat = first_new / (1.0 - BETA_ONE**STEP)
    second_hat = second_new / (1.0 - BETA_TWO**STEP)
    vectors_new = vectors - RATE_VEC * first_hat / (jnp.sqrt(second_hat) + ADAM_EPS)
    return (
        block_out,
        grad_in,
        *unstored(*grads),
        *unstored(*new_moms),
        *unstored(*new_weights),
        first_new,
        second_new,
        vectors_new,
        grad_vectors[:, 9 * D :],
    )


def solution(mesh):
    weights = (
        P(None, "fsdp", None, "tp"),
        P(None, "tp", "fsdp"),
        P(None, "fsdp", "tp"),
        P(None, "tp", "fsdp"),
    )
    rows = (P("fsdp", None), P("fsdp", None))
    return jax.shard_map(
        shards,
        mesh=mesh,
        in_specs=rows + weights + weights + (P(), P(), P(), P()),
        out_specs=rows + weights + weights + weights + (P(), P(), P(), P()),
        check_vma=False,
    )
```

```python
import functools
import math

import jax
import jax.numpy as jnp
import numpy as np
from jax import lax
from jax.experimental import pallas as pl
from jax.experimental.pallas import tpu as pltpu
from jax.sharding import PartitionSpec as P

D = 768
HEAD = 64
ROT = 16
FF = 3072
LAYERS = 2
SEQ_DEV = 64
STEP = 10
PAIR = 2 * HEAD
BLK = 256
KINDS = 4

MASKED = -1000000000.0
EPS_NORM = 1e-05
NS_A = 3.4445
NS_B = -4.775
NS_C = 2.0315
MOMENTUM = 0.95
RATE_MAT = 0.02
SHRINK = 0.99
RATE_VEC = 0.25
BETA_ONE = 0.9
BETA_TWO = 0.95
ADAM_EPS = 1e-08
ROOM_ATTEND = 16

bf16 = jnp.bfloat16
f32 = jnp.float32


def permute(x, pairs):
    return lax.ppermute(x, "fsdp", pairs)


def xor_pairs(count, by):
    return [(i, i ^ by) for i in range(count)]


def core_swap(x):
    count = lax.axis_size("tp")
    return lax.ppermute(x, "tp", [(i, i ^ 1) for i in range(count)])


def shifted(x, by):
    devices = lax.axis_size("fsdp")
    return lax.ppermute(
        x, "fsdp", [(i, i + by) for i in range(devices) if 0 <= i + by < devices]
    )


def on_grid():
    return lax.axis_size("fsdp") == 16


def place():
    index = lax.axis_index("fsdp")
    inner = lax.axis_size("fsdp") // KINDS
    bits = [(index // 2) % 2, index % 2] if on_grid() else [index * 0, index * 0]
    parts = [lax.axis_index("tp"), index // inner, *bits, index]
    return jnp.stack([p.astype(jnp.int32) for p in parts])


class Task:
    def __init__(self, steps):
        self.steps = steps
        self.result = None
        self.flying = None
        self.resume(None)

    def resume(self, arrived):
        try:
            self.flying = self.steps.send(arrived)
        except StopIteration as stop:
            self.result = stop.value
            self.flying = None


def advance(tasks, *arrays):
    tasks = [t for t in tasks if t.flying is not None]
    arrived, arrays = lax.optimization_barrier(([t.flying for t in tasks], arrays))
    for task, got in zip(tasks, arrived):
        task.resume(got)
    return arrays if len(arrays) != 1 else arrays[0]


def gather_steps(where, piece, cut, apart=False, pause=False):
    rows, cols = piece.shape
    if not on_grid():
        full = lax.all_gather(piece, "fsdp", axis=0, tiled=True)
        return full[:, :cut], full[:, cut:]
        yield
    got = []
    for group in ((1, 2), (3,)) if apart else ((1, 2, 3),):
        got += yield [permute(piece, xor_pairs(16, 4 * by)) for by in group]
    part_a, part_b = join_planes(where, [piece] + got, cut)
    if pause:
        part_a, part_b = yield [part_a, part_b]
    got_a, got_b = yield [permute(part_a, xor_pairs(16, 1)), permute(part_b, xor_pairs(16, 2))]
    part_a, part_b = join_chips(where, part_a, got_a, part_b, got_b, False)
    got_a, got_b = yield [permute(part_a, xor_pairs(16, 2)), permute(part_b, xor_pairs(16, 1))]
    part_a, part_b = join_chips(where, part_a, got_a, part_b, got_b, True)
    return part_a.reshape(16 * rows, -1), part_b.reshape(16 * rows, -1)


def natural(keep, send, axis):
    shape = (4, 1, 2, -1) if axis == 1 else (4, 2, 1, -1)
    parts = [m.reshape(shape + (m.shape[-1],)) for m in (keep, send)]
    full = jnp.concatenate(parts, axis=axis)
    return full.reshape(-1, keep.shape[-1])


def scatter_steps(where, keep_a, send_a, keep_b, send_b, pause=False, apart=False):
    if not on_grid():
        full = jnp.concatenate([natural(keep_a, send_a, 1), natural(keep_b, send_b, 2)], axis=1)
        return [lax.psum_scatter(full, "fsdp", scatter_dimension=0, tiled=True)]
        yield
    got_a, got_b = yield [permute(send_a, xor_pairs(16, 2)), permute(send_b, xor_pairs(16, 1))]
    keep_a, send_a, keep_b, send_b = add_split(where, keep_a, got_a, keep_b, got_b)
    if pause:
        keep_a, send_a, keep_b, send_b = yield [keep_a, send_a, keep_b, send_b]
    got_a, got_b = yield [permute(send_a, xor_pairs(16, 1)), permute(send_b, xor_pairs(16, 2))]
    own, *sends = add_planes(where, keep_a, got_a, keep_b, got_b)
    if pause:
        own, *sends = yield [own, *sends]
    got = [own]
    for group in ((0, 1), (2,)) if apart else ((0, 1, 2),):
        got += yield [permute(sends[i], xor_pairs(16, 4 * (i + 1))) for i in group]
    return got


def window_steps(half, span):
    got = yield [shifted(half, step) for step in range(span, 0, -1)]
    got = jnp.concatenate(got, axis=0)
    (other,) = yield [core_swap(got)]
    return got, other


def window_back_steps(keep, give, span, pause=False):
    (got,) = yield [core_swap(give)]
    half = (keep.astype(f32) + got.astype(f32)).astype(bf16).reshape(span, -1, keep.shape[-1])
    if pause:
        (half,) = yield [half]
    back = yield [shifted(half[span - step], -step) for step in range(span, 0, -1)]
    return back


def sum_steps(x):
    count = lax.axis_size("fsdp")
    step = 1
    while step < count:
        (got,) = yield [permute(x, xor_pairs(count, step))]
        x = x + got
        step *= 2
    (got,) = yield [core_swap(x)]
    return x + got


def owner_steps(own, sends):
    count = lax.axis_size("fsdp")
    inner = count // KINDS
    core = lax.axis_index("tp")
    rows, width = own.shape[1:]
    got = yield [permute(sends[by - 1], xor_pairs(count, by * inner)) for by in range(1, KINDS)]
    terms = [own] + list(got)
    give = jnp.stack([jnp.where(core == 0, m[1], m[0]) for m in terms])
    part_a = jnp.stack([jnp.where(core == 0, m[0], m[1]) for m in terms])
    part_a, part_b = yield [part_a, core_swap(give)]
    bits = inner.bit_length() - 1
    shape = (KINDS,) + (1,) * bits + (rows, width)
    part_a, part_b = part_a.reshape(shape), part_b.reshape(shape)
    for step in range(bits):
        bit_a, bit_b = step, bits - 1 - step
        got_a, got_b = yield [
            permute(part_a, xor_pairs(count, 1 << bit_a)),
            permute(part_b, xor_pairs(count, 1 << bit_b)),
        ]
        part_a = jnp.concatenate([part_a, got_a], axis=1 + bit_a)
        part_b = jnp.concatenate([part_b, got_b], axis=1 + bit_b)
    return [m.reshape(count * rows, width) for m in (part_a, part_b)]


SMALL = pl.CostEstimate(flops=1, bytes_accessed=1, transcendentals=0)
SCALARS = pl.BlockSpec(memory_space=pltpu.SMEM)
NT = (((1,), (1,)), ((), ()))
TN = (((0,), (0,)), ((), ()))


def dot(a, b, how=(((1,), (0,)), ((), ()))):
    return lax.dot_general(a, b, how, preferred_element_type=f32)


def whole(*shape):
    return pl.BlockSpec(shape, lambda *_: (0,) * len(shape))


def shaped(*shapes_and_kinds):
    return [jax.ShapeDtypeStruct(shape, kind) for shape, kind in shapes_and_kinds]


def call(kernel, name, grid, in_specs, out_specs, out_shape, scratch=(), room=8):
    return pl.pallas_call(
        kernel,
        grid=grid,
        in_specs=in_specs,
        out_specs=out_specs,
        out_shape=out_shape,
        scratch_shapes=list(scratch),
        compiler_params=pltpu.CompilerParams(vmem_limit_bytes=room << 20),
        cost_estimate=SMALL,
        name=name,
    )


def join_planes_kernel(cut, where_ref, *refs):
    *pieces, out_a, out_b = refs
    quarter = where_ref[1]
    for by, piece in enumerate(pieces):
        plane = quarter ^ by
        out_a[plane] = piece[:, :cut]
        out_b[plane] = piece[:, cut:]


def join_planes(where, pieces, cut):
    rows, cols = pieces[0].shape
    shapes = [(4, rows, cut), (4, rows, cols - cut)]
    return call(
        functools.partial(join_planes_kernel, cut),
        "join_planes",
        (1,),
        [SCALARS] + [whole(rows, cols)] * 4,
        [whole(*shape) for shape in shapes],
        shaped(*[(shape, bf16) for shape in shapes]),
    )(where, *pieces)


def join_chips_kernel(last, where_ref, own_a, got_a, own_b, got_b, out_a, out_b):
    y, x = where_ref[2], where_ref[3]
    if not last:
        out_a[0, x], out_a[0, 1 - x] = own_a[0], got_a[0]
        out_b[0, y], out_b[0, 1 - y] = own_b[0], got_b[0]
    else:
        out_a[0, y], out_a[0, 1 - y] = own_a[0], got_a[0]
        for side in range(2):
            out_b[0, side, x], out_b[0, side, 1 - x] = own_b[0, side], got_b[0, side]


def join_chips(where, own_a, got_a, own_b, got_b, last):
    rows = own_a.shape[-2]
    ins, outs = ((2, rows), (2, 2, rows)) if last else ((rows,), (2, rows))

    def spec(shape, width):
        return pl.BlockSpec((1,) + shape + (width,), lambda i: (i,) + (0,) * (len(shape) + 1))

    wide_a, wide_b = own_a.shape[-1], own_b.shape[-1]
    return call(
        functools.partial(join_chips_kernel, last),
        "join_chips",
        (4,),
        [SCALARS, spec(ins, wide_a), spec(ins, wide_a), spec(ins, wide_b), spec(ins, wide_b)],
        [spec(outs, wide_a), spec(outs, wide_b)],
        shaped(((4,) + outs + (wide_a,), bf16), ((4,) + outs + (wide_b,), bf16)),
    )(where, own_a, got_a, own_b, got_b)


def add_split_kernel(where_ref, keep_a, got_a, keep_b, got_b, out_ka, out_sa, out_kb, out_sb):
    rows = keep_a.shape[0] // 8
    for bit, keep, got, out_k, out_s in (
        (where_ref[3], keep_a, got_a, out_ka, out_sa),
        (where_ref[2], keep_b, got_b, out_kb, out_sb),
    ):
        for z in range(4):
            for flip, out in ((0, out_k), (1, out_s)):
                at = pl.ds(pl.multiple_of((2 * z + (bit ^ flip)) * rows, 16), rows)
                total = keep[at, :].astype(f32) + got[at, :].astype(f32)
                out[z * rows : (z + 1) * rows, :] = total.astype(bf16)


def add_split(where, keep_a, got_a, keep_b, got_b):
    rows, wide_a = keep_a.shape
    wide_b = keep_b.shape[1]
    outs = [(rows // 2, wide_a)] * 2 + [(rows // 2, wide_b)] * 2
    return call(
        add_split_kernel,
        "add_split",
        (1,),
        [SCALARS] + [whole(rows, wide_a)] * 2 + [whole(rows, wide_b)] * 2,
        [whole(*shape) for shape in outs],
        shaped(*[(shape, bf16) for shape in outs]),
        room=12,
    )(where, keep_a, got_a, keep_b, got_b)


def add_planes_kernel(where_ref, keep_a, got_a, keep_b, got_b, *outs):
    rows = keep_a.shape[0] // 4
    cut = keep_a.shape[1]
    for by, out in enumerate(outs):
        at = pl.ds(pl.multiple_of((where_ref[1] ^ by) * rows, 16), rows)
        out[:, :cut] = (keep_a[at, :].astype(f32) + got_a[at, :].astype(f32)).astype(bf16)
        out[:, cut:] = (keep_b[at, :].astype(f32) + got_b[at, :].astype(f32)).astype(bf16)


def add_planes(where, keep_a, got_a, keep_b, got_b):
    rows, wide_a = keep_a.shape
    wide_b = keep_b.shape[1]
    shape = (rows // 4, wide_a + wide_b)
    return call(
        add_planes_kernel,
        "add_planes",
        (1,),
        [SCALARS] + [whole(rows, wide_a)] * 2 + [whole(rows, wide_b)] * 2,
        [whole(*shape)] * 4,
        shaped(*[(shape, bf16)] * 4),
    )(where, keep_a, got_a, keep_b, got_b)


def setup_kernel(len_ref, where_ref, freq_ref, table_ref, start_ref, scal_ref):
    rows, total = start_ref.shape[1], table_ref.shape[1]
    base = where_ref[4] * rows
    first = base - (total - rows)
    half = ROT // 2

    def starts_of(index):
        end, out = jnp.int32(0), jnp.zeros_like(index)
        for i in range(len_ref.shape[0]):
            end = end + len_ref[i]
            out = jnp.where(index >= end, end, out)
        return out

    lane = lax.broadcasted_iota(jnp.int32, (BLK, PAIR), 1) % HEAD
    for c in range(total // BLK):
        at = slice(c * BLK, (c + 1) * BLK)
        index = first + c * BLK + lax.broadcasted_iota(jnp.int32, (BLK, PAIR), 0)
        phase = (index - starts_of(index)).astype(f32) * freq_ref[...]
        sine = jnp.sin(phase)
        table_ref[0, at, :] = jnp.cos(phase)
        table_ref[1, at, :] = jnp.where(lane < half, -sine, 0.0)
        table_ref[2, at, :] = jnp.where((lane >= half) & (lane < ROT), sine, 0.0)
    start_ref[...] = starts_of(base + lax.broadcasted_iota(jnp.int32, start_ref.shape, 1))
    own = (total - rows) // BLK
    scal_ref[0] = base
    scal_ref[1] = jnp.minimum((starts_of(base + BLK) - first) // BLK, own)
    scal_ref[2] = (starts_of(base) - first) // BLK


def setup(lengths, where, rows, total):
    lane = np.arange(PAIR) % HEAD
    freqs = np.exp((lane % (ROT // 2)) * (-2.0 * math.log(10000.0) / ROT))
    freqs = np.where(lane < ROT, freqs, 0.0).astype(np.float32)[None]
    return call(
        setup_kernel,
        "setup",
        (1,),
        [SCALARS, SCALARS, whole(1, PAIR)],
        [whole(3, total, PAIR), whole(8, rows), SCALARS],
        shaped(((3, total, PAIR), f32), ((8, rows), jnp.int32), ((3,), jnp.int32)),
        room=8,
    )(lengths, where, jnp.asarray(freqs))


def unit_rows(x):
    centered = x - jnp.mean(x, axis=-1, keepdims=True)
    inverse = lax.rsqrt(jnp.mean(centered * centered, axis=-1, keepdims=True) + EPS_NORM)
    return centered * inverse, inverse


def norm_kernel(where_ref, vec_ref, x_ref, a_ref, b_ref, half_ref):
    unit, _ = unit_rows(x_ref[...].astype(f32))
    a = (unit * vec_ref[:, :D] + vec_ref[:, D : 2 * D]).astype(bf16)
    a_ref[...] = a
    b_ref[...] = (unit * vec_ref[:, 2 * D : 3 * D] + vec_ref[:, 3 * D : 4 * D]).astype(bf16)
    half_ref[...] = jnp.where(where_ref[0] == 0, unit[:, : D // 2], unit[:, D // 2 :]).astype(bf16)


def add_norm_kernel(where_ref, old_ref, vec_ref, x_ref, part_ref, got_ref, new_ref, *outs):
    x = x_ref[...].astype(f32) + part_ref[...].astype(f32) + got_ref[...].astype(f32)
    x = x + old_ref[:, 4 * D : 5 * D] + old_ref[:, 5 * D : 6 * D]
    new_ref[...] = x
    if outs:
        norm_kernel(where_ref, vec_ref, new_ref, *outs)


def norm_rows(where, vec, x, old_vec=None, part=None, got=None, normed=True):
    rows = x.shape[0]
    step = rows // 4
    block = lambda width: pl.BlockSpec((step, width), lambda i: (i, 0))
    flat = whole(1, vec.shape[1])
    out = [((rows, D), bf16), ((rows, D), bf16), ((rows, D // 2), bf16)] if normed else []
    if part is None:
        specs, kernel, args = [flat, block(D)], norm_kernel, (vec, x)
    else:
        specs, kernel = [flat, flat] + [block(D)] * 3, add_norm_kernel
        args, out = (old_vec, vec, x, part, got), [((rows, D), f32)] + out
    return call(
        kernel,
        "norm_rows",
        (4,),
        [SCALARS] + specs,
        [block(shape[1]) for shape, _ in out],
        shaped(*out),
    )(where, *args)


def rope(u, tables, sign):
    half = ROT // 2
    return u * tables[0] + sign * (
        pltpu.roll(u, PAIR - half, 1) * tables[1] + pltpu.roll(u, half, 1) * tables[2]
    )


def window_block(before, where_ref, vec_ref, own_ref, half_ref, other_ref):
    half, other = half_ref[...], other_ref[...]
    first = jnp.where(where_ref[0] == 0, half, other)
    second = jnp.where(where_ref[0] == 0, other, half)
    unit = jnp.concatenate([first, second], axis=1).astype(f32)
    earlier = (unit * vec_ref[:, :D] + vec_ref[:, D : 2 * D]).astype(bf16)
    return jnp.where(pl.program_id(0) < before, earlier, own_ref[...]), unit


def qkv_kernel(
    before, where_ref, own_ref, half_ref, other_ref, wa_ref, wb_ref, vec_ref, table_ref,
    q_ref, k_ref, v_ref, vt_ref,
):
    width = q_ref.shape[1]
    over = wa_ref.shape[1] - width
    a, _ = window_block(before, where_ref, vec_ref, own_ref, half_ref, other_ref)
    tables = [table_ref[i] for i in range(3)]
    bias = [
        vec_ref[:, pl.ds(pl.multiple_of((6 + c) * D + where_ref[0] * width, PAIR), width)]
        for c in range(3)
    ]

    @pl.when(pl.program_id(0) == before)
    def _():
        pre = dot(a, wa_ref[:, :width]) + bias[0]
        for p in range(width // PAIR):
            at = slice(p * PAIR, (p + 1) * PAIR)
            q_ref[:, at] = (rope(pre[:, at], tables, 1.0) * HEAD ** (-0.5)).astype(bf16)

    front, rest = dot(a, wa_ref[:, width:]), dot(a, wb_ref[...])
    values = (rest[:, width - over :] + bias[2]).astype(bf16)
    v_ref[...] = values
    vt_ref[...] = jnp.transpose(values)
    pre = jnp.concatenate([front, rest[:, : width - over]], axis=1) + bias[1]
    for p in range(width // PAIR):
        at = slice(p * PAIR, (p + 1) * PAIR)
        k_ref[:, at] = rope(pre[:, at], tables, 1.0).astype(bf16)


def window_specs(rows, before):
    earlier = pl.BlockSpec((rows, D // 2), lambda i: (jnp.minimum(i, before - 1), 0))
    return [whole(rows, D), earlier, earlier]


def qkv_forward(where, own, half, other, weights, vec, tables):
    rows, total = own.shape[0], tables.shape[1]
    width = (weights[0].shape[1] + weights[1].shape[1]) // 3
    before = total // rows - 1
    flat = pl.BlockSpec((rows, width), lambda i: (i, 0))
    return call(
        functools.partial(qkv_kernel, before),
        "qkv_forward",
        (total // rows,),
        [SCALARS]
        + window_specs(rows, before)
        + [whole(*weights[0].shape), whole(*weights[1].shape), whole(*vec.shape)]
        + [pl.BlockSpec((3, rows, PAIR), lambda i: (0, i, 0))],
        [whole(rows, width), flat, flat, pl.BlockSpec((width, rows), lambda i: (0, i))],
        shaped(
            ((rows, width), bf16),
            ((total, width), bf16),
            ((total, width), bf16),
            ((width, total), bf16),
        ),
        room=14,
    )(where, own, half, other, *weights, vec, tables)


def qkv_back_kernel(
    before, more, where_ref, dq_ref, dk_ref, dv_ref, own_ref, half_ref, other_ref, wa_ref, wb_ref, table_ref,
    vec_ref, *refs,
):
    more_refs, refs = refs[:more], refs[more:]
    ka_ref, sa_ref, kb_ref, sb_ref, da_ref, keep_ref, give_ref, sum_ref, far_ref, pre_ref, acc_ref = refs
    width = dq_ref.shape[1]
    cut = wa_ref.shape[1]
    step = pl.program_id(0)
    tables = [table_ref[i] for i in range(3)]

    @pl.when(step == 0)
    def _():
        acc_ref[...] = jnp.zeros_like(acc_ref)
        sum_ref[...] = jnp.zeros_like(sum_ref)
        far_ref[...] = jnp.zeros_like(far_ref)

    def put(at, value):
        pre_ref[:, at] = value
        sum_ref[:, at] += jnp.sum(value.astype(f32), axis=0, keepdims=True)

    a, unit = window_block(before, where_ref, vec_ref, own_ref, half_ref, other_ref)
    turned = jnp.transpose(a)
    for p in range(width // PAIR):
        at = slice(p * PAIR, (p + 1) * PAIR)
        put(
            slice(width + p * PAIR, width + (p + 1) * PAIR),
            rope(dk_ref[:, at].astype(f32), tables, -1.0).astype(bf16),
        )
    put(slice(2 * width, 3 * width), dv_ref[...])

    @pl.when(step < before)
    def _():
        acc_ref[:, width:] += dot(turned, pre_ref[:, width:])
        da = dot(pre_ref[:, width:cut], wa_ref[:, width:], NT) + dot(pre_ref[:, cut:], wb_ref[...], NT)
        far_ref[0:1, :] += jnp.sum(da * unit, axis=0, keepdims=True)
        far_ref[1:2, :] += jnp.sum(da, axis=0, keepdims=True)
        low, high = da[:, : D // 2].astype(bf16), da[:, D // 2 :].astype(bf16)
        keep_ref[...] = jnp.where(where_ref[0] == 0, low, high)
        give_ref[...] = jnp.where(where_ref[0] == 0, high, low)

    @pl.when(step == before)
    def _():
        for p in range(width // PAIR):
            at = slice(p * PAIR, (p + 1) * PAIR)
            query = rope(dq_ref[:, at].astype(f32), tables, -1.0) * HEAD ** (-0.5)
            put(at, query.astype(bf16))
        acc_ref[...] += dot(turned, pre_ref[...])
        da_ref[...] = dot(pre_ref[:, :cut], wa_ref[...], NT) + dot(pre_ref[:, cut:], wb_ref[...], NT)
        part = acc_ref.shape[0] // 16
        for flip, out_a, out_b in ((0, ka_ref, kb_ref), (1, sa_ref, sb_ref)):
            for z in range(4):
                at = pl.ds(pl.multiple_of((2 * z + (where_ref[2] ^ flip)) * 2 * part, 16), 2 * part)
                out_a[2 * z * part : (2 * z + 2) * part, :cut] = acc_ref[at, :cut].astype(bf16)
                for y in range(2):
                    row = (2 * z + y) * part
                    at = pl.ds(pl.multiple_of(2 * row + (where_ref[3] ^ flip) * part, 16), part)
                    out_b[row : row + part, : 3 * width - cut] = acc_ref[at, cut:].astype(bf16)
        for ref, out in zip(more_refs, (ka_ref, sa_ref, kb_ref, sb_ref)):
            out[:, out.shape[1] - ref.shape[1] :] = ref[...]


def qkv_backward(where, dq, dk, dv, own, half, other, weights, tables, vec, more=()):
    rows, width = dq.shape
    total = tables.shape[1]
    before = total // rows - 1
    cut = weights[0].shape[1]
    each = pl.BlockSpec((rows, width), lambda i: (i, 0))
    earlier = pl.BlockSpec((rows, D // 2), lambda i: (jnp.minimum(i, before - 1), 0))
    behind = (more[0].shape[1], more[2].shape[1]) if more else (0, 0)
    splits = [(D // 2, cut + behind[0])] * 2 + [(D // 2, 3 * width - cut + behind[1])] * 2
    return call(
        functools.partial(qkv_back_kernel, before, len(more)),
        "qkv_backward",
        (total // rows,),
        [SCALARS, whole(rows, width), each, each]
        + window_specs(rows, before)
        + [whole(*weights[0].shape), whole(*weights[1].shape)]
        + [pl.BlockSpec((3, rows, PAIR), lambda i: (0, i, 0)), whole(*vec.shape)]
        + [whole(*m.shape) for m in more],
        [whole(*shape) for shape in splits]
        + [whole(rows, D), earlier, earlier, whole(1, 3 * width), whole(8, D)],
        shaped(
            *[(shape, bf16) for shape in splits],
            ((rows, D), f32),
            ((total - rows, D // 2), bf16),
            ((total - rows, D // 2), bf16),
            ((1, 3 * width), f32),
            ((8, D), f32),
        ),
        [pltpu.VMEM((rows, 3 * width), bf16), pltpu.VMEM((D, 3 * width), f32)],
        room=18,
    )(where, dq, dk, dv, own, half, other, *weights, tables, vec, *more)


def low_lanes():
    return lax.broadcasted_iota(jnp.int32, (1, PAIR), 1) < HEAD


def both_heads(x):
    low = low_lanes()
    zero = jnp.zeros_like(x[:BLK])
    parts = []
    for at in range(0, x.shape[0], BLK):
        block = x[at : at + BLK]
        parts += [jnp.where(low, block, zero), jnp.where(low, zero, block)]
    return jnp.concatenate(parts, axis=0)


def both_columns(first, second):
    parts = []
    for at in range(0, first.shape[1], BLK):
        parts += [first[:, at : at + BLK], second[:, at : at + BLK]]
    return jnp.concatenate(parts, axis=1)


def key_loops(scal_ref, blocks, own, work):
    work(own + 1, slice(2 * BLK, 4 * BLK))
    low_all, low_first = scal_ref[1], scal_ref[2]

    def full(i, carry):
        work(own - i, slice(0, 4 * BLK))
        return carry

    def first_only(i, carry):
        work(low_all - 1 - i, slice(0, 2 * BLK))
        return carry

    lax.fori_loop(0, own - low_all + 1, full, 0)
    lax.fori_loop(0, low_all - low_first, first_only, 0)


def attend_kernel(scal_ref, q_ref, start_ref, k_ref, vt_ref, o_ref, lse_ref, q2_ref, m_ref, l_ref, acc_ref):
    rows, total = q_ref.shape[0], k_ref.shape[0]
    pairs = q_ref.shape[1] // PAIR
    base = scal_ref[0]
    m_ref[...] = jnp.full_like(m_ref, -1e30)
    l_ref[...] = jnp.zeros_like(l_ref)
    acc_ref[...] = jnp.zeros_like(acc_ref)
    for p in range(pairs):
        q2_ref[p] = both_heads(q_ref[:, p * PAIR : (p + 1) * PAIR])
    starts = both_columns(start_ref[0:1, :], start_ref[0:1, :])
    index = base + lax.broadcasted_iota(jnp.int32, (1, rows), 1)
    index = both_columns(index, index)

    def work(kb, cols):
        at = pl.ds(pl.multiple_of(kb * BLK, BLK), BLK)
        key_index = base - (total - rows) + kb * BLK + lax.broadcasted_iota(jnp.int32, (BLK, 1), 0)
        seen = (key_index >= starts[:, cols]) & (key_index <= index[:, cols])
        for p in range(pairs):
            lanes = slice(p * PAIR, (p + 1) * PAIR)
            s = jnp.where(seen, dot(k_ref[at, lanes], q2_ref[p, cols, :], NT), MASKED)
            m_old = m_ref[p, 0:1, cols]
            m_new = jnp.maximum(m_old, jnp.max(s, axis=0, keepdims=True))
            scale = jnp.exp(m_old - m_new)
            e = jnp.exp(s - m_new)
            m_ref[p, 0:1, cols] = m_new
            l_ref[p, 0:1, cols] = l_ref[p, 0:1, cols] * scale + jnp.sum(e, axis=0, keepdims=True)
            acc_ref[p, :, cols] = acc_ref[p, :, cols] * scale + dot(vt_ref[lanes, at], e.astype(bf16))

    key_loops(scal_ref, total // BLK, (total - rows) // BLK, work)
    for p in range(pairs):
        total_p = l_ref[p, 0:1, :]
        acc = acc_ref[p] / total_p
        lse_ref[p, 0:1, :] = m_ref[p, 0:1, :] + jnp.log(total_p)
        for qb in range(rows // BLK):
            first = acc[:HEAD, 2 * qb * BLK : (2 * qb + 1) * BLK]
            second = acc[HEAD:, (2 * qb + 1) * BLK : (2 * qb + 2) * BLK]
            o_ref[qb * BLK : (qb + 1) * BLK, p * PAIR : (p + 1) * PAIR] = jnp.transpose(
                jnp.concatenate([first, second], axis=0)
            ).astype(bf16)


def attend(scalars, q, start_rows, k, vt):
    rows, width = q.shape
    total = k.shape[0]
    pairs = width // PAIR
    return pl.pallas_call(
        attend_kernel,
        grid=(1,),
        in_specs=[
            pl.BlockSpec(memory_space=pltpu.SMEM),
            whole(rows, width),
            whole(8, rows),
            whole(total, width),
            whole(width, total),
        ],
        out_specs=[whole(rows, width), whole(pairs, 8, 2 * rows)],
        out_shape=[
            jax.ShapeDtypeStruct((rows, width), bf16),
            jax.ShapeDtypeStruct((pairs, 8, 2 * rows), f32),
        ],
        scratch_shapes=[
            pltpu.VMEM((pairs, 2 * rows, PAIR), bf16),
            pltpu.VMEM((pairs, 8, 2 * rows), f32),
            pltpu.VMEM((pairs, 8, 2 * rows), f32),
            pltpu.VMEM((pairs, PAIR, 2 * rows), f32),
        ],
        compiler_params=pltpu.CompilerParams(vmem_limit_bytes=ROOM_ATTEND << 20),
        cost_estimate=SMALL,
        name="attend",
    )(scalars, q, start_rows, k, vt)


def attend_back_kernel(
    scal_ref, q_ref, g_ref, o_ref, lse_ref, start_ref, k_ref, v_ref,
    dq_ref, dk_ref, dv_ref, q2_ref, g2_ref, delta_ref, acc_ref,
):
    rows, total = q_ref.shape[0], k_ref.shape[0]
    pairs = q_ref.shape[1] // PAIR
    base = scal_ref[0]
    dk_ref[...] = jnp.zeros_like(dk_ref)
    dv_ref[...] = jnp.zeros_like(dv_ref)
    acc_ref[...] = jnp.zeros_like(acc_ref)
    which = lax.broadcasted_iota(jnp.int32, (8, PAIR), 0)
    lane = lax.broadcasted_iota(jnp.int32, (8, PAIR), 1)
    chosen = (which == lane // HEAD).astype(f32)
    for p in range(pairs):
        lanes = slice(p * PAIR, (p + 1) * PAIR)
        g = g_ref[:, lanes]
        q2_ref[p] = both_heads(q_ref[:, lanes])
        g2_ref[p] = both_heads(g)
        delta = lax.dot_general(
            chosen,
            g.astype(f32) * o_ref[:, lanes].astype(f32),
            NT,
            precision=lax.Precision.HIGHEST,
            preferred_element_type=f32,
        )
        delta_ref[p, 0:1, :] = both_columns(delta[0:1, :], delta[1:2, :])
    starts = both_columns(start_ref[0:1, :], start_ref[0:1, :])
    index = base + lax.broadcasted_iota(jnp.int32, (1, rows), 1)
    index = both_columns(index, index)

    def work(kb, cols):
        at = pl.ds(pl.multiple_of(kb * BLK, BLK), BLK)
        key_index = base - (total - rows) + kb * BLK + lax.broadcasted_iota(jnp.int32, (BLK, 1), 0)
        seen = (key_index >= starts[:, cols]) & (key_index <= index[:, cols])
        for p in range(pairs):
            lanes = slice(p * PAIR, (p + 1) * PAIR)
            keys, q2, g2 = k_ref[at, lanes], q2_ref[p, cols, :], g2_ref[p, cols, :]
            s = jnp.where(seen, dot(keys, q2, NT), MASKED)
            prob = jnp.exp(s - lse_ref[p, 0:1, cols])
            d_prob = dot(v_ref[at, lanes], g2, NT)
            d_score = (prob * (d_prob - delta_ref[p, 0:1, cols])).astype(bf16)
            dv_ref[at, lanes] = dot(prob.astype(bf16), g2).astype(bf16)
            dk_ref[at, lanes] = dot(d_score, q2).astype(bf16)
            acc_ref[p, cols, :] += dot(d_score, keys, TN)

    key_loops(scal_ref, total // BLK, (total - rows) // BLK, work)
    low = low_lanes()
    for p in range(pairs):
        for qb in range(rows // BLK):
            first = acc_ref[p, 2 * qb * BLK : (2 * qb + 1) * BLK, :]
            second = acc_ref[p, (2 * qb + 1) * BLK : (2 * qb + 2) * BLK, :]
            dq_ref[qb * BLK : (qb + 1) * BLK, p * PAIR : (p + 1) * PAIR] = jnp.where(
                low, first, second
            ).astype(bf16)


def attend_back(scalars, q, g, o, lse, start_rows, k, v):
    rows, width = q.shape
    total = k.shape[0]
    pairs = width // PAIR
    return pl.pallas_call(
        attend_back_kernel,
        grid=(1,),
        in_specs=[
            pl.BlockSpec(memory_space=pltpu.SMEM),
            whole(rows, width),
            whole(rows, width),
            whole(rows, width),
            whole(pairs, 8, 2 * rows),
            whole(8, rows),
            whole(total, width),
            whole(total, width),
        ],
        out_specs=[whole(rows, width), whole(total, width), whole(total, width)],
        out_shape=[
            jax.ShapeDtypeStruct((rows, width), bf16),
            jax.ShapeDtypeStruct((total, width), bf16),
            jax.ShapeDtypeStruct((total, width), bf16),
        ],
        scratch_shapes=[
            pltpu.VMEM((pairs, 2 * rows, PAIR), bf16),
            pltpu.VMEM((pairs, 2 * rows, PAIR), bf16),
            pltpu.VMEM((pairs, 8, 2 * rows), f32),
            pltpu.VMEM((pairs, 2 * rows, PAIR), f32),
        ],
        compiler_params=pltpu.CompilerParams(vmem_limit_bytes=ROOM_ATTEND << 20),
        cost_estimate=SMALL,
        name="attend_back",
    )(scalars, q, g, o, lse, start_rows, k, v)


def ffn_kernel(
    where_ref, a_ref, up0_ref, up1_ref, dn0_ref, dn1_ref, outa_ref, outb_ref, vec_ref, mix_ref,
    hid_ref, slope_ref, out_ref, acc_ref,
):
    step = pl.program_id(0)
    over_a = outa_ref.shape[1]
    over_b = mix_ref.shape[1] - over_a
    hidden = pl.num_programs(0) * 2 * BLK

    @pl.when(step == 0)
    def _():
        acc_ref[...] = dot(mix_ref[:, :over_a], outa_ref[...], NT) + dot(
            mix_ref[:, over_a:], outb_ref[:, :over_b], NT
        )

    a = a_ref[...]
    total = acc_ref[...]
    for i, (up, down) in enumerate(((up0_ref, dn0_ref), (up1_ref, dn1_ref))):
        at = slice(i * BLK, (i + 1) * BLK)
        first = 9 * D + where_ref[0] * hidden + (2 * step + i) * BLK
        u = dot(a, up[...]) + vec_ref[:, pl.ds(pl.multiple_of(first, BLK), BLK)]
        phi = 0.5 * (1.0 + lax.erf(u * (1.0 / math.sqrt(2.0))))
        slope = phi + u * jnp.exp(-0.5 * u * u) * (1.0 / math.sqrt(2.0 * math.pi))
        slope_ref[:, at] = slope.astype(bf16)
        low = (u * phi).astype(bf16)
        hid_ref[:, at] = low
        total = total + dot(low, down[...], NT)
    acc_ref[...] = total

    @pl.when(step == pl.num_programs(0) - 1)
    def _():
        out_ref[...] = acc_ref[...].astype(bf16)


def ffn_weights(hidden, skip):
    steps = hidden // BLK
    return [
        pl.BlockSpec((D, BLK), lambda i: (0, 2 * i)),
        pl.BlockSpec((D, BLK), lambda i: (0, 2 * i + 1)),
        pl.BlockSpec((D, BLK), lambda i: (0, skip + 2 * i)),
        pl.BlockSpec((D, BLK), lambda i: (0, skip + 2 * i + 1)),
        pl.BlockSpec((D, BLK), lambda i: (0, 0 if skip else steps)),
        pl.BlockSpec((D, BLK), lambda i: (0, skip + steps)),
    ]


def ffn_forward(where, a, wa, wb, skip, vec, mixed, hidden):
    rows, width = a.shape[0], mixed.shape[1]
    wide = pl.BlockSpec((rows, 2 * BLK), lambda i: (0, i))
    return call(
        ffn_kernel,
        "ffn_forward",
        (hidden // (2 * BLK),),
        [SCALARS, whole(rows, D)]
        + ffn_weights(hidden, skip)
        + [whole(*vec.shape), whole(rows, width)],
        [wide, wide, whole(rows, D)],
        shaped(((rows, hidden), bf16), ((rows, hidden), bf16), ((rows, D), bf16)),
        [pltpu.VMEM((rows, D), f32)],
        room=12,
    )(where, a, wa, wa, wb, wb, wb if skip else wa, wb, vec, mixed)


def ffn_back_kernel(
    where_ref, g_ref, a_ref, up0_ref, up1_ref, dn0_ref, dn1_ref, outa_ref, outb_ref,
    slope_ref, hid_ref, mix_ref,
    ka_ref, sa_ref, kb_ref, sb_ref, da_ref, gmix_ref, sum_ref, ay_ref, gy_ref, gx_ref,
):
    step = pl.program_id(0)
    last = pl.num_programs(0) - 1
    over_a = outa_ref.shape[1]
    over_b = mix_ref.shape[1] - over_a
    half = ka_ref.shape[0]
    part = half // 8

    @pl.when(step == 0)
    def _():
        da_ref[...] = jnp.zeros_like(da_ref)
        for turned, split_y, split_x in (
            (jnp.transpose(a_ref[...]), ay_ref, None),
            (jnp.transpose(g_ref[...]), gy_ref, gx_ref),
        ):
            for z in range(4):
                for y in range(2):
                    row = (2 * z + y) * 2 * part
                    to = pl.multiple_of((where_ref[2] ^ y) * half + 2 * z * part, 16)
                    split_y[pl.ds(to, 2 * part), :] = turned[row : row + 2 * part]
                    for x in range(2) if split_x is not None else ():
                        to = pl.multiple_of((where_ref[3] ^ x) * half + (2 * z + y) * part, 16)
                        split_x[pl.ds(to, part), :] = turned[row + x * part : row + (x + 1) * part]

    @pl.when(step < last)
    def _():
        g = g_ref[...]
        total = da_ref[...]
        grad = dot(gx_ref[...], hid_ref[...]).astype(bf16)
        kb_ref[...], sb_ref[...] = grad[:half], grad[half:]
        for i, (up, down) in enumerate(((up0_ref, dn0_ref), (up1_ref, dn1_ref))):
            at = slice(i * BLK, (i + 1) * BLK)
            d_pre = (dot(g, down[...]) * slope_ref[:, at].astype(f32)).astype(bf16)
            sum_ref[:, at] = jnp.sum(d_pre.astype(f32), axis=0, keepdims=True)
            grad = dot(ay_ref[...], d_pre).astype(bf16)
            ka_ref[:, at], sa_ref[:, at] = grad[:half], grad[half:]
            total = total + dot(d_pre, up[...], NT)
        da_ref[...] = total

    @pl.when(step == last)
    def _():
        g = g_ref[...]
        gmix_ref[:, :over_a] = dot(g, outa_ref[...]).astype(bf16)
        gmix_ref[:, over_a:] = dot(g, outb_ref[:, :over_b]).astype(bf16)
        grad = dot(gy_ref[...], mix_ref[:, :over_a]).astype(bf16)
        ka_ref[:, :over_a], sa_ref[:, :over_a] = grad[:half], grad[half:]
        grad = dot(gx_ref[...], mix_ref[:, over_a:]).astype(bf16)
        kb_ref[:, :over_b], sb_ref[:, :over_b] = grad[:half], grad[half:]


def ffn_backward(where, g, a, wa, wb, skip, slope, hid, mixed):
    rows, width = mixed.shape
    hidden = hid.shape[1]
    steps = hidden // (2 * BLK)
    upto = lambda i: (0, jnp.minimum(i, steps - 1))
    weights = []
    for spec in ffn_weights(hidden, skip):
        weights.append(
            pl.BlockSpec(spec.block_shape, lambda i, f=spec.index_map: f(jnp.minimum(i, steps - 1)))
        )
    wide = pl.BlockSpec((rows, 2 * BLK), upto)
    split = pl.BlockSpec((D // 2, 2 * BLK), lambda i: (0, i))
    wide_a, wide_b = hidden + BLK, hidden + width - BLK
    return call(
        ffn_back_kernel,
        "ffn_backward",
        (steps + 1,),
        [SCALARS, whole(rows, D), whole(rows, D)] + weights + [wide, wide, whole(rows, width)],
        [split] * 4
        + [whole(rows, D), whole(rows, width), pl.BlockSpec((1, 2 * BLK), upto)],
        shaped(
            *[((D // 2, wide_a), bf16)] * 2,
            *[((D // 2, wide_b), bf16)] * 2,
            ((rows, D), f32),
            ((rows, width), bf16),
            ((1, hidden), f32),
        ),
        [pltpu.VMEM((D, rows), bf16)] * 3,
        room=18,
    )(where, g, a, wa, wa, wb, wb, wb if skip else wa, wb, slope, hid, mixed)


def with_half(where_ref, da_ref, back_refs):
    half = sum(ref[...].astype(f32) for ref in back_refs)
    zero = jnp.zeros_like(half)
    first = jnp.where(where_ref[0] == 0, half, zero)
    return da_ref[...] + jnp.concatenate([first, half - first], axis=1)


def joint_kernel(where_ref, vec_ref, da_ref, db_ref, *refs):
    *back_refs, out_ref = refs
    da = with_half(where_ref, da_ref, back_refs)
    out_ref[...] = (da * vec_ref[:, :D] + db_ref[...] * vec_ref[:, 2 * D : 3 * D]).astype(bf16)


def row_call(kernel, name, where, vec, rows_in, outs, steps=4):
    rows = rows_in[0].shape[0]
    block = lambda width: pl.BlockSpec((rows // steps, width), lambda i: (i, 0))
    return call(
        kernel,
        name,
        (steps,),
        [SCALARS, whole(*vec.shape)] + [block(m.shape[1]) for m in rows_in],
        [block(shape[1]) for shape, _ in outs],
        shaped(*outs),
    )(where, vec, *rows_in)


def next_kernel(where_ref, vec_ref, grad_ref, own_ref, got_ref, x_ref, out_ref, low_ref):
    unit, inverse = unit_rows(x_ref[...].astype(f32))
    joint = own_ref[...].astype(f32) + got_ref[...].astype(f32)
    centered = joint - jnp.mean(joint, axis=-1, keepdims=True)
    grad = grad_ref[...].astype(f32) + inverse * (
        centered - unit * jnp.mean(joint * unit, axis=-1, keepdims=True)
    )
    out_ref[...] = grad
    low_ref[...] = grad.astype(bf16)


def vector_kernel(where_ref, qkv_ref, up_ref, far_ref, grad_ref, x_ref, da_ref, db_ref, out_ref):
    core = where_ref[0]
    width, hidden = qkv_ref.shape[1] // 3, up_ref.shape[1]

    @pl.when(pl.program_id(0) == 0)
    def _():
        out_ref[...] = jnp.zeros_like(out_ref)
        for c in range(3):
            to = pl.multiple_of((6 + c) * D + core * width, PAIR)
            out_ref[:, pl.ds(to, width)] = qkv_ref[:, c * width : (c + 1) * width]
        out_ref[:, pl.ds(pl.multiple_of(9 * D + core * hidden, PAIR), hidden)] = up_ref[...]
        for i in range(2):
            out_ref[:, i * D : (i + 1) * D] = far_ref[i : i + 1, :]

    unit, _ = unit_rows(x_ref[...].astype(f32))
    da, db = da_ref[...], db_ref[...]
    first = (core == 0).astype(f32)
    bias = jnp.sum(grad_ref[...].astype(f32), axis=0, keepdims=True) * first
    for i, term in enumerate((da * unit, da, db * unit, db)):
        out_ref[:, i * D : (i + 1) * D] += jnp.sum(term, axis=0, keepdims=True)
    out_ref[:, 4 * D : 5 * D] += bias
    out_ref[:, 5 * D : 6 * D] += bias


def vector_row(where, qkv_sum, up_sum, far, grad, x, da, db):
    rows, steps = grad.shape[0], 4
    block = lambda width: pl.BlockSpec((rows // steps, width), lambda i: (i, 0))
    rows_in = [grad, x, da, db]
    size = 9 * D + FF
    return call(
        vector_kernel,
        "vector_row",
        (steps,),
        [SCALARS, whole(*qkv_sum.shape), whole(*up_sum.shape), whole(*far.shape)] + [block(m.shape[1]) for m in rows_in],
        [whole(1, size)],
        shaped(((1, size), f32)),
    )(where, qkv_sum, up_sum, far, *rows_in)[0]


def qkv_cuts(width):
    low = 3 * width // 256 * 128
    return low + 128, low


def settle_kernel(counts, where_ref, *refs):
    refs = list(refs)
    terms = [[refs.pop(0) for _ in range(n)] for n in counts]
    moms, refs = refs[:KINDS], refs[KINDS:]
    grads, refs = refs[:KINDS], refs[KINDS:]
    news, refs = refs[:KINDS], refs[KINDS:]
    *sends, pad_ref = refs
    layers, _, rows, width = moms[0].shape
    hidden = moms[2].shape[2]
    cuts = qkv_cuts(width)
    pad_ref[...] = jnp.zeros_like(pad_ref)

    def total(parts, at):
        return sum(part[:, at].astype(f32) for part in parts)

    for layer in range(layers):
        ahead, cut = sum(cuts[:layer]), cuts[layer]
        first = total(terms[2], slice(ahead, ahead + cut))
        ahead, rest = sum(cuts) + layer * 3 * width - ahead, 3 * width - cut
        second = total(terms[2], slice(ahead, ahead + rest))
        qkv = jnp.concatenate([first, second], axis=1)
        up = total(terms[layer], slice(0, hidden))
        out_a = total(terms[layer], slice(hidden, hidden + BLK))
        down = total(terms[layer], slice(hidden + BLK, 2 * hidden + BLK))
        out_b = total(terms[layer], slice(2 * hidden + BLK, 2 * hidden + width))
        out = jnp.concatenate([out_a, out_b], axis=1)
        for c in range(3):
            grad = qkv[:, c * width : (c + 1) * width]
            new = MOMENTUM * moms[0][layer, c] + grad
            grads[0][layer, c], news[0][layer, c] = grad, new
            pad_ref[layer, :, c * width : (c + 1) * width] = new.astype(bf16)
        for kind, grad in ((1, out), (2, up), (3, down)):
            new = MOMENTUM * moms[kind][layer] + grad
            grads[kind][layer], news[kind][layer] = grad, new
            pad_ref[layer, :, kind * hidden : kind * hidden + grad.shape[1]] = new.astype(bf16)
    for by, send in enumerate(sends):
        at = pl.ds(pl.multiple_of((where_ref[1] ^ by) * hidden, PAIR), hidden)
        for layer in range(layers):
            send[layer] = pad_ref[layer, :, at]


def settle(where, terms, moms):
    rows, hidden = moms[2].shape[1:]
    flat = [m for group in terms for m in group]
    send = (LAYERS, rows, hidden)
    outs = [(m.shape, f32) for m in moms] * 2 + [(send, bf16)] * KINDS
    got = call(
        functools.partial(settle_kernel, [len(group) for group in terms]),
        "settle",
        (1,),
        [SCALARS] + [whole(*m.shape) for m in flat] + [whole(*m.shape) for m in moms],
        [whole(*shape) for shape, _ in outs],
        shaped(*outs),
        [pltpu.VMEM((LAYERS, rows, KINDS * hidden), bf16)],
        room=12,
    )(where, *flat, *moms)
    return got[:KINDS], got[KINDS : 2 * KINDS], got[2 * KINDS :]


def update_kernel(where_ref, *refs):
    backs, swapped = refs[:KINDS], refs[KINDS]
    masters, outs = refs[KINDS + 1 : 2 * KINDS + 1], refs[2 * KINDS + 1 : 3 * KINDS + 1]
    kept_ref = refs[-1]
    layers, _, rows, width = masters[0].shape
    for slot in range(KINDS):
        kept_ref[slot] = backs[slot][0]
    for layer in range(layers):
        mine = where_ref[0] == layer
        for kind in range(KINDS):
            slot = where_ref[1] ^ kind
            made = jnp.where(mine, kept_ref[slot], swapped[slot]).astype(f32)
            made = made * (-RATE_MAT * math.sqrt((3 * D, D, FF, FF)[kind]))
            if kind == 0:
                for c in range(3):
                    step = made[:, c * width : (c + 1) * width]
                    outs[0][layer, c] = masters[0][layer, c] * SHRINK + step
            else:
                outs[kind][layer] = masters[kind][layer] * SHRINK + made[:, : outs[kind].shape[2]]


def update(where, backs, swapped, masters):
    return call(
        update_kernel,
        "update",
        (1,),
        [SCALARS] + [whole(*m.shape) for m in (*backs, swapped, *masters)],
        [whole(*m.shape) for m in masters],
        shaped(*[(m.shape, f32) for m in masters]),
        [pltpu.VMEM(swapped.shape, bf16)],
    )(where, *backs, swapped, *masters)


def orth_kernel(inner, *refs):
    ins, outs = refs[:2], refs[2 : 2 + KINDS]
    x_ref, gram_ref, mix_ref = refs[2 + KINDS :]
    rows, width = ins[0].shape
    part, chunk = 256, 512
    blocks = rows // part
    total = jnp.zeros((1, 1), f32)
    for ref in ins:
        for i in range(blocks):
            v = ref[i * part : (i + 1) * part, :].astype(f32)
            total = total + jnp.sum(v * v).reshape(1, 1)
    inverse = 1.0 / (jnp.sqrt(total) + 1e-07)
    for i, ref in enumerate(ins):
        x_ref[:, i * width : (i + 1) * width] = (ref[...].astype(f32) * inverse).astype(bf16)

    def spread(ref, i, j, value):
        low = value.astype(bf16)
        ref[i * part : (i + 1) * part, j * part : (j + 1) * part] = low
        if j > i:
            ref[j * part : (j + 1) * part, i * part : (i + 1) * part] = jnp.transpose(low)

    def mixer():
        for i in range(blocks):
            at = slice(i * part, (i + 1) * part)
            gram = dot(x_ref[at, :], x_ref[i * part :, :], NT)
            for j in range(i, blocks):
                spread(gram_ref, i, j, gram[:, (j - i) * part : (j - i + 1) * part])
        for i in range(blocks):
            at = slice(i * part, (i + 1) * part)
            square = dot(gram_ref[at, :], gram_ref[:, i * part :])
            mixed = NS_B * gram_ref[at, i * part :].astype(f32) + NS_C * square
            for j in range(i, blocks):
                spread(mix_ref, i, j, mixed[:, (j - i) * part : (j - i + 1) * part])

    def sweep(_, carry):
        mixer()
        for c in range(2 * width // chunk):
            cols = slice(c * chunk, (c + 1) * chunk)
            x = x_ref[:, cols]
            y = NS_A * x.astype(f32) + dot(mix_ref[...], x)
            x_ref[:, cols] = y.astype(bf16)
        return carry

    lax.fori_loop(0, 4, sweep, 0)
    mixer()
    size = outs[0].shape[1]
    firsts = [by * inner * size for by in range(KINDS)]
    mine = jnp.concatenate([mix_ref[first : first + size, :] for first in firsts], axis=0)
    for half in range(2):
        cols = slice(half * width, (half + 1) * width)
        made = dot(mine, x_ref[:, cols])
        for by, out in enumerate(outs):
            x = x_ref[firsts[by] : firsts[by] + size, cols].astype(f32)
            out[half] = (NS_A * x + made[by * size : (by + 1) * size]).astype(bf16)


def orthogonalize(parts, inner):
    rows, width = parts[0].shape
    shape = (2, rows // (KINDS * inner), width)
    return call(
        functools.partial(orth_kernel, inner),
        "orthogonalize",
        (1,),
        [whole(rows, width)] * 2,
        [whole(*shape)] * KINDS,
        shaped(*[(shape, bf16)] * KINDS),
        [
            pltpu.VMEM((rows, 2 * width), bf16),
            pltpu.VMEM((rows, rows), bf16),
            pltpu.VMEM((rows, rows), bf16),
        ],
        room=20,
    )(*parts)


def shards(
    tokens,
    cotangent,
    w_qkv,
    w_out,
    w_up,
    w_down,
    mom_qkv,
    mom_out,
    mom_up,
    mom_down,
    vectors,
    vec_first,
    vec_second,
    lengths,
):
    tok_rows = tokens.shape[0]
    row_part = w_qkv.shape[1]
    head_part = w_qkv.shape[-1]
    hidden_part = w_up.shape[-1]
    widths = (3 * head_part, head_part, hidden_part, hidden_part)
    over = BLK
    cut_qkv = qkv_cuts(head_part)
    cut_rest = hidden_part + over
    fsdp_count = lax.axis_size("fsdp")
    core = lax.axis_index("tp")
    longest = SEQ_DEV * fsdp_count
    span = (tok_rows + longest - 2) // tok_rows
    where = place()

    def stored(qkv, out, up, down):
        return [qkv.transpose(0, 2, 1, 3), out.transpose(0, 2, 1), up, down.transpose(0, 2, 1)]

    def unstored(qkv, out, up, down):
        return [qkv.transpose(0, 2, 1, 3), out.transpose(0, 2, 1), up, down.transpose(0, 2, 1)]

    def qkv_piece(mats, layer):
        low = mats[0][layer].astype(bf16)
        return jnp.concatenate([low[c] for c in range(3)], axis=1)

    def rest_piece(mats, layer):
        out, up, down = [m[layer].astype(bf16) for m in mats[1:]]
        return jnp.concatenate([up, out[:, :over], down, out[:, over:]], axis=1)

    masters = stored(w_qkv, w_out, w_up, w_down)
    moments = stored(mom_qkv, mom_out, mom_up, mom_down)

    qkv_0 = Task(gather_steps(where, qkv_piece(masters, 0), cut_qkv[0]))
    vecs = [vectors[layer : layer + 1] for layer in range(LAYERS)]
    a0, b0, half = norm_rows(where, vecs[0], tokens)
    rest, half, lengths, *later = advance(
        [qkv_0], rest_piece(masters, 0), half, lengths, *masters
    )
    rest_0 = Task(gather_steps(where, rest, cut_rest, True))
    half, lengths, *later = advance([qkv_0, rest_0], half, lengths, *later)
    win_0 = Task(window_steps(half, span))
    tables, start_rows, scalars = setup(lengths, where, tok_rows, (span + 1) * tok_rows)
    tables, start_rows, scalars, *later = advance(
        [qkv_0, rest_0, win_0], tables, start_rows, scalars, *later
    )
    qkv_1 = Task(gather_steps(where, qkv_piece(later, 1), cut_qkv[1], False, True))
    wq0 = qkv_0.result
    tables, *later = advance([win_0], tables, *later)
    q, k, v, vt = qkv_forward(where, a0, *win_0.result, wq0, vecs[0], tables)
    q, k, v, vt, *later = advance([rest_0, qkv_1], q, k, v, vt, *later)
    rest_1 = Task(gather_steps(where, rest_piece(later, 1), hidden_part, False, True))
    mixed, lse = attend(scalars, q, start_rows, k, vt)
    mixed, lse, b0 = advance([rest_0, rest_1], mixed, lse, b0)
    mixed, b0, wa, wb = advance([rest_1, qkv_1], mixed, b0, *rest_0.result)
    hid, slope, partial = ffn_forward(where, b0, wa, wb, 0, vecs[0], mixed, hidden_part)
    partial = advance([rest_1, qkv_1], partial)
    kept = [(tokens, a0, win_0.result, b0, q, k, v, mixed, lse, hid, slope)]
    weights = [(wq0, wa, wb, 0)]
    got = core_swap(partial)
    x1, a1, b1, half = norm_rows(where, vecs[1], tokens, vecs[0], partial, got)
    win_1 = Task(window_steps(half, span))
    a1, b1 = advance([win_1, qkv_1], a1, b1)
    a1, b1 = advance([win_1], a1, b1)
    wq1 = qkv_1.result
    q, k, v, vt = qkv_forward(where, a1, *win_1.result, wq1, vecs[1], tables)
    mixed, lse = attend(scalars, q, start_rows, k, vt)
    mixed, lse, b1, q, k, v = advance([rest_1], mixed, lse, b1, q, k, v)
    wa, wb = rest_1.result
    hid, slope, partial = ffn_forward(where, b1, wa, wb, 1, vecs[1], mixed, hidden_part)
    kept.append((x1, a1, win_1.result, b1, q, k, v, mixed, lse, hid, slope))
    weights.append((wq1, wa, wb, 1))

    def own_gradients(grad_low, layer):
        _, _, _, b, _, _, _, mixed, _, hid, slope = kept[layer]
        _, wa, wb, skip = weights[layer]
        return ffn_backward(where, grad_low, b, wa, wb, skip, slope, hid, mixed)

    def attention_gradients(g_mixed, layer, more=()):
        _, a, win, _, q, k, v, mixed, lse, _, _ = kept[layer]
        dq, dk, dv = attend_back(scalars, q, g_mixed, mixed, lse, start_rows, k, v)
        return qkv_backward(where, dq, dk, dv, a, *win, weights[layer][0], tables, vecs[layer], more)

    def joint_of(da, db, back, layer):
        rows_in = [da, db] + list(back)
        return row_call(joint_kernel, "joint", where, vecs[layer], rows_in, [(da.shape, bf16)])[0]

    def next_grad(grad, joint, got, layer):
        outs = [(joint.shape, f32), (joint.shape, bf16)]
        rows_in = [grad, joint, got, kept[layer][0]]
        return row_call(next_kernel, "next_grad", where, vecs[layer], rows_in, outs)

    *split, db1, g_mixed, up_sum1 = own_gradients(cotangent, 1)
    *split, g_mixed, partial, db1 = advance([], *split, g_mixed, partial, db1)
    rest_1 = Task(scatter_steps(where, *split, True))
    *split1, da1, keep, give, pre_sum1, far1 = attention_gradients(g_mixed, 1)
    *split1, da1, keep, give, partial = advance([], *split1, da1, keep, give, partial)
    back_1 = Task(window_back_steps(keep, give, span))
    da1, partial = advance([back_1, rest_1], da1, partial)
    da1, partial = advance([back_1, rest_1], da1, partial)
    joint = joint_of(da1, db1, back_1.result, 1)
    got = core_swap(joint)
    grad_x0, grad_low = next_grad(cotangent, joint, got, 1)
    *split, db0, g_mixed, up_sum0 = own_gradients(grad_low, 0)
    *split, g_mixed, da1, db0, partial = advance([rest_1], *split, g_mixed, da1, db0, partial)
    *split, g_mixed = advance([rest_1], *split, g_mixed)
    rest_0 = Task(scatter_steps(where, *split, False, True))
    *split, da0, keep, give, pre_sum0, far0 = attention_gradients(g_mixed, 0, split1)
    *split, da0, keep, give, da1, db1, partial = advance(
        [rest_0, rest_1], *split, da0, keep, give, da1, db1, partial
    )
    both_qkv = Task(scatter_steps(where, *split, True))
    back_0 = Task(window_back_steps(keep, give, span, True))
    row_0 = vector_row(where, pre_sum0, up_sum0, far0, grad_x0, kept[0][0], da0, db0)
    row_1 = vector_row(where, pre_sum1, up_sum1, far1, cotangent, kept[1][0], da1, db1)
    rows_both, partial = advance(
        [rest_0, both_qkv], jnp.concatenate([row_0, row_1], axis=0), partial
    )
    rows_both, partial = advance([both_qkv], rows_both, partial)
    vec_sum = Task(sum_steps(rows_both))
    partial = advance([both_qkv, rest_0, back_0, vec_sum], partial)
    partial = advance([both_qkv], partial)
    got = core_swap(partial)
    block_out = norm_rows(where, vecs[1], kept[1][0], vecs[1], partial, got, False)[0]
    block_out = advance([both_qkv, rest_0], block_out)
    terms = [rest_0.result, rest_1.result, both_qkv.result]
    grads, new_moms, blocks = settle(where, terms, moments)
    owned = Task(owner_steps(blocks[0], blocks[1:]))
    advance([owned, vec_sum])
    advance([owned])
    while owned.flying is not None:
        advance([owned, vec_sum])

    inner = fsdp_count // KINDS
    parts = advance([back_0], *owned.result)
    made = orthogonalize(parts, inner)
    *made, da0 = advance([back_0], *made, da0)
    backs = [made[0]] + [
        permute(made[by], xor_pairs(fsdp_count, by * inner)) for by in range(1, KINDS)
    ]
    joint = joint_of(da0, db0, back_0.result, 0)
    got = core_swap(joint)
    grad_in, _ = next_grad(grad_x0, joint, got, 0)
    grad_in = advance([vec_sum], grad_in)
    while vec_sum.flying is not None:
        grad_in = advance([vec_sum], grad_in)
    grad_vectors = vec_sum.result
    grad_in, grad_vectors, *backs = advance([], grad_in, grad_vectors, *backs)
    swapped = core_swap(jnp.stack([m[1] for m in backs]))
    new_weights = update(where, backs, swapped, masters)

    first_new = BETA_ONE * vec_first + (1.0 - BETA_ONE) * grad_vectors
    second_new = BETA_TWO * vec_second + (1.0 - BETA_TWO) * grad_vectors * grad_vectors
    first_hat = first_new / (1.0 - BETA_ONE**STEP)
    second_hat = second_new / (1.0 - BETA_TWO**STEP)
    vectors_new = vectors - RATE_VEC * first_hat / (jnp.sqrt(second_hat) + ADAM_EPS)
    return (
        block_out,
        grad_in,
        *unstored(*grads),
        *unstored(*new_moms),
        *unstored(*new_weights),
        first_new,
        second_new,
        vectors_new,
        grad_vectors[:, 9 * D :],
    )


def solution(mesh):
    weights = (
        P(None, "fsdp", None, "tp"),
        P(None, "tp", "fsdp"),
        P(None, "fsdp", "tp"),
        P(None, "tp", "fsdp"),
    )
    rows = (P("fsdp", None), P("fsdp", None))
    return jax.shard_map(
        shards,
        mesh=mesh,
        in_specs=rows + weights + weights + (P(), P(), P(), P()),
        out_specs=rows + weights + weights + weights + (P(), P(), P(), P()),
        check_vma=False,
    )
```

```python
import functools
import math

import jax
import jax.numpy as jnp
import numpy as np
from jax import lax
from jax.experimental import pallas as pl
from jax.experimental.pallas import tpu as pltpu
from jax.sharding import PartitionSpec as P

D = 768
HEAD = 64
ROT = 16
FF = 3072
LAYERS = 2
SEQ_DEV = 64
STEP = 10
PAIR = 2 * HEAD
BLK = 256
KINDS = 4

MASKED = -1000000000.0
EPS_NORM = 1e-05
NS_A = 3.4445
NS_B = -4.775
NS_C = 2.0315
MOMENTUM = 0.95
RATE_MAT = 0.02
SHRINK = 0.99
RATE_VEC = 0.25
BETA_ONE = 0.9
BETA_TWO = 0.95
ADAM_EPS = 1e-08
ROOM_ATTEND = 16

bf16 = jnp.bfloat16
f32 = jnp.float32


def permute(x, pairs):
    return lax.ppermute(x, "fsdp", pairs)


def xor_pairs(count, by):
    return [(i, i ^ by) for i in range(count)]


def core_swap(x):
    count = lax.axis_size("tp")
    return lax.ppermute(x, "tp", [(i, i ^ 1) for i in range(count)])


def shifted(x, by):
    devices = lax.axis_size("fsdp")
    return lax.ppermute(
        x, "fsdp", [(i, i + by) for i in range(devices) if 0 <= i + by < devices]
    )


def on_grid():
    return lax.axis_size("fsdp") == 16


def place():
    index = lax.axis_index("fsdp")
    inner = lax.axis_size("fsdp") // KINDS
    bits = [(index // 2) % 2, index % 2] if on_grid() else [index * 0, index * 0]
    parts = [lax.axis_index("tp"), index // inner, *bits, index]
    return jnp.stack([p.astype(jnp.int32) for p in parts])


class Task:
    def __init__(self, steps):
        self.steps = steps
        self.result = None
        self.flying = None
        self.resume(None)

    def resume(self, arrived):
        try:
            self.flying = self.steps.send(arrived)
        except StopIteration as stop:
            self.result = stop.value
            self.flying = None


def advance(tasks, *arrays):
    tasks = [t for t in tasks if t.flying is not None]
    arrived, arrays = lax.optimization_barrier(([t.flying for t in tasks], arrays))
    for task, got in zip(tasks, arrived):
        task.resume(got)
    return arrays if len(arrays) != 1 else arrays[0]


def gather_steps(where, piece, cut, apart=False, pause=False):
    rows, cols = piece.shape
    if not on_grid():
        full = lax.all_gather(piece, "fsdp", axis=0, tiled=True)
        return full[:, :cut], full[:, cut:]
        yield
    got = []
    for group in ((1, 2), (3,)) if apart else ((1, 2, 3),):
        got += yield [permute(piece, xor_pairs(16, 4 * by)) for by in group]
    part_a, part_b = join_planes(where, [piece] + got, cut)
    if pause:
        part_a, part_b = yield [part_a, part_b]
    got_a, got_b = yield [permute(part_a, xor_pairs(16, 1)), permute(part_b, xor_pairs(16, 2))]
    part_a, part_b = join_chips(where, part_a, got_a, part_b, got_b, False)
    got_a, got_b = yield [permute(part_a, xor_pairs(16, 2)), permute(part_b, xor_pairs(16, 1))]
    part_a, part_b = join_chips(where, part_a, got_a, part_b, got_b, True)
    return part_a.reshape(16 * rows, -1), part_b.reshape(16 * rows, -1)


def natural(keep, send, axis):
    shape = (4, 1, 2, -1) if axis == 1 else (4, 2, 1, -1)
    parts = [m.reshape(shape + (m.shape[-1],)) for m in (keep, send)]
    full = jnp.concatenate(parts, axis=axis)
    return full.reshape(-1, keep.shape[-1])


def scatter_steps(where, keep_a, send_a, keep_b, send_b, pause=False, apart=False):
    if not on_grid():
        full = jnp.concatenate([natural(keep_a, send_a, 1), natural(keep_b, send_b, 2)], axis=1)
        return [lax.psum_scatter(full, "fsdp", scatter_dimension=0, tiled=True)]
        yield
    got_a, got_b = yield [permute(send_a, xor_pairs(16, 2)), permute(send_b, xor_pairs(16, 1))]
    keep_a, send_a, keep_b, send_b = add_split(where, keep_a, got_a, keep_b, got_b)
    if pause:
        keep_a, send_a, keep_b, send_b = yield [keep_a, send_a, keep_b, send_b]
    got_a, got_b = yield [permute(send_a, xor_pairs(16, 1)), permute(send_b, xor_pairs(16, 2))]
    own, *sends = add_planes(where, keep_a, got_a, keep_b, got_b)
    if pause:
        own, *sends = yield [own, *sends]
    got = [own]
    for group in ((0, 1), (2,)) if apart else ((0, 1, 2),):
        got += yield [permute(sends[i], xor_pairs(16, 4 * (i + 1))) for i in group]
    return got


def window_steps(half, span):
    got = yield [shifted(half, step) for step in range(span, 0, -1)]
    got = jnp.concatenate(got, axis=0)
    (other,) = yield [core_swap(got)]
    return got, other


def window_back_steps(keep, give, span, pause=False):
    (got,) = yield [core_swap(give)]
    half = (keep.astype(f32) + got.astype(f32)).astype(bf16).reshape(span, -1, keep.shape[-1])
    if pause:
        (half,) = yield [half]
    back = yield [shifted(half[span - step], -step) for step in range(span, 0, -1)]
    return back


def sum_steps(x):
    count = lax.axis_size("fsdp")
    step = 1
    while step < count:
        (got,) = yield [permute(x, xor_pairs(count, step))]
        x = x + got
        step *= 2
    (got,) = yield [core_swap(x)]
    return x + got


def owner_steps(own, sends):
    count = lax.axis_size("fsdp")
    inner = count // KINDS
    core = lax.axis_index("tp")
    rows, width = own.shape[1:]
    got = yield [permute(sends[by - 1], xor_pairs(count, by * inner)) for by in range(1, KINDS)]
    terms = [own] + list(got)
    give = jnp.stack([jnp.where(core == 0, m[1], m[0]) for m in terms])
    part_a = jnp.stack([jnp.where(core == 0, m[0], m[1]) for m in terms])
    part_a, part_b = yield [part_a, core_swap(give)]
    bits = inner.bit_length() - 1
    shape = (KINDS,) + (1,) * bits + (rows, width)
    part_a, part_b = part_a.reshape(shape), part_b.reshape(shape)
    for step in range(bits):
        bit_a, bit_b = step, bits - 1 - step
        got_a, got_b = yield [
            permute(part_a, xor_pairs(count, 1 << bit_a)),
            permute(part_b, xor_pairs(count, 1 << bit_b)),
        ]
        part_a = jnp.concatenate([part_a, got_a], axis=1 + bit_a)
        part_b = jnp.concatenate([part_b, got_b], axis=1 + bit_b)
    return [m.reshape(count * rows, width) for m in (part_a, part_b)]


SMALL = pl.CostEstimate(flops=1, bytes_accessed=1, transcendentals=0)
SCALARS = pl.BlockSpec(memory_space=pltpu.SMEM)
NT = (((1,), (1,)), ((), ()))
TN = (((0,), (0,)), ((), ()))


def dot(a, b, how=(((1,), (0,)), ((), ()))):
    return lax.dot_general(a, b, how, preferred_element_type=f32)


def whole(*shape):
    return pl.BlockSpec(shape, lambda *_: (0,) * len(shape))


def shaped(*shapes_and_kinds):
    return [jax.ShapeDtypeStruct(shape, kind) for shape, kind in shapes_and_kinds]


def call(kernel, name, grid, in_specs, out_specs, out_shape, scratch=(), room=8):
    return pl.pallas_call(
        kernel,
        grid=grid,
        in_specs=in_specs,
        out_specs=out_specs,
        out_shape=out_shape,
        scratch_shapes=list(scratch),
        compiler_params=pltpu.CompilerParams(vmem_limit_bytes=room << 20),
        cost_estimate=SMALL,
        name=name,
    )


def join_planes_kernel(cut, where_ref, *refs):
    *pieces, out_a, out_b = refs
    quarter = where_ref[1]
    for by, piece in enumerate(pieces):
        plane = quarter ^ by
        out_a[plane] = piece[:, :cut]
        out_b[plane] = piece[:, cut:]


def join_planes(where, pieces, cut):
    rows, cols = pieces[0].shape
    shapes = [(4, rows, cut), (4, rows, cols - cut)]
    return call(
        functools.partial(join_planes_kernel, cut),
        "join_planes",
        (1,),
        [SCALARS] + [whole(rows, cols)] * 4,
        [whole(*shape) for shape in shapes],
        shaped(*[(shape, bf16) for shape in shapes]),
    )(where, *pieces)


def join_chips_kernel(last, where_ref, own_a, got_a, own_b, got_b, out_a, out_b):
    y, x = where_ref[2], where_ref[3]
    if not last:
        out_a[0, x], out_a[0, 1 - x] = own_a[0], got_a[0]
        out_b[0, y], out_b[0, 1 - y] = own_b[0], got_b[0]
    else:
        out_a[0, y], out_a[0, 1 - y] = own_a[0], got_a[0]
        for side in range(2):
            out_b[0, side, x], out_b[0, side, 1 - x] = own_b[0, side], got_b[0, side]


def join_chips(where, own_a, got_a, own_b, got_b, last):
    rows = own_a.shape[-2]
    ins, outs = ((2, rows), (2, 2, rows)) if last else ((rows,), (2, rows))

    def spec(shape, width):
        return pl.BlockSpec((1,) + shape + (width,), lambda i: (i,) + (0,) * (len(shape) + 1))

    wide_a, wide_b = own_a.shape[-1], own_b.shape[-1]
    return call(
        functools.partial(join_chips_kernel, last),
        "join_chips",
        (4,),
        [SCALARS, spec(ins, wide_a), spec(ins, wide_a), spec(ins, wide_b), spec(ins, wide_b)],
        [spec(outs, wide_a), spec(outs, wide_b)],
        shaped(((4,) + outs + (wide_a,), bf16), ((4,) + outs + (wide_b,), bf16)),
    )(where, own_a, got_a, own_b, got_b)


def add_split_kernel(where_ref, keep_a, got_a, keep_b, got_b, out_ka, out_sa, out_kb, out_sb):
    rows = keep_a.shape[0] // 8
    for bit, keep, got, out_k, out_s in (
        (where_ref[3], keep_a, got_a, out_ka, out_sa),
        (where_ref[2], keep_b, got_b, out_kb, out_sb),
    ):
        for z in range(4):
            for flip, out in ((0, out_k), (1, out_s)):
                at = pl.ds(pl.multiple_of((2 * z + (bit ^ flip)) * rows, 16), rows)
                total = keep[at, :].astype(f32) + got[at, :].astype(f32)
                out[z * rows : (z + 1) * rows, :] = total.astype(bf16)


def add_split(where, keep_a, got_a, keep_b, got_b):
    rows, wide_a = keep_a.shape
    wide_b = keep_b.shape[1]
    outs = [(rows // 2, wide_a)] * 2 + [(rows // 2, wide_b)] * 2
    return call(
        add_split_kernel,
        "add_split",
        (1,),
        [SCALARS] + [whole(rows, wide_a)] * 2 + [whole(rows, wide_b)] * 2,
        [whole(*shape) for shape in outs],
        shaped(*[(shape, bf16) for shape in outs]),
        room=12,
    )(where, keep_a, got_a, keep_b, got_b)


def add_planes_kernel(where_ref, keep_a, got_a, keep_b, got_b, *outs):
    rows = keep_a.shape[0] // 4
    cut = keep_a.shape[1]
    for by, out in enumerate(outs):
        at = pl.ds(pl.multiple_of((where_ref[1] ^ by) * rows, 16), rows)
        out[:, :cut] = (keep_a[at, :].astype(f32) + got_a[at, :].astype(f32)).astype(bf16)
        out[:, cut:] = (keep_b[at, :].astype(f32) + got_b[at, :].astype(f32)).astype(bf16)


def add_planes(where, keep_a, got_a, keep_b, got_b):
    rows, wide_a = keep_a.shape
    wide_b = keep_b.shape[1]
    shape = (rows // 4, wide_a + wide_b)
    return call(
        add_planes_kernel,
        "add_planes",
        (1,),
        [SCALARS] + [whole(rows, wide_a)] * 2 + [whole(rows, wide_b)] * 2,
        [whole(*shape)] * 4,
        shaped(*[(shape, bf16)] * 4),
    )(where, keep_a, got_a, keep_b, got_b)


def setup_kernel(len_ref, where_ref, freq_ref, table_ref, start_ref, scal_ref):
    rows, total = start_ref.shape[1], table_ref.shape[1]
    base = where_ref[4] * rows
    first = base - (total - rows)
    half = ROT // 2

    def starts_of(index):
        end, out = jnp.int32(0), jnp.zeros_like(index)
        for i in range(len_ref.shape[0]):
            end = end + len_ref[i]
            out = jnp.where(index >= end, end, out)
        return out

    lane = lax.broadcasted_iota(jnp.int32, (BLK, PAIR), 1) % HEAD
    for c in range(total // BLK):
        at = slice(c * BLK, (c + 1) * BLK)
        index = first + c * BLK + lax.broadcasted_iota(jnp.int32, (BLK, PAIR), 0)
        phase = (index - starts_of(index)).astype(f32) * freq_ref[...]
        sine = jnp.sin(phase)
        table_ref[0, at, :] = jnp.cos(phase)
        table_ref[1, at, :] = jnp.where(lane < half, -sine, 0.0)
        table_ref[2, at, :] = jnp.where((lane >= half) & (lane < ROT), sine, 0.0)
    start_ref[...] = starts_of(base + lax.broadcasted_iota(jnp.int32, start_ref.shape, 1))
    own = (total - rows) // BLK
    scal_ref[0] = base
    scal_ref[1] = jnp.minimum((starts_of(base + BLK) - first) // BLK, own)
    scal_ref[2] = (starts_of(base) - first) // BLK


def setup(lengths, where, rows, total):
    lane = np.arange(PAIR) % HEAD
    freqs = np.exp((lane % (ROT // 2)) * (-2.0 * math.log(10000.0) / ROT))
    freqs = np.where(lane < ROT, freqs, 0.0).astype(np.float32)[None]
    return call(
        setup_kernel,
        "setup",
        (1,),
        [SCALARS, SCALARS, whole(1, PAIR)],
        [whole(3, total, PAIR), whole(8, rows), SCALARS],
        shaped(((3, total, PAIR), f32), ((8, rows), jnp.int32), ((3,), jnp.int32)),
        room=8,
    )(lengths, where, jnp.asarray(freqs))


def unit_rows(x):
    centered = x - jnp.mean(x, axis=-1, keepdims=True)
    inverse = lax.rsqrt(jnp.mean(centered * centered, axis=-1, keepdims=True) + EPS_NORM)
    return centered * inverse, inverse


def norm_kernel(where_ref, vec_ref, x_ref, a_ref, b_ref, half_ref):
    unit, _ = unit_rows(x_ref[...].astype(f32))
    a = (unit * vec_ref[:, :D] + vec_ref[:, D : 2 * D]).astype(bf16)
    a_ref[...] = a
    b_ref[...] = (unit * vec_ref[:, 2 * D : 3 * D] + vec_ref[:, 3 * D : 4 * D]).astype(bf16)
    half_ref[...] = jnp.where(where_ref[0] == 0, unit[:, : D // 2], unit[:, D // 2 :]).astype(bf16)


def add_norm_kernel(where_ref, old_ref, vec_ref, x_ref, part_ref, got_ref, new_ref, *outs):
    x = x_ref[...].astype(f32) + part_ref[...].astype(f32) + got_ref[...].astype(f32)
    x = x + old_ref[:, 4 * D : 5 * D] + old_ref[:, 5 * D : 6 * D]
    new_ref[...] = x
    if outs:
        norm_kernel(where_ref, vec_ref, new_ref, *outs)


def norm_rows(where, vec, x, old_vec=None, part=None, got=None, normed=True):
    rows = x.shape[0]
    step = rows // 4
    block = lambda width: pl.BlockSpec((step, width), lambda i: (i, 0))
    flat = whole(1, vec.shape[1])
    out = [((rows, D), bf16), ((rows, D), bf16), ((rows, D // 2), bf16)] if normed else []
    if part is None:
        specs, kernel, args = [flat, block(D)], norm_kernel, (vec, x)
    else:
        specs, kernel = [flat, flat] + [block(D)] * 3, add_norm_kernel
        args, out = (old_vec, vec, x, part, got), [((rows, D), f32)] + out
    return call(
        kernel,
        "norm_rows",
        (4,),
        [SCALARS] + specs,
        [block(shape[1]) for shape, _ in out],
        shaped(*out),
    )(where, *args)


def rope(u, tables, sign):
    half = ROT // 2
    return u * tables[0] + sign * (
        pltpu.roll(u, PAIR - half, 1) * tables[1] + pltpu.roll(u, half, 1) * tables[2]
    )


def window_block(before, where_ref, vec_ref, own_ref, half_ref, other_ref):
    half, other = half_ref[...], other_ref[...]
    first = jnp.where(where_ref[0] == 0, half, other)
    second = jnp.where(where_ref[0] == 0, other, half)
    unit = jnp.concatenate([first, second], axis=1).astype(f32)
    earlier = (unit * vec_ref[:, :D] + vec_ref[:, D : 2 * D]).astype(bf16)
    return jnp.where(pl.program_id(0) < before, earlier, own_ref[...]), unit


def qkv_kernel(
    before, where_ref, own_ref, half_ref, other_ref, wa_ref, wb_ref, vec_ref, table_ref,
    q_ref, k_ref, v_ref, vt_ref,
):
    width = q_ref.shape[1]
    over = wa_ref.shape[1] - width
    a, _ = window_block(before, where_ref, vec_ref, own_ref, half_ref, other_ref)
    tables = [table_ref[i] for i in range(3)]
    bias = [
        vec_ref[:, pl.ds(pl.multiple_of((6 + c) * D + where_ref[0] * width, PAIR), width)]
        for c in range(3)
    ]

    @pl.when(pl.program_id(0) == before)
    def _():
        pre = dot(a, wa_ref[:, :width]) + bias[0]
        for p in range(width // PAIR):
            at = slice(p * PAIR, (p + 1) * PAIR)
            q_ref[:, at] = (rope(pre[:, at], tables, 1.0) * HEAD ** (-0.5)).astype(bf16)

    front, rest = dot(a, wa_ref[:, width:]), dot(a, wb_ref[...])
    values = (rest[:, width - over :] + bias[2]).astype(bf16)
    v_ref[...] = values
    vt_ref[...] = jnp.transpose(values)
    pre = jnp.concatenate([front, rest[:, : width - over]], axis=1) + bias[1]
    for p in range(width // PAIR):
        at = slice(p * PAIR, (p + 1) * PAIR)
        k_ref[:, at] = rope(pre[:, at], tables, 1.0).astype(bf16)


def window_specs(rows, before):
    earlier = pl.BlockSpec((rows, D // 2), lambda i: (jnp.minimum(i, before - 1), 0))
    return [whole(rows, D), earlier, earlier]


def qkv_forward(where, own, half, other, weights, vec, tables):
    rows, total = own.shape[0], tables.shape[1]
    width = (weights[0].shape[1] + weights[1].shape[1]) // 3
    before = total // rows - 1
    flat = pl.BlockSpec((rows, width), lambda i: (i, 0))
    return call(
        functools.partial(qkv_kernel, before),
        "qkv_forward",
        (total // rows,),
        [SCALARS]
        + window_specs(rows, before)
        + [whole(*weights[0].shape), whole(*weights[1].shape), whole(*vec.shape)]
        + [pl.BlockSpec((3, rows, PAIR), lambda i: (0, i, 0))],
        [whole(rows, width), flat, flat, pl.BlockSpec((width, rows), lambda i: (0, i))],
        shaped(
            ((rows, width), bf16),
            ((total, width), bf16),
            ((total, width), bf16),
            ((width, total), bf16),
        ),
        room=14,
    )(where, own, half, other, *weights, vec, tables)


def qkv_back_kernel(
    before, more, where_ref, dq_ref, dk_ref, dv_ref, own_ref, half_ref, other_ref, wa_ref, wb_ref, table_ref,
    vec_ref, *refs,
):
    more_refs, refs = refs[:more], refs[more:]
    ka_ref, sa_ref, kb_ref, sb_ref, da_ref, keep_ref, give_ref, sum_ref, far_ref, pre_ref, acc_ref = refs
    width = dq_ref.shape[1]
    cut = wa_ref.shape[1]
    step = pl.program_id(0)
    tables = [table_ref[i] for i in range(3)]

    @pl.when(step == 0)
    def _():
        acc_ref[...] = jnp.zeros_like(acc_ref)
        sum_ref[...] = jnp.zeros_like(sum_ref)
        far_ref[...] = jnp.zeros_like(far_ref)

    def put(at, value):
        pre_ref[:, at] = value
        sum_ref[:, at] += jnp.sum(value.astype(f32), axis=0, keepdims=True)

    a, unit = window_block(before, where_ref, vec_ref, own_ref, half_ref, other_ref)
    turned = jnp.transpose(a)
    for p in range(width // PAIR):
        at = slice(p * PAIR, (p + 1) * PAIR)
        put(
            slice(width + p * PAIR, width + (p + 1) * PAIR),
            rope(dk_ref[:, at].astype(f32), tables, -1.0).astype(bf16),
        )
    put(slice(2 * width, 3 * width), dv_ref[...])

    @pl.when(step < before)
    def _():
        acc_ref[:, width:] += dot(turned, pre_ref[:, width:])
        da = dot(pre_ref[:, width:cut], wa_ref[:, width:], NT) + dot(pre_ref[:, cut:], wb_ref[...], NT)
        far_ref[0:1, :] += jnp.sum(da * unit, axis=0, keepdims=True)
        far_ref[1:2, :] += jnp.sum(da, axis=0, keepdims=True)
        low, high = da[:, : D // 2].astype(bf16), da[:, D // 2 :].astype(bf16)
        keep_ref[...] = jnp.where(where_ref[0] == 0, low, high)
        give_ref[...] = jnp.where(where_ref[0] == 0, high, low)

    @pl.when(step == before)
    def _():
        for p in range(width // PAIR):
            at = slice(p * PAIR, (p + 1) * PAIR)
            query = rope(dq_ref[:, at].astype(f32), tables, -1.0) * HEAD ** (-0.5)
            put(at, query.astype(bf16))
        acc_ref[...] += dot(turned, pre_ref[...])
        da_ref[...] = dot(pre_ref[:, :cut], wa_ref[...], NT) + dot(pre_ref[:, cut:], wb_ref[...], NT)
        part = acc_ref.shape[0] // 16
        for flip, out_a, out_b in ((0, ka_ref, kb_ref), (1, sa_ref, sb_ref)):
            for z in range(4):
                at = pl.ds(pl.multiple_of((2 * z + (where_ref[2] ^ flip)) * 2 * part, 16), 2 * part)
                out_a[2 * z * part : (2 * z + 2) * part, :cut] = acc_ref[at, :cut].astype(bf16)
                for y in range(2):
                    row = (2 * z + y) * part
                    at = pl.ds(pl.multiple_of(2 * row + (where_ref[3] ^ flip) * part, 16), part)
                    out_b[row : row + part, : 3 * width - cut] = acc_ref[at, cut:].astype(bf16)
        for ref, out in zip(more_refs, (ka_ref, sa_ref, kb_ref, sb_ref)):
            out[:, out.shape[1] - ref.shape[1] :] = ref[...]


def qkv_backward(where, dq, dk, dv, own, half, other, weights, tables, vec, more=()):
    rows, width = dq.shape
    total = tables.shape[1]
    before = total // rows - 1
    cut = weights[0].shape[1]
    each = pl.BlockSpec((rows, width), lambda i: (i, 0))
    earlier = pl.BlockSpec((rows, D // 2), lambda i: (jnp.minimum(i, before - 1), 0))
    behind = (more[0].shape[1], more[2].shape[1]) if more else (0, 0)
    splits = [(D // 2, cut + behind[0])] * 2 + [(D // 2, 3 * width - cut + behind[1])] * 2
    return call(
        functools.partial(qkv_back_kernel, before, len(more)),
        "qkv_backward",
        (total // rows,),
        [SCALARS, whole(rows, width), each, each]
        + window_specs(rows, before)
        + [whole(*weights[0].shape), whole(*weights[1].shape)]
        + [pl.BlockSpec((3, rows, PAIR), lambda i: (0, i, 0)), whole(*vec.shape)]
        + [whole(*m.shape) for m in more],
        [whole(*shape) for shape in splits]
        + [whole(rows, D), earlier, earlier, whole(1, 3 * width), whole(8, D)],
        shaped(
            *[(shape, bf16) for shape in splits],
            ((rows, D), f32),
            ((total - rows, D // 2), bf16),
            ((total - rows, D // 2), bf16),
            ((1, 3 * width), f32),
            ((8, D), f32),
        ),
        [pltpu.VMEM((rows, 3 * width), bf16), pltpu.VMEM((D, 3 * width), f32)],
        room=18,
    )(where, dq, dk, dv, own, half, other, *weights, tables, vec, *more)


def low_lanes():
    return lax.broadcasted_iota(jnp.int32, (1, PAIR), 1) < HEAD


def both_heads(x):
    low = low_lanes()
    zero = jnp.zeros_like(x[:BLK])
    parts = []
    for at in range(0, x.shape[0], BLK):
        block = x[at : at + BLK]
        parts += [jnp.where(low, block, zero), jnp.where(low, zero, block)]
    return jnp.concatenate(parts, axis=0)


def both_columns(first, second):
    parts = []
    for at in range(0, first.shape[1], BLK):
        parts += [first[:, at : at + BLK], second[:, at : at + BLK]]
    return jnp.concatenate(parts, axis=1)


def key_loops(scal_ref, blocks, own, work):
    work(own + 1, slice(2 * BLK, 4 * BLK))
    low_all, low_first = scal_ref[1], scal_ref[2]

    def full(i, carry):
        work(own - i, slice(0, 4 * BLK))
        return carry

    def first_only(i, carry):
        work(low_all - 1 - i, slice(0, 2 * BLK))
        return carry

    lax.fori_loop(0, own - low_all + 1, full, 0)
    lax.fori_loop(0, low_all - low_first, first_only, 0)


def attend_kernel(scal_ref, q_ref, start_ref, k_ref, vt_ref, o_ref, lse_ref, q2_ref, m_ref, l_ref, acc_ref):
    rows, total = q_ref.shape[0], k_ref.shape[0]
    pairs = q_ref.shape[1] // PAIR
    base = scal_ref[0]
    m_ref[...] = jnp.full_like(m_ref, -1e30)
    l_ref[...] = jnp.zeros_like(l_ref)
    acc_ref[...] = jnp.zeros_like(acc_ref)
    for p in range(pairs):
        q2_ref[p] = both_heads(q_ref[:, p * PAIR : (p + 1) * PAIR])
    starts = both_columns(start_ref[0:1, :], start_ref[0:1, :])
    index = base + lax.broadcasted_iota(jnp.int32, (1, rows), 1)
    index = both_columns(index, index)

    def work(kb, cols):
        at = pl.ds(pl.multiple_of(kb * BLK, BLK), BLK)
        key_index = base - (total - rows) + kb * BLK + lax.broadcasted_iota(jnp.int32, (BLK, 1), 0)
        seen = (key_index >= starts[:, cols]) & (key_index <= index[:, cols])
        for p in range(pairs):
            lanes = slice(p * PAIR, (p + 1) * PAIR)
            s = jnp.where(seen, dot(k_ref[at, lanes], q2_ref[p, cols, :], NT), MASKED)
            m_old = m_ref[p, 0:1, cols]
            m_new = jnp.maximum(m_old, jnp.max(s, axis=0, keepdims=True))
            scale = jnp.exp(m_old - m_new)
            e = jnp.exp(s - m_new)
            m_ref[p, 0:1, cols] = m_new
            l_ref[p, 0:1, cols] = l_ref[p, 0:1, cols] * scale + jnp.sum(e, axis=0, keepdims=True)
            acc_ref[p, :, cols] = acc_ref[p, :, cols] * scale + dot(vt_ref[lanes, at], e.astype(bf16))

    key_loops(scal_ref, total // BLK, (total - rows) // BLK, work)
    for p in range(pairs):
        total_p = l_ref[p, 0:1, :]
        acc = acc_ref[p] / total_p
        lse_ref[p, 0:1, :] = m_ref[p, 0:1, :] + jnp.log(total_p)
        for qb in range(rows // BLK):
            first = acc[:HEAD, 2 * qb * BLK : (2 * qb + 1) * BLK]
            second = acc[HEAD:, (2 * qb + 1) * BLK : (2 * qb + 2) * BLK]
            o_ref[qb * BLK : (qb + 1) * BLK, p * PAIR : (p + 1) * PAIR] = jnp.transpose(
                jnp.concatenate([first, second], axis=0)
            ).astype(bf16)


def attend(scalars, q, start_rows, k, vt):
    rows, width = q.shape
    total = k.shape[0]
    pairs = width // PAIR
    return pl.pallas_call(
        attend_kernel,
        grid=(1,),
        in_specs=[
            pl.BlockSpec(memory_space=pltpu.SMEM),
            whole(rows, width),
            whole(8, rows),
            whole(total, width),
            whole(width, total),
        ],
        out_specs=[whole(rows, width), whole(pairs, 8, 2 * rows)],
        out_shape=[
            jax.ShapeDtypeStruct((rows, width), bf16),
            jax.ShapeDtypeStruct((pairs, 8, 2 * rows), f32),
        ],
        scratch_shapes=[
            pltpu.VMEM((pairs, 2 * rows, PAIR), bf16),
            pltpu.VMEM((pairs, 8, 2 * rows), f32),
            pltpu.VMEM((pairs, 8, 2 * rows), f32),
            pltpu.VMEM((pairs, PAIR, 2 * rows), f32),
        ],
        compiler_params=pltpu.CompilerParams(vmem_limit_bytes=ROOM_ATTEND << 20),
        cost_estimate=SMALL,
        name="attend",
    )(scalars, q, start_rows, k, vt)


def attend_back_kernel(
    scal_ref, q_ref, g_ref, o_ref, lse_ref, start_ref, k_ref, v_ref,
    dq_ref, dk_ref, dv_ref, q2_ref, g2_ref, delta_ref, acc_ref,
):
    rows, total = q_ref.shape[0], k_ref.shape[0]
    pairs = q_ref.shape[1] // PAIR
    base = scal_ref[0]
    dk_ref[...] = jnp.zeros_like(dk_ref)
    dv_ref[...] = jnp.zeros_like(dv_ref)
    acc_ref[...] = jnp.zeros_like(acc_ref)
    which = lax.broadcasted_iota(jnp.int32, (8, PAIR), 0)
    lane = lax.broadcasted_iota(jnp.int32, (8, PAIR), 1)
    chosen = (which == lane // HEAD).astype(f32)
    for p in range(pairs):
        lanes = slice(p * PAIR, (p + 1) * PAIR)
        g = g_ref[:, lanes]
        q2_ref[p] = both_heads(q_ref[:, lanes])
        g2_ref[p] = both_heads(g)
        delta = lax.dot_general(
            chosen,
            g.astype(f32) * o_ref[:, lanes].astype(f32),
            NT,
            precision=lax.Precision.HIGHEST,
            preferred_element_type=f32,
        )
        delta_ref[p, 0:1, :] = both_columns(delta[0:1, :], delta[1:2, :])
    starts = both_columns(start_ref[0:1, :], start_ref[0:1, :])
    index = base + lax.broadcasted_iota(jnp.int32, (1, rows), 1)
    index = both_columns(index, index)

    def work(kb, cols):
        at = pl.ds(pl.multiple_of(kb * BLK, BLK), BLK)
        key_index = base - (total - rows) + kb * BLK + lax.broadcasted_iota(jnp.int32, (BLK, 1), 0)
        seen = (key_index >= starts[:, cols]) & (key_index <= index[:, cols])
        for p in range(pairs):
            lanes = slice(p * PAIR, (p + 1) * PAIR)
            keys, q2, g2 = k_ref[at, lanes], q2_ref[p, cols, :], g2_ref[p, cols, :]
            s = jnp.where(seen, dot(keys, q2, NT), MASKED)
            prob = jnp.exp(s - lse_ref[p, 0:1, cols])
            d_prob = dot(v_ref[at, lanes], g2, NT)
            d_score = (prob * (d_prob - delta_ref[p, 0:1, cols])).astype(bf16)
            dv_ref[at, lanes] = dot(prob.astype(bf16), g2).astype(bf16)
            dk_ref[at, lanes] = dot(d_score, q2).astype(bf16)
            acc_ref[p, cols, :] += dot(d_score, keys, TN)

    key_loops(scal_ref, total // BLK, (total - rows) // BLK, work)
    low = low_lanes()
    for p in range(pairs):
        for qb in range(rows // BLK):
            first = acc_ref[p, 2 * qb * BLK : (2 * qb + 1) * BLK, :]
            second = acc_ref[p, (2 * qb + 1) * BLK : (2 * qb + 2) * BLK, :]
            dq_ref[qb * BLK : (qb + 1) * BLK, p * PAIR : (p + 1) * PAIR] = jnp.where(
                low, first, second
            ).astype(bf16)


def attend_back(scalars, q, g, o, lse, start_rows, k, v):
    rows, width = q.shape
    total = k.shape[0]
    pairs = width // PAIR
    return pl.pallas_call(
        attend_back_kernel,
        grid=(1,),
        in_specs=[
            pl.BlockSpec(memory_space=pltpu.SMEM),
            whole(rows, width),
            whole(rows, width),
            whole(rows, width),
            whole(pairs, 8, 2 * rows),
            whole(8, rows),
            whole(total, width),
            whole(total, width),
        ],
        out_specs=[whole(rows, width), whole(total, width), whole(total, width)],
        out_shape=[
            jax.ShapeDtypeStruct((rows, width), bf16),
            jax.ShapeDtypeStruct((total, width), bf16),
            jax.ShapeDtypeStruct((total, width), bf16),
        ],
        scratch_shapes=[
            pltpu.VMEM((pairs, 2 * rows, PAIR), bf16),
            pltpu.VMEM((pairs, 2 * rows, PAIR), bf16),
            pltpu.VMEM((pairs, 8, 2 * rows), f32),
            pltpu.VMEM((pairs, 2 * rows, PAIR), f32),
        ],
        compiler_params=pltpu.CompilerParams(vmem_limit_bytes=ROOM_ATTEND << 20),
        cost_estimate=SMALL,
        name="attend_back",
    )(scalars, q, g, o, lse, start_rows, k, v)


def ffn_kernel(
    where_ref, a_ref, up0_ref, up1_ref, dn0_ref, dn1_ref, outa_ref, outb_ref, vec_ref, mix_ref,
    hid_ref, slope_ref, out_ref, acc_ref,
):
    step = pl.program_id(0)
    over_a = outa_ref.shape[1]
    over_b = mix_ref.shape[1] - over_a
    hidden = pl.num_programs(0) * 2 * BLK

    @pl.when(step == 0)
    def _():
        acc_ref[...] = dot(mix_ref[:, :over_a], outa_ref[...], NT) + dot(
            mix_ref[:, over_a:], outb_ref[:, :over_b], NT
        )

    a = a_ref[...]
    total = acc_ref[...]
    for i, (up, down) in enumerate(((up0_ref, dn0_ref), (up1_ref, dn1_ref))):
        at = slice(i * BLK, (i + 1) * BLK)
        first = 9 * D + where_ref[0] * hidden + (2 * step + i) * BLK
        u = dot(a, up[...]) + vec_ref[:, pl.ds(pl.multiple_of(first, BLK), BLK)]
        phi = 0.5 * (1.0 + lax.erf(u * (1.0 / math.sqrt(2.0))))
        slope = phi + u * jnp.exp(-0.5 * u * u) * (1.0 / math.sqrt(2.0 * math.pi))
        slope_ref[:, at] = slope.astype(bf16)
        low = (u * phi).astype(bf16)
        hid_ref[:, at] = low
        total = total + dot(low, down[...], NT)
    acc_ref[...] = total

    @pl.when(step == pl.num_programs(0) - 1)
    def _():
        out_ref[...] = acc_ref[...].astype(bf16)


def ffn_weights(hidden, skip):
    steps = hidden // BLK
    return [
        pl.BlockSpec((D, BLK), lambda i: (0, 2 * i)),
        pl.BlockSpec((D, BLK), lambda i: (0, 2 * i + 1)),
        pl.BlockSpec((D, BLK), lambda i: (0, skip + 2 * i)),
        pl.BlockSpec((D, BLK), lambda i: (0, skip + 2 * i + 1)),
        pl.BlockSpec((D, BLK), lambda i: (0, 0 if skip else steps)),
        pl.BlockSpec((D, BLK), lambda i: (0, skip + steps)),
    ]


def ffn_forward(where, a, wa, wb, skip, vec, mixed, hidden):
    rows, width = a.shape[0], mixed.shape[1]
    wide = pl.BlockSpec((rows, 2 * BLK), lambda i: (0, i))
    return call(
        ffn_kernel,
        "ffn_forward",
        (hidden // (2 * BLK),),
        [SCALARS, whole(rows, D)]
        + ffn_weights(hidden, skip)
        + [whole(*vec.shape), whole(rows, width)],
        [wide, wide, whole(rows, D)],
        shaped(((rows, hidden), bf16), ((rows, hidden), bf16), ((rows, D), bf16)),
        [pltpu.VMEM((rows, D), f32)],
        room=12,
    )(where, a, wa, wa, wb, wb, wb if skip else wa, wb, vec, mixed)


def ffn_back_kernel(
    where_ref, g_ref, a_ref, up0_ref, up1_ref, dn0_ref, dn1_ref, outa_ref, outb_ref,
    slope_ref, hid_ref, mix_ref,
    ka_ref, sa_ref, kb_ref, sb_ref, da_ref, gmix_ref, sum_ref, ay_ref, gy_ref, gx_ref,
):
    step = pl.program_id(0)
    last = pl.num_programs(0) - 1
    over_a = outa_ref.shape[1]
    over_b = mix_ref.shape[1] - over_a
    half = ka_ref.shape[0]
    part = half // 8

    @pl.when(step == 0)
    def _():
        da_ref[...] = jnp.zeros_like(da_ref)
        for turned, split_y, split_x in (
            (jnp.transpose(a_ref[...]), ay_ref, None),
            (jnp.transpose(g_ref[...]), gy_ref, gx_ref),
        ):
            for z in range(4):
                for y in range(2):
                    row = (2 * z + y) * 2 * part
                    to = pl.multiple_of((where_ref[2] ^ y) * half + 2 * z * part, 16)
                    split_y[pl.ds(to, 2 * part), :] = turned[row : row + 2 * part]
                    for x in range(2) if split_x is not None else ():
                        to = pl.multiple_of((where_ref[3] ^ x) * half + (2 * z + y) * part, 16)
                        split_x[pl.ds(to, part), :] = turned[row + x * part : row + (x + 1) * part]

    @pl.when(step < last)
    def _():
        g = g_ref[...]
        total = da_ref[...]
        grad = dot(gx_ref[...], hid_ref[...]).astype(bf16)
        kb_ref[...], sb_ref[...] = grad[:half], grad[half:]
        for i, (up, down) in enumerate(((up0_ref, dn0_ref), (up1_ref, dn1_ref))):
            at = slice(i * BLK, (i + 1) * BLK)
            d_pre = (dot(g, down[...]) * slope_ref[:, at].astype(f32)).astype(bf16)
            sum_ref[:, at] = jnp.sum(d_pre.astype(f32), axis=0, keepdims=True)
            grad = dot(ay_ref[...], d_pre).astype(bf16)
            ka_ref[:, at], sa_ref[:, at] = grad[:half], grad[half:]
            total = total + dot(d_pre, up[...], NT)
        da_ref[...] = total

    @pl.when(step == last)
    def _():
        g = g_ref[...]
        gmix_ref[:, :over_a] = dot(g, outa_ref[...]).astype(bf16)
        gmix_ref[:, over_a:] = dot(g, outb_ref[:, :over_b]).astype(bf16)
        grad = dot(gy_ref[...], mix_ref[:, :over_a]).astype(bf16)
        ka_ref[:, :over_a], sa_ref[:, :over_a] = grad[:half], grad[half:]
        grad = dot(gx_ref[...], mix_ref[:, over_a:]).astype(bf16)
        kb_ref[:, :over_b], sb_ref[:, :over_b] = grad[:half], grad[half:]


def ffn_backward(where, g, a, wa, wb, skip, slope, hid, mixed):
    rows, width = mixed.shape
    hidden = hid.shape[1]
    steps = hidden // (2 * BLK)
    upto = lambda i: (0, jnp.minimum(i, steps - 1))
    weights = []
    for spec in ffn_weights(hidden, skip):
        weights.append(
            pl.BlockSpec(spec.block_shape, lambda i, f=spec.index_map: f(jnp.minimum(i, steps - 1)))
        )
    wide = pl.BlockSpec((rows, 2 * BLK), upto)
    split = pl.BlockSpec((D // 2, 2 * BLK), lambda i: (0, i))
    wide_a, wide_b = hidden + BLK, hidden + width - BLK
    return call(
        ffn_back_kernel,
        "ffn_backward",
        (steps + 1,),
        [SCALARS, whole(rows, D), whole(rows, D)] + weights + [wide, wide, whole(rows, width)],
        [split] * 4
        + [whole(rows, D), whole(rows, width), pl.BlockSpec((1, 2 * BLK), upto)],
        shaped(
            *[((D // 2, wide_a), bf16)] * 2,
            *[((D // 2, wide_b), bf16)] * 2,
            ((rows, D), f32),
            ((rows, width), bf16),
            ((1, hidden), f32),
        ),
        [pltpu.VMEM((D, rows), bf16)] * 3,
        room=18,
    )(where, g, a, wa, wa, wb, wb, wb if skip else wa, wb, slope, hid, mixed)


def with_half(where_ref, da_ref, back_refs):
    half = sum(ref[...].astype(f32) for ref in back_refs)
    zero = jnp.zeros_like(half)
    first = jnp.where(where_ref[0] == 0, half, zero)
    return da_ref[...] + jnp.concatenate([first, half - first], axis=1)


def joint_kernel(where_ref, vec_ref, da_ref, db_ref, *refs):
    *back_refs, out_ref = refs
    da = with_half(where_ref, da_ref, back_refs)
    out_ref[...] = (da * vec_ref[:, :D] + db_ref[...] * vec_ref[:, 2 * D : 3 * D]).astype(bf16)


def row_call(kernel, name, where, vec, rows_in, outs, steps=4):
    rows = rows_in[0].shape[0]
    block = lambda width: pl.BlockSpec((rows // steps, width), lambda i: (i, 0))
    return call(
        kernel,
        name,
        (steps,),
        [SCALARS, whole(*vec.shape)] + [block(m.shape[1]) for m in rows_in],
        [block(shape[1]) for shape, _ in outs],
        shaped(*outs),
    )(where, vec, *rows_in)


def next_kernel(where_ref, vec_ref, grad_ref, own_ref, got_ref, x_ref, out_ref, low_ref):
    unit, inverse = unit_rows(x_ref[...].astype(f32))
    joint = own_ref[...].astype(f32) + got_ref[...].astype(f32)
    centered = joint - jnp.mean(joint, axis=-1, keepdims=True)
    grad = grad_ref[...].astype(f32) + inverse * (
        centered - unit * jnp.mean(joint * unit, axis=-1, keepdims=True)
    )
    out_ref[...] = grad
    low_ref[...] = grad.astype(bf16)


def vector_kernel(where_ref, qkv_ref, up_ref, far_ref, grad_ref, x_ref, da_ref, db_ref, out_ref):
    core = where_ref[0]
    width, hidden = qkv_ref.shape[1] // 3, up_ref.shape[1]

    @pl.when(pl.program_id(0) == 0)
    def _():
        out_ref[...] = jnp.zeros_like(out_ref)
        for c in range(3):
            to = pl.multiple_of((6 + c) * D + core * width, PAIR)
            out_ref[:, pl.ds(to, width)] = qkv_ref[:, c * width : (c + 1) * width]
        out_ref[:, pl.ds(pl.multiple_of(9 * D + core * hidden, PAIR), hidden)] = up_ref[...]
        for i in range(2):
            out_ref[:, i * D : (i + 1) * D] = far_ref[i : i + 1, :]

    unit, _ = unit_rows(x_ref[...].astype(f32))
    da, db = da_ref[...], db_ref[...]
    first = (core == 0).astype(f32)
    bias = jnp.sum(grad_ref[...].astype(f32), axis=0, keepdims=True) * first
    for i, term in enumerate((da * unit, da, db * unit, db)):
        out_ref[:, i * D : (i + 1) * D] += jnp.sum(term, axis=0, keepdims=True)
    out_ref[:, 4 * D : 5 * D] += bias
    out_ref[:, 5 * D : 6 * D] += bias


def vector_row(where, qkv_sum, up_sum, far, grad, x, da, db):
    rows, steps = grad.shape[0], 4
    block = lambda width: pl.BlockSpec((rows // steps, width), lambda i: (i, 0))
    rows_in = [grad, x, da, db]
    size = 9 * D + FF
    return call(
        vector_kernel,
        "vector_row",
        (steps,),
        [SCALARS, whole(*qkv_sum.shape), whole(*up_sum.shape), whole(*far.shape)] + [block(m.shape[1]) for m in rows_in],
        [whole(1, size)],
        shaped(((1, size), f32)),
    )(where, qkv_sum, up_sum, far, *rows_in)[0]


def qkv_cuts(width):
    low = 3 * width // 256 * 128
    return low + 128, low


def settle_kernel(counts, where_ref, *refs):
    refs = list(refs)
    terms = [[refs.pop(0) for _ in range(n)] for n in counts]
    moms, refs = refs[:KINDS], refs[KINDS:]
    grads, refs = refs[:KINDS], refs[KINDS:]
    news, refs = refs[:KINDS], refs[KINDS:]
    *sends, pad_ref = refs
    layers, _, rows, width = moms[0].shape
    hidden = moms[2].shape[2]
    cuts = qkv_cuts(width)
    pad_ref[...] = jnp.zeros_like(pad_ref)

    def total(parts, at):
        return sum(part[:, at].astype(f32) for part in parts)

    for layer in range(layers):
        ahead, cut = sum(cuts[:layer]), cuts[layer]
        first = total(terms[2], slice(ahead, ahead + cut))
        ahead, rest = sum(cuts) + layer * 3 * width - ahead, 3 * width - cut
        second = total(terms[2], slice(ahead, ahead + rest))
        qkv = jnp.concatenate([first, second], axis=1)
        up = total(terms[layer], slice(0, hidden))
        out_a = total(terms[layer], slice(hidden, hidden + BLK))
        down = total(terms[layer], slice(hidden + BLK, 2 * hidden + BLK))
        out_b = total(terms[layer], slice(2 * hidden + BLK, 2 * hidden + width))
        out = jnp.concatenate([out_a, out_b], axis=1)
        for c in range(3):
            grad = qkv[:, c * width : (c + 1) * width]
            new = MOMENTUM * moms[0][layer, c] + grad
            grads[0][layer, c], news[0][layer, c] = grad, new
            pad_ref[layer, :, c * width : (c + 1) * width] = new.astype(bf16)
        for kind, grad in ((1, out), (2, up), (3, down)):
            new = MOMENTUM * moms[kind][layer] + grad
            grads[kind][layer], news[kind][layer] = grad, new
            pad_ref[layer, :, kind * hidden : kind * hidden + grad.shape[1]] = new.astype(bf16)
    for by, send in enumerate(sends):
        at = pl.ds(pl.multiple_of((where_ref[1] ^ by) * hidden, PAIR), hidden)
        for layer in range(layers):
            send[layer] = pad_ref[layer, :, at]


def settle(where, terms, moms):
    rows, hidden = moms[2].shape[1:]
    flat = [m for group in terms for m in group]
    send = (LAYERS, rows, hidden)
    outs = [(m.shape, f32) for m in moms] * 2 + [(send, bf16)] * KINDS
    got = call(
        functools.partial(settle_kernel, [len(group) for group in terms]),
        "settle",
        (1,),
        [SCALARS] + [whole(*m.shape) for m in flat] + [whole(*m.shape) for m in moms],
        [whole(*shape) for shape, _ in outs],
        shaped(*outs),
        [pltpu.VMEM((LAYERS, rows, KINDS * hidden), bf16)],
        room=12,
    )(where, *flat, *moms)
    return got[:KINDS], got[KINDS : 2 * KINDS], got[2 * KINDS :]


def update_kernel(where_ref, *refs):
    backs, swapped = refs[:KINDS], refs[KINDS]
    masters, outs = refs[KINDS + 1 : 2 * KINDS + 1], refs[2 * KINDS + 1 : 3 * KINDS + 1]
    kept_ref = refs[-1]
    layers, _, rows, width = masters[0].shape
    for slot in range(KINDS):
        kept_ref[slot] = backs[slot][0]
    for layer in range(layers):
        mine = where_ref[0] == layer
        for kind in range(KINDS):
            slot = where_ref[1] ^ kind
            made = jnp.where(mine, kept_ref[slot], swapped[slot]).astype(f32)
            made = made * (-RATE_MAT * math.sqrt((3 * D, D, FF, FF)[kind]))
            if kind == 0:
                for c in range(3):
                    step = made[:, c * width : (c + 1) * width]
                    outs[0][layer, c] = masters[0][layer, c] * SHRINK + step
            else:
                outs[kind][layer] = masters[kind][layer] * SHRINK + made[:, : outs[kind].shape[2]]


def update(where, backs, swapped, masters):
    return call(
        update_kernel,
        "update",
        (1,),
        [SCALARS] + [whole(*m.shape) for m in (*backs, swapped, *masters)],
        [whole(*m.shape) for m in masters],
        shaped(*[(m.shape, f32) for m in masters]),
        [pltpu.VMEM(swapped.shape, bf16)],
    )(where, *backs, swapped, *masters)


def orth_kernel(inner, *refs):
    ins, outs = refs[:2], refs[2 : 2 + KINDS]
    x_ref, gram_ref, mix_ref = refs[2 + KINDS :]
    rows, width = ins[0].shape
    part, chunk = 256, 512
    blocks = rows // part
    total = jnp.zeros((1, 1), f32)
    for ref in ins:
        for i in range(blocks):
            v = ref[i * part : (i + 1) * part, :].astype(f32)
            total = total + jnp.sum(v * v).reshape(1, 1)
    inverse = 1.0 / (jnp.sqrt(total) + 1e-07)
    for i, ref in enumerate(ins):
        x_ref[:, i * width : (i + 1) * width] = (ref[...].astype(f32) * inverse).astype(bf16)

    def spread(ref, i, j, value):
        low = value.astype(bf16)
        ref[i * part : (i + 1) * part, j * part : (j + 1) * part] = low
        if j > i:
            ref[j * part : (j + 1) * part, i * part : (i + 1) * part] = jnp.transpose(low)

    def mixer():
        for i in range(blocks):
            at = slice(i * part, (i + 1) * part)
            gram = dot(x_ref[at, :], x_ref[i * part :, :], NT)
            for j in range(i, blocks):
                spread(gram_ref, i, j, gram[:, (j - i) * part : (j - i + 1) * part])
        for i in range(blocks):
            at = slice(i * part, (i + 1) * part)
            square = dot(gram_ref[at, :], gram_ref[:, i * part :])
            mixed = NS_B * gram_ref[at, i * part :].astype(f32) + NS_C * square
            for j in range(i, blocks):
                spread(mix_ref, i, j, mixed[:, (j - i) * part : (j - i + 1) * part])

    def sweep(_, carry):
        mixer()
        for c in range(2 * width // chunk):
            cols = slice(c * chunk, (c + 1) * chunk)
            x = x_ref[:, cols]
            y = NS_A * x.astype(f32) + dot(mix_ref[...], x)
            x_ref[:, cols] = y.astype(bf16)
        return carry

    lax.fori_loop(0, 4, sweep, 0)
    mixer()
    size = outs[0].shape[1]
    firsts = [by * inner * size for by in range(KINDS)]
    mine = jnp.concatenate([mix_ref[first : first + size, :] for first in firsts], axis=0)
    for half in range(2):
        cols = slice(half * width, (half + 1) * width)
        made = dot(mine, x_ref[:, cols])
        for by, out in enumerate(outs):
            x = x_ref[firsts[by] : firsts[by] + size, cols].astype(f32)
            out[half] = (NS_A * x + made[by * size : (by + 1) * size]).astype(bf16)


def orthogonalize(parts, inner):
    rows, width = parts[0].shape
    shape = (2, rows // (KINDS * inner), width)
    return call(
        functools.partial(orth_kernel, inner),
        "orthogonalize",
        (1,),
        [whole(rows, width)] * 2,
        [whole(*shape)] * KINDS,
        shaped(*[(shape, bf16)] * KINDS),
        [
            pltpu.VMEM((rows, 2 * width), bf16),
            pltpu.VMEM((rows, rows), bf16),
            pltpu.VMEM((rows, rows), bf16),
        ],
        room=20,
    )(*parts)


def shards(
    tokens,
    cotangent,
    w_qkv,
    w_out,
    w_up,
    w_down,
    mom_qkv,
    mom_out,
    mom_up,
    mom_down,
    vectors,
    vec_first,
    vec_second,
    lengths,
):
    tok_rows = tokens.shape[0]
    row_part = w_qkv.shape[1]
    head_part = w_qkv.shape[-1]
    hidden_part = w_up.shape[-1]
    widths = (3 * head_part, head_part, hidden_part, hidden_part)
    over = BLK
    cut_qkv = qkv_cuts(head_part)
    cut_rest = hidden_part + over
    fsdp_count = lax.axis_size("fsdp")
    core = lax.axis_index("tp")
    longest = SEQ_DEV * fsdp_count
    span = (tok_rows + longest - 2) // tok_rows
    where = place()

    def stored(qkv, out, up, down):
        return [qkv.transpose(0, 2, 1, 3), out.transpose(0, 2, 1), up, down.transpose(0, 2, 1)]

    def unstored(qkv, out, up, down):
        return [qkv.transpose(0, 2, 1, 3), out.transpose(0, 2, 1), up, down.transpose(0, 2, 1)]

    def qkv_piece(mats, layer):
        low = mats[0][layer].astype(bf16)
        return jnp.concatenate([low[c] for c in range(3)], axis=1)

    def rest_piece(mats, layer):
        out, up, down = [m[layer].astype(bf16) for m in mats[1:]]
        return jnp.concatenate([up, out[:, :over], down, out[:, over:]], axis=1)

    masters = stored(w_qkv, w_out, w_up, w_down)
    moments = stored(mom_qkv, mom_out, mom_up, mom_down)

    qkv_0 = Task(gather_steps(where, qkv_piece(masters, 0), cut_qkv[0]))
    vecs = [vectors[layer : layer + 1] for layer in range(LAYERS)]
    a0, b0, half = norm_rows(where, vecs[0], tokens)
    rest, half, lengths, *later = advance(
        [qkv_0], rest_piece(masters, 0), half, lengths, *masters
    )
    rest_0 = Task(gather_steps(where, rest, cut_rest, True))
    half, lengths, *later = advance([qkv_0, rest_0], half, lengths, *later)
    win_0 = Task(window_steps(half, span))
    tables, start_rows, scalars = setup(lengths, where, tok_rows, (span + 1) * tok_rows)
    tables, start_rows, scalars, *later = advance(
        [qkv_0, rest_0, win_0], tables, start_rows, scalars, *later
    )
    qkv_1 = Task(gather_steps(where, qkv_piece(later, 1), cut_qkv[1], False, True))
    wq0 = qkv_0.result
    tables, *later = advance([win_0], tables, *later)
    q, k, v, vt = qkv_forward(where, a0, *win_0.result, wq0, vecs[0], tables)
    q, k, v, vt, *later = advance([rest_0, qkv_1], q, k, v, vt, *later)
    rest_1 = Task(gather_steps(where, rest_piece(later, 1), cut_rest, False, True))
    mixed, lse = attend(scalars, q, start_rows, k, vt)
    mixed, lse, b0 = advance([rest_0, rest_1], mixed, lse, b0)
    mixed, b0, wa, wb = advance([rest_1, qkv_1], mixed, b0, *rest_0.result)
    hid, slope, partial = ffn_forward(where, b0, wa, wb, 0, vecs[0], mixed, hidden_part)
    partial = advance([rest_1, qkv_1], partial)
    kept = [(tokens, a0, win_0.result, b0, q, k, v, mixed, lse, hid, slope)]
    weights = [(wq0, wa, wb, 0)]
    got = core_swap(partial)
    x1, a1, b1, half = norm_rows(where, vecs[1], tokens, vecs[0], partial, got)
    win_1 = Task(window_steps(half, span))
    a1, b1 = advance([win_1, qkv_1], a1, b1)
    a1, b1 = advance([win_1], a1, b1)
    wq1 = qkv_1.result
    q, k, v, vt = qkv_forward(where, a1, *win_1.result, wq1, vecs[1], tables)
    mixed, lse = attend(scalars, q, start_rows, k, vt)
    mixed, lse, b1, q, k, v = advance([rest_1], mixed, lse, b1, q, k, v)
    wa, wb = rest_1.result
    hid, slope, partial = ffn_forward(where, b1, wa, wb, 0, vecs[1], mixed, hidden_part)
    kept.append((x1, a1, win_1.result, b1, q, k, v, mixed, lse, hid, slope))
    weights.append((wq1, wa, wb, 0))

    def own_gradients(grad_low, layer):
        _, _, _, b, _, _, _, mixed, _, hid, slope = kept[layer]
        _, wa, wb, skip = weights[layer]
        return ffn_backward(where, grad_low, b, wa, wb, skip, slope, hid, mixed)

    def attention_gradients(g_mixed, layer, more=()):
        _, a, win, _, q, k, v, mixed, lse, _, _ = kept[layer]
        dq, dk, dv = attend_back(scalars, q, g_mixed, mixed, lse, start_rows, k, v)
        return qkv_backward(where, dq, dk, dv, a, *win, weights[layer][0], tables, vecs[layer], more)

    def joint_of(da, db, back, layer):
        rows_in = [da, db] + list(back)
        return row_call(joint_kernel, "joint", where, vecs[layer], rows_in, [(da.shape, bf16)])[0]

    def next_grad(grad, joint, got, layer):
        outs = [(joint.shape, f32), (joint.shape, bf16)]
        rows_in = [grad, joint, got, kept[layer][0]]
        return row_call(next_kernel, "next_grad", where, vecs[layer], rows_in, outs)

    *split, db1, g_mixed, up_sum1 = own_gradients(cotangent, 1)
    *split, g_mixed, partial, db1 = advance([], *split, g_mixed, partial, db1)
    rest_1 = Task(scatter_steps(where, *split, True))
    *split1, da1, keep, give, pre_sum1, far1 = attention_gradients(g_mixed, 1)
    *split1, da1, keep, give, partial = advance([], *split1, da1, keep, give, partial)
    back_1 = Task(window_back_steps(keep, give, span))
    da1, partial = advance([back_1, rest_1], da1, partial)
    da1, partial = advance([back_1, rest_1], da1, partial)
    joint = joint_of(da1, db1, back_1.result, 1)
    got = core_swap(joint)
    grad_x0, grad_low = next_grad(cotangent, joint, got, 1)
    *split, db0, g_mixed, up_sum0 = own_gradients(grad_low, 0)
    *split, g_mixed, da1, db0, partial = advance([rest_1], *split, g_mixed, da1, db0, partial)
    *split, g_mixed = advance([rest_1], *split, g_mixed)
    rest_0 = Task(scatter_steps(where, *split, False, True))
    *split, da0, keep, give, pre_sum0, far0 = attention_gradients(g_mixed, 0, split1)
    *split, da0, keep, give, da1, db1, partial = advance(
        [rest_0, rest_1], *split, da0, keep, give, da1, db1, partial
    )
    both_qkv = Task(scatter_steps(where, *split, True))
    back_0 = Task(window_back_steps(keep, give, span, True))
    row_0 = vector_row(where, pre_sum0, up_sum0, far0, grad_x0, kept[0][0], da0, db0)
    row_1 = vector_row(where, pre_sum1, up_sum1, far1, cotangent, kept[1][0], da1, db1)
    rows_both, partial = advance(
        [rest_0, both_qkv], jnp.concatenate([row_0, row_1], axis=0), partial
    )
    rows_both, partial = advance([both_qkv], rows_both, partial)
    vec_sum = Task(sum_steps(rows_both))
    partial = advance([both_qkv, rest_0, back_0, vec_sum], partial)
    partial = advance([both_qkv], partial)
    got = core_swap(partial)
    block_out = norm_rows(where, vecs[1], kept[1][0], vecs[1], partial, got, False)[0]
    block_out = advance([both_qkv, rest_0], block_out)
    terms = [rest_0.result, rest_1.result, both_qkv.result]
    grads, new_moms, blocks = settle(where, terms, moments)
    owned = Task(owner_steps(blocks[0], blocks[1:]))
    advance([owned, vec_sum])
    advance([owned])
    while owned.flying is not None:
        advance([owned, vec_sum])

    inner = fsdp_count // KINDS
    parts = advance([back_0], *owned.result)
    made = orthogonalize(parts, inner)
    *made, da0 = advance([back_0], *made, da0)
    backs = [made[0]] + [
        permute(made[by], xor_pairs(fsdp_count, by * inner)) for by in range(1, KINDS)
    ]
    joint = joint_of(da0, db0, back_0.result, 0)
    got = core_swap(joint)
    grad_in, _ = next_grad(grad_x0, joint, got, 0)
    grad_in = advance([vec_sum], grad_in)
    while vec_sum.flying is not None:
        grad_in = advance([vec_sum], grad_in)
    grad_vectors = vec_sum.result
    grad_in, grad_vectors, *backs = advance([], grad_in, grad_vectors, *backs)
    swapped = core_swap(jnp.stack([m[1] for m in backs]))
    new_weights = update(where, backs, swapped, masters)

    first_new = BETA_ONE * vec_first + (1.0 - BETA_ONE) * grad_vectors
    second_new = BETA_TWO * vec_second + (1.0 - BETA_TWO) * grad_vectors * grad_vectors
    first_hat = first_new / (1.0 - BETA_ONE**STEP)
    second_hat = second_new / (1.0 - BETA_TWO**STEP)
    vectors_new = vectors - RATE_VEC * first_hat / (jnp.sqrt(second_hat) + ADAM_EPS)
    return (
        block_out,
        grad_in,
        *unstored(*grads),
        *unstored(*new_moms),
        *unstored(*new_weights),
        first_new,
        second_new,
        vectors_new,
        grad_vectors[:, 9 * D :],
    )


def solution(mesh):
    weights = (
        P(None, "fsdp", None, "tp"),
        P(None, "tp", "fsdp"),
        P(None, "fsdp", "tp"),
        P(None, "tp", "fsdp"),
    )
    rows = (P("fsdp", None), P("fsdp", None))
    return jax.shard_map(
        shards,
        mesh=mesh,
        in_specs=rows + weights + weights + (P(), P(), P(), P()),
        out_specs=rows + weights + weights + weights + (P(), P(), P(), P()),
        check_vma=False,
    )
```
